32 devices in a mesh: grp: 2 (over x), lat: 16 (over z, y, core).
Axes of the slice: x: 2, y: 2, z: 4, core: 2. Of those that a mesh axis runs over, the one named last changes fastest.
Arguments:
- fields: bfloat16 [2, 32, 128, 384], P('grp', 'lat'), may hold values from -6 to 6
- cotangent: bfloat16 [2, 32, 128, 384], P('grp', 'lat'), may hold values from -6 to 6
- ocean_kernels: bfloat16 [2, 3, 3, 192, 192], replicated, may hold values from -0.15625 to 0.15625
- atmos_kernels: bfloat16 [2, 3, 3, 384, 384], replicated, may hold values from -0.109375 to 0.109375
- ocean_surface: bfloat16 [192, 4], replicated, may hold values from -0.4375 to 0.4375
- ocean_coupling: bfloat16 [4, 192], replicated, may hold values from -3 to 3
- atmos_flux: bfloat16 [384, 4], replicated, may hold values from -0.3125 to 0.3125
- atmos_coupling: bfloat16 [4, 384], replicated, may hold values from -3 to 3
- row_map: int32 [32], P('lat'), may hold values from 0 to 31, as said below
- wet_mask: int32 [32, 256], P('lat'), may hold values 0 or 1
Outputs:
- next_fields: bfloat16 [2, 32, 128, 384], P('grp', 'lat')
- field_grads: bfloat16 [2, 32, 128, 384], P('grp', 'lat')
- ocean_kernel_grad: float32 [663552], P(('grp', 'lat'))
- atmos_kernel_grad: float32 [2654208], P(('grp', 'lat'))
The draws below stay inside these ranges and needn't reach their ends.
Inputs may be any that keep to these rules, and one draw needn't show every extreme that they name: row_map never falls, keeps each ocean row in its own band of 2 rows, and maps the first and last row of every band to that band's first and last row.
All inputs are finite; a program needn't handle non-finite values. No bound on the sum of `wet_mask` on one device may be relied on, other than what follows from the above.
Results may differ from the reference program's by a relative error of at most 0.0065.
Values may be sent and summed in bfloat16 or wider, within the bound.
No kernel may reach another device: no remote copies, remote signals or barrier semaphores. Data moves between devices by JAX's collectives and lax.ppermute only.
A program may use at most 128 MiB of HBM per device.

```python
import math
import jax
import jax.numpy as jnp
from jax import lax

BAND = 2
LON = 128
COCEAN = 192
CATMOS = 384
NSURF = 4
ROWS = 32


def draw_row_map(key, part):
    key = jax.random.fold_in(key, 11)
    band_total = ROWS // BAND
    picks = jax.random.randint(key, (band_total, BAND), 0, BAND)
    picks = jnp.sort(picks, axis=1)
    picks = picks.at[:, 0].set(0).at[:, BAND - 1].set(BAND - 1)
    starts = (jnp.arange(band_total, dtype=jnp.int32) * BAND)[:, None]
    return (picks + starts).reshape(ROWS).astype(jnp.int32)


def touch_ends(entries, key, smallest, largest):
    longest = entries.shape.index(max(entries.shape))
    spots = []
    for shift in (0, 1):
        where = [jax.random.randint(jax.random.fold_in(key, axis), (), 0, length) for axis, length in enumerate(entries.shape)]
        where[longest] = (where[longest] + shift) % entries.shape[longest]
        spots.append(tuple(where))
    return entries.at[spots[0]].set(smallest).at[spots[1]].set(largest)


def block_levels(rng, dims, shards, smallest, top_value):
    level = 1.0
    for position, parts in shards:
        steps = jax.random.uniform(jax.random.fold_in(jax.random.fold_in(rng, 6), position), (parts,), jnp.float32, smallest / len(shards), top_value / len(shards))
        level = level * jnp.repeat(jnp.exp(steps), dims[position] // parts).reshape((-1,) + (1,) * (len(dims) - 1 - position))
    return level


def scatter_about(stream_key, dims, scale, reach, cuts=(), kind=jnp.bfloat16):
    entries = jax.random.normal(stream_key, dims, jnp.float32) * scale
    if len(cuts) > 0:
        entries = block_levels(stream_key, dims, cuts, -0.22, 0.18) * entries
    return jnp.clip(entries, min=-reach, max=reach).astype(kind)


def setup_inputs(seed: int = 0) -> dict:
    streams_of = jax.random.split(jax.random.key(seed), 11)
    return {
        "fields": scatter_about(streams_of[0], (2, ROWS, LON, CATMOS), 1.0, 6.0, ((0, 2), (1, 16))),
        "cotangent": scatter_about(streams_of[1], (2, ROWS, LON, CATMOS), 1.0, 6.0, ((0, 2), (1, 16))),
        "ocean_kernels": scatter_about(streams_of[2], (2, 3, 3, COCEAN, COCEAN), (9 * COCEAN) ** -0.5, 0.15625),
        "atmos_kernels": scatter_about(streams_of[3], (2, 3, 3, CATMOS, CATMOS), (9 * CATMOS) ** -0.5, 0.109375),
        "ocean_surface": scatter_about(streams_of[4], (COCEAN, NSURF), COCEAN ** -0.5, 0.4375),
        "ocean_coupling": scatter_about(streams_of[5], (NSURF, COCEAN), NSURF ** -0.5, 3.0),
        "atmos_flux": scatter_about(streams_of[6], (CATMOS, NSURF), CATMOS ** -0.5, 0.3125),
        "atmos_coupling": scatter_about(streams_of[7], (NSURF, CATMOS), NSURF ** -0.5, 3.0),
        "row_map": draw_row_map(jax.random.fold_in(streams_of[10], 71), 0),
        "wet_mask": touch_ends((jax.random.randint(streams_of[9], (ROWS, 2 * LON), 0, 4) < 3).astype(jnp.int32), jax.random.fold_in(streams_of[9], 1), 0, 1),
    }


HIGHEST = lax.Precision.HIGHEST
GELU_SCALE = 0.7978845608028654
GELU_CUBIC = 0.044715

def gelu_value(inputs):
    inside = GELU_SCALE * (inputs + GELU_CUBIC * inputs * inputs * inputs)
    return 0.5 * inputs * (1.0 + jnp.tanh(inside))

def gelu_slope(inputs):
    tangent = jnp.tanh(GELU_SCALE * (inputs + GELU_CUBIC * inputs * inputs * inputs))
    return 0.5 * (1.0 + tangent) + 0.5 * inputs * (1.0 - tangent * tangent) * GELU_SCALE * (1.0 + 3.0 * GELU_CUBIC * inputs * inputs)

def rank_terms(weights, matrix):
    total = weights[0][:, None] * matrix[0][None, :]
    for index in range(1, matrix.shape[0]):
        total = total + weights[index][:, None] * matrix[index][None, :]
    return total

def project_rows(values, matrix):
    return jnp.stack([lax.optimization_barrier(jnp.sum(values * matrix[index][None, :], axis=1)) for index in range(matrix.shape[0])])

def narrow_dot(values, matrix):
    return jnp.dot(values.astype(jnp.float32), matrix.astype(jnp.float32), precision=HIGHEST, preferred_element_type=jnp.float32)

def convolve(values, kernel):
    row_count, col_count, channels = values.shape
    padded = jnp.pad(values, ((1, 1), (1, 1), (0, 0)))
    total = jnp.zeros((row_count * col_count, kernel.shape[3]), jnp.float32)
    for row_tap in range(3):
        for col_tap in range(3):
            piece = padded[row_tap:row_tap + row_count, col_tap:col_tap + col_count].reshape(row_count * col_count, channels)
            total = total + jnp.dot(piece, kernel[row_tap, col_tap], preferred_element_type=jnp.float32)
    return total.reshape(row_count, col_count, kernel.shape[3])

def kernel_grad(values, outgrad, factor):
    row_count, col_count, channels = values.shape
    padded = jnp.pad(values, ((1, 1), (1, 1), (0, 0))).astype(jnp.float32)
    flat_grad = outgrad.reshape(row_count * col_count, -1).astype(jnp.float32)
    blocks = []
    for row_tap in range(3):
        for col_tap in range(3):
            piece = padded[row_tap:row_tap + row_count, col_tap:col_tap + col_count].reshape(row_count * col_count, channels)
            blocks.append(lax.dot_general(piece, flat_grad, (((0,), (0,)), ((), ())), precision=HIGHEST, preferred_element_type=jnp.float32))
    return jnp.stack(blocks).reshape(-1) * factor

def flip_kernel(kernel):
    return jnp.flip(kernel, (0, 1)).transpose(0, 1, 3, 2)

def component(values, outgrad, kernels, factor):
    first_out = convolve(values, kernels[0])
    hidden = gelu_value(first_out).astype(jnp.bfloat16)
    next_values = (values.astype(jnp.float32) + convolve(hidden, kernels[1])).astype(jnp.bfloat16)
    back_hidden = convolve(outgrad, flip_kernel(kernels[1]))
    first_grad = (back_hidden * gelu_slope(first_out)).astype(jnp.bfloat16)
    input_grad = outgrad.astype(jnp.float32) + convolve(first_grad, flip_kernel(kernels[0]))
    grads = jnp.concatenate([kernel_grad(values, first_grad, factor), kernel_grad(hidden, outgrad, factor)])
    return (next_values, input_grad, grads)

def reference(fields, cotangent, ocean_kernels, atmos_kernels, ocean_surface, ocean_coupling, atmos_flux, atmos_coupling, row_map, wet_mask):
    ocean_field = fields[0].reshape(ROWS, 2 * LON, COCEAN)
    atmos_field = fields[1]
    select = (row_map[None, :] == jnp.arange(ROWS, dtype=jnp.int32)[:, None]).astype(jnp.float32)
    wetness = wet_mask.astype(jnp.float32).reshape(ROWS, LON, 2)
    covered = jnp.einsum('ar,rlt->al', select, wetness, precision=HIGHEST)
    inverse = 1.0 / jnp.maximum(covered, 1.0)
    projected = narrow_dot(ocean_field.reshape(-1, COCEAN), ocean_surface).T
    summed = lax.optimization_barrier(jnp.sum(projected.reshape(NSURF, ROWS, LON, 2) * wetness[None], axis=3))
    surface = jnp.einsum('ar,frl->fal', select, summed, precision=HIGHEST) * inverse[None]
    flux_out = narrow_dot(atmos_field.reshape(-1, CATMOS), atmos_flux).T.reshape(NSURF, ROWS, LON)
    rows_flux = jnp.einsum('ar,fal->frl', select, flux_out, precision=HIGHEST)
    spread = (rows_flux[..., None] * wetness[None]).reshape(NSURF, -1)
    ocean_term = rank_terms(spread, ocean_coupling.astype(jnp.float32))
    ocean_in = (ocean_field.reshape(-1, COCEAN).astype(jnp.float32) + ocean_term).astype(jnp.bfloat16).reshape(ROWS, 2 * LON, COCEAN)
    atmos_term = rank_terms(surface.reshape(NSURF, -1), atmos_coupling.astype(jnp.float32))
    atmos_in = (atmos_field.reshape(-1, CATMOS).astype(jnp.float32) + atmos_term).astype(jnp.bfloat16).reshape(ROWS, LON, CATMOS)
    ocean_next, ocean_back, ocean_grads = component(ocean_in, cotangent[0].reshape(ROWS, 2 * LON, COCEAN), ocean_kernels, 1.0 / math.sqrt(ROWS * 2 * LON))
    atmos_next, atmos_back, atmos_grads = component(atmos_in, cotangent[1], atmos_kernels, 1.0 / math.sqrt(ROWS * LON))
    weighted = project_rows(ocean_back.reshape(-1, COCEAN), ocean_coupling.astype(jnp.float32))
    weighted_sum = lax.optimization_barrier(jnp.sum(weighted.reshape(NSURF, ROWS, LON, 2) * wetness[None], axis=3))
    flux_grad = jnp.einsum('ar,frl->fal', select, weighted_sum, precision=HIGHEST)
    surface_grad = project_rows(atmos_back.reshape(-1, CATMOS), atmos_coupling.astype(jnp.float32)).reshape(NSURF, ROWS, LON)
    rows_back = jnp.einsum('ar,fal->frl', select, surface_grad * inverse[None], precision=HIGHEST)
    spread_back = (rows_back[..., None] * wetness[None]).reshape(NSURF, -1)
    ocean_extra = rank_terms(spread_back, ocean_surface.astype(jnp.float32).T)
    ocean_grad = (ocean_back.reshape(-1, COCEAN) + ocean_extra).astype(jnp.bfloat16).reshape(ROWS, LON, CATMOS)
    atmos_extra = rank_terms(flux_grad.reshape(NSURF, -1), atmos_flux.astype(jnp.float32).T)
    atmos_grad = (atmos_back.reshape(-1, CATMOS) + atmos_extra).astype(jnp.bfloat16).reshape(ROWS, LON, CATMOS)
    next_fields = jnp.stack([ocean_next.reshape(ROWS, LON, CATMOS), atmos_next])
    field_grads = jnp.stack([ocean_grad, atmos_grad])
    return (next_fields, field_grads, ocean_grads, atmos_grads)
```

```python
import functools
import math

import jax
import jax.numpy as jnp
from jax import lax
from jax.experimental import pallas as pl
from jax.experimental.pallas import tpu as pltpu
from jax.sharding import PartitionSpec as P

HIGHEST = lax.Precision.HIGHEST
GELU_SCALE = 0.7978845608028654
GELU_CUBIC = 0.044715
F32 = jnp.float32
BF16 = jnp.bfloat16
WHOLE = pl.BlockSpec(memory_space=pltpu.VMEM)
IN_PLACE = pl.BlockSpec(memory_space=pl.ANY)
VMEM_LIMIT = 50 * 1024 * 1024

NN = (((1,), (0,)), ((), ()))
NT = (((1,), (1,)), ((), ()))
TN = (((0,), (0,)), ((), ()))


def shape(dims, kind):
    return jax.ShapeDtypeStruct(dims, kind)


def call(kernel, outs, inputs, in_specs=None, scratch=(), flops=0, moved=0, name=None):
    return pl.pallas_call(
        kernel,
        out_shape=outs,
        in_specs=in_specs or [WHOLE] * len(inputs),
        out_specs=jax.tree.map(lambda _: WHOLE, outs),
        scratch_shapes=list(scratch),
        compiler_params=pltpu.CompilerParams(vmem_limit_bytes=VMEM_LIMIT),
        cost_estimate=pl.CostEstimate(flops=flops, bytes_accessed=moved, transcendentals=0),
        name=name,
    )(*inputs)


def on_ocean():
    return lax.axis_index("grp") == 0


def dot(left, right, dims=NN, precision=None):
    return lax.dot_general(left, right, dims, precision=precision, preferred_element_type=F32)


def moved_cells(values, axis, cols):
    count = values.shape[axis]
    place = lax.rem(lax.broadcasted_iota(jnp.int32, values.shape, axis), cols)
    before = jnp.where(place == 0, 0.0, pltpu.roll(values, 1, axis))
    after = jnp.where(place == cols - 1, 0.0, pltpu.roll(values, count - 1, axis))
    return before, after


def pack_kernel(x_ref, g_ref, wet_ref, up_ref, down_ref, own_ref, *, cols):
    wet = wet_ref[...].astype(F32)
    source = lax.broadcasted_iota(jnp.int32, (2 * cols, 2 * cols), 0)
    target = lax.broadcasted_iota(jnp.int32, (2 * cols, 2 * cols), 1)
    wanted = 2 * lax.rem(target, cols) + jnp.where(target >= cols, 1, 0)
    chooser = (source == wanted).astype(F32).astype(BF16)
    padded = jnp.concatenate([wet, jnp.zeros((14, 2 * cols), F32)], axis=0)
    apart = dot(padded.astype(BF16), chooser)
    wide = jnp.concatenate([apart, jnp.zeros((16, x_ref.shape[2] - 2 * cols), F32)], axis=1)
    own_ref[...] = wide.astype(BF16)
    other = pltpu.roll(wide, 15, 0)
    up_ref[0:cols, :] = x_ref[1]
    up_ref[cols : 2 * cols, :] = g_ref[1]
    up_ref[2 * cols :, :] = other.astype(BF16)
    down_ref[0:cols, :] = x_ref[0]
    down_ref[cols : 2 * cols, :] = g_ref[0]
    down_ref[2 * cols :, :] = wide.astype(BF16)


def expand_kernel(raw_ref, out_ref):
    narrow = raw_ref.shape[2]

    @pl.when(on_ocean())
    def _():
        row = lax.broadcasted_iota(jnp.int32, (narrow, 2 * narrow), 0)
        col = lax.broadcasted_iota(jnp.int32, (narrow, 2 * narrow), 1)
        to_left = (row == col).astype(F32).astype(BF16)
        to_right = (row + narrow == col).astype(F32).astype(BF16)
        nothing = jnp.zeros((narrow, 2 * narrow), BF16)

        def step(index, carry):
            first, middle, last = (raw_ref[3 * index + tap] for tap in range(3))
            out_ref[3 * index, 0:narrow, :] = nothing
            out_ref[3 * index, narrow:, :] = dot(first, to_left).astype(BF16)
            even = dot(middle, to_left) + dot(first, to_right)
            odd = dot(last, to_left) + dot(middle, to_right)
            out_ref[3 * index + 1, 0:narrow, :] = even.astype(BF16)
            out_ref[3 * index + 1, narrow:, :] = odd.astype(BF16)
            out_ref[3 * index + 2, 0:narrow, :] = dot(last, to_right).astype(BF16)
            out_ref[3 * index + 2, narrow:, :] = nothing
            return carry

        lax.fori_loop(0, raw_ref.shape[0] // 3, step, 0)


def outgoing_kernel(
    x_ref, g_ref, low_ref, high_ref, own_ref, terms_ref,
    xpad_ref, gpad_ref, wet_ref, early_ref, sent_ref, *, cols,
):
    for pad_ref, own, start in ((xpad_ref, x_ref, 0), (gpad_ref, g_ref, cols)):
        pad_ref[0:cols, :] = low_ref[start : start + cols, :]
        pad_ref[cols : 2 * cols, :] = own[0]
        pad_ref[2 * cols : 3 * cols, :] = own[1]
        pad_ref[3 * cols : 4 * cols, :] = high_ref[start : start + cols, :]
    low_wet = low_ref[2 * cols :, :].astype(F32)
    high_wet = high_ref[2 * cols :, :].astype(F32)
    own_wet = own_ref[...].astype(F32)
    halves = []
    for start in (0, cols):
        lanes = slice(start, start + cols)
        rows = (low_wet[0:1, lanes], own_wet[0:1, lanes], own_wet[1:2, lanes], high_wet[0:1, lanes])
        halves.append(jnp.concatenate(rows, axis=1))
    first_wet, second_wet = halves
    inverse = 1.0 / jnp.maximum(first_wet + second_wet, 1.0)
    wet_ref[0:1, :] = first_wet
    wet_ref[1:2, :] = second_wet
    wet_ref[2:3, :] = inverse
    wet_ref[3:8, :] = jnp.zeros((5, 4 * cols), F32)
    xpad = xpad_ref[...]
    projected = dot(terms_ref[0:8, :].astype(BF16), xpad, NT)
    mixed = (projected[0:4] * first_wet + projected[4:8] * second_wet) * inverse
    sent_ref[...] = jnp.where(on_ocean(), mixed, projected[0:4])
    early_ref[...] = jnp.where(on_ocean(), gpad_ref[...], xpad)


def fetch(atmos_ref, ocean_ref, where, buffer, sem):
    @pl.when(on_ocean())
    def _():
        pltpu.make_async_copy(ocean_ref.at[where], buffer, sem).start()

    @pl.when(jnp.logical_not(on_ocean()))
    def _():
        pltpu.make_async_copy(atmos_ref.at[where], buffer, sem).start()

    return pltpu.make_async_copy(atmos_ref.at[where], buffer, sem)


def with_columns(pad, cols):
    before, after = moved_cells(pad.astype(F32), 0, cols)
    return before.astype(BF16), pad, after.astype(BF16)


def conv(pad, weight_ref, base, cols):
    taps = with_columns(pad, cols)
    joined = jnp.concatenate(taps, axis=1)
    rows = pad.shape[0] - 2 * cols
    channels = pad.shape[1]
    total = None
    for tap in range(3):
        kernel = weight_ref[base + 3 * tap : base + 3 * tap + 3].reshape(3 * channels, channels)
        part = dot(joined[cols * tap : cols * tap + rows], kernel)
        total = part if total is None else total + part
    return total


def conv_back(pad, weight_ref, base, cols):
    taps = with_columns(pad, cols)
    rows = pad.shape[0] - 2 * cols
    total = None
    for row_tap in range(3):
        for col_tap in range(3):
            kernel = weight_ref[base + 8 - (3 * row_tap + col_tap)]
            part = dot(taps[col_tap][cols * row_tap : cols * row_tap + rows], kernel, NT)
            total = part if total is None else total + part
    return total


def back_kernel(gpad_ref, atmos_ref, ocean_ref, out_ref, buffer, sem, *, cols):
    copy = fetch(atmos_ref, ocean_ref, pl.ds(9, 9), buffer, sem)
    copy.wait()
    out_ref[...] = conv_back(gpad_ref[...], buffer, 0, cols)


def spread(arrived, wet, mixing, terms):
    first_wet, second_wet = wet
    both = jnp.concatenate([arrived * first_wet, arrived * second_wet], axis=0)
    alone = jnp.concatenate([arrived, jnp.zeros_like(arrived)], axis=0)
    return dot(jnp.where(mixing, both, alone), terms, TN, HIGHEST)


def first_kernel(
    xpad_ref, wet_ref, arrived_ref, terms_ref, back_ref, atmos_ref, ocean_ref,
    u_ref, stay_ref, give_ref, up_ref, down_ref, buffer, sem, *, cols,
):
    copy = fetch(atmos_ref, ocean_ref, pl.ds(0, 9), buffer, sem)
    wet = wet_ref[0:1, :], wet_ref[1:2, :]
    coupled = spread(arrived_ref[...], wet, on_ocean(), terms_ref[8:16, :])
    u = (xpad_ref[...].astype(F32) + coupled).astype(BF16)
    u_ref[...] = u
    copy.wait()
    first = conv(u, buffer, 0, cols)
    tangent = jnp.tanh(GELU_SCALE * (first + GELU_CUBIC * first * first * first))
    hidden = (0.5 * first * (1.0 + tangent)).astype(BF16)
    slope = 0.5 * (1.0 + tangent) + 0.5 * first * (1.0 - tangent * tangent) * GELU_SCALE * (
        1.0 + 3.0 * GELU_CUBIC * first * first
    )
    first_grad = (back_ref[...] * slope).astype(BF16)
    stay_ref[...] = jnp.where(on_ocean(), first_grad, hidden)
    give_ref[...] = jnp.where(on_ocean(), hidden, first_grad)
    up_ref[0:cols, :] = hidden[cols:]
    up_ref[cols:, :] = first_grad[cols:]
    down_ref[0:cols, :] = hidden[:cols]
    down_ref[cols:, :] = first_grad[:cols]


def grad_atmos(pad, own, pad_is_input, cols, store):
    rows = own.shape[0]
    if pad_is_input:
        middle = pad.T
        before, after = moved_cells(middle, 1, cols)
        lefts = [part.astype(BF16) for part in (before, middle, after)]
        right = own.astype(BF16)
        for tap in range(9):
            start = cols * (tap // 3)
            store(tap, dot(lefts[tap % 3][:, start : start + rows], right))
    else:
        left = own.T.astype(BF16)
        before, after = moved_cells(pad, 0, cols)
        rights = [part.astype(BF16) for part in (after, pad, before)]
        for tap in range(9):
            start = cols * (2 - tap // 3)
            store(tap, dot(left, rights[tap % 3][start : start + rows]))


def grad_ocean(pad, own, pad_is_input, cols, store):
    rows, channels = own.shape
    narrow = channels // 2
    wide = -(-narrow // 128) * 128

    def apart(values):
        lane = lax.broadcasted_iota(jnp.int32, values.shape, 1)
        even = jnp.where(lane < narrow, values, 0.0)
        odd = jnp.where(lane < narrow, pltpu.roll(values, narrow, 1), 0.0)
        return even[:, :wide], odd[:, :wide]

    if pad_is_input:
        middle = pad.T
        before, after = moved_cells(middle, 1, cols)
        even, odd = middle[:narrow].astype(BF16), middle[narrow:].astype(BF16)
        pairs = (
            (before[narrow:].astype(BF16), even),
            (even, odd),
            (odd, after[:narrow].astype(BF16)),
        )
        right = jnp.concatenate(apart(own), axis=0).astype(BF16)
        for tap in range(9):
            start = cols * (tap // 3)
            pieces = [part[:, start : start + rows] for part in pairs[tap % 3]]
            store(tap, dot(jnp.concatenate(pieces, axis=1), right))
    else:
        turned = own.T.astype(BF16)
        left = jnp.concatenate([turned[:narrow], turned[narrow:]], axis=1)
        even, odd = apart(pad)
        odd_before = moved_cells(odd, 0, cols)[0].astype(BF16)
        even_after = moved_cells(even, 0, cols)[1].astype(BF16)
        even, odd = even.astype(BF16), odd.astype(BF16)
        pairs = ((odd, even_after), (even, odd), (odd_before, even))
        for tap in range(9):
            start = cols * (2 - tap // 3)
            pieces = [part[start : start + rows] for part in pairs[tap % 3]]
            store(tap, dot(left, jnp.concatenate(pieces, axis=0)))


def both_grads(
    early_ref, upad_ref, gpad_ref, stay_ref, late_ref, sent_ref, coupling_ref, atmos_out, ocean_out, cols
):
    channels = upad_ref.shape[1]
    narrow = channels // 2

    def store_atmos(tap, value):
        atmos_out[channels * tap : channels * (tap + 1), :] = value

    def store_ocean(tap, value):
        for piece in range(ocean_out.shape[0]):
            lanes = slice(128 * piece, 128 * (piece + 1))
            ocean_out[piece, narrow * tap : narrow * (tap + 1), :] = value[:, lanes]

    @pl.when(on_ocean())
    def _():
        added = dot(sent_ref[...], coupling_ref[...].astype(F32), TN, HIGHEST)
        other = (early_ref[...].astype(F32) + added).astype(BF16).astype(F32)
        grad_ocean(upad_ref[...].astype(F32), stay_ref[...].astype(F32), True, cols, store_ocean)
        grad_atmos(other, late_ref[...].astype(F32), True, cols, store_atmos)

    @pl.when(jnp.logical_not(on_ocean()))
    def _():
        grad_atmos(gpad_ref[...].astype(F32), stay_ref[...].astype(F32), False, cols, store_atmos)
        grad_ocean(early_ref[...].astype(F32), late_ref[...].astype(F32), False, cols, store_ocean)


def grads_kernel(*refs, cols, chunks):
    ins, (out_ref, atmos_all, ocean_all) = refs[:7], refs[7:]
    both_grads(*ins, atmos_all, ocean_all, cols)
    channels = out_ref.shape[2]
    pieces = ocean_all.shape[0]
    atmos_rows = atmos_all.shape[0] // chunks
    ocean_rows = atmos_rows // 4
    taken = out_ref.shape[1] - atmos_rows
    spare = ocean_all.shape[1] - ocean_rows * 2 * chunks
    if spare:
        ocean_all[:, ocean_rows * 2 * chunks :, :] = jnp.zeros((pieces, spare, 128), F32)
    for chunk in range(chunks):
        upper = atmos_all[atmos_rows * chunk : atmos_rows * (chunk + 1), :]
        start = 2 * ocean_rows * chunk
        blank = jnp.zeros((taken, channels - 128 * pieces), F32)
        even, odd = (
            jnp.concatenate([ocean_all.at[piece][pl.ds(start + odd, taken, 2), :] for piece in range(pieces)] + [blank], axis=1)
            for odd in range(2)
        )
        odd = pltpu.roll(odd, channels // 2, 1)
        out_ref[chunk] = jnp.concatenate([upper, even + odd], axis=0).astype(BF16)


def plain_grads_kernel(*refs, cols):
    both_grads(*refs, cols)


def finish_kernel(total_ref, atmos_ref, ocean_ref, *, atmos_factor, ocean_factor):
    channels = total_ref.shape[1]
    pieces = channels // 128
    atmos_rows = atmos_ref.shape[0] // pieces
    ocean_rows = ocean_ref.shape[0] // pieces
    total = total_ref[...].astype(F32)
    for piece in range(pieces):
        lanes = slice(128 * piece, 128 * (piece + 1))
        atmos_ref[pl.ds(piece, atmos_rows, pieces), :] = total[:atmos_rows, lanes] * atmos_factor
        ocean_ref[pl.ds(piece, ocean_rows, pieces), :] = (
            total[atmos_rows : atmos_rows + ocean_rows, lanes] * ocean_factor
        )


def next_kernel(
    stay_ref, give_ref, low_ref, high_ref, upad_ref, gpad_ref, wet_ref, terms_ref, atmos_ref, ocean_ref,
    next_ref, grad_ref, sent_ref, buffer, sem, *, cols,
):
    copy = fetch(atmos_ref, ocean_ref, pl.ds(0, 18), buffer, sem)
    hidden = jnp.where(on_ocean(), give_ref[...], stay_ref[...])
    first_grad = jnp.where(on_ocean(), stay_ref[...], give_ref[...])
    hidden_pad = jnp.concatenate([low_ref[0:cols, :], hidden, high_ref[0:cols, :]], axis=0)
    first_pad = jnp.concatenate([low_ref[cols:, :], first_grad, high_ref[cols:, :]], axis=0)
    own = slice(cols, 3 * cols)
    copy.wait()
    grad = gpad_ref[own, :].astype(F32) + conv_back(first_pad, buffer, 0, cols)
    grad_ref[...] = grad
    weighted = dot(terms_ref[8:16, :], grad, NT, HIGHEST)
    mixed = weighted[0:4] * wet_ref[0:1, own] + weighted[4:8] * wet_ref[1:2, own]
    sent_ref[...] = jnp.where(on_ocean(), mixed, weighted[0:4])
    second = conv(hidden_pad, buffer, 9, cols)
    values = (upad_ref[own, :].astype(F32) + second).astype(BF16)
    next_ref[0] = values[:cols]
    next_ref[1] = values[cols:]


def last_kernel(grad_ref, arrived_ref, wet_ref, terms_ref, out_ref, *, cols):
    own = slice(cols, 3 * cols)
    wet = wet_ref[0:1, own], wet_ref[1:2, own]
    arrived = jnp.where(on_ocean(), arrived_ref[...] * wet_ref[2:3, own], arrived_ref[...])
    added = spread(arrived, wet, on_ocean(), terms_ref[0:8, :])
    values = (grad_ref[...] + added).astype(BF16)
    out_ref[0] = values[:cols]
    out_ref[1] = values[cols:]


def swapped(value, axis, mask):
    pairs = [(source, source ^ mask) for source in range(lax.axis_size(axis))]
    return lax.ppermute(value, axis, pairs)


def halo(up, down):
    count = lax.axis_size("lat")
    forward = [(i, i + 1) for i in range(count - 1)]
    backward = [(target, source) for source, target in forward]
    return lax.ppermute(up, "lat", forward), lax.ppermute(down, "lat", backward)


def local(
    fields,
    cotangent,
    ocean_kernels,
    atmos_kernels,
    ocean_surface,
    ocean_coupling,
    atmos_flux,
    atmos_coupling,
    row_map,
    wet_mask,
):
    x, g = fields[0], cotangent[0]
    bands, cols, channels = x.shape
    narrow = channels // 2
    cells = bands * cols
    count = lax.axis_size("lat")
    is_ocean = lax.axis_index("grp") == 0
    atmos_factor = 1.0 / math.sqrt(bands * count * cols)
    ocean_factor = 1.0 / math.sqrt(bands * count * 2 * cols)
    bound = functools.partial

    blank = jnp.zeros((4, narrow), BF16)
    gap = jnp.zeros((4, channels), BF16)
    surface = ocean_surface.T
    ocean_terms = jnp.concatenate(
        [
            jnp.concatenate([surface, blank], axis=1),
            jnp.concatenate([blank, surface], axis=1),
            jnp.concatenate([ocean_coupling, blank], axis=1),
            jnp.concatenate([blank, ocean_coupling], axis=1),
        ],
        axis=0,
    )
    atmos_terms = jnp.concatenate([atmos_flux.T, gap, atmos_coupling, gap], axis=0)
    terms = jnp.where(is_ocean, ocean_terms, atmos_terms).astype(F32)

    edge = shape((2 * cols + 16, channels), BF16)
    up, down, own_wet = call(
        bound(pack_kernel, cols=cols), [edge, edge, shape((16, channels), BF16)], [x, g, wet_mask], name="pack"
    )
    low, high = halo(up, down)
    atmos_flat = atmos_kernels.reshape(18, channels, channels)
    ocean_flat = call(
        expand_kernel,
        shape((18, channels, channels), BF16),
        [ocean_kernels.reshape(18, narrow, narrow)],
        flops=2 * 36 * narrow * narrow * channels,
        moved=18 * channels * channels * 2,
        name="expand",
    )
    pad = shape((2 * cells, channels), BF16)
    xpad, gpad, wet, early, sent = call(
        bound(outgoing_kernel, cols=cols),
        [pad, pad, shape((8, 2 * cells), F32), pad, shape((4, 2 * cells), F32)],
        [x, g, low, high, own_wet, terms],
        name="outgoing",
    )
    arrived = swapped(sent, "grp", 1)
    other_early = swapped(early, "grp", 1)
    one_conv = 2 * 9 * cells * channels * channels
    weight_bytes = 9 * channels * channels * 2
    buffer = [pltpu.VMEM((9, channels, channels), BF16), pltpu.SemaphoreType.DMA]
    back = call(
        bound(back_kernel, cols=cols),
        shape((cells, channels), F32),
        [gpad, atmos_flat, ocean_flat],
        [WHOLE, IN_PLACE, IN_PLACE],
        buffer,
        flops=one_conv,
        moved=weight_bytes,
        name="back",
    )
    half = shape((cells, channels), BF16)
    upad, stay, give, up, down = call(
        bound(first_kernel, cols=cols),
        [pad, half, half, half, half],
        [xpad, wet, arrived, terms, back, atmos_flat, ocean_flat],
        [WHOLE] * 5 + [IN_PLACE] * 2,
        buffer,
        flops=one_conv,
        moved=weight_bytes,
        name="first",
    )
    late = swapped(give, "grp", 1)

    atmos_rows = 9 * channels // count
    ocean_rows = 9 * narrow // count
    inputs = [other_early, upad, gpad, stay, late, sent, atmos_coupling]
    wide = -(-narrow // 128) * 128
    if 9 * channels % (8 * count) == 0 and ocean_rows % 2 == 0:
        tall = -(-(atmos_rows + ocean_rows // 2) // 16) * 16
        taken = tall - atmos_rows
        spare = max(0, 2 * taken - ocean_rows)
        parts = call(
            bound(grads_kernel, cols=cols, chunks=count),
            shape((count, tall, channels), BF16),
            inputs,
            None,
            [
                pltpu.VMEM((9 * channels, channels), F32),
                pltpu.VMEM((wide // 128, 9 * narrow + -(-spare // 8) * 8, 128), F32),
            ],
            flops=2 * one_conv,
            moved=count * tall * channels * 2,
            name="grads",
        )
        total = lax.psum_scatter(parts, "lat", scatter_dimension=0, tiled=True)[0]
        atmos_chunk, ocean_chunk = call(
            bound(finish_kernel, atmos_factor=atmos_factor, ocean_factor=ocean_factor),
            [
                shape((atmos_rows * channels // 128, 128), F32),
                shape((ocean_rows * narrow // 128, 128), F32),
            ],
            [total],
            name="finish",
        )
        atmos_total, ocean_total = atmos_chunk.reshape(-1), ocean_chunk.reshape(-1)
    else:
        atmos_all, ocean_all = call(
            bound(plain_grads_kernel, cols=cols),
            [shape((9 * channels, channels), F32), shape((wide // 128, 9 * narrow, 128), F32)],
            inputs,
            flops=2 * one_conv,
            name="grads",
        )
        atmos_total = atmos_factor * lax.psum_scatter(
            atmos_all.reshape(-1), "lat", scatter_dimension=0, tiled=True
        )
        ocean_all = jnp.concatenate([ocean_all[piece] for piece in range(wide // 128)], axis=1)
        ocean_total = ocean_factor * lax.psum_scatter(
            ocean_all[:, :narrow].reshape(-1), "lat", scatter_dimension=0, tiled=True
        )

    low, high = halo(up, down)
    next_field, grad, sent_back = call(
        bound(next_kernel, cols=cols),
        [shape(x.shape, BF16), shape((cells, channels), F32), shape((4, cells), F32)],
        [stay, give, low, high, upad, gpad, wet, terms, atmos_flat, ocean_flat],
        [WHOLE] * 8 + [IN_PLACE] * 2,
        [pltpu.VMEM((18, channels, channels), BF16), pltpu.SemaphoreType.DMA],
        flops=2 * one_conv,
        moved=2 * weight_bytes,
        name="next",
    )
    returned = swapped(sent_back, "grp", 1)
    field_grad = call(
        bound(last_kernel, cols=cols), shape(x.shape, BF16), [grad, returned, wet, terms], name="last"
    )
    return (next_field[None], field_grad[None], ocean_total, atmos_total)


def solution(mesh):
    in_specs = (
        P("grp", "lat", None, None),
        P("grp", "lat", None, None),
        P(),
        P(),
        P(),
        P(),
        P(),
        P(),
        P("lat"),
        P("lat", None),
    )
    out_specs = (
        P("grp", "lat", None, None),
        P("grp", "lat", None, None),
        P(("grp", "lat")),
        P(("grp", "lat")),
    )
    return jax.shard_map(local, mesh=mesh, in_specs=in_specs, out_specs=out_specs, check_vma=False)
```

```python
import functools
import math

import jax
import jax.numpy as jnp
from jax import lax
from jax.experimental import pallas as pl
from jax.experimental.pallas import tpu as pltpu
from jax.sharding import PartitionSpec as P

HIGHEST = lax.Precision.HIGHEST
GELU_SCALE = 0.7978845608028654
GELU_CUBIC = 0.044715
F32 = jnp.float32
BF16 = jnp.bfloat16
WHOLE = pl.BlockSpec(memory_space=pltpu.VMEM)
IN_PLACE = pl.BlockSpec(memory_space=pl.ANY)
VMEM_LIMIT = 50 * 1024 * 1024

NN = (((1,), (0,)), ((), ()))
NT = (((1,), (1,)), ((), ()))
TN = (((0,), (0,)), ((), ()))


def shape(dims, kind):
    return jax.ShapeDtypeStruct(dims, kind)


def call(kernel, outs, inputs, in_specs=None, scratch=(), flops=0, moved=0, name=None):
    return pl.pallas_call(
        kernel,
        out_shape=outs,
        in_specs=in_specs or [WHOLE] * len(inputs),
        out_specs=jax.tree.map(lambda _: WHOLE, outs),
        scratch_shapes=list(scratch),
        compiler_params=pltpu.CompilerParams(vmem_limit_bytes=VMEM_LIMIT),
        cost_estimate=pl.CostEstimate(flops=flops, bytes_accessed=moved, transcendentals=0),
        name=name,
    )(*inputs)


def on_ocean():
    return lax.axis_index("grp") == 0


def dot(left, right, dims=NN, precision=None):
    return lax.dot_general(left, right, dims, precision=precision, preferred_element_type=F32)


def moved_cells(values, axis, cols):
    count = values.shape[axis]
    place = lax.rem(lax.broadcasted_iota(jnp.int32, values.shape, axis), cols)
    before = jnp.where(place == 0, 0.0, pltpu.roll(values, 1, axis))
    after = jnp.where(place == cols - 1, 0.0, pltpu.roll(values, count - 1, axis))
    return before, after


def pack_kernel(x_ref, g_ref, wet_ref, up_ref, down_ref, own_ref, *, cols):
    wet = wet_ref[...].astype(F32)
    source = lax.broadcasted_iota(jnp.int32, (2 * cols, 2 * cols), 0)
    target = lax.broadcasted_iota(jnp.int32, (2 * cols, 2 * cols), 1)
    wanted = 2 * lax.rem(target, cols) + jnp.where(target >= cols, 1, 0)
    chooser = (source == wanted).astype(F32).astype(BF16)
    padded = jnp.concatenate([wet, jnp.zeros((14, 2 * cols), F32)], axis=0)
    apart = dot(padded.astype(BF16), chooser)
    wide = jnp.concatenate([apart, jnp.zeros((16, x_ref.shape[2] - 2 * cols), F32)], axis=1)
    own_ref[...] = wide.astype(BF16)
    other = pltpu.roll(wide, 15, 0)
    up_ref[0:cols, :] = x_ref[1]
    up_ref[cols : 2 * cols, :] = g_ref[1]
    up_ref[2 * cols :, :] = other.astype(BF16)
    down_ref[0:cols, :] = x_ref[0]
    down_ref[cols : 2 * cols, :] = g_ref[0]
    down_ref[2 * cols :, :] = wide.astype(BF16)


def expand_kernel(raw_ref, out_ref):
    narrow = raw_ref.shape[2]

    @pl.when(on_ocean())
    def _():
        row = lax.broadcasted_iota(jnp.int32, (narrow, 2 * narrow), 0)
        col = lax.broadcasted_iota(jnp.int32, (narrow, 2 * narrow), 1)
        to_left = (row == col).astype(F32).astype(BF16)
        to_right = (row + narrow == col).astype(F32).astype(BF16)
        nothing = jnp.zeros((narrow, 2 * narrow), BF16)

        def step(index, carry):
            first, middle, last = (raw_ref[3 * index + tap] for tap in range(3))
            out_ref[3 * index, 0:narrow, :] = nothing
            out_ref[3 * index, narrow:, :] = dot(first, to_left).astype(BF16)
            even = dot(middle, to_left) + dot(first, to_right)
            odd = dot(last, to_left) + dot(middle, to_right)
            out_ref[3 * index + 1, 0:narrow, :] = even.astype(BF16)
            out_ref[3 * index + 1, narrow:, :] = odd.astype(BF16)
            out_ref[3 * index + 2, 0:narrow, :] = dot(last, to_right).astype(BF16)
            out_ref[3 * index + 2, narrow:, :] = nothing
            return carry

        lax.fori_loop(0, raw_ref.shape[0] // 3, step, 0)


def outgoing_kernel(
    x_ref, g_ref, low_ref, high_ref, own_ref, terms_ref,
    xpad_ref, gpad_ref, wet_ref, early_ref, sent_ref, *, cols,
):
    for pad_ref, own, start in ((xpad_ref, x_ref, 0), (gpad_ref, g_ref, cols)):
        pad_ref[0:cols, :] = low_ref[start : start + cols, :]
        pad_ref[cols : 2 * cols, :] = own[0]
        pad_ref[2 * cols : 3 * cols, :] = own[1]
        pad_ref[3 * cols : 4 * cols, :] = high_ref[start : start + cols, :]
    low_wet = low_ref[2 * cols :, :].astype(F32)
    high_wet = high_ref[2 * cols :, :].astype(F32)
    own_wet = own_ref[...].astype(F32)
    halves = []
    for start in (0, cols):
        lanes = slice(start, start + cols)
        rows = (low_wet[0:1, lanes], own_wet[0:1, lanes], own_wet[1:2, lanes], high_wet[0:1, lanes])
        halves.append(jnp.concatenate(rows, axis=1))
    first_wet, second_wet = halves
    inverse = 1.0 / jnp.maximum(first_wet + second_wet, 1.0)
    wet_ref[0:1, :] = first_wet
    wet_ref[1:2, :] = second_wet
    wet_ref[2:3, :] = inverse
    wet_ref[3:8, :] = jnp.zeros((5, 4 * cols), F32)
    xpad = xpad_ref[...]
    projected = dot(terms_ref[0:8, :].astype(BF16), xpad, NT)
    mixed = (projected[0:4] * first_wet + projected[4:8] * second_wet) * inverse
    sent_ref[...] = jnp.where(on_ocean(), mixed, projected[0:4])
    early_ref[...] = jnp.where(on_ocean(), gpad_ref[...], xpad)


def fetch(atmos_ref, ocean_ref, where, buffer, sem):
    @pl.when(on_ocean())
    def _():
        pltpu.make_async_copy(ocean_ref.at[where], buffer, sem).start()

    @pl.when(jnp.logical_not(on_ocean()))
    def _():
        pltpu.make_async_copy(atmos_ref.at[where], buffer, sem).start()

    return pltpu.make_async_copy(atmos_ref.at[where], buffer, sem)


def with_columns(pad, cols):
    before, after = moved_cells(pad.astype(F32), 0, cols)
    return before.astype(BF16), pad, after.astype(BF16)


def conv(pad, weight_ref, base, cols):
    taps = with_columns(pad, cols)
    joined = jnp.concatenate(taps, axis=1)
    rows = pad.shape[0] - 2 * cols
    channels = pad.shape[1]
    total = None
    for tap in range(3):
        kernel = weight_ref[base + 3 * tap : base + 3 * tap + 3].reshape(3 * channels, channels)
        part = dot(joined[cols * tap : cols * tap + rows], kernel)
        total = part if total is None else total + part
    return total


def conv_back(pad, weight_ref, base, cols):
    taps = with_columns(pad, cols)
    rows = pad.shape[0] - 2 * cols
    total = None
    for row_tap in range(3):
        for col_tap in range(3):
            kernel = weight_ref[base + 8 - (3 * row_tap + col_tap)]
            part = dot(taps[col_tap][cols * row_tap : cols * row_tap + rows], kernel, NT)
            total = part if total is None else total + part
    return total


def back_kernel(gpad_ref, atmos_ref, ocean_ref, out_ref, buffer, sem, *, cols):
    copy = fetch(atmos_ref, ocean_ref, pl.ds(9, 9), buffer, sem)
    copy.wait()
    out_ref[...] = conv_back(gpad_ref[...], buffer, 0, cols)


def spread(arrived, wet, mixing, terms):
    first_wet, second_wet = wet
    both = jnp.concatenate([arrived * first_wet, arrived * second_wet], axis=0)
    alone = jnp.concatenate([arrived, jnp.zeros_like(arrived)], axis=0)
    return dot(jnp.where(mixing, both, alone), terms, TN, HIGHEST)


def first_kernel(
    xpad_ref, wet_ref, arrived_ref, terms_ref, back_ref, atmos_ref, ocean_ref,
    u_ref, stay_ref, give_ref, up_ref, down_ref, buffer, sem, *, cols,
):
    copy = fetch(atmos_ref, ocean_ref, pl.ds(0, 9), buffer, sem)
    wet = wet_ref[0:1, :], wet_ref[1:2, :]
    coupled = spread(arrived_ref[...], wet, on_ocean(), terms_ref[8:16, :])
    u = (xpad_ref[...].astype(F32) + coupled).astype(BF16)
    u_ref[...] = u
    copy.wait()
    first = conv(u, buffer, 0, cols)
    tangent = jnp.tanh(GELU_SCALE * (first + GELU_CUBIC * first * first * first))
    hidden = (0.5 * first * (1.0 + tangent)).astype(BF16)
    slope = 0.5 * (1.0 + tangent) + 0.5 * first * (1.0 - tangent * tangent) * GELU_SCALE * (
        1.0 + 3.0 * GELU_CUBIC * first * first
    )
    first_grad = (back_ref[...] * slope).astype(BF16)
    stay_ref[...] = jnp.where(on_ocean(), first_grad, hidden)
    give_ref[...] = jnp.where(on_ocean(), hidden, first_grad)
    up_ref[0:cols, :] = hidden[cols:]
    up_ref[cols:, :] = first_grad[cols:]
    down_ref[0:cols, :] = hidden[:cols]
    down_ref[cols:, :] = first_grad[:cols]


def grad_atmos(pad, own, pad_is_input, cols, store):
    rows = own.shape[0]
    if pad_is_input:
        middle = pad.T
        before, after = moved_cells(middle, 1, cols)
        lefts = [part.astype(BF16) for part in (before, middle, after)]
        right = own.astype(BF16)
        for tap in range(9):
            start = cols * (tap // 3)
            store(tap, dot(lefts[tap % 3][:, start : start + rows], right))
    else:
        left = own.T.astype(BF16)
        before, after = moved_cells(pad, 0, cols)
        rights = [part.astype(BF16) for part in (after, pad, before)]
        for tap in range(9):
            start = cols * (2 - tap // 3)
            store(tap, dot(left, rights[tap % 3][start : start + rows]))


def grad_ocean(pad, own, pad_is_input, cols, store):
    rows, channels = own.shape
    narrow = channels // 2
    wide = -(-narrow // 128) * 128

    def apart(values):
        lane = lax.broadcasted_iota(jnp.int32, values.shape, 1)
        even = jnp.where(lane < narrow, values, 0.0)
        odd = jnp.where(lane < narrow, pltpu.roll(values, narrow, 1), 0.0)
        return even[:, :wide], odd[:, :wide]

    if pad_is_input:
        middle = pad.T
        before, after = moved_cells(middle, 1, cols)
        even, odd = middle[:narrow].astype(BF16), middle[narrow:].astype(BF16)
        pairs = (
            (before[narrow:].astype(BF16), even),
            (even, odd),
            (odd, after[:narrow].astype(BF16)),
        )
        right = jnp.concatenate(apart(own), axis=0).astype(BF16)
        for tap in range(9):
            start = cols * (tap // 3)
            pieces = [part[:, start : start + rows] for part in pairs[tap % 3]]
            store(tap, dot(jnp.concatenate(pieces, axis=1), right))
    else:
        turned = own.T.astype(BF16)
        left = jnp.concatenate([turned[:narrow], turned[narrow:]], axis=1)
        even, odd = apart(pad)
        odd_before = moved_cells(odd, 0, cols)[0].astype(BF16)
        even_after = moved_cells(even, 0, cols)[1].astype(BF16)
        even, odd = even.astype(BF16), odd.astype(BF16)
        pairs = ((odd, even_after), (even, odd), (odd_before, even))
        for tap in range(9):
            start = cols * (2 - tap // 3)
            pieces = [part[start : start + rows] for part in pairs[tap % 3]]
            store(tap, dot(left, jnp.concatenate(pieces, axis=0)))


def both_grads(
    early_ref, upad_ref, gpad_ref, stay_ref, late_ref, sent_ref, coupling_ref, atmos_out, ocean_out, cols
):
    channels = upad_ref.shape[1]
    narrow = channels // 2

    def store_atmos(tap, value):
        atmos_out[channels * tap : channels * (tap + 1), :] = value

    def store_ocean(tap, value):
        for piece in range(ocean_out.shape[0]):
            lanes = slice(128 * piece, 128 * (piece + 1))
            ocean_out[piece, narrow * tap : narrow * (tap + 1), :] = value[:, lanes]

    @pl.when(on_ocean())
    def _():
        added = dot(sent_ref[...], coupling_ref[...].astype(F32), TN, HIGHEST)
        other = (early_ref[...].astype(F32) + added).astype(BF16).astype(F32)
        grad_ocean(upad_ref[...].astype(F32), stay_ref[...].astype(F32), True, cols, store_ocean)
        grad_atmos(other, late_ref[...].astype(F32), True, cols, store_atmos)

    @pl.when(jnp.logical_not(on_ocean()))
    def _():
        grad_atmos(gpad_ref[...].astype(F32), stay_ref[...].astype(F32), False, cols, store_atmos)
        grad_ocean(early_ref[...].astype(F32), late_ref[...].astype(F32), False, cols, store_ocean)


def grads_kernel(*refs, cols, chunks):
    ins, (keep_ref, send_ref, atmos_all, ocean_all) = refs[:7], refs[7:]
    both_grads(*ins, atmos_all, ocean_all, cols)
    channels = keep_ref.shape[2]
    pieces = ocean_all.shape[0]
    atmos_rows = atmos_all.shape[0] // chunks
    ocean_rows = atmos_rows // 2
    taken = keep_ref.shape[1] - atmos_rows
    spare = ocean_all.shape[1] - ocean_rows * chunks
    if spare:
        ocean_all[:, ocean_rows * chunks :, :] = jnp.zeros((pieces, spare, 128), F32)
    core = lax.rem(lax.axis_index("lat"), 2)
    blank = jnp.zeros((taken, channels - 128 * pieces), F32)
    for out_ref, side in ((send_ref, 1 - core), (keep_ref, core)):
        for pair in range(chunks // 2):
            start = pl.multiple_of(atmos_rows * (2 * pair + side), 8)
            upper = atmos_all[pl.ds(start, atmos_rows), :]
            start = ocean_rows * (2 * pair + side)
            halves = []
            for odd in range(2):
                parts = [ocean_all.at[piece][pl.ds(start + odd, taken, 2), :] for piece in range(pieces)]
                halves.append(jnp.concatenate(parts + [blank], axis=1))
            lower = halves[0] + pltpu.roll(halves[1], channels // 2, 1)
            out_ref[pair] = jnp.concatenate([upper, lower], axis=0).astype(BF16)


def own_bit(bit):
    return lax.rem(lax.shift_right_logical(lax.axis_index("lat"), bit), 2)


def halve(keep_ref, came_ref, keep_out, send_out, bit, rows):
    own = own_bit(bit)
    for out_ref, side in ((send_out, 1 - own), (keep_out, own)):
        for outer in range(keep_ref.shape[0]):
            for inner in range(keep_ref.shape[2]):
                total = keep_ref[outer, side, inner, rows, :].astype(F32)
                total = total + came_ref[outer, side, inner, rows, :].astype(F32)
                out_ref[outer, inner] = total.astype(BF16)


def split_kernel(keep_ref, came_ref, first_keep, first_send, second_keep, second_send, *, cut):
    tall = keep_ref.shape[3]
    halve(keep_ref, came_ref, first_keep, first_send, 1, slice(0, cut))
    views = [ref.reshape(2, 2, 2, *keep_ref.shape[3:]) for ref in (keep_ref, came_ref)]
    halve(*views, second_keep, second_send, 2, slice(cut, tall))


def halve_kernel(keep_ref, came_ref, keep_out, send_out, *, bit):
    halve(keep_ref, came_ref, keep_out, send_out, bit, slice(None))


def halved(keep, came, bit, dims):
    outer, inner, rows, channels = dims[0], dims[1], keep.shape[-2], keep.shape[-1]
    keep, came = (part.reshape(outer, 2, inner, rows, channels) for part in (keep, came))
    out = shape((outer, inner, rows, channels), BF16)
    return call(
        functools.partial(halve_kernel, bit=bit),
        [out, out],
        [keep, came],
        moved=8 * outer * inner * rows * channels,
        name="halve",
    )


def scatter_sum(keep, send):
    pairs, tall, channels = keep.shape
    came = swapped(send, "lat", 1)
    cut = -(-tall // 32) * 16
    first, second = shape((4, 1, cut, channels), BF16), shape((2, 2, tall - cut, channels), BF16)
    keep, came = (part.reshape(4, 2, 1, tall, channels) for part in (keep, came))
    first_keep, first_send, second_keep, second_send = call(
        functools.partial(split_kernel, cut=cut),
        [first, first, second, second],
        [keep, came],
        moved=6 * pairs * tall * channels,
        name="split",
    )
    first_came = swapped(first_send, "lat", 2)
    second_came = swapped(second_send, "lat", 4)
    first_keep, first_send = halved(first_keep, first_came, 2, (2, 1))
    first_came = swapped(first_send, "lat", 4)
    second_keep, second_send = halved(second_keep, second_came, 3, (1, 2))
    second_came = swapped(second_send, "lat", 8)
    first_keep, first_send = halved(first_keep, first_came, 3, (1, 1))
    first_came = swapped(first_send, "lat", 8)
    second_keep, second_send = halved(second_keep, second_came, 1, (1, 1))
    second_came = swapped(second_send, "lat", 2)
    return [part.reshape(-1, channels) for part in (first_keep, first_came, second_keep, second_came)]


def plain_grads_kernel(*refs, cols):
    both_grads(*refs, cols)


def finish_kernel(
    first_ref, first_came, second_ref, second_came, atmos_ref, ocean_ref, *, atmos_factor, ocean_factor
):
    channels = first_ref.shape[1]
    pieces = channels // 128
    atmos_rows = atmos_ref.shape[0] // pieces
    ocean_rows = ocean_ref.shape[0] // pieces
    first = first_ref[...].astype(F32) + first_came[...].astype(F32)
    second = second_ref[...].astype(F32) + second_came[...].astype(F32)
    total = jnp.concatenate([first, second], axis=0)
    for piece in range(pieces):
        lanes = slice(128 * piece, 128 * (piece + 1))
        atmos_ref[pl.ds(piece, atmos_rows, pieces), :] = total[:atmos_rows, lanes] * atmos_factor
        ocean_ref[pl.ds(piece, ocean_rows, pieces), :] = (
            total[atmos_rows : atmos_rows + ocean_rows, lanes] * ocean_factor
        )


def next_kernel(
    stay_ref, give_ref, low_ref, high_ref, upad_ref, gpad_ref, wet_ref, terms_ref, atmos_ref, ocean_ref,
    next_ref, grad_ref, sent_ref, buffer, sem, *, cols,
):
    copy = fetch(atmos_ref, ocean_ref, pl.ds(0, 18), buffer, sem)
    hidden = jnp.where(on_ocean(), give_ref[...], stay_ref[...])
    first_grad = jnp.where(on_ocean(), stay_ref[...], give_ref[...])
    hidden_pad = jnp.concatenate([low_ref[0:cols, :], hidden, high_ref[0:cols, :]], axis=0)
    first_pad = jnp.concatenate([low_ref[cols:, :], first_grad, high_ref[cols:, :]], axis=0)
    own = slice(cols, 3 * cols)
    copy.wait()
    grad = gpad_ref[own, :].astype(F32) + conv_back(first_pad, buffer, 0, cols)
    grad_ref[...] = grad
    weighted = dot(terms_ref[8:16, :], grad, NT, HIGHEST)
    mixed = weighted[0:4] * wet_ref[0:1, own] + weighted[4:8] * wet_ref[1:2, own]
    sent_ref[...] = jnp.where(on_ocean(), mixed, weighted[0:4])
    second = conv(hidden_pad, buffer, 9, cols)
    values = (upad_ref[own, :].astype(F32) + second).astype(BF16)
    next_ref[0] = values[:cols]
    next_ref[1] = values[cols:]


def last_kernel(grad_ref, arrived_ref, wet_ref, terms_ref, out_ref, *, cols):
    own = slice(cols, 3 * cols)
    wet = wet_ref[0:1, own], wet_ref[1:2, own]
    arrived = jnp.where(on_ocean(), arrived_ref[...] * wet_ref[2:3, own], arrived_ref[...])
    added = spread(arrived, wet, on_ocean(), terms_ref[0:8, :])
    values = (grad_ref[...] + added).astype(BF16)
    out_ref[0] = values[:cols]
    out_ref[1] = values[cols:]


def swapped(value, axis, mask):
    pairs = [(source, source ^ mask) for source in range(lax.axis_size(axis))]
    return lax.ppermute(value, axis, pairs)


def halo(up, down):
    count = lax.axis_size("lat")
    forward = [(i, i + 1) for i in range(count - 1)]
    backward = [(target, source) for source, target in forward]
    return lax.ppermute(up, "lat", forward), lax.ppermute(down, "lat", backward)


def local(
    fields,
    cotangent,
    ocean_kernels,
    atmos_kernels,
    ocean_surface,
    ocean_coupling,
    atmos_flux,
    atmos_coupling,
    row_map,
    wet_mask,
):
    x, g = fields[0], cotangent[0]
    bands, cols, channels = x.shape
    narrow = channels // 2
    cells = bands * cols
    count = lax.axis_size("lat")
    is_ocean = lax.axis_index("grp") == 0
    atmos_factor = 1.0 / math.sqrt(bands * count * cols)
    ocean_factor = 1.0 / math.sqrt(bands * count * 2 * cols)
    bound = functools.partial

    blank = jnp.zeros((4, narrow), BF16)
    gap = jnp.zeros((4, channels), BF16)
    surface = ocean_surface.T
    ocean_terms = jnp.concatenate(
        [
            jnp.concatenate([surface, blank], axis=1),
            jnp.concatenate([blank, surface], axis=1),
            jnp.concatenate([ocean_coupling, blank], axis=1),
            jnp.concatenate([blank, ocean_coupling], axis=1),
        ],
        axis=0,
    )
    atmos_terms = jnp.concatenate([atmos_flux.T, gap, atmos_coupling, gap], axis=0)
    terms = jnp.where(is_ocean, ocean_terms, atmos_terms).astype(F32)

    edge = shape((2 * cols + 16, channels), BF16)
    up, down, own_wet = call(
        bound(pack_kernel, cols=cols), [edge, edge, shape((16, channels), BF16)], [x, g, wet_mask], name="pack"
    )
    low, high = halo(up, down)
    atmos_flat = atmos_kernels.reshape(18, channels, channels)
    ocean_flat = call(
        expand_kernel,
        shape((18, channels, channels), BF16),
        [ocean_kernels.reshape(18, narrow, narrow)],
        flops=2 * 36 * narrow * narrow * channels,
        moved=18 * channels * channels * 2,
        name="expand",
    )
    pad = shape((2 * cells, channels), BF16)
    xpad, gpad, wet, early, sent = call(
        bound(outgoing_kernel, cols=cols),
        [pad, pad, shape((8, 2 * cells), F32), pad, shape((4, 2 * cells), F32)],
        [x, g, low, high, own_wet, terms],
        name="outgoing",
    )
    arrived = swapped(sent, "grp", 1)
    other_early = swapped(early, "grp", 1)
    one_conv = 2 * 9 * cells * channels * channels
    weight_bytes = 9 * channels * channels * 2
    buffer = [pltpu.VMEM((9, channels, channels), BF16), pltpu.SemaphoreType.DMA]
    back = call(
        bound(back_kernel, cols=cols),
        shape((cells, channels), F32),
        [gpad, atmos_flat, ocean_flat],
        [WHOLE, IN_PLACE, IN_PLACE],
        buffer,
        flops=one_conv,
        moved=weight_bytes,
        name="back",
    )
    half = shape((cells, channels), BF16)
    upad, stay, give, up, down = call(
        bound(first_kernel, cols=cols),
        [pad, half, half, half, half],
        [xpad, wet, arrived, terms, back, atmos_flat, ocean_flat],
        [WHOLE] * 5 + [IN_PLACE] * 2,
        buffer,
        flops=one_conv,
        moved=weight_bytes,
        name="first",
    )
    late = swapped(give, "grp", 1)

    atmos_rows = 9 * channels // count
    ocean_rows = 9 * narrow // count
    inputs = [other_early, upad, gpad, stay, late, sent, atmos_coupling]
    wide = -(-narrow // 128) * 128
    if count == 16 and 9 * channels % (8 * count) == 0 and ocean_rows % 2 == 0:
        tall = -(-(atmos_rows + ocean_rows // 2) // 16) * 16
        taken = tall - atmos_rows
        spare = max(0, 2 * taken - ocean_rows)
        part = shape((count // 2, tall, channels), BF16)
        keep, send = call(
            bound(grads_kernel, cols=cols, chunks=count),
            [part, part],
            inputs,
            None,
            [
                pltpu.VMEM((9 * channels, channels), F32),
                pltpu.VMEM((wide // 128, 9 * narrow + -(-spare // 8) * 8, 128), F32),
            ],
            flops=2 * one_conv,
            moved=count * tall * channels * 2,
            name="grads",
        )
        atmos_chunk, ocean_chunk = call(
            bound(finish_kernel, atmos_factor=atmos_factor, ocean_factor=ocean_factor),
            [
                shape((atmos_rows * channels // 128, 128), F32),
                shape((ocean_rows * narrow // 128, 128), F32),
            ],
            scatter_sum(keep, send),
            name="finish",
        )
        atmos_total, ocean_total = atmos_chunk.reshape(-1), ocean_chunk.reshape(-1)
    else:
        atmos_all, ocean_all = call(
            bound(plain_grads_kernel, cols=cols),
            [shape((9 * channels, channels), F32), shape((wide // 128, 9 * narrow, 128), F32)],
            inputs,
            flops=2 * one_conv,
            name="grads",
        )
        atmos_total = atmos_factor * lax.psum_scatter(
            atmos_all.reshape(-1), "lat", scatter_dimension=0, tiled=True
        )
        ocean_all = jnp.concatenate([ocean_all[piece] for piece in range(wide // 128)], axis=1)
        ocean_total = ocean_factor * lax.psum_scatter(
            ocean_all[:, :narrow].reshape(-1), "lat", scatter_dimension=0, tiled=True
        )

    low, high = halo(up, down)
    next_field, grad, sent_back = call(
        bound(next_kernel, cols=cols),
        [shape(x.shape, BF16), shape((cells, channels), F32), shape((4, cells), F32)],
        [stay, give, low, high, upad, gpad, wet, terms, atmos_flat, ocean_flat],
        [WHOLE] * 8 + [IN_PLACE] * 2,
        [pltpu.VMEM((18, channels, channels), BF16), pltpu.SemaphoreType.DMA],
        flops=2 * one_conv,
        moved=2 * weight_bytes,
        name="next",
    )
    returned = swapped(sent_back, "grp", 1)
    field_grad = call(
        bound(last_kernel, cols=cols), shape(x.shape, BF16), [grad, returned, wet, terms], name="last"
    )
    return (next_field[None], field_grad[None], ocean_total, atmos_total)


def solution(mesh):
    in_specs = (
        P("grp", "lat", None, None),
        P("grp", "lat", None, None),
        P(),
        P(),
        P(),
        P(),
        P(),
        P(),
        P("lat"),
        P("lat", None),
    )
    out_specs = (
        P("grp", "lat", None, None),
        P("grp", "lat", None, None),
        P(("grp", "lat")),
        P(("grp", "lat")),
    )
    return jax.shard_map(local, mesh=mesh, in_specs=in_specs, out_specs=out_specs, check_vma=False)
```

```python
import functools
import math

import jax
import jax.numpy as jnp
from jax import lax
from jax.experimental import pallas as pl
from jax.experimental.pallas import tpu as pltpu
from jax.sharding import PartitionSpec as P

HIGHEST = lax.Precision.HIGHEST
GELU_SCALE = 0.7978845608028654
GELU_CUBIC = 0.044715
F32 = jnp.float32
BF16 = jnp.bfloat16
WHOLE = pl.BlockSpec(memory_space=pltpu.VMEM)
IN_PLACE = pl.BlockSpec(memory_space=pltpu.HBM)
ANYWHERE = pl.BlockSpec(memory_space=pl.ANY)
VMEM_LIMIT = 32 * 1024 * 1024
MOST_VMEM = 52 * 1024 * 1024
PACE = 8
PACK_VMEM = 62 * 1024 * 1024

NN = (((1,), (0,)), ((), ()))
NT = (((1,), (1,)), ((), ()))
TN = (((0,), (0,)), ((), ()))


def shape(dims, kind):
    return jax.ShapeDtypeStruct(dims, kind)


def call(kernel, outs, inputs, in_specs=None, scratch=(), flops=0, moved=0, name=None, limit=VMEM_LIMIT, out_spec=WHOLE):
    return pl.pallas_call(
        kernel,
        out_shape=outs,
        in_specs=in_specs or [WHOLE] * len(inputs),
        out_specs=jax.tree.map(lambda _: out_spec, outs),
        scratch_shapes=list(scratch),
        compiler_params=pltpu.CompilerParams(vmem_limit_bytes=limit),
        cost_estimate=pl.CostEstimate(flops=flops, bytes_accessed=moved, transcendentals=0),
        name=name,
    )(*inputs)


def on_ocean():
    return lax.axis_index("grp") == 0


def dot(left, right, dims=NN, precision=None):
    return lax.dot_general(left, right, dims, precision=precision, preferred_element_type=F32)


def moved_cells(values, axis, cols):
    count = values.shape[axis]
    place = lax.rem(lax.broadcasted_iota(jnp.int32, values.shape, axis), cols)
    before = jnp.where(place == 0, 0.0, pltpu.roll(values, 1, axis))
    after = jnp.where(place == cols - 1, 0.0, pltpu.roll(values, count - 1, axis))
    return before, after


def wet_halves(wet, cols, channels):
    source = lax.broadcasted_iota(jnp.int32, (2 * cols, 2 * cols), 0)
    target = lax.broadcasted_iota(jnp.int32, (2 * cols, 2 * cols), 1)
    wanted = 2 * lax.rem(target, cols) + jnp.where(target >= cols, 1, 0)
    chooser = (source == wanted).astype(F32).astype(BF16)
    padded = jnp.concatenate([wet.astype(F32), jnp.zeros((14, 2 * cols), F32)], axis=0)
    apart = dot(padded.astype(BF16), chooser)
    return jnp.concatenate([apart, jnp.zeros((16, channels - 2 * cols), F32)], axis=1)


def pack_kernel(x_any, g_any, wet_any, up_any, down_any, wet_ref, edge_ref, wet_sem, sems, *, cols):
    fetch = pltpu.make_async_copy(wet_any, wet_ref, wet_sem)
    fetch.start()
    copies = []
    for row, out_any in ((1, up_any), (0, down_any)):
        for part, source in enumerate((x_any, g_any)):
            target = out_any.at[pl.ds(part * cols, cols), :]
            copies.append(pltpu.make_async_copy(source.at[row], target, sems.at[row, part]))
            copies[-1].start()
    fetch.wait()
    wide = wet_halves(wet_ref[...], cols, edge_ref.shape[2])
    edge_ref[0] = wide.astype(BF16)
    edge_ref[1] = pltpu.roll(wide, 15, 0).astype(BF16)
    for row, out_any in ((1, up_any), (0, down_any)):
        target = out_any.at[pl.ds(2 * cols, 16), :]
        copies.append(pltpu.make_async_copy(edge_ref.at[row], target, sems.at[row, 2]))
        copies[-1].start()
    for copy in copies:
        copy.wait()


def hold_kernel(x_any, g_any, wet_any, x_ref, g_ref, own_ref, wet_ref, sems, *, cols):
    pairs = ((wet_any, wet_ref), (x_any, x_ref), (g_any, g_ref))
    copies = [pltpu.make_async_copy(*pair, sems.at[index]) for index, pair in enumerate(pairs)]
    for copy in copies:
        copy.start()
    copies[0].wait()
    own_ref[...] = wet_halves(wet_ref[...], cols, own_ref.shape[1]).astype(BF16)
    copies[1].wait()
    copies[2].wait()


def outgoing_kernel(
    x_ref, g_ref, low_ref, high_ref, own_ref, terms_ref,
    xpad_ref, gpad_ref, wet_ref, early_ref, sent_ref, *, cols,
):
    for pad_ref, own, start in ((xpad_ref, x_ref, 0), (gpad_ref, g_ref, cols)):
        pad_ref[0:cols, :] = low_ref[start : start + cols, :]
        pad_ref[cols : 2 * cols, :] = own[0]
        pad_ref[2 * cols : 3 * cols, :] = own[1]
        pad_ref[3 * cols : 4 * cols, :] = high_ref[start : start + cols, :]
    low_wet = low_ref[2 * cols :, :].astype(F32)
    high_wet = high_ref[2 * cols :, :].astype(F32)
    own_wet = own_ref[...].astype(F32)
    halves = []
    for start in (0, cols):
        lanes = slice(start, start + cols)
        rows = (low_wet[0:1, lanes], own_wet[0:1, lanes], own_wet[1:2, lanes], high_wet[0:1, lanes])
        halves.append(jnp.concatenate(rows, axis=1))
    first_wet, second_wet = halves
    inverse = 1.0 / jnp.maximum(first_wet + second_wet, 1.0)
    wet_ref[0:1, :] = first_wet
    wet_ref[1:2, :] = second_wet
    wet_ref[2:3, :] = inverse
    wet_ref[3:8, :] = jnp.zeros((5, 4 * cols), F32)
    xpad = xpad_ref[...]
    projected = dot(terms_ref[0:8, :].astype(BF16), xpad, NT)
    mixed = (projected[0:4] * first_wet + projected[4:8] * second_wet) * inverse
    sent_ref[...] = jnp.where(on_ocean(), mixed, projected[0:4])
    early_ref[...] = jnp.where(on_ocean(), gpad_ref[...], xpad)


def halves_apart(values, narrow):
    wide = -(-narrow // 128) * 128
    lane = lax.broadcasted_iota(jnp.int32, values.shape, 1)
    even = jnp.where(lane < narrow, values, 0.0)
    odd = jnp.where(lane < narrow, pltpu.roll(values, narrow, 1), 0.0)
    return even[:, :wide], odd[:, :wide]


def halves_with_columns(pad, cols):
    even, odd = halves_apart(pad.astype(F32), pad.shape[1] // 2)
    odd_before = moved_cells(odd, 0, cols)[0].astype(BF16)
    even_after = moved_cells(even, 0, cols)[1].astype(BF16)
    even, odd = even.astype(BF16), odd.astype(BF16)
    return (odd_before, even, odd), (even, odd, even_after)


def with_columns(pad, cols):
    before, after = moved_cells(pad.astype(F32), 0, cols)
    return before.astype(BF16), pad, after.astype(BF16)


def conv_scratch(channels):
    narrow = channels // 2
    wide = -(-narrow // 128) * 128
    return [
        pltpu.VMEM((9, channels, channels), BF16),
        pltpu.VMEM((9, wide, narrow), BF16),
        pltpu.SemaphoreType.DMA((3,)),
    ]


def convolve(pad_ref, out_ref, atmos_ref, ocean_ref, layer, flipped, scratch, cols, meanwhile=None):
    atmos_buffer, ocean_buffer, sems = scratch
    order = (2, 1, 0) if flipped else (0, 1, 2)
    channels = atmos_buffer.shape[2]
    narrow = ocean_buffer.shape[2]
    rows = out_ref.shape[0]

    def atmos_copy(group):
        taps = pl.ds(9 * layer + 3 * group, 3)
        return pltpu.make_async_copy(atmos_ref.at[taps], atmos_buffer.at[pl.ds(3 * group, 3)], sems.at[group])

    def ocean_copy(group):
        taps = pl.ds(9 * layer + 3 * group, 3)
        target = ocean_buffer.at[pl.ds(3 * group, 3), pl.ds(0, narrow), :]
        return pltpu.make_async_copy(ocean_ref.at[taps], target, sems.at[group])

    @pl.when(on_ocean())
    def _():
        for group in order:
            ocean_copy(group).start()
        gap = ocean_buffer.shape[1] - narrow
        if gap:
            ocean_buffer[:, narrow:, :] = jnp.zeros((9, gap, narrow), BF16)
        if meanwhile is not None:
            meanwhile()
        evens, odds = halves_with_columns(pad_ref[...], cols)
        total = None
        if not flipped:
            even, odd = jnp.concatenate(evens, axis=1), jnp.concatenate(odds, axis=1)
        for row_tap, group in enumerate(order):
            ocean_copy(group).wait()
            span = slice(cols * row_tap, cols * row_tap + rows)
            if flipped:
                part = None
                for col_tap in range(3):
                    left = jnp.concatenate([evens[col_tap][span], odds[col_tap][span]], axis=0)
                    kernel = ocean_buffer[8 - (3 * row_tap + col_tap), 0:narrow, :]
                    piece = dot(left[:, :narrow], kernel, NT)
                    part = piece if part is None else part + piece
            else:
                kernel = ocean_buffer[3 * group : 3 * group + 3].reshape(3 * ocean_buffer.shape[1], narrow)
                part = dot(jnp.concatenate([even[span], odd[span]], axis=0), kernel)
            total = part if total is None else total + part
        out_ref[...] = jnp.concatenate([total[:rows], total[rows:]], axis=1)

    @pl.when(jnp.logical_not(on_ocean()))
    def _():
        for group in order:
            atmos_copy(group).start()
        if meanwhile is not None:
            meanwhile()
        taps = with_columns(pad_ref[...], cols)
        total = None
        if not flipped:
            joined = jnp.concatenate(taps, axis=1)
        for row_tap, group in enumerate(order):
            atmos_copy(group).wait()
            span = slice(cols * row_tap, cols * row_tap + rows)
            if flipped:
                part = None
                for col_tap in range(3):
                    piece = dot(taps[col_tap][span], atmos_buffer[8 - (3 * row_tap + col_tap)], NT)
                    part = piece if part is None else part + piece
            else:
                kernel = atmos_buffer[3 * group : 3 * group + 3].reshape(3 * channels, channels)
                part = dot(joined[span], kernel)
            total = part if total is None else total + part
        out_ref[...] = total


def back_kernel(gpad_ref, atmos_ref, ocean_ref, out_ref, *scratch, cols):
    convolve(gpad_ref, out_ref, atmos_ref, ocean_ref, 1, True, scratch, cols)


def spread(arrived, wet, mixing, terms):
    first_wet, second_wet = wet
    both = jnp.concatenate([arrived * first_wet, arrived * second_wet], axis=0)
    alone = jnp.concatenate([arrived, jnp.zeros_like(arrived)], axis=0)
    return dot(jnp.where(mixing, both, alone), terms, TN, HIGHEST)


def first_kernel(
    xpad_ref, wet_ref, arrived_ref, terms_ref, back_ref, atmos_ref, ocean_ref,
    u_ref, stay_ref, give_ref, up_ref, down_ref, first_ref, *scratch, cols,
):
    def couple():
        wet = wet_ref[0:1, :], wet_ref[1:2, :]
        coupled = spread(arrived_ref[...], wet, on_ocean(), terms_ref[8:16, :])
        u_ref[...] = (xpad_ref[...].astype(F32) + coupled).astype(BF16)

    convolve(u_ref, first_ref, atmos_ref, ocean_ref, 0, False, scratch, cols, couple)
    first = first_ref[...]
    tangent = jnp.tanh(GELU_SCALE * (first + GELU_CUBIC * first * first * first))
    hidden = (0.5 * first * (1.0 + tangent)).astype(BF16)
    slope = 0.5 * (1.0 + tangent) + 0.5 * first * (1.0 - tangent * tangent) * GELU_SCALE * (
        1.0 + 3.0 * GELU_CUBIC * first * first
    )
    first_grad = (back_ref[...] * slope).astype(BF16)
    stay_ref[...] = jnp.where(on_ocean(), first_grad, hidden)
    give_ref[...] = jnp.where(on_ocean(), hidden, first_grad)
    up_ref[0:cols, :] = hidden[cols:]
    up_ref[cols:, :] = first_grad[cols:]
    down_ref[0:cols, :] = hidden[:cols]
    down_ref[cols:, :] = first_grad[:cols]


def grad_atmos(pad, own, pad_is_input, cols, store):
    rows = own.shape[0]
    if pad_is_input:
        middle = pad.T
        before, after = moved_cells(middle, 1, cols)
        lefts = [part.astype(BF16) for part in (before, middle, after)]
        right = own.astype(BF16)
        for tap in range(9):
            start = cols * (tap // 3)
            store(tap, dot(lefts[tap % 3][:, start : start + rows], right))
    else:
        left = own.T.astype(BF16)
        before, after = moved_cells(pad, 0, cols)
        rights = [part.astype(BF16) for part in (after, pad, before)]
        for tap in range(9):
            start = cols * (2 - tap // 3)
            store(tap, dot(left, rights[tap % 3][start : start + rows]))


def grad_ocean(pad, own, pad_is_input, cols, store):
    rows, channels = own.shape
    narrow = channels // 2

    if pad_is_input:
        middle = pad.T
        before, after = moved_cells(middle, 1, cols)
        even, odd = middle[:narrow].astype(BF16), middle[narrow:].astype(BF16)
        pairs = (
            (before[narrow:].astype(BF16), even),
            (even, odd),
            (odd, after[:narrow].astype(BF16)),
        )
        right = jnp.concatenate(halves_apart(own, narrow), axis=0).astype(BF16)
        for tap in range(9):
            start = cols * (tap // 3)
            pieces = [part[:, start : start + rows] for part in pairs[tap % 3]]
            store(tap, dot(jnp.concatenate(pieces, axis=1), right))
    else:
        turned = own.T.astype(BF16)
        left = jnp.concatenate([turned[:narrow], turned[narrow:]], axis=1)
        even, odd = halves_apart(pad, narrow)
        odd_before = moved_cells(odd, 0, cols)[0].astype(BF16)
        even_after = moved_cells(even, 0, cols)[1].astype(BF16)
        even, odd = even.astype(BF16), odd.astype(BF16)
        pairs = ((odd, even_after), (even, odd), (odd_before, even))
        for tap in range(9):
            start = cols * (2 - tap // 3)
            pieces = [part[start : start + rows] for part in pairs[tap % 3]]
            store(tap, dot(left, jnp.concatenate(pieces, axis=0)))


def store_into(out_ref):
    def store(tap, value):
        if len(out_ref.shape) == 2:
            rows = value.shape[0]
            out_ref[rows * tap : rows * (tap + 1), :] = value
        else:
            rows = value.shape[0]
            for piece in range(out_ref.shape[0]):
                lanes = slice(128 * piece, 128 * (piece + 1))
                out_ref[piece, rows * tap : rows * (tap + 1), :] = value[:, lanes]

    return store


def own_grads_kernel(upad_ref, gpad_ref, stay_ref, atmos_out, ocean_out, *, cols):
    stay = stay_ref[...].astype(F32)

    @pl.when(on_ocean())
    def _():
        grad_ocean(upad_ref[...].astype(F32), stay, True, cols, store_into(ocean_out))

    @pl.when(jnp.logical_not(on_ocean()))
    def _():
        grad_atmos(gpad_ref[...].astype(F32), stay, False, cols, store_into(atmos_out))


def other_grads(early_ref, late_ref, sent_ref, coupling_ref, atmos_out, ocean_out, cols):
    late = late_ref[...].astype(F32)
    early = early_ref[...].astype(F32)

    @pl.when(on_ocean())
    def _():
        added = dot(sent_ref[...], coupling_ref[...].astype(F32), TN, HIGHEST)
        other = (early + added).astype(BF16).astype(F32)
        grad_atmos(other, late, True, cols, store_into(atmos_out))

    @pl.when(jnp.logical_not(on_ocean()))
    def _():
        grad_ocean(early, late, False, cols, store_into(ocean_out))


def chunk_rows(keep_ref, send_ref, atmos_all, ocean_all, chunks):
    channels = keep_ref.shape[2]
    pieces = ocean_all.shape[0]
    atmos_rows = atmos_all.shape[0] // chunks
    ocean_rows = atmos_rows // 2
    taken = keep_ref.shape[1] - atmos_rows
    core = lax.rem(lax.axis_index("lat"), 2)
    blank = jnp.zeros((taken, channels - 128 * pieces), F32)
    for out_ref, side in ((send_ref, 1 - core), (keep_ref, core)):
        for pair in range(chunks // 2):
            start = pl.multiple_of(atmos_rows * (2 * pair + side), 8)
            upper = atmos_all[pl.ds(start, atmos_rows), :]
            start = ocean_rows * (2 * pair + side)
            halves = []
            for odd in range(2):
                parts = [ocean_all.at[piece][pl.ds(start + odd, taken, 2), :] for piece in range(pieces)]
                halves.append(jnp.concatenate(parts + [blank], axis=1))
            lower = halves[0] + pltpu.roll(halves[1], channels // 2, 1)
            out_ref[pair] = jnp.concatenate([upper, lower], axis=0).astype(BF16)


def grads_kernel(
    early_ref, late_ref, sent_ref, coupling_ref, atmos_in, ocean_in,
    keep_ref, send_ref, atmos_all, ocean_all, *, cols, chunks,
):
    other_grads(early_ref, late_ref, sent_ref, coupling_ref, atmos_all, ocean_all, cols)

    @pl.when(on_ocean())
    def _():
        chunk_rows(keep_ref, send_ref, atmos_all, ocean_in, chunks)

    @pl.when(jnp.logical_not(on_ocean()))
    def _():
        chunk_rows(keep_ref, send_ref, atmos_in, ocean_all, chunks)


def plain_grads_kernel(
    early_ref, late_ref, sent_ref, coupling_ref, atmos_in, ocean_in, atmos_out, ocean_out, *, cols
):
    @pl.when(on_ocean())
    def _():
        ocean_out[...] = ocean_in[...]

    @pl.when(jnp.logical_not(on_ocean()))
    def _():
        atmos_out[...] = atmos_in[...]

    other_grads(early_ref, late_ref, sent_ref, coupling_ref, atmos_out, ocean_out, cols)


def own_bit(bit):
    return lax.rem(lax.shift_right_logical(lax.axis_index("lat"), bit), 2)


def halve(keep_ref, came_ref, keep_out, send_out, bit, rows):
    own = own_bit(bit)
    for out_ref, side in ((send_out, 1 - own), (keep_out, own)):
        for outer in range(keep_ref.shape[0]):
            for inner in range(keep_ref.shape[2]):
                total = keep_ref[outer, side, inner, rows, :].astype(F32)
                total = total + came_ref[outer, side, inner, rows, :].astype(F32)
                out_ref[outer, inner] = total.astype(BF16)


def split_kernel(keep_ref, came_ref, done_ref, first_keep, first_send, second_keep, second_send, *, cut):
    tall = keep_ref.shape[3]
    halve(keep_ref, came_ref, first_keep, first_send, 1, slice(0, cut))
    views = [ref.reshape(2, 2, 2, *keep_ref.shape[3:]) for ref in (keep_ref, came_ref)]
    halve(*views, second_keep, second_send, 2, slice(cut, tall))


def halve_kernel(keep_ref, came_ref, *refs, bit):
    keep_out, send_out = refs[-2:]
    halve(keep_ref, came_ref, keep_out, send_out, bit, slice(None))


def halved(keep, came, bit, dims, after=()):
    outer, inner, rows, channels = dims[0], dims[1], keep.shape[-2], keep.shape[-1]
    keep, came = (part.reshape(outer, 2, inner, rows, channels) for part in (keep, came))
    out = shape((outer, inner, rows, channels), BF16)
    return call(
        functools.partial(halve_kernel, bit=bit),
        [out, out],
        [keep, came, *after],
        [WHOLE] * 2 + [IN_PLACE] * len(after),
        moved=8 * outer * inner * rows * channels,
        name="halve",
    )


def scatter_sum(keep, came, done_before, done_next):
    pairs, tall, channels = keep.shape
    cut = -(-tall // 32) * 16
    first, second = shape((4, 1, cut, channels), BF16), shape((2, 2, tall - cut, channels), BF16)
    keep, came = (part.reshape(4, 2, 1, tall, channels) for part in (keep, came))
    first_keep, first_send, second_keep, second_send = call(
        functools.partial(split_kernel, cut=cut),
        [first, first, second, second],
        [keep, came, done_before],
        [WHOLE] * 2 + [ANYWHERE],
        moved=6 * pairs * tall * channels,
        name="split",
    )
    first_came = swapped(first_send, "lat", 2)
    second_came = swapped(second_send, "lat", 4)
    first_keep, first_send = halved(first_keep, first_came, 2, (2, 1), done_next)
    first_came = swapped(first_send, "lat", 4)
    second_keep, second_send = halved(second_keep, second_came, 3, (1, 2))
    second_came = swapped(second_send, "lat", 8)
    first_keep, first_send = halved(first_keep, first_came, 3, (1, 1))
    first_came = swapped(first_send, "lat", 8)
    second_keep, second_send = halved(second_keep, second_came, 1, (1, 1))
    second_came = swapped(second_send, "lat", 2)
    return [part.reshape(-1, channels) for part in (first_keep, first_came, second_keep, second_came)]


def finish_kernel(
    first_ref, first_came, second_ref, second_came, atmos_ref, ocean_ref, *, atmos_factor, ocean_factor
):
    channels = first_ref.shape[1]
    pieces = channels // 128
    atmos_rows = atmos_ref.shape[0] // pieces
    ocean_rows = ocean_ref.shape[0] // pieces
    first = first_ref[...].astype(F32) + first_came[...].astype(F32)
    second = second_ref[...].astype(F32) + second_came[...].astype(F32)
    total = jnp.concatenate([first, second], axis=0)
    for piece in range(pieces):
        lanes = slice(128 * piece, 128 * (piece + 1))
        atmos_ref[pl.ds(piece, atmos_rows, pieces), :] = total[:atmos_rows, lanes] * atmos_factor
        ocean_ref[pl.ds(piece, ocean_rows, pieces), :] = (
            total[atmos_rows : atmos_rows + ocean_rows, lanes] * ocean_factor
        )


def input_grad_kernel(
    stay_ref, give_ref, low_ref, high_ref, gpad_ref, wet_ref, terms_ref, atmos_ref, ocean_ref,
    grad_ref, sent_ref, pad_ref, *scratch, cols,
):
    def gather():
        pad_ref[0:cols, :] = low_ref[cols:, :]
        pad_ref[cols : 3 * cols, :] = jnp.where(on_ocean(), stay_ref[...], give_ref[...])
        pad_ref[3 * cols :, :] = high_ref[cols:, :]

    own = slice(cols, 3 * cols)
    convolve(pad_ref, grad_ref, atmos_ref, ocean_ref, 0, True, scratch, cols, gather)
    grad = gpad_ref[own, :].astype(F32) + grad_ref[...]
    grad_ref[...] = grad
    weighted = dot(terms_ref[8:16, :], grad, NT, HIGHEST)
    mixed = weighted[0:4] * wet_ref[0:1, own] + weighted[4:8] * wet_ref[1:2, own]
    sent_ref[...] = jnp.where(on_ocean(), mixed, weighted[0:4])


def next_kernel(
    stay_ref, give_ref, low_ref, high_ref, upad_ref, atmos_ref, ocean_ref,
    next_ref, mark_ref, second_ref, pad_ref, *scratch, cols,
):
    def gather():
        pad_ref[0:cols, :] = low_ref[0:cols, :]
        pad_ref[cols : 3 * cols, :] = jnp.where(on_ocean(), give_ref[...], stay_ref[...])
        pad_ref[3 * cols :, :] = high_ref[0:cols, :]

    own = slice(cols, 3 * cols)
    convolve(pad_ref, second_ref, atmos_ref, ocean_ref, 1, False, scratch, cols, gather)
    values = (upad_ref[own, :].astype(F32) + second_ref[...]).astype(BF16)
    next_ref[0] = values[:cols]
    next_ref[1] = values[cols:]
    mark_ref[...] = jnp.zeros_like(mark_ref)


def last_kernel(grad_ref, arrived_ref, wet_ref, terms_ref, out_ref, mark_ref, *, cols):
    own = slice(cols, 3 * cols)
    wet = wet_ref[0:1, own], wet_ref[1:2, own]
    arrived = jnp.where(on_ocean(), arrived_ref[...] * wet_ref[2:3, own], arrived_ref[...])
    added = spread(arrived, wet, on_ocean(), terms_ref[0:8, :])
    values = (grad_ref[...] + added).astype(BF16)
    out_ref[0] = values[:cols]
    out_ref[1] = values[cols:]
    mark_ref[...] = jnp.zeros_like(mark_ref)


def swapped(value, axis, mask):
    pairs = [(source, source ^ mask) for source in range(lax.axis_size(axis))]
    return lax.ppermute(value, axis, pairs)


def halo(up, down):
    count = lax.axis_size("lat")
    forward = [(i, i + 1) for i in range(count - 1)]
    backward = [(target, source) for source, target in forward]
    return lax.ppermute(up, "lat", forward), lax.ppermute(down, "lat", backward)


def local(
    fields,
    cotangent,
    ocean_kernels,
    atmos_kernels,
    ocean_surface,
    ocean_coupling,
    atmos_flux,
    atmos_coupling,
    row_map,
    wet_mask,
):
    x, g = fields[0], cotangent[0]
    bands, cols, channels = x.shape
    narrow = channels // 2
    cells = bands * cols
    count = lax.axis_size("lat")
    is_ocean = lax.axis_index("grp") == 0
    atmos_factor = 1.0 / math.sqrt(bands * count * cols)
    ocean_factor = 1.0 / math.sqrt(bands * count * 2 * cols)
    bound = functools.partial

    blank = jnp.zeros((4, narrow), BF16)
    gap = jnp.zeros((4, channels), BF16)
    surface = ocean_surface.T
    ocean_terms = jnp.concatenate(
        [
            jnp.concatenate([surface, blank], axis=1),
            jnp.concatenate([blank, surface], axis=1),
            jnp.concatenate([ocean_coupling, blank], axis=1),
            jnp.concatenate([blank, ocean_coupling], axis=1),
        ],
        axis=0,
    )
    atmos_terms = jnp.concatenate([atmos_flux.T, gap, atmos_coupling, gap], axis=0)
    terms = jnp.where(is_ocean, ocean_terms, atmos_terms).astype(F32)

    edge = shape((2 * cols + 16, channels), BF16)
    kept = shape(x.shape, BF16)
    up, down = call(
        bound(pack_kernel, cols=cols),
        [edge, edge],
        [x, g, wet_mask],
        [IN_PLACE] * 3,
        [
            pltpu.VMEM(wet_mask.shape, jnp.int32),
            pltpu.VMEM((2, 16, channels), BF16),
            pltpu.SemaphoreType.DMA,
            pltpu.SemaphoreType.DMA((2, 3)),
        ],
        out_spec=ANYWHERE,
        name="pack",
        limit=PACK_VMEM,
    )
    low, high = halo(up, down)
    x, g, own_wet = call(
        bound(hold_kernel, cols=cols),
        [kept, kept, shape((16, channels), BF16)],
        [x, g, wet_mask],
        [IN_PLACE] * 3,
        [pltpu.VMEM(wet_mask.shape, jnp.int32), pltpu.SemaphoreType.DMA((3,))],
        flops=PACE * 10**8,
        name="hold",
        limit=MOST_VMEM,
    )
    atmos_flat = atmos_kernels.reshape(18, channels, channels)
    ocean_flat = ocean_kernels.reshape(18, narrow, narrow)
    pad = shape((2 * cells, channels), BF16)
    xpad, gpad, wet, early, sent = call(
        bound(outgoing_kernel, cols=cols),
        [pad, pad, shape((8, 2 * cells), F32), pad, shape((4, 2 * cells), F32)],
        [x, g, low, high, own_wet, terms],
        name="outgoing",
    )
    arrived = swapped(sent, "grp", 1)
    other_early = swapped(early, "grp", 1)
    conv_cost = dict(limit=MOST_VMEM, flops=PACE * 9 * cells * channels * channels, moved=9 * channels * channels * 2)
    grad_cost = dict(conv_cost, limit=VMEM_LIMIT)
    back = call(
        bound(back_kernel, cols=cols),
        shape((cells, channels), F32),
        [gpad, atmos_flat, ocean_flat],
        [WHOLE, IN_PLACE, IN_PLACE],
        conv_scratch(channels),
        **conv_cost,
        name="back",
    )
    half = shape((cells, channels), BF16)
    upad, stay, give, up, down = call(
        bound(first_kernel, cols=cols),
        [pad, half, half, half, half],
        [xpad, wet, arrived, terms, back, atmos_flat, ocean_flat],
        [WHOLE] * 5 + [IN_PLACE] * 2,
        [pltpu.VMEM((cells, channels), F32)] + conv_scratch(channels),
        **conv_cost,
        name="first",
    )
    late = swapped(give, "grp", 1)

    atmos_rows = 9 * channels // count
    ocean_rows = 9 * narrow // count
    wide = -(-narrow // 128) * 128
    chunked = count == 16 and 9 * channels % (8 * count) == 0 and ocean_rows % 2 == 0
    tall = -(-(atmos_rows + ocean_rows // 2) // 16) * 16
    spare = max(0, 2 * (tall - atmos_rows) - ocean_rows) if chunked else 0
    ocean_tall = 9 * narrow + -(-spare // 8) * 8
    sums = [shape((9 * channels, channels), F32), shape((wide // 128, ocean_tall, 128), F32)]
    atmos_sum, ocean_sum = call(
        bound(own_grads_kernel, cols=cols), sums, [upad, gpad, stay], **grad_cost, name="own_grads"
    )
    inputs = [other_early, late, sent, atmos_coupling, atmos_sum, ocean_sum]
    if chunked:
        part = shape((count // 2, tall, channels), BF16)
        keep, send = call(
            bound(grads_kernel, cols=cols, chunks=count),
            [part, part],
            inputs,
            None,
            [pltpu.VMEM(out.shape, F32) for out in sums],
            **grad_cost,
            name="grads",
        )
        came = swapped(send, "lat", 1)
    else:
        atmos_all, ocean_all = call(
            bound(plain_grads_kernel, cols=cols), sums, inputs, **grad_cost, name="grads"
        )

    low, high = halo(up, down)
    grad, sent_back = call(
        bound(input_grad_kernel, cols=cols),
        [shape((cells, channels), F32), shape((4, cells), F32)],
        [stay, give, low, high, gpad, wet, terms, atmos_flat, ocean_flat],
        [WHOLE] * 7 + [IN_PLACE] * 2,
        [pltpu.VMEM((2 * cells, channels), BF16)] + conv_scratch(channels),
        **conv_cost,
        name="input_grad",
    )
    returned = swapped(sent_back, "grp", 1)
    mark = shape((8, 128), F32)
    next_field, next_mark = call(
        bound(next_kernel, cols=cols),
        [shape(x.shape, BF16), mark],
        [stay, give, low, high, upad, atmos_flat, ocean_flat],
        [WHOLE] * 5 + [IN_PLACE] * 2,
        [pltpu.VMEM((cells, channels), F32), pltpu.VMEM((2 * cells, channels), BF16)] + conv_scratch(channels),
        **conv_cost,
        name="next",
    )
    field_grad, last_mark = call(
        bound(last_kernel, cols=cols),
        [shape(x.shape, BF16), mark],
        [grad, returned, wet, terms],
        name="last",
    )

    if chunked:
        atmos_chunk, ocean_chunk = call(
            bound(finish_kernel, atmos_factor=atmos_factor, ocean_factor=ocean_factor),
            [
                shape((atmos_rows * channels // 128, 128), F32),
                shape((ocean_rows * narrow // 128, 128), F32),
            ],
            scatter_sum(keep, came, sent_back, (next_mark, last_mark)),
            name="finish",
        )
        atmos_total, ocean_total = atmos_chunk.reshape(-1), ocean_chunk.reshape(-1)
    else:
        atmos_total = atmos_factor * lax.psum_scatter(
            atmos_all.reshape(-1), "lat", scatter_dimension=0, tiled=True
        )
        ocean_all = jnp.concatenate([ocean_all[piece] for piece in range(wide // 128)], axis=1)
        ocean_total = ocean_factor * lax.psum_scatter(
            ocean_all[:, :narrow].reshape(-1), "lat", scatter_dimension=0, tiled=True
        )
    return (next_field[None], field_grad[None], ocean_total, atmos_total)


def solution(mesh):
    in_specs = (
        P("grp", "lat", None, None),
        P("grp", "lat", None, None),
        P(),
        P(),
        P(),
        P(),
        P(),
        P(),
        P("lat"),
        P("lat", None),
    )
    out_specs = (
        P("grp", "lat", None, None),
        P("grp", "lat", None, None),
        P(("grp", "lat")),
        P(("grp", "lat")),
    )
    return jax.shard_map(local, mesh=mesh, in_specs=in_specs, out_specs=out_specs, check_vma=False)
```

```python
import functools
import math

import jax
import jax.numpy as jnp
from jax import lax
from jax.experimental import pallas as pl
from jax.experimental.pallas import tpu as pltpu
from jax.sharding import PartitionSpec as P

HIGHEST = lax.Precision.HIGHEST
GELU_SCALE = 0.7978845608028654
GELU_CUBIC = 0.044715
F32 = jnp.float32
BF16 = jnp.bfloat16
WHOLE = pl.BlockSpec(memory_space=pltpu.VMEM)
IN_PLACE = pl.BlockSpec(memory_space=pltpu.HBM)
ANYWHERE = pl.BlockSpec(memory_space=pl.ANY)
VMEM_LIMIT = 32 * 1024 * 1024
PACE = 8
PACK_VMEM = 62 * 1024 * 1024
HOLD_VMEM = 42 * 1024 * 1024

NN = (((1,), (0,)), ((), ()))
NT = (((1,), (1,)), ((), ()))
TN = (((0,), (0,)), ((), ()))


def shape(dims, kind):
    return jax.ShapeDtypeStruct(dims, kind)


def call(kernel, outs, inputs, in_specs=None, scratch=(), flops=0, moved=0, name=None, limit=VMEM_LIMIT, out_spec=WHOLE):
    return pl.pallas_call(
        kernel,
        out_shape=outs,
        in_specs=in_specs or [WHOLE] * len(inputs),
        out_specs=jax.tree.map(lambda _: out_spec, outs),
        scratch_shapes=list(scratch),
        compiler_params=pltpu.CompilerParams(vmem_limit_bytes=limit),
        cost_estimate=pl.CostEstimate(flops=flops, bytes_accessed=moved, transcendentals=0),
        name=name,
    )(*inputs)


def on_ocean():
    return lax.axis_index("grp") == 0


def dot(left, right, dims=NN, precision=None):
    return lax.dot_general(left, right, dims, precision=precision, preferred_element_type=F32)


def moved_cells(values, axis, cols):
    count = values.shape[axis]
    place = lax.rem(lax.broadcasted_iota(jnp.int32, values.shape, axis), cols)
    before = jnp.where(place == 0, 0.0, pltpu.roll(values, 1, axis))
    after = jnp.where(place == cols - 1, 0.0, pltpu.roll(values, count - 1, axis))
    return before, after


def wet_halves(wet, cols, channels):
    source = lax.broadcasted_iota(jnp.int32, (2 * cols, 2 * cols), 0)
    target = lax.broadcasted_iota(jnp.int32, (2 * cols, 2 * cols), 1)
    wanted = 2 * lax.rem(target, cols) + jnp.where(target >= cols, 1, 0)
    chooser = (source == wanted).astype(F32).astype(BF16)
    padded = jnp.concatenate([wet.astype(F32), jnp.zeros((14, 2 * cols), F32)], axis=0)
    apart = dot(padded.astype(BF16), chooser)
    return jnp.concatenate([apart, jnp.zeros((16, channels - 2 * cols), F32)], axis=1)


def pack_kernel(
    x_any, g_any, wet_any, up_ref, down_ref, early_ref, x_ref, g_ref, wet_ref, sems, *, cols
):
    pairs = ((wet_any, wet_ref), (x_any, x_ref), (g_any, g_ref))
    copies = [pltpu.make_async_copy(*pair, sems.at[index]) for index, pair in enumerate(pairs)]
    for copy in copies:
        copy.start()
    copies[0].wait()
    wide = wet_halves(wet_ref[...], cols, x_ref.shape[2])
    up_ref[2 * cols :, :] = pltpu.roll(wide, 15, 0).astype(BF16)
    down_ref[2 * cols :, :] = wide.astype(BF16)
    copies[1].wait()
    copies[2].wait()
    for row, out_ref in ((1, up_ref), (0, down_ref)):
        out_ref[0:cols, :] = x_ref[row]
        out_ref[cols : 2 * cols, :] = g_ref[row]
        early_ref[row * cols : (row + 1) * cols, :] = jnp.where(on_ocean(), g_ref[row], x_ref[row])


def hold_kernel(
    x_any, g_any, wet_any, atmos_any, ocean_any,
    x_ref, g_ref, own_ref, atmos_ref, ocean_ref, wet_ref, sems, weight_sem, *, cols,
):
    pairs = ((wet_any, wet_ref), (x_any, x_ref), (g_any, g_ref))
    copies = [pltpu.make_async_copy(*pair, sems.at[index]) for index, pair in enumerate(pairs)]
    narrow = ocean_ref.shape[2]
    ocean_copy = pltpu.make_async_copy(ocean_any, ocean_ref.at[:, pl.ds(0, narrow), :], weight_sem)
    atmos_copy = pltpu.make_async_copy(atmos_any, atmos_ref, weight_sem)
    for copy in copies:
        copy.start()

    @pl.when(on_ocean())
    def _():
        ocean_copy.start()
        gap = ocean_ref.shape[1] - narrow
        if gap:
            ocean_ref[:, narrow:, :] = jnp.zeros((ocean_ref.shape[0], gap, narrow), BF16)

    @pl.when(jnp.logical_not(on_ocean()))
    def _():
        atmos_copy.start()

    copies[0].wait()
    own_ref[...] = wet_halves(wet_ref[...], cols, own_ref.shape[1]).astype(BF16)
    copies[1].wait()
    copies[2].wait()

    @pl.when(on_ocean())
    def _():
        ocean_copy.wait()

    @pl.when(jnp.logical_not(on_ocean()))
    def _():
        atmos_copy.wait()


def outgoing_kernel(
    x_ref, g_ref, low_ref, high_ref, own_ref, terms_ref,
    xpad_ref, gpad_ref, wet_ref, early_ref, sent_ref, *, cols,
):
    for pad_ref, own, start in ((xpad_ref, x_ref, 0), (gpad_ref, g_ref, cols)):
        pad_ref[0:cols, :] = low_ref[start : start + cols, :]
        pad_ref[cols : 2 * cols, :] = own[0]
        pad_ref[2 * cols : 3 * cols, :] = own[1]
        pad_ref[3 * cols : 4 * cols, :] = high_ref[start : start + cols, :]
    low_wet = low_ref[2 * cols :, :].astype(F32)
    high_wet = high_ref[2 * cols :, :].astype(F32)
    own_wet = own_ref[...].astype(F32)
    halves = []
    for start in (0, cols):
        lanes = slice(start, start + cols)
        rows = (low_wet[0:1, lanes], own_wet[0:1, lanes], own_wet[1:2, lanes], high_wet[0:1, lanes])
        halves.append(jnp.concatenate(rows, axis=1))
    first_wet, second_wet = halves
    inverse = 1.0 / jnp.maximum(first_wet + second_wet, 1.0)
    wet_ref[0:1, :] = first_wet
    wet_ref[1:2, :] = second_wet
    wet_ref[2:3, :] = inverse
    wet_ref[3:8, :] = jnp.zeros((5, 4 * cols), F32)
    xpad = xpad_ref[...]
    projected = dot(terms_ref[0:8, :].astype(BF16), xpad, NT)
    mixed = (projected[0:4] * first_wet + projected[4:8] * second_wet) * inverse
    sent_ref[...] = jnp.where(on_ocean(), mixed, projected[0:4])
    early_ref[0:cols, :] = jnp.where(on_ocean(), gpad_ref[0:cols, :], xpad_ref[0:cols, :])
    early_ref[cols:, :] = jnp.where(on_ocean(), gpad_ref[3 * cols :, :], xpad_ref[3 * cols :, :])


def halves_apart(values, narrow):
    wide = -(-narrow // 128) * 128
    lane = lax.broadcasted_iota(jnp.int32, values.shape, 1)
    even = jnp.where(lane < narrow, values, 0.0)
    odd = jnp.where(lane < narrow, pltpu.roll(values, narrow, 1), 0.0)
    return even[:, :wide], odd[:, :wide]


def halves_with_columns(pad, cols):
    even, odd = halves_apart(pad.astype(F32), pad.shape[1] // 2)
    odd_before = moved_cells(odd, 0, cols)[0].astype(BF16)
    even_after = moved_cells(even, 0, cols)[1].astype(BF16)
    even, odd = even.astype(BF16), odd.astype(BF16)
    return (odd_before, even, odd), (even, odd, even_after)


def with_columns(pad, cols):
    before, after = moved_cells(pad.astype(F32), 0, cols)
    return before.astype(BF16), pad, after.astype(BF16)


def convolve(pad, out_ref, atmos_ref, ocean_ref, layer, flipped, cols):
    base = 9 * layer
    channels = atmos_ref.shape[2]
    wide, narrow = ocean_ref.shape[1:]
    rows = out_ref.shape[0]

    def summed(pick):
        total = None
        for row_tap in range(3):
            part = pick(row_tap, slice(cols * row_tap, cols * row_tap + rows))
            total = part if total is None else total + part
        return total

    @pl.when(on_ocean())
    def _():
        evens, odds = halves_with_columns(pad, cols)
        if flipped:

            def pick(row_tap, span):
                part = None
                for col_tap in range(3):
                    left = jnp.concatenate([evens[col_tap][span], odds[col_tap][span]], axis=0)
                    kernel = ocean_ref[base + 8 - (3 * row_tap + col_tap), 0:narrow, :]
                    piece = dot(left[:, :narrow], kernel, NT)
                    part = piece if part is None else part + piece
                return part

        else:
            even, odd = jnp.concatenate(evens, axis=1), jnp.concatenate(odds, axis=1)

            def pick(row_tap, span):
                first = base + 3 * row_tap
                kernel = ocean_ref[first : first + 3].reshape(3 * wide, narrow)
                return dot(jnp.concatenate([even[span], odd[span]], axis=0), kernel)

        total = summed(pick)
        out_ref[...] = jnp.concatenate([total[:rows], total[rows:]], axis=1)

    @pl.when(jnp.logical_not(on_ocean()))
    def _():
        taps = with_columns(pad, cols)
        if flipped:

            def pick(row_tap, span):
                part = None
                for col_tap in range(3):
                    piece = dot(taps[col_tap][span], atmos_ref[base + 8 - (3 * row_tap + col_tap)], NT)
                    part = piece if part is None else part + piece
                return part

        else:
            joined = jnp.concatenate(taps, axis=1)

            def pick(row_tap, span):
                first = base + 3 * row_tap
                return dot(joined[span], atmos_ref[first : first + 3].reshape(3 * channels, channels))

        out_ref[...] = summed(pick)


def back_kernel(gpad_ref, atmos_ref, ocean_ref, out_ref, *, cols):
    convolve(gpad_ref[...], out_ref, atmos_ref, ocean_ref, 1, True, cols)


def spread(arrived, wet, mixing, terms):
    first_wet, second_wet = wet
    both = jnp.concatenate([arrived * first_wet, arrived * second_wet], axis=0)
    alone = jnp.concatenate([arrived, jnp.zeros_like(arrived)], axis=0)
    return dot(jnp.where(mixing, both, alone), terms, TN, HIGHEST)


def first_kernel(
    xpad_ref, wet_ref, arrived_ref, terms_ref, back_ref, atmos_ref, ocean_ref,
    u_ref, stay_ref, give_ref, up_ref, down_ref, first_ref, *, cols,
):
    wet = wet_ref[0:1, :], wet_ref[1:2, :]
    coupled = spread(arrived_ref[...], wet, on_ocean(), terms_ref[8:16, :])
    u = (xpad_ref[...].astype(F32) + coupled).astype(BF16)
    u_ref[...] = u
    convolve(u, first_ref, atmos_ref, ocean_ref, 0, False, cols)
    first = first_ref[...]
    tangent = jnp.tanh(GELU_SCALE * (first + GELU_CUBIC * first * first * first))
    hidden = (0.5 * first * (1.0 + tangent)).astype(BF16)
    slope = 0.5 * (1.0 + tangent) + 0.5 * first * (1.0 - tangent * tangent) * GELU_SCALE * (
        1.0 + 3.0 * GELU_CUBIC * first * first
    )
    first_grad = (back_ref[...] * slope).astype(BF16)
    stay_ref[...] = jnp.where(on_ocean(), first_grad, hidden)
    give_ref[...] = jnp.where(on_ocean(), hidden, first_grad)
    up_ref[0:cols, :] = hidden[cols:]
    up_ref[cols:, :] = first_grad[cols:]
    down_ref[0:cols, :] = hidden[:cols]
    down_ref[cols:, :] = first_grad[:cols]


def grad_atmos(pad, own, pad_is_input, cols, store):
    rows = own.shape[0]
    if pad_is_input:
        middle = pad.T
        before, after = moved_cells(middle, 1, cols)
        lefts = [part.astype(BF16) for part in (before, middle, after)]
        right = own.astype(BF16)
        for tap in range(9):
            start = cols * (tap // 3)
            store(tap, dot(lefts[tap % 3][:, start : start + rows], right))
    else:
        left = own.T.astype(BF16)
        before, after = moved_cells(pad, 0, cols)
        rights = [part.astype(BF16) for part in (after, pad, before)]
        for tap in range(9):
            start = cols * (2 - tap // 3)
            store(tap, dot(left, rights[tap % 3][start : start + rows]))


def grad_ocean(pad, own, pad_is_input, cols, store):
    rows, channels = own.shape
    narrow = channels // 2

    if pad_is_input:
        middle = pad.T
        before, after = moved_cells(middle, 1, cols)
        even, odd = middle[:narrow].astype(BF16), middle[narrow:].astype(BF16)
        pairs = (
            (before[narrow:].astype(BF16), even),
            (even, odd),
            (odd, after[:narrow].astype(BF16)),
        )
        right = jnp.concatenate(halves_apart(own, narrow), axis=0).astype(BF16)
        for tap in range(9):
            start = cols * (tap // 3)
            pieces = [part[:, start : start + rows] for part in pairs[tap % 3]]
            store(tap, dot(jnp.concatenate(pieces, axis=1), right))
    else:
        turned = own.T.astype(BF16)
        left = jnp.concatenate([turned[:narrow], turned[narrow:]], axis=1)
        even, odd = halves_apart(pad, narrow)
        odd_before = moved_cells(odd, 0, cols)[0].astype(BF16)
        even_after = moved_cells(even, 0, cols)[1].astype(BF16)
        even, odd = even.astype(BF16), odd.astype(BF16)
        pairs = ((odd, even_after), (even, odd), (odd_before, even))
        for tap in range(9):
            start = cols * (2 - tap // 3)
            pieces = [part[start : start + rows] for part in pairs[tap % 3]]
            store(tap, dot(left, jnp.concatenate(pieces, axis=0)))


def store_into(out_ref):
    def store(tap, value):
        if len(out_ref.shape) == 2:
            rows = value.shape[0]
            out_ref[rows * tap : rows * (tap + 1), :] = value
        else:
            rows = value.shape[0]
            for piece in range(out_ref.shape[0]):
                lanes = slice(128 * piece, 128 * (piece + 1))
                out_ref[piece, rows * tap : rows * (tap + 1), :] = value[:, lanes]

    return store


def own_grads_kernel(upad_ref, gpad_ref, stay_ref, atmos_out, ocean_out, *, cols):
    stay = stay_ref[...].astype(F32)

    @pl.when(on_ocean())
    def _():
        grad_ocean(upad_ref[...].astype(F32), stay, True, cols, store_into(ocean_out))

    @pl.when(jnp.logical_not(on_ocean()))
    def _():
        grad_atmos(gpad_ref[...].astype(F32), stay, False, cols, store_into(atmos_out))


def other_grads(early_ref, edge_ref, late_ref, sent_ref, coupling_ref, atmos_out, ocean_out, cols):
    late = late_ref[...].astype(F32)
    early = jnp.concatenate([edge_ref[0:cols, :], early_ref[...], edge_ref[cols:, :]], axis=0).astype(F32)

    @pl.when(on_ocean())
    def _():
        added = dot(sent_ref[...], coupling_ref[...].astype(F32), TN, HIGHEST)
        other = (early + added).astype(BF16).astype(F32)
        grad_atmos(other, late, True, cols, store_into(atmos_out))

    @pl.when(jnp.logical_not(on_ocean()))
    def _():
        grad_ocean(early, late, False, cols, store_into(ocean_out))


def chunk_rows(keep_ref, send_ref, atmos_all, ocean_all, chunks):
    channels = keep_ref.shape[2]
    pieces = ocean_all.shape[0]
    atmos_rows = atmos_all.shape[0] // chunks
    ocean_rows = atmos_rows // 2
    taken = keep_ref.shape[1] - atmos_rows
    core = lax.rem(lax.axis_index("lat"), 2)
    blank = jnp.zeros((taken, channels - 128 * pieces), F32)
    for out_ref, side in ((send_ref, 1 - core), (keep_ref, core)):
        for pair in range(chunks // 2):
            start = pl.multiple_of(atmos_rows * (2 * pair + side), 8)
            upper = atmos_all[pl.ds(start, atmos_rows), :]
            start = ocean_rows * (2 * pair + side)
            halves = []
            for odd in range(2):
                parts = [ocean_all.at[piece][pl.ds(start + odd, taken, 2), :] for piece in range(pieces)]
                halves.append(jnp.concatenate(parts + [blank], axis=1))
            lower = halves[0] + pltpu.roll(halves[1], channels // 2, 1)
            out_ref[pair] = jnp.concatenate([upper, lower], axis=0).astype(BF16)


def grads_kernel(
    early_ref, edge_ref, late_ref, sent_ref, coupling_ref, atmos_in, ocean_in, low_any, high_any,
    keep_ref, send_ref, atmos_all, ocean_all, *, cols, chunks,
):
    other_grads(early_ref, edge_ref, late_ref, sent_ref, coupling_ref, atmos_all, ocean_all, cols)

    @pl.when(on_ocean())
    def _():
        chunk_rows(keep_ref, send_ref, atmos_all, ocean_in, chunks)

    @pl.when(jnp.logical_not(on_ocean()))
    def _():
        chunk_rows(keep_ref, send_ref, atmos_in, ocean_all, chunks)


def plain_grads_kernel(
    early_ref, edge_ref, late_ref, sent_ref, coupling_ref, atmos_in, ocean_in, atmos_out, ocean_out, *, cols
):
    @pl.when(on_ocean())
    def _():
        ocean_out[...] = ocean_in[...]

    @pl.when(jnp.logical_not(on_ocean()))
    def _():
        atmos_out[...] = atmos_in[...]

    other_grads(early_ref, edge_ref, late_ref, sent_ref, coupling_ref, atmos_out, ocean_out, cols)


def own_bit(bit):
    return lax.rem(lax.shift_right_logical(lax.axis_index("lat"), bit), 2)


def halve(keep_ref, came_ref, keep_out, send_out, bit, rows):
    own = own_bit(bit)
    for out_ref, side in ((send_out, 1 - own), (keep_out, own)):
        for outer in range(keep_ref.shape[0]):
            for inner in range(keep_ref.shape[2]):
                total = keep_ref[outer, side, inner, rows, :].astype(F32)
                total = total + came_ref[outer, side, inner, rows, :].astype(F32)
                out_ref[outer, inner] = total.astype(BF16)


def split_kernel(keep_ref, came_ref, done_ref, first_keep, first_send, second_keep, second_send, *, cut):
    tall = keep_ref.shape[3]
    halve(keep_ref, came_ref, first_keep, first_send, 1, slice(0, cut))
    views = [ref.reshape(2, 2, 2, *keep_ref.shape[3:]) for ref in (keep_ref, came_ref)]
    halve(*views, second_keep, second_send, 2, slice(cut, tall))


def halve_kernel(keep_ref, came_ref, *refs, bit):
    keep_out, send_out = refs[-2:]
    halve(keep_ref, came_ref, keep_out, send_out, bit, slice(None))


def halved(keep, came, bit, dims, after=()):
    outer, inner, rows, channels = dims[0], dims[1], keep.shape[-2], keep.shape[-1]
    keep, came = (part.reshape(outer, 2, inner, rows, channels) for part in (keep, came))
    out = shape((outer, inner, rows, channels), BF16)
    return call(
        functools.partial(halve_kernel, bit=bit),
        [out, out],
        [keep, came, *after],
        [WHOLE] * 2 + [IN_PLACE] * len(after),
        moved=8 * outer * inner * rows * channels,
        name="halve",
    )


def scatter_sum(keep, came, done_before, done_next):
    pairs, tall, channels = keep.shape
    cut = -(-tall // 32) * 16
    first, second = shape((4, 1, cut, channels), BF16), shape((2, 2, tall - cut, channels), BF16)
    keep, came = (part.reshape(4, 2, 1, tall, channels) for part in (keep, came))
    first_keep, first_send, second_keep, second_send = call(
        functools.partial(split_kernel, cut=cut),
        [first, first, second, second],
        [keep, came, done_before],
        [WHOLE] * 2 + [ANYWHERE],
        moved=6 * pairs * tall * channels,
        name="split",
    )
    first_came = swapped(first_send, "lat", 2)
    second_came = swapped(second_send, "lat", 4)
    first_keep, first_send = halved(first_keep, first_came, 2, (2, 1), done_next)
    first_came = swapped(first_send, "lat", 4)
    second_keep, second_send = halved(second_keep, second_came, 3, (1, 2))
    second_came = swapped(second_send, "lat", 8)
    first_keep, first_send = halved(first_keep, first_came, 3, (1, 1))
    first_came = swapped(first_send, "lat", 8)
    second_keep, second_send = halved(second_keep, second_came, 1, (1, 1))
    second_came = swapped(second_send, "lat", 2)
    return [part.reshape(-1, channels) for part in (first_keep, first_came, second_keep, second_came)]


def finish_kernel(
    first_ref, first_came, second_ref, second_came, atmos_ref, ocean_ref, *, atmos_factor, ocean_factor
):
    channels = first_ref.shape[1]
    pieces = channels // 128
    atmos_rows = atmos_ref.shape[0] // pieces
    ocean_rows = ocean_ref.shape[0] // pieces
    first = first_ref[...].astype(F32) + first_came[...].astype(F32)
    second = second_ref[...].astype(F32) + second_came[...].astype(F32)
    total = jnp.concatenate([first, second], axis=0)
    for piece in range(pieces):
        lanes = slice(128 * piece, 128 * (piece + 1))
        atmos_ref[pl.ds(piece, atmos_rows, pieces), :] = total[:atmos_rows, lanes] * atmos_factor
        ocean_ref[pl.ds(piece, ocean_rows, pieces), :] = (
            total[atmos_rows : atmos_rows + ocean_rows, lanes] * ocean_factor
        )


def input_grad_kernel(
    stay_ref, give_ref, low_ref, high_ref, gpad_ref, wet_ref, terms_ref, atmos_ref, ocean_ref,
    grad_ref, sent_ref, *, cols,
):
    middle = jnp.where(on_ocean(), stay_ref[...], give_ref[...])
    pad = jnp.concatenate([low_ref[cols:, :], middle, high_ref[cols:, :]], axis=0)
    own = slice(cols, 3 * cols)
    convolve(pad, grad_ref, atmos_ref, ocean_ref, 0, True, cols)
    grad = gpad_ref[own, :].astype(F32) + grad_ref[...]
    grad_ref[...] = grad
    weighted = dot(terms_ref[8:16, :], grad, NT, HIGHEST)
    mixed = weighted[0:4] * wet_ref[0:1, own] + weighted[4:8] * wet_ref[1:2, own]
    sent_ref[...] = jnp.where(on_ocean(), mixed, weighted[0:4])


def next_kernel(
    stay_ref, give_ref, low_ref, high_ref, upad_ref, atmos_ref, ocean_ref,
    next_ref, mark_ref, second_ref, *, cols,
):
    middle = jnp.where(on_ocean(), give_ref[...], stay_ref[...])
    pad = jnp.concatenate([low_ref[0:cols, :], middle, high_ref[0:cols, :]], axis=0)
    own = slice(cols, 3 * cols)
    convolve(pad, second_ref, atmos_ref, ocean_ref, 1, False, cols)
    values = (upad_ref[own, :].astype(F32) + second_ref[...]).astype(BF16)
    next_ref[0] = values[:cols]
    next_ref[1] = values[cols:]
    mark_ref[...] = jnp.zeros_like(mark_ref)


def last_kernel(grad_ref, arrived_ref, wet_ref, terms_ref, out_ref, mark_ref, *, cols):
    own = slice(cols, 3 * cols)
    wet = wet_ref[0:1, own], wet_ref[1:2, own]
    arrived = jnp.where(on_ocean(), arrived_ref[...] * wet_ref[2:3, own], arrived_ref[...])
    added = spread(arrived, wet, on_ocean(), terms_ref[0:8, :])
    values = (grad_ref[...] + added).astype(BF16)
    out_ref[0] = values[:cols]
    out_ref[1] = values[cols:]
    mark_ref[...] = jnp.zeros_like(mark_ref)


def swapped(value, axis, mask):
    pairs = [(source, source ^ mask) for source in range(lax.axis_size(axis))]
    return lax.ppermute(value, axis, pairs)


def halo(up, down):
    count = lax.axis_size("lat")
    forward = [(i, i + 1) for i in range(count - 1)]
    backward = [(target, source) for source, target in forward]
    return lax.ppermute(up, "lat", forward), lax.ppermute(down, "lat", backward)


def local(
    fields,
    cotangent,
    ocean_kernels,
    atmos_kernels,
    ocean_surface,
    ocean_coupling,
    atmos_flux,
    atmos_coupling,
    row_map,
    wet_mask,
):
    x, g = fields[0], cotangent[0]
    bands, cols, channels = x.shape
    narrow = channels // 2
    cells = bands * cols
    count = lax.axis_size("lat")
    is_ocean = lax.axis_index("grp") == 0
    atmos_factor = 1.0 / math.sqrt(bands * count * cols)
    ocean_factor = 1.0 / math.sqrt(bands * count * 2 * cols)
    bound = functools.partial

    blank = jnp.zeros((4, narrow), BF16)
    gap = jnp.zeros((4, channels), BF16)
    surface = ocean_surface.T
    ocean_terms = jnp.concatenate(
        [
            jnp.concatenate([surface, blank], axis=1),
            jnp.concatenate([blank, surface], axis=1),
            jnp.concatenate([ocean_coupling, blank], axis=1),
            jnp.concatenate([blank, ocean_coupling], axis=1),
        ],
        axis=0,
    )
    atmos_terms = jnp.concatenate([atmos_flux.T, gap, atmos_coupling, gap], axis=0)
    terms = jnp.where(is_ocean, ocean_terms, atmos_terms).astype(F32)

    edge = shape((2 * cols + 16, channels), BF16)
    kept = shape(x.shape, BF16)
    half = shape((cells, channels), BF16)
    up, down, own_early = call(
        bound(pack_kernel, cols=cols),
        [edge, edge, half],
        [x, g, wet_mask],
        [IN_PLACE] * 3,
        [
            pltpu.VMEM(x.shape, BF16),
            pltpu.VMEM(x.shape, BF16),
            pltpu.VMEM(wet_mask.shape, jnp.int32),
            pltpu.SemaphoreType.DMA((3,)),
        ],
        name="pack",
        limit=PACK_VMEM,
    )
    low, high = halo(up, down)
    other_early = swapped(own_early, "grp", 1)
    wide = -(-narrow // 128) * 128
    x, g, own_wet, atmos_flat, ocean_flat = call(
        bound(hold_kernel, cols=cols),
        [
            kept,
            kept,
            shape((16, channels), BF16),
            shape((18, channels, channels), BF16),
            shape((18, wide, narrow), BF16),
        ],
        [
            x,
            g,
            wet_mask,
            atmos_kernels.reshape(18, channels, channels),
            ocean_kernels.reshape(18, narrow, narrow),
        ],
        [IN_PLACE] * 5,
        [
            pltpu.VMEM(wet_mask.shape, jnp.int32),
            pltpu.SemaphoreType.DMA((3,)),
            pltpu.SemaphoreType.DMA,
        ],
        flops=PACE * 10**8,
        name="hold",
        limit=HOLD_VMEM,
    )
    pad = shape((2 * cells, channels), BF16)
    xpad, gpad, wet, edges, sent = call(
        bound(outgoing_kernel, cols=cols),
        [pad, pad, shape((8, 2 * cells), F32), half, shape((4, 2 * cells), F32)],
        [x, g, low, high, own_wet, terms],
        name="outgoing",
    )
    arrived = swapped(sent, "grp", 1)
    other_edges = swapped(edges, "grp", 1)
    conv_cost = dict(flops=PACE * 9 * cells * channels * channels, moved=9 * channels * channels * 2)
    back = call(
        bound(back_kernel, cols=cols),
        shape((cells, channels), F32),
        [gpad, atmos_flat, ocean_flat],
        **conv_cost,
        name="back",
    )
    upad, stay, give, up, down = call(
        bound(first_kernel, cols=cols),
        [pad, half, half, half, half],
        [xpad, wet, arrived, terms, back, atmos_flat, ocean_flat],
        None,
        [pltpu.VMEM((cells, channels), F32)],
        **conv_cost,
        name="first",
    )
    late = swapped(give, "grp", 1)
    low, high = halo(up, down)

    atmos_rows = 9 * channels // count
    ocean_rows = 9 * narrow // count
    chunked = count == 16 and 9 * channels % (8 * count) == 0 and ocean_rows % 2 == 0
    tall = -(-(atmos_rows + ocean_rows // 2) // 16) * 16
    spare = max(0, 2 * (tall - atmos_rows) - ocean_rows) if chunked else 0
    ocean_tall = 9 * narrow + -(-spare // 8) * 8
    sums = [shape((9 * channels, channels), F32), shape((wide // 128, ocean_tall, 128), F32)]
    atmos_sum, ocean_sum = call(
        bound(own_grads_kernel, cols=cols), sums, [upad, gpad, stay], **conv_cost, name="own_grads"
    )
    inputs = [other_early, other_edges, late, sent, atmos_coupling, atmos_sum, ocean_sum]
    if chunked:
        part = shape((count // 2, tall, channels), BF16)
        keep, send = call(
            bound(grads_kernel, cols=cols, chunks=count),
            [part, part],
            inputs + [low, high],
            [WHOLE] * len(inputs) + [ANYWHERE] * 2,
            [pltpu.VMEM(out.shape, F32) for out in sums],
            **conv_cost,
            name="grads",
        )
        came = swapped(send, "lat", 1)
    else:
        atmos_all, ocean_all = call(
            bound(plain_grads_kernel, cols=cols), sums, inputs, **conv_cost, name="grads"
        )

    grad, sent_back = call(
        bound(input_grad_kernel, cols=cols),
        [shape((cells, channels), F32), shape((4, cells), F32)],
        [stay, give, low, high, gpad, wet, terms, atmos_flat, ocean_flat],
        **conv_cost,
        name="input_grad",
    )
    returned = swapped(sent_back, "grp", 1)
    mark = shape((8, 128), F32)
    next_field, next_mark = call(
        bound(next_kernel, cols=cols),
        [shape(x.shape, BF16), mark],
        [stay, give, low, high, upad, atmos_flat, ocean_flat],
        None,
        [pltpu.VMEM((cells, channels), F32)],
        **conv_cost,
        name="next",
    )
    field_grad, last_mark = call(
        bound(last_kernel, cols=cols),
        [shape(x.shape, BF16), mark],
        [grad, returned, wet, terms],
        name="last",
    )

    if chunked:
        atmos_chunk, ocean_chunk = call(
            bound(finish_kernel, atmos_factor=atmos_factor, ocean_factor=ocean_factor),
            [
                shape((atmos_rows * channels // 128, 128), F32),
                shape((ocean_rows * narrow // 128, 128), F32),
            ],
            scatter_sum(keep, came, sent_back, (next_mark, last_mark)),
            name="finish",
        )
        atmos_total, ocean_total = atmos_chunk.reshape(-1), ocean_chunk.reshape(-1)
    else:
        atmos_total = atmos_factor * lax.psum_scatter(
            atmos_all.reshape(-1), "lat", scatter_dimension=0, tiled=True
        )
        ocean_all = jnp.concatenate([ocean_all[piece] for piece in range(wide // 128)], axis=1)
        ocean_total = ocean_factor * lax.psum_scatter(
            ocean_all[:, :narrow].reshape(-1), "lat", scatter_dimension=0, tiled=True
        )
    return (next_field[None], field_grad[None], ocean_total, atmos_total)


def solution(mesh):
    in_specs = (
        P("grp", "lat", None, None),
        P("grp", "lat", None, None),
        P(),
        P(),
        P(),
        P(),
        P(),
        P(),
        P("lat"),
        P("lat", None),
    )
    out_specs = (
        P("grp", "lat", None, None),
        P("grp", "lat", None, None),
        P(("grp", "lat")),
        P(("grp", "lat")),
    )
    return jax.shard_map(local, mesh=mesh, in_specs=in_specs, out_specs=out_specs, check_vma=False)
```

```python
import functools
import math

import jax
import jax.numpy as jnp
from jax import lax
from jax.experimental import pallas as pl
from jax.experimental.pallas import tpu as pltpu
from jax.sharding import PartitionSpec as P

HIGHEST = lax.Precision.HIGHEST
GELU_SCALE = 0.7978845608028654
GELU_CUBIC = 0.044715
F32 = jnp.float32
BF16 = jnp.bfloat16
WHOLE = pl.BlockSpec(memory_space=pltpu.VMEM)
IN_PLACE = pl.BlockSpec(memory_space=pltpu.HBM)
ANYWHERE = pl.BlockSpec(memory_space=pl.ANY)
VMEM_LIMIT = 20 * 1024 * 1024
PACE = 8
PACK_VMEM = 62 * 1024 * 1024
HOLD_VMEM = 42 * 1024 * 1024

NN = (((1,), (0,)), ((), ()))
NT = (((1,), (1,)), ((), ()))
TN = (((0,), (0,)), ((), ()))


def shape(dims, kind):
    return jax.ShapeDtypeStruct(dims, kind)


def call(kernel, outs, inputs, in_specs=None, scratch=(), flops=0, moved=0, name=None, limit=VMEM_LIMIT, out_spec=WHOLE):
    return pl.pallas_call(
        kernel,
        out_shape=outs,
        in_specs=in_specs or [WHOLE] * len(inputs),
        out_specs=jax.tree.map(lambda _: out_spec, outs),
        scratch_shapes=list(scratch),
        compiler_params=pltpu.CompilerParams(vmem_limit_bytes=limit),
        cost_estimate=pl.CostEstimate(flops=flops, bytes_accessed=moved, transcendentals=0),
        name=name,
    )(*inputs)


def on_ocean():
    return lax.axis_index("grp") == 0


def dot(left, right, dims=NN, precision=None):
    return lax.dot_general(left, right, dims, precision=precision, preferred_element_type=F32)


def moved_cells(values, axis, cols):
    count = values.shape[axis]
    place = lax.rem(lax.broadcasted_iota(jnp.int32, values.shape, axis), cols)
    before = jnp.where(place == 0, 0.0, pltpu.roll(values, 1, axis))
    after = jnp.where(place == cols - 1, 0.0, pltpu.roll(values, count - 1, axis))
    return before, after


def wet_halves(wet, cols, channels):
    source = lax.broadcasted_iota(jnp.int32, (2 * cols, 2 * cols), 0)
    target = lax.broadcasted_iota(jnp.int32, (2 * cols, 2 * cols), 1)
    wanted = 2 * lax.rem(target, cols) + jnp.where(target >= cols, 1, 0)
    chooser = (source == wanted).astype(F32).astype(BF16)
    padded = jnp.concatenate([wet.astype(F32), jnp.zeros((14, 2 * cols), F32)], axis=0)
    apart = dot(padded.astype(BF16), chooser)
    return jnp.concatenate([apart, jnp.zeros((16, channels - 2 * cols), F32)], axis=1)


def own_bit(bit):
    return lax.rem(lax.shift_right_logical(lax.axis_index("lat"), bit), 2)


def pack_kernel(
    x_any, g_any, wet_any, near_ref, far_ref, early_ref, own_ref, x_ref, g_ref, wet_ref, sems, *, cols
):
    pairs = ((wet_any, wet_ref), (x_any, x_ref), (g_any, g_ref))
    copies = [pltpu.make_async_copy(*pair, sems.at[index]) for index, pair in enumerate(pairs)]
    for copy in copies:
        copy.start()
    core = own_bit(0)
    copies[0].wait()
    wide = wet_halves(wet_ref[...], cols, x_ref.shape[2])
    other = pltpu.roll(wide, 15, 0)
    own_ref[4 * cols :, :] = wide.astype(BF16)
    far_ref[2 * cols :, :] = jnp.where(core == 0, wide, other).astype(BF16)
    near_ref[2 * cols :, :] = jnp.where(core == 0, other, wide).astype(BF16)
    copies[1].wait()
    copies[2].wait()
    for part, ref in enumerate((x_ref, g_ref)):
        far_ref[part * cols : (part + 1) * cols, :] = ref[core]
        near_ref[part * cols : (part + 1) * cols, :] = ref[1 - core]
        own_ref[2 * part * cols : (2 * part + 1) * cols, :] = ref[0]
        own_ref[(2 * part + 1) * cols : (2 * part + 2) * cols, :] = ref[1]
    for row in range(2):
        early_ref[row * cols : (row + 1) * cols, :] = jnp.where(on_ocean(), g_ref[row], x_ref[row])


def hold_kernel(own_in, atmos_any, ocean_any, own_ref, atmos_ref, ocean_ref, sem):
    narrow = ocean_ref.shape[2]
    ocean_copy = pltpu.make_async_copy(ocean_any, ocean_ref.at[:, pl.ds(0, narrow), :], sem)
    atmos_copy = pltpu.make_async_copy(atmos_any, atmos_ref, sem)

    @pl.when(on_ocean())
    def _():
        ocean_copy.start()
        gap = ocean_ref.shape[1] - narrow
        if gap:
            ocean_ref[:, narrow:, :] = jnp.zeros((ocean_ref.shape[0], gap, narrow), BF16)

    @pl.when(jnp.logical_not(on_ocean()))
    def _():
        atmos_copy.start()

    own_ref[...] = own_in[...]

    @pl.when(on_ocean())
    def _():
        ocean_copy.wait()

    @pl.when(jnp.logical_not(on_ocean()))
    def _():
        atmos_copy.wait()


def low_and_high(near, far):
    core = own_bit(0)
    return jnp.where(core == 0, far, near), jnp.where(core == 0, near, far)


def outgoing_kernel(
    own_ref, near_ref, far_ref, terms_ref, xpad_ref, gpad_ref, wet_ref, edge_ref, sent_ref, *, cols
):
    low, high = low_and_high(near_ref[...], far_ref[...])
    for part, pad_ref in enumerate((xpad_ref, gpad_ref)):
        pad_ref[0:cols, :] = low[part * cols : (part + 1) * cols]
        pad_ref[cols : 3 * cols, :] = own_ref[2 * part * cols : 2 * (part + 1) * cols, :]
        pad_ref[3 * cols : 4 * cols, :] = high[part * cols : (part + 1) * cols]
    low_wet = low[2 * cols :].astype(F32)
    high_wet = high[2 * cols :].astype(F32)
    own_wet = own_ref[4 * cols :, :].astype(F32)
    halves = []
    for start in (0, cols):
        lanes = slice(start, start + cols)
        rows = (low_wet[0:1, lanes], own_wet[0:1, lanes], own_wet[1:2, lanes], high_wet[0:1, lanes])
        halves.append(jnp.concatenate(rows, axis=1))
    first_wet, second_wet = halves
    inverse = 1.0 / jnp.maximum(first_wet + second_wet, 1.0)
    wet_ref[0:1, :] = first_wet
    wet_ref[1:2, :] = second_wet
    wet_ref[2:3, :] = inverse
    wet_ref[3:8, :] = jnp.zeros((5, 4 * cols), F32)
    xpad = xpad_ref[...]
    projected = dot(terms_ref[0:8, :].astype(BF16), xpad, NT)
    mixed = (projected[0:4] * first_wet + projected[4:8] * second_wet) * inverse
    sent_ref[...] = jnp.where(on_ocean(), mixed, projected[0:4])
    edge_ref[0:cols, :] = jnp.where(on_ocean(), gpad_ref[0:cols, :], xpad_ref[0:cols, :])
    edge_ref[cols:, :] = jnp.where(on_ocean(), gpad_ref[3 * cols :, :], xpad_ref[3 * cols :, :])


def halves_apart(values, narrow):
    wide = -(-narrow // 128) * 128
    lane = lax.broadcasted_iota(jnp.int32, values.shape, 1)
    even = jnp.where(lane < narrow, values, 0.0)
    odd = jnp.where(lane < narrow, pltpu.roll(values, narrow, 1), 0.0)
    return even[:, :wide], odd[:, :wide]


def halves_with_columns(pad, cols):
    even, odd = halves_apart(pad.astype(F32), pad.shape[1] // 2)
    odd_before = moved_cells(odd, 0, cols)[0].astype(BF16)
    even_after = moved_cells(even, 0, cols)[1].astype(BF16)
    even, odd = even.astype(BF16), odd.astype(BF16)
    return (odd_before, even, odd), (even, odd, even_after)


def with_columns(pad, cols):
    before, after = moved_cells(pad.astype(F32), 0, cols)
    return before.astype(BF16), pad, after.astype(BF16)


def convolve(pad, out_ref, atmos_ref, ocean_ref, layer, flipped, cols):
    base = 9 * layer
    channels = atmos_ref.shape[2]
    wide, narrow = ocean_ref.shape[1:]
    rows = out_ref.shape[0]

    def summed(pick):
        total = None
        for row_tap in range(3):
            part = pick(row_tap, slice(cols * row_tap, cols * row_tap + rows))
            total = part if total is None else total + part
        return total

    @pl.when(on_ocean())
    def _():
        evens, odds = halves_with_columns(pad, cols)
        if flipped:

            def pick(row_tap, span):
                part = None
                for col_tap in range(3):
                    left = jnp.concatenate([evens[col_tap][span], odds[col_tap][span]], axis=0)
                    kernel = ocean_ref[base + 8 - (3 * row_tap + col_tap), 0:narrow, :]
                    piece = dot(left[:, :narrow], kernel, NT)
                    part = piece if part is None else part + piece
                return part

        else:
            even, odd = jnp.concatenate(evens, axis=1), jnp.concatenate(odds, axis=1)

            def pick(row_tap, span):
                first = base + 3 * row_tap
                kernel = ocean_ref[first : first + 3].reshape(3 * wide, narrow)
                return dot(jnp.concatenate([even[span], odd[span]], axis=0), kernel)

        total = summed(pick)
        out_ref[...] = jnp.concatenate([total[:rows], total[rows:]], axis=1)

    @pl.when(jnp.logical_not(on_ocean()))
    def _():
        taps = with_columns(pad, cols)
        if flipped:

            def pick(row_tap, span):
                part = None
                for col_tap in range(3):
                    piece = dot(taps[col_tap][span], atmos_ref[base + 8 - (3 * row_tap + col_tap)], NT)
                    part = piece if part is None else part + piece
                return part

        else:
            joined = jnp.concatenate(taps, axis=1)

            def pick(row_tap, span):
                first = base + 3 * row_tap
                return dot(joined[span], atmos_ref[first : first + 3].reshape(3 * channels, channels))

        out_ref[...] = summed(pick)


def back_kernel(gpad_ref, atmos_ref, ocean_ref, out_ref, *, cols):
    convolve(gpad_ref[...], out_ref, atmos_ref, ocean_ref, 1, True, cols)


def spread(arrived, wet, mixing, terms):
    first_wet, second_wet = wet
    both = jnp.concatenate([arrived * first_wet, arrived * second_wet], axis=0)
    alone = jnp.concatenate([arrived, jnp.zeros_like(arrived)], axis=0)
    return dot(jnp.where(mixing, both, alone), terms, TN, HIGHEST)


def first_kernel(
    xpad_ref, wet_ref, arrived_ref, terms_ref, back_ref, atmos_ref, ocean_ref,
    u_ref, stay_ref, give_ref, first_ref, *, cols,
):
    wet = wet_ref[0:1, :], wet_ref[1:2, :]
    coupled = spread(arrived_ref[...], wet, on_ocean(), terms_ref[8:16, :])
    u = (xpad_ref[...].astype(F32) + coupled).astype(BF16)
    u_ref[...] = u
    convolve(u, first_ref, atmos_ref, ocean_ref, 0, False, cols)
    first = first_ref[...]
    tangent = jnp.tanh(GELU_SCALE * (first + GELU_CUBIC * first * first * first))
    hidden = (0.5 * first * (1.0 + tangent)).astype(BF16)
    slope = 0.5 * (1.0 + tangent) + 0.5 * first * (1.0 - tangent * tangent) * GELU_SCALE * (
        1.0 + 3.0 * GELU_CUBIC * first * first
    )
    first_grad = (back_ref[...] * slope).astype(BF16)
    stay_ref[...] = jnp.where(on_ocean(), first_grad, hidden)
    give_ref[...] = jnp.where(on_ocean(), hidden, first_grad)


def grad_atmos(pad, own, pad_is_input, cols, store):
    rows = own.shape[0]
    if pad_is_input:
        middle = pad.T
        before, after = moved_cells(middle, 1, cols)
        lefts = [part.astype(BF16) for part in (before, middle, after)]
        right = own.astype(BF16)
        for tap in range(9):
            start = cols * (tap // 3)
            store(tap, dot(lefts[tap % 3][:, start : start + rows], right))
    else:
        left = own.T.astype(BF16)
        before, after = moved_cells(pad, 0, cols)
        rights = [part.astype(BF16) for part in (after, pad, before)]
        for tap in range(9):
            start = cols * (2 - tap // 3)
            store(tap, dot(left, rights[tap % 3][start : start + rows]))


def grad_ocean(pad, own, pad_is_input, cols, store):
    rows, channels = own.shape
    narrow = channels // 2

    if pad_is_input:
        middle = pad.T
        before, after = moved_cells(middle, 1, cols)
        even, odd = middle[:narrow].astype(BF16), middle[narrow:].astype(BF16)
        pairs = (
            (before[narrow:].astype(BF16), even),
            (even, odd),
            (odd, after[:narrow].astype(BF16)),
        )
        right = jnp.concatenate(halves_apart(own, narrow), axis=0).astype(BF16)
        for tap in range(9):
            start = cols * (tap // 3)
            pieces = [part[:, start : start + rows] for part in pairs[tap % 3]]
            store(tap, dot(jnp.concatenate(pieces, axis=1), right))
    else:
        turned = own.T.astype(BF16)
        left = jnp.concatenate([turned[:narrow], turned[narrow:]], axis=1)
        even, odd = halves_apart(pad, narrow)
        odd_before = moved_cells(odd, 0, cols)[0].astype(BF16)
        even_after = moved_cells(even, 0, cols)[1].astype(BF16)
        even, odd = even.astype(BF16), odd.astype(BF16)
        pairs = ((odd, even_after), (even, odd), (odd_before, even))
        for tap in range(9):
            start = cols * (2 - tap // 3)
            pieces = [part[start : start + rows] for part in pairs[tap % 3]]
            store(tap, dot(left, jnp.concatenate(pieces, axis=0)))


def store_into(out_ref):
    def store(tap, value):
        if len(out_ref.shape) == 2:
            rows = value.shape[0]
            out_ref[rows * tap : rows * (tap + 1), :] = value
        else:
            rows = value.shape[0]
            for piece in range(out_ref.shape[0]):
                lanes = slice(128 * piece, 128 * (piece + 1))
                out_ref[piece, rows * tap : rows * (tap + 1), :] = value[:, lanes]

    return store


def hidden_and_grad(stay_ref, give_ref):
    stay, give = stay_ref[...], give_ref[...]
    return jnp.where(on_ocean(), give, stay), jnp.where(on_ocean(), stay, give)


def own_grads_kernel(
    upad_ref, gpad_ref, stay_ref, give_ref, atmos_out, ocean_out, near_ref, far_ref, *, cols
):
    stay = stay_ref[...].astype(F32)
    core = own_bit(0)
    hidden, first_grad = hidden_and_grad(stay_ref, give_ref)
    for part, values in enumerate((hidden, first_grad)):
        target = slice(part * cols, (part + 1) * cols)
        far_ref[target, :] = jnp.where(core == 0, values[:cols], values[cols:])
        near_ref[target, :] = jnp.where(core == 0, values[cols:], values[:cols])

    @pl.when(on_ocean())
    def _():
        grad_ocean(upad_ref[...].astype(F32), stay, True, cols, store_into(ocean_out))

    @pl.when(jnp.logical_not(on_ocean()))
    def _():
        grad_atmos(gpad_ref[...].astype(F32), stay, False, cols, store_into(atmos_out))


def other_grads_kernel(
    early_ref, edge_ref, late_ref, sent_ref, coupling_ref, atmos_out, ocean_out, *, cols
):
    late = late_ref[...].astype(F32)
    early = jnp.concatenate([edge_ref[0:cols, :], early_ref[...], edge_ref[cols:, :]], axis=0).astype(F32)

    @pl.when(on_ocean())
    def _():
        added = dot(sent_ref[...], coupling_ref[...].astype(F32), TN, HIGHEST)
        other = (early + added).astype(BF16).astype(F32)
        grad_atmos(other, late, True, cols, store_into(atmos_out))

    @pl.when(jnp.logical_not(on_ocean()))
    def _():
        grad_ocean(early, late, False, cols, store_into(ocean_out))


def chunk_rows(keep_ref, send_ref, atmos_all, ocean_all, chunks):
    channels = keep_ref.shape[2]
    pieces = ocean_all.shape[0]
    atmos_rows = atmos_all.shape[0] // chunks
    ocean_rows = atmos_rows // 2
    taken = keep_ref.shape[1] - atmos_rows
    core = lax.rem(lax.axis_index("lat"), 2)
    blank = jnp.zeros((taken, channels - 128 * pieces), F32)
    for out_ref, side in ((send_ref, 1 - core), (keep_ref, core)):
        for pair in range(chunks // 2):
            start = pl.multiple_of(atmos_rows * (2 * pair + side), 8)
            upper = atmos_all[pl.ds(start, atmos_rows), :]
            start = ocean_rows * (2 * pair + side)
            halves = []
            for odd in range(2):
                parts = [ocean_all.at[piece][pl.ds(start + odd, taken, 2), :] for piece in range(pieces)]
                halves.append(jnp.concatenate(parts + [blank], axis=1))
            lower = halves[0] + pltpu.roll(halves[1], channels // 2, 1)
            out_ref[pair] = jnp.concatenate([upper, lower], axis=0).astype(BF16)


def chunk_kernel(
    atmos_own, ocean_own, atmos_other, ocean_other, near_any, far_any, keep_ref, send_ref, *, chunks
):
    @pl.when(on_ocean())
    def _():
        chunk_rows(keep_ref, send_ref, atmos_other, ocean_own, chunks)

    @pl.when(jnp.logical_not(on_ocean()))
    def _():
        chunk_rows(keep_ref, send_ref, atmos_own, ocean_other, chunks)


def halve(keep_ref, came_ref, keep_out, send_out, bit, rows):
    own = own_bit(bit)
    for out_ref, side in ((send_out, 1 - own), (keep_out, own)):
        for outer in range(keep_ref.shape[0]):
            for inner in range(keep_ref.shape[2]):
                total = keep_ref[outer, side, inner, rows, :].astype(F32)
                total = total + came_ref[outer, side, inner, rows, :].astype(F32)
                out_ref[outer, inner] = total.astype(BF16)


def split_kernel(keep_ref, came_ref, done_ref, *outs, cuts):
    by_z = [ref.reshape(2, 2, 2, *keep_ref.shape[3:]) for ref in (keep_ref, came_ref)]
    start = 0
    for index, rows in enumerate(cuts):
        refs, bit = (by_z, 2) if index == 1 else ((keep_ref, came_ref), 1)
        halve(*refs, *outs[2 * index : 2 * index + 2], bit, slice(start, start + rows))
        start += rows


def halve_kernel(keep_ref, came_ref, *refs, bit):
    keep_out, send_out, mark_ref = refs[-3:]
    halve(keep_ref, came_ref, keep_out, send_out, bit, slice(None))
    mark_ref[...] = jnp.zeros_like(mark_ref)


MARK = shape((8, 128), F32)


def halved(keep, came, bit, dims, after):
    outer, inner, rows, channels = dims[0], dims[1], keep.shape[-2], keep.shape[-1]
    keep, came = (part.reshape(outer, 2, inner, rows, channels) for part in (keep, came))
    out = shape((outer, inner, rows, channels), BF16)
    return call(
        functools.partial(halve_kernel, bit=bit),
        [out, out, MARK],
        [keep, came, *after],
        [WHOLE] * 2 + [ANYWHERE] * len(after),
        moved=8 * outer * inner * rows * channels,
        name="halve",
    )


def scatter_sum(keep, came, done_before, done_next):
    pairs, tall, channels = keep.shape
    cuts = [16 * (tall // 16 * part // 17) for part in (6, 6)]
    cuts.append(tall - sum(cuts))
    outs = []
    for index, rows in enumerate(cuts):
        outs += [shape(((2, 2) if index == 1 else (4, 1)) + (rows, channels), BF16)] * 2
    keep, came = (part.reshape(4, 2, 1, tall, channels) for part in (keep, came))
    parts = call(
        functools.partial(split_kernel, cuts=cuts),
        outs,
        [keep, came, done_before],
        [WHOLE] * 2 + [ANYWHERE],
        moved=6 * pairs * tall * channels,
        name="split",
    )
    a_keep, a_send, b_keep, b_send, c_keep, c_send = parts
    a_came = swapped(a_send, "lat", 2)
    b_came = swapped(b_send, "lat", 4)
    c_came = swapped(c_send, "lat", 2)
    a_keep, a_send, mark = halved(a_keep, a_came, 2, (2, 1), done_next)
    a_came = swapped(a_send, "lat", 4)
    b_keep, b_send, mark = halved(b_keep, b_came, 3, (1, 2), [mark])
    b_came = swapped(b_send, "lat", 8)
    c_keep, c_send, mark = halved(c_keep, c_came, 2, (2, 1), [mark])
    c_came = swapped(c_send, "lat", 4)
    a_keep, a_send, mark = halved(a_keep, a_came, 3, (1, 1), [mark])
    a_came = swapped(a_send, "lat", 8)
    b_keep, b_send, mark = halved(b_keep, b_came, 1, (1, 1), [mark])
    b_came = swapped(b_send, "lat", 2)
    c_keep, c_send, mark = halved(c_keep, c_came, 3, (1, 1), [mark])
    c_came = swapped(c_send, "lat", 8)
    return [part.reshape(-1, channels) for part in (a_keep, a_came, b_keep, b_came, c_keep, c_came)]


def finish_kernel(*refs, atmos_factor, ocean_factor):
    parts, (atmos_ref, ocean_ref) = refs[:-2], refs[-2:]
    channels = parts[0].shape[1]
    pieces = channels // 128
    atmos_rows = atmos_ref.shape[0] // pieces
    ocean_rows = ocean_ref.shape[0] // pieces
    sums = [
        parts[index][...].astype(F32) + parts[index + 1][...].astype(F32)
        for index in range(0, len(parts), 2)
    ]
    total = jnp.concatenate(sums, axis=0)
    for piece in range(pieces):
        lanes = slice(128 * piece, 128 * (piece + 1))
        atmos_ref[pl.ds(piece, atmos_rows, pieces), :] = total[:atmos_rows, lanes] * atmos_factor
        ocean_ref[pl.ds(piece, ocean_rows, pieces), :] = (
            total[atmos_rows : atmos_rows + ocean_rows, lanes] * ocean_factor
        )


def input_grad_kernel(
    stay_ref, give_ref, near_ref, far_ref, gpad_ref, wet_ref, terms_ref, atmos_ref, ocean_ref,
    grad_ref, sent_ref, *, cols,
):
    middle = hidden_and_grad(stay_ref, give_ref)[1]
    low, high = low_and_high(near_ref[cols:, :], far_ref[cols:, :])
    pad = jnp.concatenate([low, middle, high], axis=0)
    own = slice(cols, 3 * cols)
    convolve(pad, grad_ref, atmos_ref, ocean_ref, 0, True, cols)
    grad = gpad_ref[own, :].astype(F32) + grad_ref[...]
    grad_ref[...] = grad
    weighted = dot(terms_ref[8:16, :], grad, NT, HIGHEST)
    mixed = weighted[0:4] * wet_ref[0:1, own] + weighted[4:8] * wet_ref[1:2, own]
    sent_ref[...] = jnp.where(on_ocean(), mixed, weighted[0:4])


def next_kernel(
    stay_ref, give_ref, near_ref, far_ref, upad_ref, atmos_ref, ocean_ref,
    next_ref, mark_ref, second_ref, *, cols,
):
    middle = hidden_and_grad(stay_ref, give_ref)[0]
    low, high = low_and_high(near_ref[0:cols, :], far_ref[0:cols, :])
    pad = jnp.concatenate([low, middle, high], axis=0)
    own = slice(cols, 3 * cols)
    convolve(pad, second_ref, atmos_ref, ocean_ref, 1, False, cols)
    values = (upad_ref[own, :].astype(F32) + second_ref[...]).astype(BF16)
    next_ref[0] = values[:cols]
    next_ref[1] = values[cols:]
    mark_ref[...] = jnp.zeros_like(mark_ref)


def last_kernel(grad_ref, arrived_ref, wet_ref, terms_ref, out_ref, mark_ref, *, cols):
    own = slice(cols, 3 * cols)
    wet = wet_ref[0:1, own], wet_ref[1:2, own]
    arrived = jnp.where(on_ocean(), arrived_ref[...] * wet_ref[2:3, own], arrived_ref[...])
    added = spread(arrived, wet, on_ocean(), terms_ref[0:8, :])
    values = (grad_ref[...] + added).astype(BF16)
    out_ref[0] = values[:cols]
    out_ref[1] = values[cols:]
    mark_ref[...] = jnp.zeros_like(mark_ref)


def swapped(value, axis, mask):
    pairs = [(source, source ^ mask) for source in range(lax.axis_size(axis))]
    return lax.ppermute(value, axis, pairs)


def halo(near, far):
    count = lax.axis_size("lat")
    pairs = [(i, i + 1 if i % 2 else i - 1) for i in range(1, count - 1)]
    return swapped(near, "lat", 1), lax.ppermute(far, "lat", pairs)


def local(
    fields,
    cotangent,
    ocean_kernels,
    atmos_kernels,
    ocean_surface,
    ocean_coupling,
    atmos_flux,
    atmos_coupling,
    row_map,
    wet_mask,
):
    x, g = fields[0], cotangent[0]
    bands, cols, channels = x.shape
    narrow = channels // 2
    cells = bands * cols
    count = lax.axis_size("lat")
    is_ocean = lax.axis_index("grp") == 0
    atmos_factor = 1.0 / math.sqrt(bands * count * cols)
    ocean_factor = 1.0 / math.sqrt(bands * count * 2 * cols)
    bound = functools.partial

    blank = jnp.zeros((4, narrow), BF16)
    gap = jnp.zeros((4, channels), BF16)
    surface = ocean_surface.T
    ocean_terms = jnp.concatenate(
        [
            jnp.concatenate([surface, blank], axis=1),
            jnp.concatenate([blank, surface], axis=1),
            jnp.concatenate([ocean_coupling, blank], axis=1),
            jnp.concatenate([blank, ocean_coupling], axis=1),
        ],
        axis=0,
    )
    atmos_terms = jnp.concatenate([atmos_flux.T, gap, atmos_coupling, gap], axis=0)
    terms = jnp.where(is_ocean, ocean_terms, atmos_terms).astype(F32)

    edge = shape((2 * cols + 16, channels), BF16)
    half = shape((cells, channels), BF16)
    near, far, own_early, own = call(
        bound(pack_kernel, cols=cols),
        [edge, edge, half, shape((2 * cells + 16, channels), BF16)],
        [x, g, wet_mask],
        [IN_PLACE] * 3,
        [
            pltpu.VMEM(x.shape, BF16),
            pltpu.VMEM(x.shape, BF16),
            pltpu.VMEM(wet_mask.shape, jnp.int32),
            pltpu.SemaphoreType.DMA((3,)),
        ],
        name="pack",
        limit=PACK_VMEM,
    )
    near, far = halo(near, far)
    other_early = swapped(own_early, "grp", 1)
    wide = -(-narrow // 128) * 128
    own, atmos_flat, ocean_flat = call(
        hold_kernel,
        [
            shape(own.shape, BF16),
            shape((18, channels, channels), BF16),
            shape((18, wide, narrow), BF16),
        ],
        [own, atmos_kernels.reshape(18, channels, channels), ocean_kernels.reshape(18, narrow, narrow)],
        [WHOLE, IN_PLACE, IN_PLACE],
        [pltpu.SemaphoreType.DMA],
        flops=PACE * 10**8,
        name="hold",
        limit=HOLD_VMEM,
    )
    pad = shape((2 * cells, channels), BF16)
    xpad, gpad, wet, edges, sent = call(
        bound(outgoing_kernel, cols=cols),
        [pad, pad, shape((8, 2 * cells), F32), half, shape((4, 2 * cells), F32)],
        [own, near, far, terms],
        name="outgoing",
    )
    arrived = swapped(sent, "grp", 1)
    other_edges = swapped(edges, "grp", 1)
    conv_cost = dict(flops=PACE * 9 * cells * channels * channels, moved=9 * channels * channels * 2)
    back = call(
        bound(back_kernel, cols=cols),
        shape((cells, channels), F32),
        [gpad, atmos_flat, ocean_flat],
        **conv_cost,
        name="back",
    )
    upad, stay, give = call(
        bound(first_kernel, cols=cols),
        [pad, half, half],
        [xpad, wet, arrived, terms, back, atmos_flat, ocean_flat],
        None,
        [pltpu.VMEM((cells, channels), F32)],
        **conv_cost,
        name="first",
    )
    late = swapped(give, "grp", 1)

    atmos_rows = 9 * channels // count
    ocean_rows = 9 * narrow // count
    chunked = count == 16 and 9 * channels % (8 * count) == 0 and ocean_rows % 2 == 0
    tall = -(-(atmos_rows + ocean_rows // 2) // 16) * 16
    spare = max(0, 2 * (tall - atmos_rows) - ocean_rows) if chunked else 0
    ocean_tall = 9 * narrow + -(-spare // 8) * 8
    sums = [shape((9 * channels, channels), F32), shape((wide // 128, ocean_tall, 128), F32)]
    atmos_sum, ocean_sum, near, far = call(
        bound(own_grads_kernel, cols=cols),
        [*sums, half, half],
        [upad, gpad, stay, give],
        **conv_cost,
        name="own_grads",
    )
    near, far = halo(near, far)
    atmos_other, ocean_other = call(
        bound(other_grads_kernel, cols=cols),
        sums,
        [other_early, other_edges, late, sent, atmos_coupling],
        **conv_cost,
        name="other_grads",
    )
    if chunked:
        part = shape((count // 2, tall, channels), BF16)
        keep, send = call(
            bound(chunk_kernel, chunks=count),
            [part, part],
            [atmos_sum, ocean_sum, atmos_other, ocean_other, near, far],
            [WHOLE] * 4 + [ANYWHERE] * 2,
            moved=4 * count * tall * channels,
            name="chunk",
        )
        came = swapped(send, "lat", 1)

    grad, sent_back = call(
        bound(input_grad_kernel, cols=cols),
        [shape((cells, channels), F32), shape((4, cells), F32)],
        [stay, give, near, far, gpad, wet, terms, atmos_flat, ocean_flat],
        **conv_cost,
        name="input_grad",
    )
    returned = swapped(sent_back, "grp", 1)
    next_field, next_mark = call(
        bound(next_kernel, cols=cols),
        [shape(x.shape, BF16), MARK],
        [stay, give, near, far, upad, atmos_flat, ocean_flat],
        None,
        [pltpu.VMEM((cells, channels), F32)],
        **conv_cost,
        name="next",
    )
    field_grad, last_mark = call(
        bound(last_kernel, cols=cols),
        [shape(x.shape, BF16), MARK],
        [grad, returned, wet, terms],
        name="last",
    )

    if chunked:
        atmos_chunk, ocean_chunk = call(
            bound(finish_kernel, atmos_factor=atmos_factor, ocean_factor=ocean_factor),
            [
                shape((atmos_rows * channels // 128, 128), F32),
                shape((ocean_rows * narrow // 128, 128), F32),
            ],
            scatter_sum(keep, came, sent_back, (next_mark, last_mark)),
            name="finish",
        )
        atmos_total, ocean_total = atmos_chunk.reshape(-1), ocean_chunk.reshape(-1)
    else:
        atmos_all = jnp.where(is_ocean, atmos_other, atmos_sum)
        ocean_all = jnp.where(is_ocean, ocean_sum, ocean_other)
        atmos_total = atmos_factor * lax.psum_scatter(
            atmos_all.reshape(-1), "lat", scatter_dimension=0, tiled=True
        )
        ocean_all = jnp.concatenate([ocean_all[piece] for piece in range(wide // 128)], axis=1)
        ocean_total = ocean_factor * lax.psum_scatter(
            ocean_all[:, :narrow].reshape(-1), "lat", scatter_dimension=0, tiled=True
        )
    return (next_field[None], field_grad[None], ocean_total, atmos_total)


def solution(mesh):
    in_specs = (
        P("grp", "lat", None, None),
        P("grp", "lat", None, None),
        P(),
        P(),
        P(),
        P(),
        P(),
        P(),
        P("lat"),
        P("lat", None),
    )
    out_specs = (
        P("grp", "lat", None, None),
        P("grp", "lat", None, None),
        P(("grp", "lat")),
        P(("grp", "lat")),
    )
    return jax.shard_map(local, mesh=mesh, in_specs=in_specs, out_specs=out_specs, check_vma=False)
```

```python
import functools
import math

import jax
import jax.numpy as jnp
from jax import lax
from jax.experimental import pallas as pl
from jax.experimental.pallas import tpu as pltpu
from jax.sharding import PartitionSpec as P

HIGHEST = lax.Precision.HIGHEST
GELU_SCALE = 0.7978845608028654
GELU_CUBIC = 0.044715
F32 = jnp.float32
BF16 = jnp.bfloat16
WHOLE = pl.BlockSpec(memory_space=pltpu.VMEM)
IN_PLACE = pl.BlockSpec(memory_space=pltpu.HBM)
ANYWHERE = pl.BlockSpec(memory_space=pl.ANY)
VMEM_LIMIT = 20 * 1024 * 1024
PACE = 8
PACK_VMEM = 62 * 1024 * 1024
HOLD_VMEM = 42 * 1024 * 1024

NN = (((1,), (0,)), ((), ()))
NT = (((1,), (1,)), ((), ()))
TN = (((0,), (0,)), ((), ()))


def shape(dims, kind):
    return jax.ShapeDtypeStruct(dims, kind)


def call(kernel, outs, inputs, in_specs=None, scratch=(), flops=0, moved=0, name=None, limit=VMEM_LIMIT, out_spec=WHOLE):
    return pl.pallas_call(
        kernel,
        out_shape=outs,
        in_specs=in_specs or [WHOLE] * len(inputs),
        out_specs=jax.tree.map(lambda _: out_spec, outs),
        scratch_shapes=list(scratch),
        compiler_params=pltpu.CompilerParams(vmem_limit_bytes=limit),
        cost_estimate=pl.CostEstimate(flops=flops, bytes_accessed=moved, transcendentals=0),
        name=name,
    )(*inputs)


def on_ocean():
    return lax.axis_index("grp") == 0


def dot(left, right, dims=NN, precision=None):
    return lax.dot_general(left, right, dims, precision=precision, preferred_element_type=F32)


def moved_cells(values, axis, cols):
    count = values.shape[axis]
    place = lax.rem(lax.broadcasted_iota(jnp.int32, values.shape, axis), cols)
    before = jnp.where(place == 0, 0.0, pltpu.roll(values, 1, axis))
    after = jnp.where(place == cols - 1, 0.0, pltpu.roll(values, count - 1, axis))
    return before, after


def wet_halves(wet, cols, channels):
    source = lax.broadcasted_iota(jnp.int32, (2 * cols, 2 * cols), 0)
    target = lax.broadcasted_iota(jnp.int32, (2 * cols, 2 * cols), 1)
    wanted = 2 * lax.rem(target, cols) + jnp.where(target >= cols, 1, 0)
    chooser = (source == wanted).astype(F32).astype(BF16)
    padded = jnp.concatenate([wet.astype(F32), jnp.zeros((14, 2 * cols), F32)], axis=0)
    apart = dot(padded.astype(BF16), chooser)
    return jnp.concatenate([apart, jnp.zeros((16, channels - 2 * cols), F32)], axis=1)


def own_bit(bit):
    return lax.rem(lax.shift_right_logical(lax.axis_index("lat"), bit), 2)


def pack_kernel(
    x_any, g_any, wet_any, near_ref, far_ref, early_ref, own_ref, x_ref, g_ref, wet_ref, sems, *, cols
):
    pairs = ((wet_any, wet_ref), (x_any, x_ref), (g_any, g_ref))
    copies = [pltpu.make_async_copy(*pair, sems.at[index]) for index, pair in enumerate(pairs)]
    for copy in copies:
        copy.start()
    core = own_bit(0)
    copies[0].wait()
    wide = wet_halves(wet_ref[...], cols, x_ref.shape[2])
    other = pltpu.roll(wide, 15, 0)
    own_ref[4 * cols :, :] = wide.astype(BF16)
    far_ref[2 * cols :, :] = jnp.where(core == 0, wide, other).astype(BF16)
    near_ref[2 * cols :, :] = jnp.where(core == 0, other, wide).astype(BF16)
    copies[1].wait()
    copies[2].wait()
    for part, ref in enumerate((x_ref, g_ref)):
        far_ref[part * cols : (part + 1) * cols, :] = ref[core]
        near_ref[part * cols : (part + 1) * cols, :] = ref[1 - core]
        own_ref[2 * part * cols : (2 * part + 1) * cols, :] = ref[0]
        own_ref[(2 * part + 1) * cols : (2 * part + 2) * cols, :] = ref[1]
    for row in range(2):
        early_ref[row * cols : (row + 1) * cols, :] = jnp.where(on_ocean(), g_ref[row], x_ref[row])


def hold_kernel(own_in, atmos_any, ocean_any, own_ref, atmos_ref, ocean_ref, sem):
    narrow = ocean_ref.shape[2]
    ocean_copy = pltpu.make_async_copy(ocean_any, ocean_ref.at[:, pl.ds(0, narrow), :], sem)
    atmos_copy = pltpu.make_async_copy(atmos_any, atmos_ref, sem)

    @pl.when(on_ocean())
    def _():
        ocean_copy.start()
        gap = ocean_ref.shape[1] - narrow
        if gap:
            ocean_ref[:, narrow:, :] = jnp.zeros((ocean_ref.shape[0], gap, narrow), BF16)

    @pl.when(jnp.logical_not(on_ocean()))
    def _():
        atmos_copy.start()

    own_ref[...] = own_in[...]

    @pl.when(on_ocean())
    def _():
        ocean_copy.wait()

    @pl.when(jnp.logical_not(on_ocean()))
    def _():
        atmos_copy.wait()


def low_and_high(near, far):
    core = own_bit(0)
    return jnp.where(core == 0, far, near), jnp.where(core == 0, near, far)


def outgoing_kernel(
    own_ref, near_ref, far_ref, terms_ref, xpad_ref, gpad_ref, wet_ref, edge_ref, sent_ref, *, cols
):
    low, high = low_and_high(near_ref[...], far_ref[...])
    for part, pad_ref in enumerate((xpad_ref, gpad_ref)):
        pad_ref[0:cols, :] = low[part * cols : (part + 1) * cols]
        pad_ref[cols : 3 * cols, :] = own_ref[2 * part * cols : 2 * (part + 1) * cols, :]
        pad_ref[3 * cols : 4 * cols, :] = high[part * cols : (part + 1) * cols]
    low_wet = low[2 * cols :].astype(F32)
    high_wet = high[2 * cols :].astype(F32)
    own_wet = own_ref[4 * cols :, :].astype(F32)
    halves = []
    for start in (0, cols):
        lanes = slice(start, start + cols)
        rows = (low_wet[0:1, lanes], own_wet[0:1, lanes], own_wet[1:2, lanes], high_wet[0:1, lanes])
        halves.append(jnp.concatenate(rows, axis=1))
    first_wet, second_wet = halves
    inverse = 1.0 / jnp.maximum(first_wet + second_wet, 1.0)
    wet_ref[0:1, :] = first_wet
    wet_ref[1:2, :] = second_wet
    wet_ref[2:3, :] = inverse
    wet_ref[3:8, :] = jnp.zeros((5, 4 * cols), F32)
    xpad = xpad_ref[...]
    projected = dot(terms_ref[0:8, :].astype(BF16), xpad, NT)
    mixed = (projected[0:4] * first_wet + projected[4:8] * second_wet) * inverse
    sent_ref[...] = jnp.where(on_ocean(), mixed, projected[0:4])
    edge_ref[0:cols, :] = jnp.where(on_ocean(), gpad_ref[0:cols, :], xpad_ref[0:cols, :])
    edge_ref[cols:, :] = jnp.where(on_ocean(), gpad_ref[3 * cols :, :], xpad_ref[3 * cols :, :])


def halves_apart(values, narrow):
    wide = -(-narrow // 128) * 128
    lane = lax.broadcasted_iota(jnp.int32, values.shape, 1)
    even = jnp.where(lane < narrow, values, 0.0)
    odd = jnp.where(lane < narrow, pltpu.roll(values, narrow, 1), 0.0)
    return even[:, :wide], odd[:, :wide]


def halves_with_columns(pad, cols):
    even, odd = halves_apart(pad.astype(F32), pad.shape[1] // 2)
    odd_before = moved_cells(odd, 0, cols)[0].astype(BF16)
    even_after = moved_cells(even, 0, cols)[1].astype(BF16)
    even, odd = even.astype(BF16), odd.astype(BF16)
    return (odd_before, even, odd), (even, odd, even_after)


def with_columns(pad, cols):
    before, after = moved_cells(pad.astype(F32), 0, cols)
    return before.astype(BF16), pad, after.astype(BF16)


def convolve(pad, out_ref, atmos_ref, ocean_ref, layer, flipped, cols):
    base = 9 * layer
    channels = atmos_ref.shape[2]
    wide, narrow = ocean_ref.shape[1:]
    rows = out_ref.shape[0]

    def summed(pick):
        total = None
        for row_tap in range(3):
            part = pick(row_tap, slice(cols * row_tap, cols * row_tap + rows))
            total = part if total is None else total + part
        return total

    @pl.when(on_ocean())
    def _():
        evens, odds = halves_with_columns(pad, cols)
        if flipped:

            def pick(row_tap, span):
                part = None
                for col_tap in range(3):
                    left = jnp.concatenate([evens[col_tap][span], odds[col_tap][span]], axis=0)
                    kernel = ocean_ref[base + 8 - (3 * row_tap + col_tap), 0:narrow, :]
                    piece = dot(left[:, :narrow], kernel, NT)
                    part = piece if part is None else part + piece
                return part

        else:
            even, odd = jnp.concatenate(evens, axis=1), jnp.concatenate(odds, axis=1)

            def pick(row_tap, span):
                first = base + 3 * row_tap
                kernel = ocean_ref[first : first + 3].reshape(3 * wide, narrow)
                return dot(jnp.concatenate([even[span], odd[span]], axis=0), kernel)

        total = summed(pick)
        out_ref[...] = jnp.concatenate([total[:rows], total[rows:]], axis=1)

    @pl.when(jnp.logical_not(on_ocean()))
    def _():
        taps = with_columns(pad, cols)
        if flipped:

            def pick(row_tap, span):
                part = None
                for col_tap in range(3):
                    piece = dot(taps[col_tap][span], atmos_ref[base + 8 - (3 * row_tap + col_tap)], NT)
                    part = piece if part is None else part + piece
                return part

        else:
            joined = jnp.concatenate(taps, axis=1)

            def pick(row_tap, span):
                first = base + 3 * row_tap
                return dot(joined[span], atmos_ref[first : first + 3].reshape(3 * channels, channels))

        out_ref[...] = summed(pick)


def back_kernel(gpad_ref, atmos_ref, ocean_ref, out_ref, *, cols):
    convolve(gpad_ref[...], out_ref, atmos_ref, ocean_ref, 1, True, cols)


def spread(arrived, wet, mixing, terms):
    first_wet, second_wet = wet
    both = jnp.concatenate([arrived * first_wet, arrived * second_wet], axis=0)
    alone = jnp.concatenate([arrived, jnp.zeros_like(arrived)], axis=0)
    return dot(jnp.where(mixing, both, alone), terms, TN, HIGHEST)


def first_kernel(
    xpad_ref, wet_ref, arrived_ref, terms_ref, back_ref, atmos_ref, ocean_ref,
    u_ref, stay_ref, give_ref, first_ref, *, cols,
):
    wet = wet_ref[0:1, :], wet_ref[1:2, :]
    coupled = spread(arrived_ref[...], wet, on_ocean(), terms_ref[8:16, :])
    u = (xpad_ref[...].astype(F32) + coupled).astype(BF16)
    u_ref[...] = u
    convolve(u, first_ref, atmos_ref, ocean_ref, 0, False, cols)
    first = first_ref[...]
    tangent = jnp.tanh(GELU_SCALE * (first + GELU_CUBIC * first * first * first))
    hidden = (0.5 * first * (1.0 + tangent)).astype(BF16)
    slope = 0.5 * (1.0 + tangent) + 0.5 * first * (1.0 - tangent * tangent) * GELU_SCALE * (
        1.0 + 3.0 * GELU_CUBIC * first * first
    )
    first_grad = (back_ref[...] * slope).astype(BF16)
    stay_ref[...] = jnp.where(on_ocean(), first_grad, hidden)
    give_ref[...] = jnp.where(on_ocean(), hidden, first_grad)


def whole_pad(early_ref, edge_ref, cols):
    parts = [edge_ref[0:cols, :], early_ref[...], edge_ref[cols:, :]]
    return jnp.concatenate(parts, axis=0).astype(F32)


def grad_atmos(pad, own, cols, store):
    rows = own.shape[0]
    left = own.T.astype(BF16)
    before, after = moved_cells(pad, 0, cols)
    rights = [part.astype(BF16) for part in (after, pad, before)]
    for tap in range(9):
        start = cols * (2 - tap // 3)
        store(tap, dot(left, rights[tap % 3][start : start + rows]))


def grad_ocean(pad, own, pad_is_input, cols, store):
    rows, channels = own.shape
    narrow = channels // 2

    if pad_is_input:
        middle = pad.T
        before, after = moved_cells(middle, 1, cols)
        even, odd = middle[:narrow].astype(BF16), middle[narrow:].astype(BF16)
        pairs = (
            (before[narrow:].astype(BF16), even),
            (even, odd),
            (odd, after[:narrow].astype(BF16)),
        )
        right = jnp.concatenate(halves_apart(own, narrow), axis=0).astype(BF16)
        for tap in range(9):
            start = cols * (tap // 3)
            pieces = [part[:, start : start + rows] for part in pairs[tap % 3]]
            store(tap, dot(jnp.concatenate(pieces, axis=1), right))
    else:
        turned = own.T.astype(BF16)
        left = jnp.concatenate([turned[:narrow], turned[narrow:]], axis=1)
        even, odd = halves_apart(pad, narrow)
        odd_before = moved_cells(odd, 0, cols)[0].astype(BF16)
        even_after = moved_cells(even, 0, cols)[1].astype(BF16)
        even, odd = even.astype(BF16), odd.astype(BF16)
        pairs = ((odd, even_after), (even, odd), (odd_before, even))
        for tap in range(9):
            start = cols * (2 - tap // 3)
            pieces = [part[start : start + rows] for part in pairs[tap % 3]]
            store(tap, dot(left, jnp.concatenate(pieces, axis=0)))


def store_into(out_ref):
    def store(tap, value):
        if len(out_ref.shape) == 2:
            rows = value.shape[0]
            out_ref[rows * tap : rows * (tap + 1), :] = value
        else:
            rows = value.shape[0]
            for piece in range(out_ref.shape[0]):
                lanes = slice(128 * piece, 128 * (piece + 1))
                out_ref[piece, rows * tap : rows * (tap + 1), :] = value[:, lanes]

    return store


def hidden_and_grad(stay_ref, give_ref):
    stay, give = stay_ref[...], give_ref[...]
    return jnp.where(on_ocean(), give, stay), jnp.where(on_ocean(), stay, give)


def shifted_inputs(pad, cols):
    middle = pad.T
    before, after = moved_cells(middle, 1, cols)
    return [part.astype(BF16) for part in (before, middle, after)]


def own_grads_kernel(
    upad_ref, gpad_ref, stay_ref, give_ref, early_ref, edge_ref, sent_ref, coupling_ref,
    atmos_out, ocean_out, near_ref, far_ref, left_ref, *, cols,
):
    stay = stay_ref[...].astype(F32)
    core = own_bit(0)
    hidden, first_grad = hidden_and_grad(stay_ref, give_ref)
    for part, values in enumerate((hidden, first_grad)):
        target = slice(part * cols, (part + 1) * cols)
        far_ref[target, :] = jnp.where(core == 0, values[:cols], values[cols:])
        near_ref[target, :] = jnp.where(core == 0, values[cols:], values[:cols])

    @pl.when(on_ocean())
    def _():
        grad_ocean(upad_ref[...].astype(F32), stay, True, cols, store_into(ocean_out))
        added = dot(sent_ref[...], coupling_ref[...].astype(F32), TN, HIGHEST)
        other = (whole_pad(early_ref, edge_ref, cols) + added).astype(BF16).astype(F32)
        for tap, left in enumerate(shifted_inputs(other, cols)):
            left_ref[tap] = left

    @pl.when(jnp.logical_not(on_ocean()))
    def _():
        grad_atmos(gpad_ref[...].astype(F32), stay, cols, store_into(atmos_out))


def other_grads_kernel(left_ref, late_ref, early_ref, edge_ref, atmos_out, ocean_out, *, cols):
    rows = late_ref.shape[0]

    @pl.when(on_ocean())
    def _():
        store = store_into(atmos_out)
        for tap in range(9):
            start = cols * (tap // 3)
            store(tap, dot(left_ref[tap % 3, :, start : start + rows], late_ref[...]))

    @pl.when(jnp.logical_not(on_ocean()))
    def _():
        late = late_ref[...].astype(F32)
        grad_ocean(whole_pad(early_ref, edge_ref, cols), late, False, cols, store_into(ocean_out))


def chunk_rows(keep_ref, send_ref, atmos_all, ocean_all, chunks):
    channels = keep_ref.shape[2]
    pieces = ocean_all.shape[0]
    atmos_rows = atmos_all.shape[0] // chunks
    ocean_rows = atmos_rows // 2
    taken = keep_ref.shape[1] - atmos_rows
    core = lax.rem(lax.axis_index("lat"), 2)
    blank = jnp.zeros((taken, channels - 128 * pieces), F32)
    for out_ref, side in ((send_ref, 1 - core), (keep_ref, core)):
        for pair in range(chunks // 2):
            start = pl.multiple_of(atmos_rows * (2 * pair + side), 8)
            upper = atmos_all[pl.ds(start, atmos_rows), :]
            start = ocean_rows * (2 * pair + side)
            halves = []
            for odd in range(2):
                parts = [ocean_all.at[piece][pl.ds(start + odd, taken, 2), :] for piece in range(pieces)]
                halves.append(jnp.concatenate(parts + [blank], axis=1))
            lower = halves[0] + pltpu.roll(halves[1], channels // 2, 1)
            out_ref[pair] = jnp.concatenate([upper, lower], axis=0).astype(BF16)


def chunk_kernel(
    atmos_own, ocean_own, atmos_other, ocean_other, far_any, near_any, keep_ref, send_ref, *, chunks
):
    @pl.when(on_ocean())
    def _():
        chunk_rows(keep_ref, send_ref, atmos_other, ocean_own, chunks)

    @pl.when(jnp.logical_not(on_ocean()))
    def _():
        chunk_rows(keep_ref, send_ref, atmos_own, ocean_other, chunks)


def halve(keep_ref, came_ref, keep_out, send_out, bit, rows):
    own = own_bit(bit)
    for out_ref, side in ((send_out, 1 - own), (keep_out, own)):
        for outer in range(keep_ref.shape[0]):
            for inner in range(keep_ref.shape[2]):
                total = keep_ref[outer, side, inner, rows, :].astype(F32)
                total = total + came_ref[outer, side, inner, rows, :].astype(F32)
                out_ref[outer, inner] = total.astype(BF16)


def split_kernel(keep_ref, came_ref, done_ref, *outs, cuts):
    by_z = [ref.reshape(2, 2, 2, *keep_ref.shape[3:]) for ref in (keep_ref, came_ref)]
    halve(keep_ref, came_ref, *outs[:2], 1, slice(0, cuts[0]))
    halve(*by_z, *outs[2:4], 2, slice(cuts[0], cuts[0] + cuts[1]))


def rest_kernel(keep_ref, came_ref, *refs, start):
    keep_out, send_out, mark_ref = refs[-3:]
    halve(keep_ref, came_ref, keep_out, send_out, 1, slice(start, keep_ref.shape[3]))
    mark_ref[...] = jnp.zeros_like(mark_ref)


def halve_kernel(keep_ref, came_ref, *refs, bit):
    keep_out, send_out, mark_ref = refs[-3:]
    halve(keep_ref, came_ref, keep_out, send_out, bit, slice(None))
    mark_ref[...] = jnp.zeros_like(mark_ref)


MARK = shape((8, 128), F32)


def halved(keep, came, bit, dims, after):
    outer, inner, rows, channels = dims[0], dims[1], keep.shape[-2], keep.shape[-1]
    keep, came = (part.reshape(outer, 2, inner, rows, channels) for part in (keep, came))
    out = shape((outer, inner, rows, channels), BF16)
    return call(
        functools.partial(halve_kernel, bit=bit),
        [out, out, MARK],
        [keep, came, *after],
        [WHOLE] * 2 + [ANYWHERE] * len(after),
        moved=8 * outer * inner * rows * channels,
        name="halve",
    )


def scatter_sum(keep, came, done_before, done_next):
    pairs, tall, channels = keep.shape
    cuts = [16 * (tall // 16 * part // 17) for part in (8, 4)]
    start = sum(cuts)
    a_out, b_out = shape((4, 1, cuts[0], channels), BF16), shape((2, 2, cuts[1], channels), BF16)
    c_out = shape((4, 1, tall - start, channels), BF16)
    keep, came = (part.reshape(4, 2, 1, tall, channels) for part in (keep, came))
    a_keep, a_send, b_keep, b_send = call(
        functools.partial(split_kernel, cuts=cuts),
        [a_out, a_out, b_out, b_out],
        [keep, came, done_before],
        [WHOLE] * 2 + [ANYWHERE],
        moved=6 * pairs * tall * channels,
        name="split",
    )
    a_came = swapped(a_send, "lat", 2)
    b_came = swapped(b_send, "lat", 4)
    c_keep, c_send, mark = call(
        functools.partial(rest_kernel, start=start),
        [c_out, c_out, MARK],
        [keep, came, *done_next],
        [WHOLE] * 2 + [ANYWHERE] * len(done_next),
        moved=6 * pairs * (tall - start) * channels,
        name="rest",
    )
    c_came = swapped(c_send, "lat", 2)
    b_keep, b_send, mark = halved(b_keep, b_came, 3, (1, 2), [mark])
    b_came = swapped(b_send, "lat", 8)
    a_keep, a_send, mark = halved(a_keep, a_came, 2, (2, 1), [mark])
    a_came = swapped(a_send, "lat", 4)
    c_keep, c_send, mark = halved(c_keep, c_came, 2, (2, 1), [mark])
    c_came = swapped(c_send, "lat", 4)
    b_keep, b_send, mark = halved(b_keep, b_came, 1, (1, 1), [mark])
    b_came = swapped(b_send, "lat", 2)
    a_keep, a_send, mark = halved(a_keep, a_came, 3, (1, 1), [mark])
    a_came = swapped(a_send, "lat", 8)
    c_keep, c_send, mark = halved(c_keep, c_came, 3, (1, 1), [mark])
    c_came = swapped(c_send, "lat", 8)
    return [part.reshape(-1, channels) for part in (a_keep, a_came, b_keep, b_came, c_keep, c_came)]


def finish_kernel(*refs, atmos_factor, ocean_factor):
    parts, (atmos_ref, ocean_ref) = refs[:-2], refs[-2:]
    channels = parts[0].shape[1]
    pieces = channels // 128
    atmos_rows = atmos_ref.shape[0] // pieces
    ocean_rows = ocean_ref.shape[0] // pieces
    sums = [
        parts[index][...].astype(F32) + parts[index + 1][...].astype(F32)
        for index in range(0, len(parts), 2)
    ]
    total = jnp.concatenate(sums, axis=0)
    for piece in range(pieces):
        lanes = slice(128 * piece, 128 * (piece + 1))
        atmos_ref[pl.ds(piece, atmos_rows, pieces), :] = total[:atmos_rows, lanes] * atmos_factor
        ocean_ref[pl.ds(piece, ocean_rows, pieces), :] = (
            total[atmos_rows : atmos_rows + ocean_rows, lanes] * ocean_factor
        )


def input_grad_kernel(
    stay_ref, give_ref, near_ref, far_ref, gpad_ref, wet_ref, terms_ref, atmos_ref, ocean_ref,
    grad_ref, sent_ref, *, cols,
):
    middle = hidden_and_grad(stay_ref, give_ref)[1]
    low, high = low_and_high(near_ref[cols:, :], far_ref[cols:, :])
    pad = jnp.concatenate([low, middle, high], axis=0)
    own = slice(cols, 3 * cols)
    convolve(pad, grad_ref, atmos_ref, ocean_ref, 0, True, cols)
    grad = gpad_ref[own, :].astype(F32) + grad_ref[...]
    grad_ref[...] = grad
    weighted = dot(terms_ref[8:16, :], grad, NT, HIGHEST)
    mixed = weighted[0:4] * wet_ref[0:1, own] + weighted[4:8] * wet_ref[1:2, own]
    sent_ref[...] = jnp.where(on_ocean(), mixed, weighted[0:4])


def next_kernel(
    stay_ref, give_ref, near_ref, far_ref, upad_ref, atmos_ref, ocean_ref,
    next_ref, mark_ref, second_ref, *, cols,
):
    middle = hidden_and_grad(stay_ref, give_ref)[0]
    low, high = low_and_high(near_ref[0:cols, :], far_ref[0:cols, :])
    pad = jnp.concatenate([low, middle, high], axis=0)
    own = slice(cols, 3 * cols)
    convolve(pad, second_ref, atmos_ref, ocean_ref, 1, False, cols)
    values = (upad_ref[own, :].astype(F32) + second_ref[...]).astype(BF16)
    next_ref[0] = values[:cols]
    next_ref[1] = values[cols:]
    mark_ref[...] = jnp.zeros_like(mark_ref)


def last_kernel(grad_ref, arrived_ref, wet_ref, terms_ref, out_ref, mark_ref, *, cols):
    own = slice(cols, 3 * cols)
    wet = wet_ref[0:1, own], wet_ref[1:2, own]
    arrived = jnp.where(on_ocean(), arrived_ref[...] * wet_ref[2:3, own], arrived_ref[...])
    added = spread(arrived, wet, on_ocean(), terms_ref[0:8, :])
    values = (grad_ref[...] + added).astype(BF16)
    out_ref[0] = values[:cols]
    out_ref[1] = values[cols:]
    mark_ref[...] = jnp.zeros_like(mark_ref)


def swapped(value, axis, mask):
    pairs = [(source, source ^ mask) for source in range(lax.axis_size(axis))]
    return lax.ppermute(value, axis, pairs)


def halo(near, far):
    count = lax.axis_size("lat")
    pairs = [(i, i + 1 if i % 2 else i - 1) for i in range(1, count - 1)]
    far = lax.ppermute(far, "lat", pairs)
    return swapped(near, "lat", 1), far


def local(
    fields,
    cotangent,
    ocean_kernels,
    atmos_kernels,
    ocean_surface,
    ocean_coupling,
    atmos_flux,
    atmos_coupling,
    row_map,
    wet_mask,
):
    x, g = fields[0], cotangent[0]
    bands, cols, channels = x.shape
    narrow = channels // 2
    cells = bands * cols
    count = lax.axis_size("lat")
    is_ocean = lax.axis_index("grp") == 0
    atmos_factor = 1.0 / math.sqrt(bands * count * cols)
    ocean_factor = 1.0 / math.sqrt(bands * count * 2 * cols)
    bound = functools.partial

    blank = jnp.zeros((4, narrow), BF16)
    gap = jnp.zeros((4, channels), BF16)
    surface = ocean_surface.T
    ocean_terms = jnp.concatenate(
        [
            jnp.concatenate([surface, blank], axis=1),
            jnp.concatenate([blank, surface], axis=1),
            jnp.concatenate([ocean_coupling, blank], axis=1),
            jnp.concatenate([blank, ocean_coupling], axis=1),
        ],
        axis=0,
    )
    atmos_terms = jnp.concatenate([atmos_flux.T, gap, atmos_coupling, gap], axis=0)
    terms = jnp.where(is_ocean, ocean_terms, atmos_terms).astype(F32)

    edge = shape((2 * cols + 16, channels), BF16)
    half = shape((cells, channels), BF16)
    near, far, own_early, own = call(
        bound(pack_kernel, cols=cols),
        [edge, edge, half, shape((2 * cells + 16, channels), BF16)],
        [x, g, wet_mask],
        [IN_PLACE] * 3,
        [
            pltpu.VMEM(x.shape, BF16),
            pltpu.VMEM(x.shape, BF16),
            pltpu.VMEM(wet_mask.shape, jnp.int32),
            pltpu.SemaphoreType.DMA((3,)),
        ],
        name="pack",
        limit=PACK_VMEM,
    )
    near, far = halo(near, far)
    other_early = swapped(own_early, "grp", 1)
    wide = -(-narrow // 128) * 128
    own, atmos_flat, ocean_flat = call(
        hold_kernel,
        [
            shape(own.shape, BF16),
            shape((18, channels, channels), BF16),
            shape((18, wide, narrow), BF16),
        ],
        [own, atmos_kernels.reshape(18, channels, channels), ocean_kernels.reshape(18, narrow, narrow)],
        [WHOLE, IN_PLACE, IN_PLACE],
        [pltpu.SemaphoreType.DMA],
        flops=PACE * 10**8,
        name="hold",
        limit=HOLD_VMEM,
    )
    pad = shape((2 * cells, channels), BF16)
    xpad, gpad, wet, edges, sent = call(
        bound(outgoing_kernel, cols=cols),
        [pad, pad, shape((8, 2 * cells), F32), half, shape((4, 2 * cells), F32)],
        [own, near, far, terms],
        name="outgoing",
    )
    arrived = swapped(sent, "grp", 1)
    other_edges = swapped(edges, "grp", 1)
    conv_cost = dict(flops=PACE * 9 * cells * channels * channels, moved=9 * channels * channels * 2)
    back = call(
        bound(back_kernel, cols=cols),
        shape((cells, channels), F32),
        [gpad, atmos_flat, ocean_flat],
        **conv_cost,
        name="back",
    )
    upad, stay, give = call(
        bound(first_kernel, cols=cols),
        [pad, half, half],
        [xpad, wet, arrived, terms, back, atmos_flat, ocean_flat],
        None,
        [pltpu.VMEM((cells, channels), F32)],
        **conv_cost,
        name="first",
    )
    late = swapped(give, "grp", 1)

    atmos_rows = 9 * channels // count
    ocean_rows = 9 * narrow // count
    chunked = count == 16 and 9 * channels % (8 * count) == 0 and ocean_rows % 2 == 0
    tall = -(-(atmos_rows + ocean_rows // 2) // 16) * 16
    spare = max(0, 2 * (tall - atmos_rows) - ocean_rows) if chunked else 0
    ocean_tall = 9 * narrow + -(-spare // 8) * 8
    sums = [shape((9 * channels, channels), F32), shape((wide // 128, ocean_tall, 128), F32)]
    atmos_sum, ocean_sum, near, far, lefts = call(
        bound(own_grads_kernel, cols=cols),
        [*sums, half, half, shape((3, channels, 2 * cells), BF16)],
        [upad, gpad, stay, give, other_early, other_edges, sent, atmos_coupling],
        **conv_cost,
        name="own_grads",
    )
    near, far = halo(near, far)
    atmos_other, ocean_other = call(
        bound(other_grads_kernel, cols=cols),
        sums,
        [lefts, late, other_early, other_edges],
        **conv_cost,
        name="other_grads",
    )
    if chunked:
        part = shape((count // 2, tall, channels), BF16)
        keep, send = call(
            bound(chunk_kernel, chunks=count),
            [part, part],
            [atmos_sum, ocean_sum, atmos_other, ocean_other, far, near],
            [WHOLE] * 4 + [ANYWHERE] * 2,
            moved=4 * count * tall * channels,
            name="chunk",
        )
        came = swapped(send, "lat", 1)

    grad, sent_back = call(
        bound(input_grad_kernel, cols=cols),
        [shape((cells, channels), F32), shape((4, cells), F32)],
        [stay, give, near, far, gpad, wet, terms, atmos_flat, ocean_flat],
        **conv_cost,
        name="input_grad",
    )
    returned = swapped(sent_back, "grp", 1)
    next_field, next_mark = call(
        bound(next_kernel, cols=cols),
        [shape(x.shape, BF16), MARK],
        [stay, give, near, far, upad, atmos_flat, ocean_flat],
        None,
        [pltpu.VMEM((cells, channels), F32)],
        **conv_cost,
        name="next",
    )
    field_grad, last_mark = call(
        bound(last_kernel, cols=cols),
        [shape(x.shape, BF16), MARK],
        [grad, returned, wet, terms],
        name="last",
    )

    if chunked:
        atmos_chunk, ocean_chunk = call(
            bound(finish_kernel, atmos_factor=atmos_factor, ocean_factor=ocean_factor),
            [
                shape((atmos_rows * channels // 128, 128), F32),
                shape((ocean_rows * narrow // 128, 128), F32),
            ],
            scatter_sum(keep, came, sent_back, (next_mark, last_mark)),
            name="finish",
        )
        atmos_total, ocean_total = atmos_chunk.reshape(-1), ocean_chunk.reshape(-1)
    else:
        atmos_all = jnp.where(is_ocean, atmos_other, atmos_sum)
        ocean_all = jnp.where(is_ocean, ocean_sum, ocean_other)
        atmos_total = atmos_factor * lax.psum_scatter(
            atmos_all.reshape(-1), "lat", scatter_dimension=0, tiled=True
        )
        ocean_all = jnp.concatenate([ocean_all[piece] for piece in range(wide // 128)], axis=1)
        ocean_total = ocean_factor * lax.psum_scatter(
            ocean_all[:, :narrow].reshape(-1), "lat", scatter_dimension=0, tiled=True
        )
    return (next_field[None], field_grad[None], ocean_total, atmos_total)


def solution(mesh):
    in_specs = (
        P("grp", "lat", None, None),
        P("grp", "lat", None, None),
        P(),
        P(),
        P(),
        P(),
        P(),
        P(),
        P("lat"),
        P("lat", None),
    )
    out_specs = (
        P("grp", "lat", None, None),
        P("grp", "lat", None, None),
        P(("grp", "lat")),
        P(("grp", "lat")),
    )
    return jax.shard_map(local, mesh=mesh, in_specs=in_specs, out_specs=out_specs, check_vma=False)
```

```python
import functools
import math

import jax
import jax.numpy as jnp
from jax import lax
from jax.experimental import pallas as pl
from jax.experimental.pallas import tpu as pltpu
from jax.sharding import PartitionSpec as P

HIGHEST = lax.Precision.HIGHEST
GELU_SCALE = 0.7978845608028654
GELU_CUBIC = 0.044715
F32 = jnp.float32
BF16 = jnp.bfloat16
WHOLE = pl.BlockSpec(memory_space=pltpu.VMEM)
IN_PLACE = pl.BlockSpec(memory_space=pltpu.HBM)
ANYWHERE = pl.BlockSpec(memory_space=pl.ANY)
VMEM_LIMIT = 20 * 1024 * 1024
PACE = 8
PACK_VMEM = 62 * 1024 * 1024
HOLD_VMEM = 42 * 1024 * 1024

NN = (((1,), (0,)), ((), ()))
NT = (((1,), (1,)), ((), ()))
TN = (((0,), (0,)), ((), ()))


def shape(dims, kind):
    return jax.ShapeDtypeStruct(dims, kind)


def call(kernel, outs, inputs, in_specs=None, scratch=(), flops=0, moved=0, name=None, limit=VMEM_LIMIT, out_spec=WHOLE):
    return pl.pallas_call(
        kernel,
        out_shape=outs,
        in_specs=in_specs or [WHOLE] * len(inputs),
        out_specs=jax.tree.map(lambda _: out_spec, outs),
        scratch_shapes=list(scratch),
        compiler_params=pltpu.CompilerParams(vmem_limit_bytes=limit),
        cost_estimate=pl.CostEstimate(flops=flops, bytes_accessed=moved, transcendentals=0),
        name=name,
    )(*inputs)


def on_ocean():
    return lax.axis_index("grp") == 0


def dot(left, right, dims=NN, precision=None):
    return lax.dot_general(left, right, dims, precision=precision, preferred_element_type=F32)


def moved_cells(values, axis, cols):
    count = values.shape[axis]
    place = lax.rem(lax.broadcasted_iota(jnp.int32, values.shape, axis), cols)
    before = jnp.where(place == 0, 0.0, pltpu.roll(values, 1, axis))
    after = jnp.where(place == cols - 1, 0.0, pltpu.roll(values, count - 1, axis))
    return before, after


def wet_halves(wet, cols, channels):
    source = lax.broadcasted_iota(jnp.int32, (2 * cols, 2 * cols), 0)
    target = lax.broadcasted_iota(jnp.int32, (2 * cols, 2 * cols), 1)
    wanted = 2 * lax.rem(target, cols) + jnp.where(target >= cols, 1, 0)
    chooser = (source == wanted).astype(F32).astype(BF16)
    padded = jnp.concatenate([wet.astype(F32), jnp.zeros((14, 2 * cols), F32)], axis=0)
    apart = dot(padded.astype(BF16), chooser)
    return jnp.concatenate([apart, jnp.zeros((16, channels - 2 * cols), F32)], axis=1)


def own_bit(bit):
    return lax.rem(lax.shift_right_logical(lax.axis_index("lat"), bit), 2)


def pack_kernel(
    x_any, g_any, wet_any, near_ref, far_ref, early_ref, own_ref, x_ref, g_ref, wet_ref, sems, *, cols
):
    pairs = ((wet_any, wet_ref), (x_any, x_ref), (g_any, g_ref))
    copies = [pltpu.make_async_copy(*pair, sems.at[index]) for index, pair in enumerate(pairs)]
    for copy in copies:
        copy.start()
    core = own_bit(0)
    copies[0].wait()
    wide = wet_halves(wet_ref[...], cols, x_ref.shape[2])
    other = pltpu.roll(wide, 15, 0)
    own_ref[4 * cols :, :] = wide.astype(BF16)
    far_ref[2 * cols :, :] = jnp.where(core == 0, wide, other).astype(BF16)
    near_ref[2 * cols :, :] = jnp.where(core == 0, other, wide).astype(BF16)
    copies[1].wait()
    copies[2].wait()
    for part, ref in enumerate((x_ref, g_ref)):
        far_ref[part * cols : (part + 1) * cols, :] = ref[core]
        near_ref[part * cols : (part + 1) * cols, :] = ref[1 - core]
        own_ref[2 * part * cols : (2 * part + 1) * cols, :] = ref[0]
        own_ref[(2 * part + 1) * cols : (2 * part + 2) * cols, :] = ref[1]
    for row in range(2):
        early_ref[row * cols : (row + 1) * cols, :] = jnp.where(on_ocean(), g_ref[row], x_ref[row])


def hold_kernel(own_in, atmos_any, ocean_any, own_ref, atmos_ref, ocean_ref, sem):
    narrow = ocean_ref.shape[2]
    ocean_copy = pltpu.make_async_copy(ocean_any, ocean_ref.at[:, pl.ds(0, narrow), :], sem)
    atmos_copy = pltpu.make_async_copy(atmos_any, atmos_ref, sem)

    @pl.when(on_ocean())
    def _():
        ocean_copy.start()
        gap = ocean_ref.shape[1] - narrow
        if gap:
            ocean_ref[:, narrow:, :] = jnp.zeros((ocean_ref.shape[0], gap, narrow), BF16)

    @pl.when(jnp.logical_not(on_ocean()))
    def _():
        atmos_copy.start()

    own_ref[...] = own_in[...]

    @pl.when(on_ocean())
    def _():
        ocean_copy.wait()

    @pl.when(jnp.logical_not(on_ocean()))
    def _():
        atmos_copy.wait()


def low_and_high(near, far):
    core = own_bit(0)
    return jnp.where(core == 0, far, near), jnp.where(core == 0, near, far)


def outgoing_kernel(
    own_ref, near_ref, far_ref, terms_ref, xpad_ref, gpad_ref, wet_ref, edge_ref, sent_ref, *, cols
):
    low, high = low_and_high(near_ref[...], far_ref[...])
    for part, pad_ref in enumerate((xpad_ref, gpad_ref)):
        pad_ref[0:cols, :] = low[part * cols : (part + 1) * cols]
        pad_ref[cols : 3 * cols, :] = own_ref[2 * part * cols : 2 * (part + 1) * cols, :]
        pad_ref[3 * cols : 4 * cols, :] = high[part * cols : (part + 1) * cols]
    low_wet = low[2 * cols :].astype(F32)
    high_wet = high[2 * cols :].astype(F32)
    own_wet = own_ref[4 * cols :, :].astype(F32)
    halves = []
    for start in (0, cols):
        lanes = slice(start, start + cols)
        rows = (low_wet[0:1, lanes], own_wet[0:1, lanes], own_wet[1:2, lanes], high_wet[0:1, lanes])
        halves.append(jnp.concatenate(rows, axis=1))
    first_wet, second_wet = halves
    inverse = 1.0 / jnp.maximum(first_wet + second_wet, 1.0)
    wet_ref[0:1, :] = first_wet
    wet_ref[1:2, :] = second_wet
    wet_ref[2:3, :] = inverse
    wet_ref[3:8, :] = jnp.zeros((5, 4 * cols), F32)
    xpad = xpad_ref[...]
    projected = dot(terms_ref[0:8, :].astype(BF16), xpad, NT)
    mixed = (projected[0:4] * first_wet + projected[4:8] * second_wet) * inverse
    sent_ref[...] = jnp.where(on_ocean(), mixed, projected[0:4])
    edge_ref[0:cols, :] = jnp.where(on_ocean(), gpad_ref[0:cols, :], xpad_ref[0:cols, :])
    edge_ref[cols:, :] = jnp.where(on_ocean(), gpad_ref[3 * cols :, :], xpad_ref[3 * cols :, :])


def halves_apart(values, narrow):
    wide = -(-narrow // 128) * 128
    lane = lax.broadcasted_iota(jnp.int32, values.shape, 1)
    even = jnp.where(lane < narrow, values, 0.0)
    odd = jnp.where(lane < narrow, pltpu.roll(values, narrow, 1), 0.0)
    return even[:, :wide], odd[:, :wide]


def halves_with_columns(pad, cols):
    even, odd = halves_apart(pad.astype(F32), pad.shape[1] // 2)
    odd_before = moved_cells(odd, 0, cols)[0].astype(BF16)
    even_after = moved_cells(even, 0, cols)[1].astype(BF16)
    even, odd = even.astype(BF16), odd.astype(BF16)
    return (odd_before, even, odd), (even, odd, even_after)


def with_columns(pad, cols):
    before, after = moved_cells(pad.astype(F32), 0, cols)
    return before.astype(BF16), pad, after.astype(BF16)


def convolve(pad, out_ref, atmos_ref, ocean_ref, layer, flipped, cols):
    base = 9 * layer
    channels = atmos_ref.shape[2]
    wide, narrow = ocean_ref.shape[1:]
    rows = out_ref.shape[0]

    def summed(pick):
        total = None
        for row_tap in range(3):
            part = pick(row_tap, slice(cols * row_tap, cols * row_tap + rows))
            total = part if total is None else total + part
        return total

    @pl.when(on_ocean())
    def _():
        evens, odds = halves_with_columns(pad, cols)
        if flipped:

            def pick(row_tap, span):
                part = None
                for col_tap in range(3):
                    left = jnp.concatenate([evens[col_tap][span], odds[col_tap][span]], axis=0)
                    kernel = ocean_ref[base + 8 - (3 * row_tap + col_tap), 0:narrow, :]
                    piece = dot(left[:, :narrow], kernel, NT)
                    part = piece if part is None else part + piece
                return part

        else:
            even, odd = jnp.concatenate(evens, axis=1), jnp.concatenate(odds, axis=1)

            def pick(row_tap, span):
                first = base + 3 * row_tap
                kernel = ocean_ref[first : first + 3].reshape(3 * wide, narrow)
                return dot(jnp.concatenate([even[span], odd[span]], axis=0), kernel)

        total = summed(pick)
        out_ref[...] = jnp.concatenate([total[:rows], total[rows:]], axis=1)

    @pl.when(jnp.logical_not(on_ocean()))
    def _():
        taps = with_columns(pad, cols)
        if flipped:

            def pick(row_tap, span):
                part = None
                for col_tap in range(3):
                    piece = dot(taps[col_tap][span], atmos_ref[base + 8 - (3 * row_tap + col_tap)], NT)
                    part = piece if part is None else part + piece
                return part

        else:
            joined = jnp.concatenate(taps, axis=1)

            def pick(row_tap, span):
                first = base + 3 * row_tap
                return dot(joined[span], atmos_ref[first : first + 3].reshape(3 * channels, channels))

        out_ref[...] = summed(pick)


def back_kernel(gpad_ref, atmos_ref, ocean_ref, out_ref, *, cols):
    convolve(gpad_ref[...], out_ref, atmos_ref, ocean_ref, 1, True, cols)


def spread(arrived, wet, mixing, terms):
    first_wet, second_wet = wet
    both = jnp.concatenate([arrived * first_wet, arrived * second_wet], axis=0)
    alone = jnp.concatenate([arrived, jnp.zeros_like(arrived)], axis=0)
    return dot(jnp.where(mixing, both, alone), terms, TN, HIGHEST)


def first_kernel(
    xpad_ref, wet_ref, arrived_ref, terms_ref, back_ref, atmos_ref, ocean_ref,
    u_ref, stay_ref, give_ref, first_ref, *, cols,
):
    wet = wet_ref[0:1, :], wet_ref[1:2, :]
    coupled = spread(arrived_ref[...], wet, on_ocean(), terms_ref[8:16, :])
    u = (xpad_ref[...].astype(F32) + coupled).astype(BF16)
    u_ref[...] = u
    convolve(u, first_ref, atmos_ref, ocean_ref, 0, False, cols)
    first = first_ref[...]
    tangent = jnp.tanh(GELU_SCALE * (first + GELU_CUBIC * first * first * first))
    hidden = (0.5 * first * (1.0 + tangent)).astype(BF16)
    slope = 0.5 * (1.0 + tangent) + 0.5 * first * (1.0 - tangent * tangent) * GELU_SCALE * (
        1.0 + 3.0 * GELU_CUBIC * first * first
    )
    first_grad = (back_ref[...] * slope).astype(BF16)
    stay_ref[...] = jnp.where(on_ocean(), first_grad, hidden)
    give_ref[...] = jnp.where(on_ocean(), hidden, first_grad)


def whole_pad(early_ref, edge_ref, cols):
    parts = [edge_ref[0:cols, :], early_ref[...], edge_ref[cols:, :]]
    return jnp.concatenate(parts, axis=0).astype(F32)


def grad_atmos(pad, own, cols, store):
    rows = own.shape[0]
    left = own.T.astype(BF16)
    before, after = moved_cells(pad, 0, cols)
    rights = [part.astype(BF16) for part in (after, pad, before)]
    for tap in range(9):
        start = cols * (2 - tap // 3)
        store(tap, dot(left, rights[tap % 3][start : start + rows]))


def grad_ocean(pad, own, pad_is_input, cols, store):
    rows, channels = own.shape
    narrow = channels // 2

    if pad_is_input:
        middle = pad.T
        before, after = moved_cells(middle, 1, cols)
        even, odd = middle[:narrow].astype(BF16), middle[narrow:].astype(BF16)
        pairs = (
            (before[narrow:].astype(BF16), even),
            (even, odd),
            (odd, after[:narrow].astype(BF16)),
        )
        right = jnp.concatenate(halves_apart(own, narrow), axis=0).astype(BF16)
        for tap in range(9):
            start = cols * (tap // 3)
            pieces = [part[:, start : start + rows] for part in pairs[tap % 3]]
            store(tap, dot(jnp.concatenate(pieces, axis=1), right))
    else:
        turned = own.T.astype(BF16)
        left = jnp.concatenate([turned[:narrow], turned[narrow:]], axis=1)
        even, odd = halves_apart(pad, narrow)
        odd_before = moved_cells(odd, 0, cols)[0].astype(BF16)
        even_after = moved_cells(even, 0, cols)[1].astype(BF16)
        even, odd = even.astype(BF16), odd.astype(BF16)
        pairs = ((odd, even_after), (even, odd), (odd_before, even))
        for tap in range(9):
            start = cols * (2 - tap // 3)
            pieces = [part[start : start + rows] for part in pairs[tap % 3]]
            store(tap, dot(left, jnp.concatenate(pieces, axis=0)))


def store_into(out_ref):
    def store(tap, value):
        if len(out_ref.shape) == 2:
            rows = value.shape[0]
            out_ref[rows * tap : rows * (tap + 1), :] = value
        else:
            rows = value.shape[0]
            for piece in range(out_ref.shape[0]):
                lanes = slice(128 * piece, 128 * (piece + 1))
                out_ref[piece, rows * tap : rows * (tap + 1), :] = value[:, lanes]

    return store


def hidden_and_grad(stay_ref, give_ref):
    stay, give = stay_ref[...], give_ref[...]
    return jnp.where(on_ocean(), give, stay), jnp.where(on_ocean(), stay, give)


def shifted_inputs(pad, cols):
    middle = pad.T
    before, after = moved_cells(middle, 1, cols)
    return [part.astype(BF16) for part in (before, middle, after)]


def own_grads_kernel(
    upad_ref, gpad_ref, stay_ref, give_ref, early_ref, edge_ref, sent_ref, coupling_ref,
    atmos_out, ocean_out, near_ref, far_ref, left_ref, *, cols,
):
    stay = stay_ref[...].astype(F32)
    core = own_bit(0)
    hidden, first_grad = hidden_and_grad(stay_ref, give_ref)
    for part, values in enumerate((hidden, first_grad)):
        target = slice(part * cols, (part + 1) * cols)
        far_ref[target, :] = jnp.where(core == 0, values[:cols], values[cols:])
        near_ref[target, :] = jnp.where(core == 0, values[cols:], values[:cols])

    @pl.when(on_ocean())
    def _():
        grad_ocean(upad_ref[...].astype(F32), stay, True, cols, store_into(ocean_out))
        added = dot(sent_ref[...], coupling_ref[...].astype(F32), TN, HIGHEST)
        other = (whole_pad(early_ref, edge_ref, cols) + added).astype(BF16).astype(F32)
        for tap, left in enumerate(shifted_inputs(other, cols)):
            left_ref[tap] = left

    @pl.when(jnp.logical_not(on_ocean()))
    def _():
        grad_atmos(gpad_ref[...].astype(F32), stay, cols, store_into(atmos_out))


def other_grads_kernel(left_ref, late_ref, early_ref, edge_ref, atmos_out, ocean_out, *, cols):
    rows = late_ref.shape[0]

    @pl.when(on_ocean())
    def _():
        store = store_into(atmos_out)
        for tap in range(9):
            start = cols * (tap // 3)
            store(tap, dot(left_ref[tap % 3, :, start : start + rows], late_ref[...]))

    @pl.when(jnp.logical_not(on_ocean()))
    def _():
        late = late_ref[...].astype(F32)
        grad_ocean(whole_pad(early_ref, edge_ref, cols), late, False, cols, store_into(ocean_out))


def chunk_rows(keep_ref, send_ref, atmos_all, ocean_all, chunks):
    channels = keep_ref.shape[2]
    pieces = ocean_all.shape[0]
    atmos_rows = atmos_all.shape[0] // chunks
    ocean_rows = atmos_rows // 2
    taken = keep_ref.shape[1] - atmos_rows
    core = lax.rem(lax.axis_index("lat"), 2)
    blank = jnp.zeros((taken, channels - 128 * pieces), F32)
    for out_ref, side in ((send_ref, 1 - core), (keep_ref, core)):
        for pair in range(chunks // 2):
            start = pl.multiple_of(atmos_rows * (2 * pair + side), 8)
            upper = atmos_all[pl.ds(start, atmos_rows), :]
            start = ocean_rows * (2 * pair + side)
            halves = []
            for odd in range(2):
                parts = [ocean_all.at[piece][pl.ds(start + odd, taken, 2), :] for piece in range(pieces)]
                halves.append(jnp.concatenate(parts + [blank], axis=1))
            lower = halves[0] + pltpu.roll(halves[1], channels // 2, 1)
            out_ref[pair] = jnp.concatenate([upper, lower], axis=0).astype(BF16)


def chunk_kernel(
    atmos_own, ocean_own, atmos_other, ocean_other, keep_ref, send_ref, *, chunks
):
    @pl.when(on_ocean())
    def _():
        chunk_rows(keep_ref, send_ref, atmos_other, ocean_own, chunks)

    @pl.when(jnp.logical_not(on_ocean()))
    def _():
        chunk_rows(keep_ref, send_ref, atmos_own, ocean_other, chunks)


def halve(keep_ref, came_ref, keep_out, send_out, bit, rows):
    own = own_bit(bit)
    for out_ref, side in ((send_out, 1 - own), (keep_out, own)):
        for outer in range(keep_ref.shape[0]):
            for inner in range(keep_ref.shape[2]):
                total = keep_ref[outer, side, inner, rows, :].astype(F32)
                total = total + came_ref[outer, side, inner, rows, :].astype(F32)
                out_ref[outer, inner] = total.astype(BF16)


def split_kernel(keep_ref, came_ref, *outs, cuts):
    by_z = [ref.reshape(2, 2, 2, *keep_ref.shape[3:]) for ref in (keep_ref, came_ref)]
    start = 0
    for index, rows in enumerate(cuts):
        refs, bit = (by_z, 2) if index == 1 else ((keep_ref, came_ref), 1)
        halve(*refs, *outs[2 * index : 2 * index + 2], bit, slice(start, start + rows))
        start += rows


def halve_kernel(keep_ref, came_ref, *refs, bit):
    keep_out, send_out, mark_ref = refs[-3:]
    halve(keep_ref, came_ref, keep_out, send_out, bit, slice(None))
    mark_ref[...] = jnp.zeros_like(mark_ref)


MARK = shape((8, 128), F32)


def halved(keep, came, bit, dims, after):
    outer, inner, rows, channels = dims[0], dims[1], keep.shape[-2], keep.shape[-1]
    keep, came = (part.reshape(outer, 2, inner, rows, channels) for part in (keep, came))
    out = shape((outer, inner, rows, channels), BF16)
    return call(
        functools.partial(halve_kernel, bit=bit),
        [out, out, MARK],
        [keep, came, *after],
        [WHOLE] * 2 + [ANYWHERE] * len(after),
        moved=8 * outer * inner * rows * channels,
        name="halve",
    )


def scatter_sum(keep, came, early_marks, late_marks):
    pairs, tall, channels = keep.shape
    cuts = [16 * (tall // 16 * part // 17) for part in (6, 6)]
    cuts.append(tall - sum(cuts))
    outs = []
    for index, rows in enumerate(cuts):
        outs += [shape(((2, 2) if index == 1 else (4, 1)) + (rows, channels), BF16)] * 2
    keep, came = (part.reshape(4, 2, 1, tall, channels) for part in (keep, came))
    parts = call(
        functools.partial(split_kernel, cuts=cuts),
        outs,
        [keep, came],
        moved=6 * pairs * tall * channels,
        name="split",
    )
    a_keep, a_send, b_keep, b_send, c_keep, c_send = parts
    a_came = swapped(a_send, "lat", 2)
    b_came = swapped(b_send, "lat", 4)
    c_came = swapped(c_send, "lat", 2)
    a_keep, a_send, mark = halved(a_keep, a_came, 2, (2, 1), early_marks)
    a_came = swapped(a_send, "lat", 4)
    b_keep, b_send, mark = halved(b_keep, b_came, 3, (1, 2), [mark])
    b_came = swapped(b_send, "lat", 8)
    c_keep, c_send, mark = halved(c_keep, c_came, 2, (2, 1), [mark, *late_marks])
    c_came = swapped(c_send, "lat", 4)
    a_keep, a_send, mark = halved(a_keep, a_came, 3, (1, 1), [mark])
    a_came = swapped(a_send, "lat", 8)
    b_keep, b_send, mark = halved(b_keep, b_came, 1, (1, 1), [mark])
    b_came = swapped(b_send, "lat", 2)
    c_keep, c_send, mark = halved(c_keep, c_came, 3, (1, 1), [mark])
    c_came = swapped(c_send, "lat", 8)
    return [part.reshape(-1, channels) for part in (a_keep, a_came, b_keep, b_came, c_keep, c_came)]


def finish_kernel(*refs, atmos_factor, ocean_factor):
    parts, (atmos_ref, ocean_ref) = refs[:-2], refs[-2:]
    channels = parts[0].shape[1]
    pieces = channels // 128
    atmos_rows = atmos_ref.shape[0] // pieces
    ocean_rows = ocean_ref.shape[0] // pieces
    sums = [
        parts[index][...].astype(F32) + parts[index + 1][...].astype(F32)
        for index in range(0, len(parts), 2)
    ]
    total = jnp.concatenate(sums, axis=0)
    for piece in range(pieces):
        lanes = slice(128 * piece, 128 * (piece + 1))
        atmos_ref[pl.ds(piece, atmos_rows, pieces), :] = total[:atmos_rows, lanes] * atmos_factor
        ocean_ref[pl.ds(piece, ocean_rows, pieces), :] = (
            total[atmos_rows : atmos_rows + ocean_rows, lanes] * ocean_factor
        )


def input_grad_kernel(
    stay_ref, give_ref, near_ref, far_ref, gpad_ref, wet_ref, terms_ref, atmos_ref, ocean_ref,
    grad_ref, sent_ref, *, cols,
):
    middle = hidden_and_grad(stay_ref, give_ref)[1]
    low, high = low_and_high(near_ref[cols:, :], far_ref[cols:, :])
    pad = jnp.concatenate([low, middle, high], axis=0)
    own = slice(cols, 3 * cols)
    convolve(pad, grad_ref, atmos_ref, ocean_ref, 0, True, cols)
    grad = gpad_ref[own, :].astype(F32) + grad_ref[...]
    grad_ref[...] = grad
    weighted = dot(terms_ref[8:16, :], grad, NT, HIGHEST)
    mixed = weighted[0:4] * wet_ref[0:1, own] + weighted[4:8] * wet_ref[1:2, own]
    sent_ref[...] = jnp.where(on_ocean(), mixed, weighted[0:4])


def next_kernel(
    stay_ref, give_ref, near_ref, far_ref, upad_ref, atmos_ref, ocean_ref,
    next_ref, mark_ref, second_ref, *, cols,
):
    middle = hidden_and_grad(stay_ref, give_ref)[0]
    low, high = low_and_high(near_ref[0:cols, :], far_ref[0:cols, :])
    pad = jnp.concatenate([low, middle, high], axis=0)
    own = slice(cols, 3 * cols)
    convolve(pad, second_ref, atmos_ref, ocean_ref, 1, False, cols)
    values = (upad_ref[own, :].astype(F32) + second_ref[...]).astype(BF16)
    next_ref[0] = values[:cols]
    next_ref[1] = values[cols:]
    mark_ref[...] = jnp.zeros_like(mark_ref)


def last_kernel(grad_ref, arrived_ref, wet_ref, terms_ref, out_ref, mark_ref, *, cols):
    own = slice(cols, 3 * cols)
    wet = wet_ref[0:1, own], wet_ref[1:2, own]
    arrived = jnp.where(on_ocean(), arrived_ref[...] * wet_ref[2:3, own], arrived_ref[...])
    added = spread(arrived, wet, on_ocean(), terms_ref[0:8, :])
    values = (grad_ref[...] + added).astype(BF16)
    out_ref[0] = values[:cols]
    out_ref[1] = values[cols:]
    mark_ref[...] = jnp.zeros_like(mark_ref)


def swapped(value, axis, mask):
    pairs = [(source, source ^ mask) for source in range(lax.axis_size(axis))]
    return lax.ppermute(value, axis, pairs)


def halo(near, far):
    count = lax.axis_size("lat")
    pairs = [(i, i + 1 if i % 2 else i - 1) for i in range(1, count - 1)]
    far = lax.ppermute(far, "lat", pairs)
    return swapped(near, "lat", 1), far


def local(
    fields,
    cotangent,
    ocean_kernels,
    atmos_kernels,
    ocean_surface,
    ocean_coupling,
    atmos_flux,
    atmos_coupling,
    row_map,
    wet_mask,
):
    x, g = fields[0], cotangent[0]
    bands, cols, channels = x.shape
    narrow = channels // 2
    cells = bands * cols
    count = lax.axis_size("lat")
    is_ocean = lax.axis_index("grp") == 0
    atmos_factor = 1.0 / math.sqrt(bands * count * cols)
    ocean_factor = 1.0 / math.sqrt(bands * count * 2 * cols)
    bound = functools.partial

    blank = jnp.zeros((4, narrow), BF16)
    gap = jnp.zeros((4, channels), BF16)
    surface = ocean_surface.T
    ocean_terms = jnp.concatenate(
        [
            jnp.concatenate([surface, blank], axis=1),
            jnp.concatenate([blank, surface], axis=1),
            jnp.concatenate([ocean_coupling, blank], axis=1),
            jnp.concatenate([blank, ocean_coupling], axis=1),
        ],
        axis=0,
    )
    atmos_terms = jnp.concatenate([atmos_flux.T, gap, atmos_coupling, gap], axis=0)
    terms = jnp.where(is_ocean, ocean_terms, atmos_terms).astype(F32)

    edge = shape((2 * cols + 16, channels), BF16)
    half = shape((cells, channels), BF16)
    near, far, own_early, own = call(
        bound(pack_kernel, cols=cols),
        [edge, edge, half, shape((2 * cells + 16, channels), BF16)],
        [x, g, wet_mask],
        [IN_PLACE] * 3,
        [
            pltpu.VMEM(x.shape, BF16),
            pltpu.VMEM(x.shape, BF16),
            pltpu.VMEM(wet_mask.shape, jnp.int32),
            pltpu.SemaphoreType.DMA((3,)),
        ],
        name="pack",
        limit=PACK_VMEM,
    )
    near, far = halo(near, far)
    other_early = swapped(own_early, "grp", 1)
    wide = -(-narrow // 128) * 128
    own, atmos_flat, ocean_flat = call(
        hold_kernel,
        [
            shape(own.shape, BF16),
            shape((18, channels, channels), BF16),
            shape((18, wide, narrow), BF16),
        ],
        [own, atmos_kernels.reshape(18, channels, channels), ocean_kernels.reshape(18, narrow, narrow)],
        [WHOLE, IN_PLACE, IN_PLACE],
        [pltpu.SemaphoreType.DMA],
        flops=PACE * 10**8,
        name="hold",
        limit=HOLD_VMEM,
    )
    pad = shape((2 * cells, channels), BF16)
    xpad, gpad, wet, edges, sent = call(
        bound(outgoing_kernel, cols=cols),
        [pad, pad, shape((8, 2 * cells), F32), half, shape((4, 2 * cells), F32)],
        [own, near, far, terms],
        name="outgoing",
    )
    arrived = swapped(sent, "grp", 1)
    other_edges = swapped(edges, "grp", 1)
    conv_cost = dict(flops=PACE * 9 * cells * channels * channels, moved=9 * channels * channels * 2)
    back = call(
        bound(back_kernel, cols=cols),
        shape((cells, channels), F32),
        [gpad, atmos_flat, ocean_flat],
        **conv_cost,
        name="back",
    )
    upad, stay, give = call(
        bound(first_kernel, cols=cols),
        [pad, half, half],
        [xpad, wet, arrived, terms, back, atmos_flat, ocean_flat],
        None,
        [pltpu.VMEM((cells, channels), F32)],
        **conv_cost,
        name="first",
    )
    late = swapped(give, "grp", 1)

    atmos_rows = 9 * channels // count
    ocean_rows = 9 * narrow // count
    chunked = count == 16 and 9 * channels % (8 * count) == 0 and ocean_rows % 2 == 0
    tall = -(-(atmos_rows + ocean_rows // 2) // 16) * 16
    spare = max(0, 2 * (tall - atmos_rows) - ocean_rows) if chunked else 0
    ocean_tall = 9 * narrow + -(-spare // 8) * 8
    sums = [shape((9 * channels, channels), F32), shape((wide // 128, ocean_tall, 128), F32)]
    atmos_sum, ocean_sum, near, far, lefts = call(
        bound(own_grads_kernel, cols=cols),
        [*sums, half, half, shape((3, channels, 2 * cells), BF16)],
        [upad, gpad, stay, give, other_early, other_edges, sent, atmos_coupling],
        **conv_cost,
        name="own_grads",
    )
    near, far = halo(near, far)
    atmos_other, ocean_other = call(
        bound(other_grads_kernel, cols=cols),
        sums,
        [lefts, late, other_early, other_edges],
        **conv_cost,
        name="other_grads",
    )
    if chunked:
        part = shape((count // 2, tall, channels), BF16)
        keep, send = call(
            bound(chunk_kernel, chunks=count),
            [part, part],
            [atmos_sum, ocean_sum, atmos_other, ocean_other],
            moved=4 * count * tall * channels,
            name="chunk",
        )
        came = swapped(send, "lat", 1)

    grad, sent_back = call(
        bound(input_grad_kernel, cols=cols),
        [shape((cells, channels), F32), shape((4, cells), F32)],
        [stay, give, near, far, gpad, wet, terms, atmos_flat, ocean_flat],
        **conv_cost,
        name="input_grad",
    )
    returned = swapped(sent_back, "grp", 1)
    next_field, next_mark = call(
        bound(next_kernel, cols=cols),
        [shape(x.shape, BF16), MARK],
        [stay, give, near, far, upad, atmos_flat, ocean_flat],
        None,
        [pltpu.VMEM((cells, channels), F32)],
        **conv_cost,
        name="next",
    )
    field_grad, last_mark = call(
        bound(last_kernel, cols=cols),
        [shape(x.shape, BF16), MARK],
        [grad, returned, wet, terms],
        name="last",
    )

    if chunked:
        atmos_chunk, ocean_chunk = call(
            bound(finish_kernel, atmos_factor=atmos_factor, ocean_factor=ocean_factor),
            [
                shape((atmos_rows * channels // 128, 128), F32),
                shape((ocean_rows * narrow // 128, 128), F32),
            ],
            scatter_sum(keep, came, [sent_back, next_mark], [last_mark]),
            name="finish",
        )
        atmos_total, ocean_total = atmos_chunk.reshape(-1), ocean_chunk.reshape(-1)
    else:
        atmos_all = jnp.where(is_ocean, atmos_other, atmos_sum)
        ocean_all = jnp.where(is_ocean, ocean_sum, ocean_other)
        atmos_total = atmos_factor * lax.psum_scatter(
            atmos_all.reshape(-1), "lat", scatter_dimension=0, tiled=True
        )
        ocean_all = jnp.concatenate([ocean_all[piece] for piece in range(wide // 128)], axis=1)
        ocean_total = ocean_factor * lax.psum_scatter(
            ocean_all[:, :narrow].reshape(-1), "lat", scatter_dimension=0, tiled=True
        )
    return (next_field[None], field_grad[None], ocean_total, atmos_total)


def solution(mesh):
    in_specs = (
        P("grp", "lat", None, None),
        P("grp", "lat", None, None),
        P(),
        P(),
        P(),
        P(),
        P(),
        P(),
        P("lat"),
        P("lat", None),
    )
    out_specs = (
        P("grp", "lat", None, None),
        P("grp", "lat", None, None),
        P(("grp", "lat")),
        P(("grp", "lat")),
    )
    return jax.shard_map(local, mesh=mesh, in_specs=in_specs, out_specs=out_specs, check_vma=False)
```

```python
import functools
import math

import jax
import jax.numpy as jnp
from jax import lax
from jax.experimental import pallas as pl
from jax.experimental.pallas import tpu as pltpu
from jax.sharding import PartitionSpec as P

HIGHEST = lax.Precision.HIGHEST
GELU_SCALE = 0.7978845608028654
GELU_CUBIC = 0.044715
F32 = jnp.float32
BF16 = jnp.bfloat16
WHOLE = pl.BlockSpec(memory_space=pltpu.VMEM)
IN_PLACE = pl.BlockSpec(memory_space=pltpu.HBM)
ANYWHERE = pl.BlockSpec(memory_space=pl.ANY)
VMEM_LIMIT = 20 * 1024 * 1024
PACE = 8
PACK_VMEM = 62 * 1024 * 1024
HOLD_VMEM = 42 * 1024 * 1024

NN = (((1,), (0,)), ((), ()))
NT = (((1,), (1,)), ((), ()))
TN = (((0,), (0,)), ((), ()))


def shape(dims, kind):
    return jax.ShapeDtypeStruct(dims, kind)


def call(kernel, outs, inputs, in_specs=None, scratch=(), flops=0, moved=0, name=None, limit=VMEM_LIMIT, out_spec=WHOLE):
    return pl.pallas_call(
        kernel,
        out_shape=outs,
        in_specs=in_specs or [WHOLE] * len(inputs),
        out_specs=jax.tree.map(lambda _: out_spec, outs),
        scratch_shapes=list(scratch),
        compiler_params=pltpu.CompilerParams(vmem_limit_bytes=limit),
        cost_estimate=pl.CostEstimate(flops=flops, bytes_accessed=moved, transcendentals=0),
        name=name,
    )(*inputs)


def on_ocean():
    return lax.axis_index("grp") == 0


def dot(left, right, dims=NN, precision=None):
    return lax.dot_general(left, right, dims, precision=precision, preferred_element_type=F32)


def moved_cells(values, axis, cols):
    count = values.shape[axis]
    place = lax.rem(lax.broadcasted_iota(jnp.int32, values.shape, axis), cols)
    before = jnp.where(place == 0, 0.0, pltpu.roll(values, 1, axis))
    after = jnp.where(place == cols - 1, 0.0, pltpu.roll(values, count - 1, axis))
    return before, after


def wet_halves(wet, cols, channels):
    source = lax.broadcasted_iota(jnp.int32, (2 * cols, 2 * cols), 0)
    target = lax.broadcasted_iota(jnp.int32, (2 * cols, 2 * cols), 1)
    wanted = 2 * lax.rem(target, cols) + jnp.where(target >= cols, 1, 0)
    chooser = (source == wanted).astype(F32).astype(BF16)
    padded = jnp.concatenate([wet.astype(F32), jnp.zeros((14, 2 * cols), F32)], axis=0)
    apart = dot(padded.astype(BF16), chooser)
    return jnp.concatenate([apart, jnp.zeros((16, channels - 2 * cols), F32)], axis=1)


def own_bit(bit):
    return lax.rem(lax.shift_right_logical(lax.axis_index("lat"), bit), 2)


def pack_kernel(
    x_any, g_any, wet_any, near_ref, far_ref, early_ref, own_ref, x_ref, g_ref, wet_ref, sems, *, cols
):
    pairs = ((wet_any, wet_ref), (x_any, x_ref), (g_any, g_ref))
    copies = [pltpu.make_async_copy(*pair, sems.at[index]) for index, pair in enumerate(pairs)]
    for copy in copies:
        copy.start()
    core = own_bit(0)
    copies[0].wait()
    wide = wet_halves(wet_ref[...], cols, x_ref.shape[2])
    other = pltpu.roll(wide, 15, 0)
    own_ref[4 * cols :, :] = wide.astype(BF16)
    far_ref[2 * cols :, :] = jnp.where(core == 0, wide, other).astype(BF16)
    near_ref[2 * cols :, :] = jnp.where(core == 0, other, wide).astype(BF16)
    copies[1].wait()
    copies[2].wait()
    for part, ref in enumerate((x_ref, g_ref)):
        far_ref[part * cols : (part + 1) * cols, :] = ref[core]
        near_ref[part * cols : (part + 1) * cols, :] = ref[1 - core]
        own_ref[2 * part * cols : (2 * part + 1) * cols, :] = ref[0]
        own_ref[(2 * part + 1) * cols : (2 * part + 2) * cols, :] = ref[1]
    for row in range(2):
        early_ref[row * cols : (row + 1) * cols, :] = jnp.where(on_ocean(), g_ref[row], x_ref[row])


def hold_kernel(own_in, atmos_any, ocean_any, own_ref, atmos_ref, ocean_ref, sem):
    narrow = ocean_ref.shape[2]
    ocean_copy = pltpu.make_async_copy(ocean_any, ocean_ref.at[:, pl.ds(0, narrow), :], sem)
    atmos_copy = pltpu.make_async_copy(atmos_any, atmos_ref, sem)

    @pl.when(on_ocean())
    def _():
        ocean_copy.start()
        gap = ocean_ref.shape[1] - narrow
        if gap:
            ocean_ref[:, narrow:, :] = jnp.zeros((ocean_ref.shape[0], gap, narrow), BF16)

    @pl.when(jnp.logical_not(on_ocean()))
    def _():
        atmos_copy.start()

    own_ref[...] = own_in[...]

    @pl.when(on_ocean())
    def _():
        ocean_copy.wait()

    @pl.when(jnp.logical_not(on_ocean()))
    def _():
        atmos_copy.wait()


def low_and_high(near, far):
    core = own_bit(0)
    return jnp.where(core == 0, far, near), jnp.where(core == 0, near, far)


def outgoing_kernel(
    own_ref, near_ref, far_ref, terms_ref, xpad_ref, gpad_ref, wet_ref, edge_ref, sent_ref, *, cols
):
    low, high = low_and_high(near_ref[...], far_ref[...])
    for part, pad_ref in enumerate((xpad_ref, gpad_ref)):
        pad_ref[0:cols, :] = low[part * cols : (part + 1) * cols]
        pad_ref[cols : 3 * cols, :] = own_ref[2 * part * cols : 2 * (part + 1) * cols, :]
        pad_ref[3 * cols : 4 * cols, :] = high[part * cols : (part + 1) * cols]
    low_wet = low[2 * cols :].astype(F32)
    high_wet = high[2 * cols :].astype(F32)
    own_wet = own_ref[4 * cols :, :].astype(F32)
    halves = []
    for start in (0, cols):
        lanes = slice(start, start + cols)
        rows = (low_wet[0:1, lanes], own_wet[0:1, lanes], own_wet[1:2, lanes], high_wet[0:1, lanes])
        halves.append(jnp.concatenate(rows, axis=1))
    first_wet, second_wet = halves
    inverse = 1.0 / jnp.maximum(first_wet + second_wet, 1.0)
    wet_ref[0:1, :] = first_wet
    wet_ref[1:2, :] = second_wet
    wet_ref[2:3, :] = inverse
    wet_ref[3:8, :] = jnp.zeros((5, 4 * cols), F32)
    xpad = xpad_ref[...]
    projected = dot(terms_ref[0:8, :].astype(BF16), xpad, NT)
    mixed = (projected[0:4] * first_wet + projected[4:8] * second_wet) * inverse
    sent_ref[...] = jnp.where(on_ocean(), mixed, projected[0:4])
    edge_ref[0:cols, :] = jnp.where(on_ocean(), gpad_ref[0:cols, :], xpad_ref[0:cols, :])
    edge_ref[cols:, :] = jnp.where(on_ocean(), gpad_ref[3 * cols :, :], xpad_ref[3 * cols :, :])


def halves_apart(values, narrow):
    wide = -(-narrow // 128) * 128
    lane = lax.broadcasted_iota(jnp.int32, values.shape, 1)
    even = jnp.where(lane < narrow, values, 0.0)
    odd = jnp.where(lane < narrow, pltpu.roll(values, narrow, 1), 0.0)
    return even[:, :wide], odd[:, :wide]


def halves_with_columns(pad, cols):
    even, odd = halves_apart(pad.astype(F32), pad.shape[1] // 2)
    odd_before = moved_cells(odd, 0, cols)[0].astype(BF16)
    even_after = moved_cells(even, 0, cols)[1].astype(BF16)
    even, odd = even.astype(BF16), odd.astype(BF16)
    return (odd_before, even, odd), (even, odd, even_after)


def with_columns(pad, cols):
    before, after = moved_cells(pad.astype(F32), 0, cols)
    return before.astype(BF16), pad, after.astype(BF16)


def convolve(pad, out_ref, atmos_ref, ocean_ref, layer, flipped, cols):
    base = 9 * layer
    channels = atmos_ref.shape[2]
    wide, narrow = ocean_ref.shape[1:]
    rows = out_ref.shape[0]

    def summed(pick):
        total = None
        for row_tap in range(3):
            part = pick(row_tap, slice(cols * row_tap, cols * row_tap + rows))
            total = part if total is None else total + part
        return total

    @pl.when(on_ocean())
    def _():
        evens, odds = halves_with_columns(pad, cols)
        if flipped:

            def pick(row_tap, span):
                part = None
                for col_tap in range(3):
                    left = jnp.concatenate([evens[col_tap][span], odds[col_tap][span]], axis=0)
                    kernel = ocean_ref[base + 8 - (3 * row_tap + col_tap), 0:narrow, :]
                    piece = dot(left[:, :narrow], kernel, NT)
                    part = piece if part is None else part + piece
                return part

        else:
            even, odd = jnp.concatenate(evens, axis=1), jnp.concatenate(odds, axis=1)

            def pick(row_tap, span):
                first = base + 3 * row_tap
                kernel = ocean_ref[first : first + 3].reshape(3 * wide, narrow)
                return dot(jnp.concatenate([even[span], odd[span]], axis=0), kernel)

        total = summed(pick)
        out_ref[...] = jnp.concatenate([total[:rows], total[rows:]], axis=1)

    @pl.when(jnp.logical_not(on_ocean()))
    def _():
        taps = with_columns(pad, cols)
        if flipped:

            def pick(row_tap, span):
                part = None
                for col_tap in range(3):
                    piece = dot(taps[col_tap][span], atmos_ref[base + 8 - (3 * row_tap + col_tap)], NT)
                    part = piece if part is None else part + piece
                return part

        else:
            joined = jnp.concatenate(taps, axis=1)

            def pick(row_tap, span):
                first = base + 3 * row_tap
                return dot(joined[span], atmos_ref[first : first + 3].reshape(3 * channels, channels))

        out_ref[...] = summed(pick)


def back_kernel(gpad_ref, atmos_ref, ocean_ref, out_ref, *, cols):
    convolve(gpad_ref[...], out_ref, atmos_ref, ocean_ref, 1, True, cols)


def spread(arrived, wet, mixing, terms):
    first_wet, second_wet = wet
    both = jnp.concatenate([arrived * first_wet, arrived * second_wet], axis=0)
    alone = jnp.concatenate([arrived, jnp.zeros_like(arrived)], axis=0)
    return dot(jnp.where(mixing, both, alone), terms, TN, HIGHEST)


def first_kernel(
    xpad_ref, wet_ref, arrived_ref, terms_ref, back_ref, atmos_ref, ocean_ref,
    u_ref, stay_ref, give_ref, near_ref, far_ref, first_ref, *, cols,
):
    wet = wet_ref[0:1, :], wet_ref[1:2, :]
    coupled = spread(arrived_ref[...], wet, on_ocean(), terms_ref[8:16, :])
    u = (xpad_ref[...].astype(F32) + coupled).astype(BF16)
    u_ref[...] = u
    convolve(u, first_ref, atmos_ref, ocean_ref, 0, False, cols)
    first = first_ref[...]
    tangent = jnp.tanh(GELU_SCALE * (first + GELU_CUBIC * first * first * first))
    hidden = (0.5 * first * (1.0 + tangent)).astype(BF16)
    slope = 0.5 * (1.0 + tangent) + 0.5 * first * (1.0 - tangent * tangent) * GELU_SCALE * (
        1.0 + 3.0 * GELU_CUBIC * first * first
    )
    first_grad = (back_ref[...] * slope).astype(BF16)
    stay_ref[...] = jnp.where(on_ocean(), first_grad, hidden)
    give_ref[...] = jnp.where(on_ocean(), hidden, first_grad)
    core = own_bit(0)
    for part, values in enumerate((hidden, first_grad)):
        target = slice(part * cols, (part + 1) * cols)
        far_ref[target, :] = jnp.where(core == 0, values[:cols], values[cols:])
        near_ref[target, :] = jnp.where(core == 0, values[cols:], values[:cols])


def whole_pad(early_ref, edge_ref, cols):
    parts = [edge_ref[0:cols, :], early_ref[...], edge_ref[cols:, :]]
    return jnp.concatenate(parts, axis=0).astype(F32)


def grad_atmos(pad, own, cols, store):
    rows = own.shape[0]
    left = own.T.astype(BF16)
    before, after = moved_cells(pad, 0, cols)
    rights = [part.astype(BF16) for part in (after, pad, before)]
    for tap in range(9):
        start = cols * (2 - tap // 3)
        store(tap, dot(left, rights[tap % 3][start : start + rows]))


def grad_ocean(pad, own, pad_is_input, cols, store):
    rows, channels = own.shape
    narrow = channels // 2

    if pad_is_input:
        middle = pad.T
        before, after = moved_cells(middle, 1, cols)
        even, odd = middle[:narrow].astype(BF16), middle[narrow:].astype(BF16)
        pairs = (
            (before[narrow:].astype(BF16), even),
            (even, odd),
            (odd, after[:narrow].astype(BF16)),
        )
        right = jnp.concatenate(halves_apart(own, narrow), axis=0).astype(BF16)
        for tap in range(9):
            start = cols * (tap // 3)
            pieces = [part[:, start : start + rows] for part in pairs[tap % 3]]
            store(tap, dot(jnp.concatenate(pieces, axis=1), right))
    else:
        turned = own.T.astype(BF16)
        left = jnp.concatenate([turned[:narrow], turned[narrow:]], axis=1)
        even, odd = halves_apart(pad, narrow)
        odd_before = moved_cells(odd, 0, cols)[0].astype(BF16)
        even_after = moved_cells(even, 0, cols)[1].astype(BF16)
        even, odd = even.astype(BF16), odd.astype(BF16)
        pairs = ((odd, even_after), (even, odd), (odd_before, even))
        for tap in range(9):
            start = cols * (2 - tap // 3)
            pieces = [part[start : start + rows] for part in pairs[tap % 3]]
            store(tap, dot(left, jnp.concatenate(pieces, axis=0)))


def store_into(out_ref):
    def store(tap, value):
        if len(out_ref.shape) == 2:
            rows = value.shape[0]
            out_ref[rows * tap : rows * (tap + 1), :] = value
        else:
            rows = value.shape[0]
            for piece in range(out_ref.shape[0]):
                lanes = slice(128 * piece, 128 * (piece + 1))
                out_ref[piece, rows * tap : rows * (tap + 1), :] = value[:, lanes]

    return store


def hidden_and_grad(stay_ref, give_ref):
    stay, give = stay_ref[...], give_ref[...]
    return jnp.where(on_ocean(), give, stay), jnp.where(on_ocean(), stay, give)


def shifted_inputs(pad, cols):
    middle = pad.T
    before, after = moved_cells(middle, 1, cols)
    return [part.astype(BF16) for part in (before, middle, after)]


def own_grads_kernel(
    upad_ref, gpad_ref, stay_ref, early_ref, edge_ref, sent_ref, coupling_ref,
    atmos_out, ocean_out, left_ref, *, cols,
):
    stay = stay_ref[...].astype(F32)

    @pl.when(on_ocean())
    def _():
        grad_ocean(upad_ref[...].astype(F32), stay, True, cols, store_into(ocean_out))
        added = dot(sent_ref[...], coupling_ref[...].astype(F32), TN, HIGHEST)
        other = (whole_pad(early_ref, edge_ref, cols) + added).astype(BF16).astype(F32)
        for tap, left in enumerate(shifted_inputs(other, cols)):
            left_ref[tap] = left

    @pl.when(jnp.logical_not(on_ocean()))
    def _():
        grad_atmos(gpad_ref[...].astype(F32), stay, cols, store_into(atmos_out))


def other_grads_kernel(left_ref, late_ref, early_ref, edge_ref, atmos_out, ocean_out, *, cols):
    rows = late_ref.shape[0]

    @pl.when(on_ocean())
    def _():
        store = store_into(atmos_out)
        for tap in range(9):
            start = cols * (tap // 3)
            store(tap, dot(left_ref[tap % 3, :, start : start + rows], late_ref[...]))

    @pl.when(jnp.logical_not(on_ocean()))
    def _():
        late = late_ref[...].astype(F32)
        grad_ocean(whole_pad(early_ref, edge_ref, cols), late, False, cols, store_into(ocean_out))


def chunk_rows(keep_ref, send_ref, atmos_all, ocean_all, chunks):
    channels = keep_ref.shape[2]
    pieces = ocean_all.shape[0]
    atmos_rows = atmos_all.shape[0] // chunks
    ocean_rows = atmos_rows // 2
    taken = keep_ref.shape[1] - atmos_rows
    core = lax.rem(lax.axis_index("lat"), 2)
    blank = jnp.zeros((taken, channels - 128 * pieces), F32)
    for out_ref, side in ((send_ref, 1 - core), (keep_ref, core)):
        for pair in range(chunks // 2):
            start = pl.multiple_of(atmos_rows * (2 * pair + side), 8)
            upper = atmos_all[pl.ds(start, atmos_rows), :]
            start = ocean_rows * (2 * pair + side)
            halves = []
            for odd in range(2):
                parts = [ocean_all.at[piece][pl.ds(start + odd, taken, 2), :] for piece in range(pieces)]
                halves.append(jnp.concatenate(parts + [blank], axis=1))
            lower = halves[0] + pltpu.roll(halves[1], channels // 2, 1)
            out_ref[pair] = jnp.concatenate([upper, lower], axis=0).astype(BF16)


def chunk_kernel(
    atmos_own, ocean_own, atmos_other, ocean_other, near_any, far_any, keep_ref, send_ref, *, chunks
):
    @pl.when(on_ocean())
    def _():
        chunk_rows(keep_ref, send_ref, atmos_other, ocean_own, chunks)

    @pl.when(jnp.logical_not(on_ocean()))
    def _():
        chunk_rows(keep_ref, send_ref, atmos_own, ocean_other, chunks)


def halve(keep_ref, came_ref, keep_out, send_out, bit, rows):
    own = own_bit(bit)
    for out_ref, side in ((send_out, 1 - own), (keep_out, own)):
        for outer in range(keep_ref.shape[0]):
            for inner in range(keep_ref.shape[2]):
                total = keep_ref[outer, side, inner, rows, :].astype(F32)
                total = total + came_ref[outer, side, inner, rows, :].astype(F32)
                out_ref[outer, inner] = total.astype(BF16)


def split_kernel(keep_ref, came_ref, done_ref, *outs, cuts):
    by_z = [ref.reshape(2, 2, 2, *keep_ref.shape[3:]) for ref in (keep_ref, came_ref)]
    start = 0
    for index, rows in enumerate(cuts):
        refs, bit = (by_z, 2) if index == 1 else ((keep_ref, came_ref), 1)
        halve(*refs, *outs[2 * index : 2 * index + 2], bit, slice(start, start + rows))
        start += rows


def halve_kernel(keep_ref, came_ref, *refs, bit):
    keep_out, send_out, mark_ref = refs[-3:]
    halve(keep_ref, came_ref, keep_out, send_out, bit, slice(None))
    mark_ref[...] = jnp.zeros_like(mark_ref)


MARK = shape((8, 128), F32)


def halved(keep, came, bit, dims, after):
    outer, inner, rows, channels = dims[0], dims[1], keep.shape[-2], keep.shape[-1]
    keep, came = (part.reshape(outer, 2, inner, rows, channels) for part in (keep, came))
    out = shape((outer, inner, rows, channels), BF16)
    return call(
        functools.partial(halve_kernel, bit=bit),
        [out, out, MARK],
        [keep, came, *after],
        [WHOLE] * 2 + [ANYWHERE] * len(after),
        moved=8 * outer * inner * rows * channels,
        name="halve",
    )


def scatter_sum(keep, came, done_before, done_next):
    pairs, tall, channels = keep.shape
    cuts = [16 * (tall // 16 * part // 17) for part in (6, 6)]
    cuts.append(tall - sum(cuts))
    outs = []
    for index, rows in enumerate(cuts):
        outs += [shape(((2, 2) if index == 1 else (4, 1)) + (rows, channels), BF16)] * 2
    keep, came = (part.reshape(4, 2, 1, tall, channels) for part in (keep, came))
    parts = call(
        functools.partial(split_kernel, cuts=cuts),
        outs,
        [keep, came, done_before],
        [WHOLE] * 2 + [ANYWHERE],
        moved=6 * pairs * tall * channels,
        name="split",
    )
    a_keep, a_send, b_keep, b_send, c_keep, c_send = parts
    a_came = swapped(a_send, "lat", 2)
    b_came = swapped(b_send, "lat", 4)
    c_came = swapped(c_send, "lat", 2)
    a_keep, a_send, mark = halved(a_keep, a_came, 2, (2, 1), done_next)
    a_came = swapped(a_send, "lat", 4)
    b_keep, b_send, mark = halved(b_keep, b_came, 3, (1, 2), [mark])
    b_came = swapped(b_send, "lat", 8)
    c_keep, c_send, mark = halved(c_keep, c_came, 2, (2, 1), [mark])
    c_came = swapped(c_send, "lat", 4)
    a_keep, a_send, mark = halved(a_keep, a_came, 3, (1, 1), [mark])
    a_came = swapped(a_send, "lat", 8)
    b_keep, b_send, mark = halved(b_keep, b_came, 1, (1, 1), [mark])
    b_came = swapped(b_send, "lat", 2)
    c_keep, c_send, mark = halved(c_keep, c_came, 3, (1, 1), [mark])
    c_came = swapped(c_send, "lat", 8)
    return [part.reshape(-1, channels) for part in (a_keep, a_came, b_keep, b_came, c_keep, c_came)]


def finish_kernel(*refs, atmos_factor, ocean_factor):
    parts, (atmos_ref, ocean_ref) = refs[:-2], refs[-2:]
    channels = parts[0].shape[1]
    pieces = channels // 128
    atmos_rows = atmos_ref.shape[0] // pieces
    ocean_rows = ocean_ref.shape[0] // pieces
    sums = [
        parts[index][...].astype(F32) + parts[index + 1][...].astype(F32)
        for index in range(0, len(parts), 2)
    ]
    total = jnp.concatenate(sums, axis=0)
    for piece in range(pieces):
        lanes = slice(128 * piece, 128 * (piece + 1))
        atmos_ref[pl.ds(piece, atmos_rows, pieces), :] = total[:atmos_rows, lanes] * atmos_factor
        ocean_ref[pl.ds(piece, ocean_rows, pieces), :] = (
            total[atmos_rows : atmos_rows + ocean_rows, lanes] * ocean_factor
        )


def input_grad_kernel(
    stay_ref, give_ref, near_ref, far_ref, gpad_ref, wet_ref, terms_ref, atmos_ref, ocean_ref,
    grad_ref, sent_ref, *, cols,
):
    middle = hidden_and_grad(stay_ref, give_ref)[1]
    low, high = low_and_high(near_ref[cols:, :], far_ref[cols:, :])
    pad = jnp.concatenate([low, middle, high], axis=0)
    own = slice(cols, 3 * cols)
    convolve(pad, grad_ref, atmos_ref, ocean_ref, 0, True, cols)
    grad = gpad_ref[own, :].astype(F32) + grad_ref[...]
    grad_ref[...] = grad
    weighted = dot(terms_ref[8:16, :], grad, NT, HIGHEST)
    mixed = weighted[0:4] * wet_ref[0:1, own] + weighted[4:8] * wet_ref[1:2, own]
    sent_ref[...] = jnp.where(on_ocean(), mixed, weighted[0:4])


def next_kernel(
    stay_ref, give_ref, near_ref, far_ref, upad_ref, atmos_ref, ocean_ref,
    next_ref, mark_ref, second_ref, *, cols,
):
    middle = hidden_and_grad(stay_ref, give_ref)[0]
    low, high = low_and_high(near_ref[0:cols, :], far_ref[0:cols, :])
    pad = jnp.concatenate([low, middle, high], axis=0)
    own = slice(cols, 3 * cols)
    convolve(pad, second_ref, atmos_ref, ocean_ref, 1, False, cols)
    values = (upad_ref[own, :].astype(F32) + second_ref[...]).astype(BF16)
    next_ref[0] = values[:cols]
    next_ref[1] = values[cols:]
    mark_ref[...] = jnp.zeros_like(mark_ref)


def last_kernel(grad_ref, arrived_ref, wet_ref, terms_ref, out_ref, mark_ref, *, cols):
    own = slice(cols, 3 * cols)
    wet = wet_ref[0:1, own], wet_ref[1:2, own]
    arrived = jnp.where(on_ocean(), arrived_ref[...] * wet_ref[2:3, own], arrived_ref[...])
    added = spread(arrived, wet, on_ocean(), terms_ref[0:8, :])
    values = (grad_ref[...] + added).astype(BF16)
    out_ref[0] = values[:cols]
    out_ref[1] = values[cols:]
    mark_ref[...] = jnp.zeros_like(mark_ref)


def swapped(value, axis, mask):
    pairs = [(source, source ^ mask) for source in range(lax.axis_size(axis))]
    return lax.ppermute(value, axis, pairs)


def halo(near, far):
    count = lax.axis_size("lat")
    pairs = [(i, i + 1 if i % 2 else i - 1) for i in range(1, count - 1)]
    far = lax.ppermute(far, "lat", pairs)
    return swapped(near, "lat", 1), far


def local(
    fields,
    cotangent,
    ocean_kernels,
    atmos_kernels,
    ocean_surface,
    ocean_coupling,
    atmos_flux,
    atmos_coupling,
    row_map,
    wet_mask,
):
    x, g = fields[0], cotangent[0]
    bands, cols, channels = x.shape
    narrow = channels // 2
    cells = bands * cols
    count = lax.axis_size("lat")
    is_ocean = lax.axis_index("grp") == 0
    atmos_factor = 1.0 / math.sqrt(bands * count * cols)
    ocean_factor = 1.0 / math.sqrt(bands * count * 2 * cols)
    bound = functools.partial

    blank = jnp.zeros((4, narrow), BF16)
    gap = jnp.zeros((4, channels), BF16)
    surface = ocean_surface.T
    ocean_terms = jnp.concatenate(
        [
            jnp.concatenate([surface, blank], axis=1),
            jnp.concatenate([blank, surface], axis=1),
            jnp.concatenate([ocean_coupling, blank], axis=1),
            jnp.concatenate([blank, ocean_coupling], axis=1),
        ],
        axis=0,
    )
    atmos_terms = jnp.concatenate([atmos_flux.T, gap, atmos_coupling, gap], axis=0)
    terms = jnp.where(is_ocean, ocean_terms, atmos_terms).astype(F32)

    edge = shape((2 * cols + 16, channels), BF16)
    half = shape((cells, channels), BF16)
    near, far, own_early, own = call(
        bound(pack_kernel, cols=cols),
        [edge, edge, half, shape((2 * cells + 16, channels), BF16)],
        [x, g, wet_mask],
        [IN_PLACE] * 3,
        [
            pltpu.VMEM(x.shape, BF16),
            pltpu.VMEM(x.shape, BF16),
            pltpu.VMEM(wet_mask.shape, jnp.int32),
            pltpu.SemaphoreType.DMA((3,)),
        ],
        name="pack",
        limit=PACK_VMEM,
    )
    near, far = halo(near, far)
    other_early = swapped(own_early, "grp", 1)
    wide = -(-narrow // 128) * 128
    own, atmos_flat, ocean_flat = call(
        hold_kernel,
        [
            shape(own.shape, BF16),
            shape((18, channels, channels), BF16),
            shape((18, wide, narrow), BF16),
        ],
        [own, atmos_kernels.reshape(18, channels, channels), ocean_kernels.reshape(18, narrow, narrow)],
        [WHOLE, IN_PLACE, IN_PLACE],
        [pltpu.SemaphoreType.DMA],
        flops=PACE * 10**8,
        name="hold",
        limit=HOLD_VMEM,
    )
    pad = shape((2 * cells, channels), BF16)
    xpad, gpad, wet, edges, sent = call(
        bound(outgoing_kernel, cols=cols),
        [pad, pad, shape((8, 2 * cells), F32), half, shape((4, 2 * cells), F32)],
        [own, near, far, terms],
        name="outgoing",
    )
    arrived = swapped(sent, "grp", 1)
    other_edges = swapped(edges, "grp", 1)
    conv_cost = dict(flops=PACE * 9 * cells * channels * channels, moved=9 * channels * channels * 2)
    back = call(
        bound(back_kernel, cols=cols),
        shape((cells, channels), F32),
        [gpad, atmos_flat, ocean_flat],
        **conv_cost,
        name="back",
    )
    upad, stay, give, near, far = call(
        bound(first_kernel, cols=cols),
        [pad, half, half, half, half],
        [xpad, wet, arrived, terms, back, atmos_flat, ocean_flat],
        None,
        [pltpu.VMEM((cells, channels), F32)],
        **conv_cost,
        name="first",
    )
    late = swapped(give, "grp", 1)

    near, far = halo(near, far)

    atmos_rows = 9 * channels // count
    ocean_rows = 9 * narrow // count
    chunked = count == 16 and 9 * channels % (8 * count) == 0 and ocean_rows % 2 == 0
    tall = -(-(atmos_rows + ocean_rows // 2) // 16) * 16
    spare = max(0, 2 * (tall - atmos_rows) - ocean_rows) if chunked else 0
    ocean_tall = 9 * narrow + -(-spare // 8) * 8
    sums = [shape((9 * channels, channels), F32), shape((wide // 128, ocean_tall, 128), F32)]
    atmos_sum, ocean_sum, lefts = call(
        bound(own_grads_kernel, cols=cols),
        [*sums, shape((3, channels, 2 * cells), BF16)],
        [upad, gpad, stay, other_early, other_edges, sent, atmos_coupling],
        **conv_cost,
        name="own_grads",
    )
    atmos_other, ocean_other = call(
        bound(other_grads_kernel, cols=cols),
        sums,
        [lefts, late, other_early, other_edges],
        **conv_cost,
        name="other_grads",
    )
    if chunked:
        part = shape((count // 2, tall, channels), BF16)
        keep, send = call(
            bound(chunk_kernel, chunks=count),
            [part, part],
            [atmos_sum, ocean_sum, atmos_other, ocean_other, near, far],
            [WHOLE] * 4 + [ANYWHERE] * 2,
            moved=4 * count * tall * channels,
            name="chunk",
        )
        came = swapped(send, "lat", 1)

    grad, sent_back = call(
        bound(input_grad_kernel, cols=cols),
        [shape((cells, channels), F32), shape((4, cells), F32)],
        [stay, give, near, far, gpad, wet, terms, atmos_flat, ocean_flat],
        **conv_cost,
        name="input_grad",
    )
    returned = swapped(sent_back, "grp", 1)
    next_field, next_mark = call(
        bound(next_kernel, cols=cols),
        [shape(x.shape, BF16), MARK],
        [stay, give, near, far, upad, atmos_flat, ocean_flat],
        None,
        [pltpu.VMEM((cells, channels), F32)],
        **conv_cost,
        name="next",
    )
    field_grad, last_mark = call(
        bound(last_kernel, cols=cols),
        [shape(x.shape, BF16), MARK],
        [grad, returned, wet, terms],
        name="last",
    )

    if chunked:
        atmos_chunk, ocean_chunk = call(
            bound(finish_kernel, atmos_factor=atmos_factor, ocean_factor=ocean_factor),
            [
                shape((atmos_rows * channels // 128, 128), F32),
                shape((ocean_rows * narrow // 128, 128), F32),
            ],
            scatter_sum(keep, came, sent_back, [next_mark, last_mark]),
            name="finish",
        )
        atmos_total, ocean_total = atmos_chunk.reshape(-1), ocean_chunk.reshape(-1)
    else:
        atmos_all = jnp.where(is_ocean, atmos_other, atmos_sum)
        ocean_all = jnp.where(is_ocean, ocean_sum, ocean_other)
        atmos_total = atmos_factor * lax.psum_scatter(
            atmos_all.reshape(-1), "lat", scatter_dimension=0, tiled=True
        )
        ocean_all = jnp.concatenate([ocean_all[piece] for piece in range(wide // 128)], axis=1)
        ocean_total = ocean_factor * lax.psum_scatter(
            ocean_all[:, :narrow].reshape(-1), "lat", scatter_dimension=0, tiled=True
        )
    return (next_field[None], field_grad[None], ocean_total, atmos_total)


def solution(mesh):
    in_specs = (
        P("grp", "lat", None, None),
        P("grp", "lat", None, None),
        P(),
        P(),
        P(),
        P(),
        P(),
        P(),
        P("lat"),
        P("lat", None),
    )
    out_specs = (
        P("grp", "lat", None, None),
        P("grp", "lat", None, None),
        P(("grp", "lat")),
        P(("grp", "lat")),
    )
    return jax.shard_map(local, mesh=mesh, in_specs=in_specs, out_specs=out_specs, check_vma=False)
```

```python
import functools
import math

import jax
import jax.numpy as jnp
from jax import lax
from jax.experimental import pallas as pl
from jax.experimental.pallas import tpu as pltpu
from jax.sharding import PartitionSpec as P

HIGHEST = lax.Precision.HIGHEST
GELU_SCALE = 0.7978845608028654
GELU_CUBIC = 0.044715
F32 = jnp.float32
BF16 = jnp.bfloat16
WHOLE = pl.BlockSpec(memory_space=pltpu.VMEM)
IN_PLACE = pl.BlockSpec(memory_space=pltpu.HBM)
ANYWHERE = pl.BlockSpec(memory_space=pl.ANY)
VMEM_LIMIT = 20 * 1024 * 1024
PACE = 8
PACK_VMEM = 62 * 1024 * 1024
HOLD_VMEM = 42 * 1024 * 1024

NN = (((1,), (0,)), ((), ()))
NT = (((1,), (1,)), ((), ()))
TN = (((0,), (0,)), ((), ()))


def shape(dims, kind):
    return jax.ShapeDtypeStruct(dims, kind)


def call(kernel, outs, inputs, in_specs=None, scratch=(), flops=0, moved=0, name=None, limit=VMEM_LIMIT, out_spec=WHOLE):
    return pl.pallas_call(
        kernel,
        out_shape=outs,
        in_specs=in_specs or [WHOLE] * len(inputs),
        out_specs=jax.tree.map(lambda _: out_spec, outs),
        scratch_shapes=list(scratch),
        compiler_params=pltpu.CompilerParams(vmem_limit_bytes=limit),
        cost_estimate=pl.CostEstimate(flops=flops, bytes_accessed=moved, transcendentals=0),
        name=name,
    )(*inputs)


def on_ocean():
    return lax.axis_index("grp") == 0


def dot(left, right, dims=NN, precision=None):
    return lax.dot_general(left, right, dims, precision=precision, preferred_element_type=F32)


def moved_cells(values, axis, cols):
    count = values.shape[axis]
    place = lax.rem(lax.broadcasted_iota(jnp.int32, values.shape, axis), cols)
    before = jnp.where(place == 0, 0.0, pltpu.roll(values, 1, axis))
    after = jnp.where(place == cols - 1, 0.0, pltpu.roll(values, count - 1, axis))
    return before, after


def wet_halves(wet, cols, channels):
    source = lax.broadcasted_iota(jnp.int32, (2 * cols, 2 * cols), 0)
    target = lax.broadcasted_iota(jnp.int32, (2 * cols, 2 * cols), 1)
    wanted = 2 * lax.rem(target, cols) + jnp.where(target >= cols, 1, 0)
    chooser = (source == wanted).astype(F32).astype(BF16)
    padded = jnp.concatenate([wet.astype(F32), jnp.zeros((14, 2 * cols), F32)], axis=0)
    apart = dot(padded.astype(BF16), chooser)
    return jnp.concatenate([apart, jnp.zeros((16, channels - 2 * cols), F32)], axis=1)


def own_bit(bit):
    return lax.rem(lax.shift_right_logical(lax.axis_index("lat"), bit), 2)


def pack_kernel(
    x_any, g_any, wet_any, near_ref, far_ref, early_ref, own_ref, x_ref, g_ref, wet_ref, sems, *, cols
):
    pairs = ((wet_any, wet_ref), (x_any, x_ref), (g_any, g_ref))
    copies = [pltpu.make_async_copy(*pair, sems.at[index]) for index, pair in enumerate(pairs)]
    for copy in copies:
        copy.start()
    core = own_bit(0)
    copies[0].wait()
    wide = wet_halves(wet_ref[...], cols, x_ref.shape[2])
    other = pltpu.roll(wide, 15, 0)
    own_ref[4 * cols :, :] = wide.astype(BF16)
    far_ref[2 * cols :, :] = jnp.where(core == 0, wide, other).astype(BF16)
    near_ref[2 * cols :, :] = jnp.where(core == 0, other, wide).astype(BF16)
    copies[1].wait()
    copies[2].wait()
    for part, ref in enumerate((x_ref, g_ref)):
        far_ref[part * cols : (part + 1) * cols, :] = ref[core]
        near_ref[part * cols : (part + 1) * cols, :] = ref[1 - core]
        own_ref[2 * part * cols : (2 * part + 1) * cols, :] = ref[0]
        own_ref[(2 * part + 1) * cols : (2 * part + 2) * cols, :] = ref[1]
    for row in range(2):
        early_ref[row * cols : (row + 1) * cols, :] = jnp.where(on_ocean(), g_ref[row], x_ref[row])


def hold_kernel(own_in, atmos_any, ocean_any, own_ref, atmos_ref, ocean_ref, sem):
    narrow = ocean_ref.shape[2]
    ocean_copy = pltpu.make_async_copy(ocean_any, ocean_ref.at[:, pl.ds(0, narrow), :], sem)
    atmos_copy = pltpu.make_async_copy(atmos_any, atmos_ref, sem)

    @pl.when(on_ocean())
    def _():
        ocean_copy.start()
        gap = ocean_ref.shape[1] - narrow
        if gap:
            ocean_ref[:, narrow:, :] = jnp.zeros((ocean_ref.shape[0], gap, narrow), BF16)

    @pl.when(jnp.logical_not(on_ocean()))
    def _():
        atmos_copy.start()

    own_ref[...] = own_in[...]

    @pl.when(on_ocean())
    def _():
        ocean_copy.wait()

    @pl.when(jnp.logical_not(on_ocean()))
    def _():
        atmos_copy.wait()


def low_and_high(near, far):
    core = own_bit(0)
    return jnp.where(core == 0, far, near), jnp.where(core == 0, near, far)


def outgoing_kernel(
    own_ref, near_ref, far_ref, terms_ref, xpad_ref, gpad_ref, wet_ref, edge_ref, sent_ref, *, cols
):
    low, high = low_and_high(near_ref[...], far_ref[...])
    for part, pad_ref in enumerate((xpad_ref, gpad_ref)):
        pad_ref[0:cols, :] = low[part * cols : (part + 1) * cols]
        pad_ref[cols : 3 * cols, :] = own_ref[2 * part * cols : 2 * (part + 1) * cols, :]
        pad_ref[3 * cols : 4 * cols, :] = high[part * cols : (part + 1) * cols]
    low_wet = low[2 * cols :].astype(F32)
    high_wet = high[2 * cols :].astype(F32)
    own_wet = own_ref[4 * cols :, :].astype(F32)
    halves = []
    for start in (0, cols):
        lanes = slice(start, start + cols)
        rows = (low_wet[0:1, lanes], own_wet[0:1, lanes], own_wet[1:2, lanes], high_wet[0:1, lanes])
        halves.append(jnp.concatenate(rows, axis=1))
    first_wet, second_wet = halves
    inverse = 1.0 / jnp.maximum(first_wet + second_wet, 1.0)
    wet_ref[0:1, :] = first_wet
    wet_ref[1:2, :] = second_wet
    wet_ref[2:3, :] = inverse
    wet_ref[3:8, :] = jnp.zeros((5, 4 * cols), F32)
    xpad = xpad_ref[...]
    projected = dot(terms_ref[0:8, :].astype(BF16), xpad, NT)
    mixed = (projected[0:4] * first_wet + projected[4:8] * second_wet) * inverse
    sent_ref[...] = jnp.where(on_ocean(), mixed, projected[0:4])
    edge_ref[0:cols, :] = jnp.where(on_ocean(), gpad_ref[0:cols, :], xpad_ref[0:cols, :])
    edge_ref[cols:, :] = jnp.where(on_ocean(), gpad_ref[3 * cols :, :], xpad_ref[3 * cols :, :])


def halves_apart(values, narrow):
    wide = -(-narrow // 128) * 128
    lane = lax.broadcasted_iota(jnp.int32, values.shape, 1)
    even = jnp.where(lane < narrow, values, 0.0)
    odd = jnp.where(lane < narrow, pltpu.roll(values, narrow, 1), 0.0)
    return even[:, :wide], odd[:, :wide]


def halves_with_columns(pad, cols):
    even, odd = halves_apart(pad.astype(F32), pad.shape[1] // 2)
    odd_before = moved_cells(odd, 0, cols)[0].astype(BF16)
    even_after = moved_cells(even, 0, cols)[1].astype(BF16)
    even, odd = even.astype(BF16), odd.astype(BF16)
    return (odd_before, even, odd), (even, odd, even_after)


def with_columns(pad, cols):
    before, after = moved_cells(pad.astype(F32), 0, cols)
    return before.astype(BF16), pad, after.astype(BF16)


def convolve(pad, out_ref, atmos_ref, ocean_ref, layer, flipped, cols):
    base = 9 * layer
    channels = atmos_ref.shape[2]
    wide, narrow = ocean_ref.shape[1:]
    rows = out_ref.shape[0]

    def summed(pick):
        total = None
        for row_tap in range(3):
            part = pick(row_tap, slice(cols * row_tap, cols * row_tap + rows))
            total = part if total is None else total + part
        return total

    @pl.when(on_ocean())
    def _():
        evens, odds = halves_with_columns(pad, cols)
        if flipped:

            def pick(row_tap, span):
                part = None
                for col_tap in range(3):
                    left = jnp.concatenate([evens[col_tap][span], odds[col_tap][span]], axis=0)
                    kernel = ocean_ref[base + 8 - (3 * row_tap + col_tap), 0:narrow, :]
                    piece = dot(left[:, :narrow], kernel, NT)
                    part = piece if part is None else part + piece
                return part

        else:
            even, odd = jnp.concatenate(evens, axis=1), jnp.concatenate(odds, axis=1)

            def pick(row_tap, span):
                first = base + 3 * row_tap
                kernel = ocean_ref[first : first + 3].reshape(3 * wide, narrow)
                return dot(jnp.concatenate([even[span], odd[span]], axis=0), kernel)

        total = summed(pick)
        out_ref[...] = jnp.concatenate([total[:rows], total[rows:]], axis=1)

    @pl.when(jnp.logical_not(on_ocean()))
    def _():
        taps = with_columns(pad, cols)
        if flipped:

            def pick(row_tap, span):
                part = None
                for col_tap in range(3):
                    piece = dot(taps[col_tap][span], atmos_ref[base + 8 - (3 * row_tap + col_tap)], NT)
                    part = piece if part is None else part + piece
                return part

        else:
            joined = jnp.concatenate(taps, axis=1)

            def pick(row_tap, span):
                first = base + 3 * row_tap
                return dot(joined[span], atmos_ref[first : first + 3].reshape(3 * channels, channels))

        out_ref[...] = summed(pick)


def back_kernel(gpad_ref, atmos_ref, ocean_ref, out_ref, *, cols):
    convolve(gpad_ref[...], out_ref, atmos_ref, ocean_ref, 1, True, cols)


def spread(arrived, wet, mixing, terms):
    first_wet, second_wet = wet
    both = jnp.concatenate([arrived * first_wet, arrived * second_wet], axis=0)
    alone = jnp.concatenate([arrived, jnp.zeros_like(arrived)], axis=0)
    return dot(jnp.where(mixing, both, alone), terms, TN, HIGHEST)


def first_kernel(
    xpad_ref, wet_ref, arrived_ref, terms_ref, back_ref, atmos_ref, ocean_ref,
    u_ref, stay_ref, give_ref, near_ref, far_ref, first_ref, *, cols,
):
    wet = wet_ref[0:1, :], wet_ref[1:2, :]
    coupled = spread(arrived_ref[...], wet, on_ocean(), terms_ref[8:16, :])
    u = (xpad_ref[...].astype(F32) + coupled).astype(BF16)
    u_ref[...] = u
    convolve(u, first_ref, atmos_ref, ocean_ref, 0, False, cols)
    first = first_ref[...]
    tangent = jnp.tanh(GELU_SCALE * (first + GELU_CUBIC * first * first * first))
    hidden = (0.5 * first * (1.0 + tangent)).astype(BF16)
    slope = 0.5 * (1.0 + tangent) + 0.5 * first * (1.0 - tangent * tangent) * GELU_SCALE * (
        1.0 + 3.0 * GELU_CUBIC * first * first
    )
    first_grad = (back_ref[...] * slope).astype(BF16)
    stay_ref[...] = jnp.where(on_ocean(), first_grad, hidden)
    give_ref[...] = jnp.where(on_ocean(), hidden, first_grad)
    core = own_bit(0)
    for part, values in enumerate((hidden, first_grad)):
        target = slice(part * cols, (part + 1) * cols)
        far_ref[target, :] = jnp.where(core == 0, values[:cols], values[cols:])
        near_ref[target, :] = jnp.where(core == 0, values[cols:], values[:cols])


def whole_pad(early_ref, edge_ref, cols):
    parts = [edge_ref[0:cols, :], early_ref[...], edge_ref[cols:, :]]
    return jnp.concatenate(parts, axis=0).astype(F32)


def grad_atmos(pad, own, cols, store):
    rows = own.shape[0]
    left = own.T.astype(BF16)
    before, after = moved_cells(pad, 0, cols)
    rights = [part.astype(BF16) for part in (after, pad, before)]
    for tap in range(9):
        start = cols * (2 - tap // 3)
        store(tap, dot(left, rights[tap % 3][start : start + rows]))


def grad_ocean(pad, own, pad_is_input, cols, store):
    rows, channels = own.shape
    narrow = channels // 2

    if pad_is_input:
        middle = pad.T
        before, after = moved_cells(middle, 1, cols)
        even, odd = middle[:narrow].astype(BF16), middle[narrow:].astype(BF16)
        pairs = (
            (before[narrow:].astype(BF16), even),
            (even, odd),
            (odd, after[:narrow].astype(BF16)),
        )
        right = jnp.concatenate(halves_apart(own, narrow), axis=0).astype(BF16)
        for tap in range(9):
            start = cols * (tap // 3)
            pieces = [part[:, start : start + rows] for part in pairs[tap % 3]]
            store(tap, dot(jnp.concatenate(pieces, axis=1), right))
    else:
        turned = own.T.astype(BF16)
        left = jnp.concatenate([turned[:narrow], turned[narrow:]], axis=1)
        even, odd = halves_apart(pad, narrow)
        odd_before = moved_cells(odd, 0, cols)[0].astype(BF16)
        even_after = moved_cells(even, 0, cols)[1].astype(BF16)
        even, odd = even.astype(BF16), odd.astype(BF16)
        pairs = ((odd, even_after), (even, odd), (odd_before, even))
        for tap in range(9):
            start = cols * (2 - tap // 3)
            pieces = [part[start : start + rows] for part in pairs[tap % 3]]
            store(tap, dot(left, jnp.concatenate(pieces, axis=0)))


def store_into(out_ref):
    def store(tap, value):
        if len(out_ref.shape) == 2:
            rows = value.shape[0]
            out_ref[rows * tap : rows * (tap + 1), :] = value
        else:
            rows = value.shape[0]
            for piece in range(out_ref.shape[0]):
                lanes = slice(128 * piece, 128 * (piece + 1))
                out_ref[piece, rows * tap : rows * (tap + 1), :] = value[:, lanes]

    return store


def near_rows(near_ref, part, cols):
    if len(near_ref.shape) == 2:
        return near_ref[part * cols : (part + 1) * cols, :]
    count, tall = near_ref.shape[0] // 2, near_ref.shape[1]
    taken = cols // count
    pieces = [near_ref[index, tall - taken :, :] for index in range(part * count, (part + 1) * count)]
    return jnp.concatenate(pieces, axis=0)


def hidden_and_grad(stay_ref, give_ref):
    stay, give = stay_ref[...], give_ref[...]
    return jnp.where(on_ocean(), give, stay), jnp.where(on_ocean(), stay, give)


def shifted_inputs(pad, cols):
    middle = pad.T
    before, after = moved_cells(middle, 1, cols)
    return [part.astype(BF16) for part in (before, middle, after)]


def own_grads_kernel(
    upad_ref, gpad_ref, stay_ref, early_ref, edge_ref, sent_ref, coupling_ref,
    atmos_out, ocean_out, left_ref, *, cols,
):
    stay = stay_ref[...].astype(F32)

    @pl.when(on_ocean())
    def _():
        grad_ocean(upad_ref[...].astype(F32), stay, True, cols, store_into(ocean_out))
        added = dot(sent_ref[...], coupling_ref[...].astype(F32), TN, HIGHEST)
        other = (whole_pad(early_ref, edge_ref, cols) + added).astype(BF16).astype(F32)
        for tap, left in enumerate(shifted_inputs(other, cols)):
            left_ref[tap] = left

    @pl.when(jnp.logical_not(on_ocean()))
    def _():
        grad_atmos(gpad_ref[...].astype(F32), stay, cols, store_into(atmos_out))


def other_grads_kernel(left_ref, late_ref, early_ref, edge_ref, atmos_out, ocean_out, *, cols):
    rows = late_ref.shape[0]

    @pl.when(on_ocean())
    def _():
        store = store_into(atmos_out)
        for tap in range(9):
            start = cols * (tap // 3)
            store(tap, dot(left_ref[tap % 3, :, start : start + rows], late_ref[...]))

    @pl.when(jnp.logical_not(on_ocean()))
    def _():
        late = late_ref[...].astype(F32)
        grad_ocean(whole_pad(early_ref, edge_ref, cols), late, False, cols, store_into(ocean_out))


def chunk_rows(out_ref, side, tall, atmos_all, ocean_all, chunks):
    channels = out_ref.shape[2]
    pieces = ocean_all.shape[0]
    atmos_rows = atmos_all.shape[0] // chunks
    ocean_rows = atmos_rows // 2
    taken = tall - atmos_rows
    blank = jnp.zeros((taken, channels - 128 * pieces), F32)
    for pair in range(chunks // 2):
        start = pl.multiple_of(atmos_rows * (2 * pair + side), 8)
        upper = atmos_all[pl.ds(start, atmos_rows), :]
        start = ocean_rows * (2 * pair + side)
        halves = []
        for odd in range(2):
            parts = [ocean_all.at[piece][pl.ds(start + odd, taken, 2), :] for piece in range(pieces)]
            halves.append(jnp.concatenate(parts + [blank], axis=1))
        lower = halves[0] + pltpu.roll(halves[1], channels // 2, 1)
        out_ref[pair, 0:tall, :] = jnp.concatenate([upper, lower], axis=0).astype(BF16)


def chunk_kernel(atmos_own, ocean_own, atmos_other, ocean_other, *refs, chunks, tall, sent):
    out_ref = refs[-1]
    core = own_bit(0)
    side = 1 - core if sent else core
    if sent:
        near_ref = refs[0]
        taken = out_ref.shape[1] - tall
        for pair in range(chunks // 2):
            out_ref[pair, tall:, :] = near_ref[pair * taken : (pair + 1) * taken, :]

    @pl.when(on_ocean())
    def _():
        chunk_rows(out_ref, side, tall, atmos_other, ocean_own, chunks)

    @pl.when(jnp.logical_not(on_ocean()))
    def _():
        chunk_rows(out_ref, side, tall, atmos_own, ocean_other, chunks)


def halve(keep_ref, came_ref, out_ref, side, rows):
    for outer in range(keep_ref.shape[0]):
        for inner in range(keep_ref.shape[2]):
            total = keep_ref[outer, side, inner, rows, :].astype(F32)
            total = total + came_ref[outer, side, inner, rows, :].astype(F32)
            out_ref[outer, inner] = total.astype(BF16)


def split_kernel(keep_ref, came_ref, *refs, cuts, sent):
    by_z = [ref.reshape(2, 2, 2, *ref.shape[3:]) for ref in (keep_ref, came_ref)]
    start = 0
    for index, rows in enumerate(cuts):
        pair, bit = (by_z, 2) if index == 1 else ((keep_ref, came_ref), 1)
        own = own_bit(bit)
        halve(*pair, refs[index], 1 - own if sent else own, slice(start, start + rows))
        start += rows
    if sent:
        refs[-1][...] = jnp.zeros_like(refs[-1])


def halve_kernel(keep_ref, came_ref, *refs, bit, marked):
    outs = refs[-3:] if marked else refs[-2:]
    own = own_bit(bit)
    halve(keep_ref, came_ref, outs[1], 1 - own, slice(None))
    halve(keep_ref, came_ref, outs[0], own, slice(None))
    if marked:
        outs[2][...] = jnp.zeros_like(outs[2])


MARK = shape((8, 128), F32)


def halved(keep, came, bit, dims, after, marked=True):
    outer, inner, rows, channels = dims[0], dims[1], keep.shape[-2], keep.shape[-1]
    keep, came = (part.reshape(outer, 2, inner, rows, channels) for part in (keep, came))
    out = shape((outer, inner, rows, channels), BF16)
    return call(
        functools.partial(halve_kernel, bit=bit, marked=marked),
        [out, out] + [MARK] * marked,
        [keep, came, *after],
        [WHOLE] * 2 + [ANYWHERE] * len(after),
        moved=8 * outer * inner * rows * channels,
        name="halve",
    )


def split(keep, came):
    pairs, tall, channels = keep.shape
    cuts = [16 * (tall // 16 * part // 17) for part in (6, 6)]
    cuts.append(tall - sum(cuts))
    outs = [
        shape(((2, 2) if index == 1 else (4, 1)) + (rows, channels), BF16) for index, rows in enumerate(cuts)
    ]
    inputs = [part.reshape(4, 2, 1, *part.shape[1:]) for part in (keep, came)]
    kept, sent = (
        call(
            functools.partial(split_kernel, cuts=cuts, sent=is_sent),
            outs + [MARK] * is_sent,
            inputs,
            moved=3 * pairs * tall * channels,
            name="split",
        )
        for is_sent in (False, True)
    )
    return kept, sent[:3], sent[3]


def scatter_sum(kept, sent, before_b, finish_last):
    (a_keep, b_keep, c_keep), (a_send, b_send, c_send) = kept, sent
    channels = a_keep.shape[-1]
    a_came = swapped(a_send, "lat", 2)
    b_came = swapped(b_send, "lat", 4)
    c_came = swapped(c_send, "lat", 2)
    b_keep, b_send, mark = halved(b_keep, b_came, 3, (1, 2), before_b)
    b_came = swapped(b_send, "lat", 8)
    mark = finish_last(mark)
    a_keep, a_send, mark = halved(a_keep, a_came, 2, (2, 1), [mark])
    a_came = swapped(a_send, "lat", 4)
    c_keep, c_send, mark = halved(c_keep, c_came, 2, (2, 1), [mark])
    c_came = swapped(c_send, "lat", 4)
    b_keep, b_send, mark = halved(b_keep, b_came, 1, (1, 1), [mark])
    b_came = swapped(b_send, "lat", 2)
    a_keep, a_send, mark = halved(a_keep, a_came, 3, (1, 1), [mark])
    a_came = swapped(a_send, "lat", 8)
    c_keep, c_send = halved(c_keep, c_came, 3, (1, 1), [mark], False)
    c_came = swapped(c_send, "lat", 8)
    return [part.reshape(-1, channels) for part in (a_keep, a_came, b_keep, b_came, c_keep, c_came)]


def finish_kernel(*refs, atmos_factor, ocean_factor):
    parts, (atmos_ref, ocean_ref) = refs[:-2], refs[-2:]
    channels = parts[0].shape[1]
    pieces = channels // 128
    atmos_rows = atmos_ref.shape[0] // pieces
    ocean_rows = ocean_ref.shape[0] // pieces
    sums = [
        parts[index][...].astype(F32) + parts[index + 1][...].astype(F32)
        for index in range(0, len(parts), 2)
    ]
    total = jnp.concatenate(sums, axis=0)
    for piece in range(pieces):
        lanes = slice(128 * piece, 128 * (piece + 1))
        atmos_ref[pl.ds(piece, atmos_rows, pieces), :] = total[:atmos_rows, lanes] * atmos_factor
        ocean_ref[pl.ds(piece, ocean_rows, pieces), :] = (
            total[atmos_rows : atmos_rows + ocean_rows, lanes] * ocean_factor
        )


def input_grad_kernel(
    stay_ref, give_ref, near_ref, far_ref, gpad_ref, wet_ref, terms_ref, atmos_ref, ocean_ref, *refs, cols
):
    grad_ref, sent_ref = refs[-2:]
    middle = hidden_and_grad(stay_ref, give_ref)[1]
    low, high = low_and_high(near_rows(near_ref, 1, cols), far_ref[cols:, :])
    pad = jnp.concatenate([low, middle, high], axis=0)
    own = slice(cols, 3 * cols)
    convolve(pad, grad_ref, atmos_ref, ocean_ref, 0, True, cols)
    grad = gpad_ref[own, :].astype(F32) + grad_ref[...]
    grad_ref[...] = grad
    weighted = dot(terms_ref[8:16, :], grad, NT, HIGHEST)
    mixed = weighted[0:4] * wet_ref[0:1, own] + weighted[4:8] * wet_ref[1:2, own]
    sent_ref[...] = jnp.where(on_ocean(), mixed, weighted[0:4])


def next_kernel(
    stay_ref, give_ref, near_ref, far_ref, upad_ref, atmos_ref, ocean_ref,
    next_ref, mark_ref, second_ref, *, cols,
):
    middle = hidden_and_grad(stay_ref, give_ref)[0]
    low, high = low_and_high(near_rows(near_ref, 0, cols), far_ref[0:cols, :])
    pad = jnp.concatenate([low, middle, high], axis=0)
    own = slice(cols, 3 * cols)
    convolve(pad, second_ref, atmos_ref, ocean_ref, 1, False, cols)
    values = (upad_ref[own, :].astype(F32) + second_ref[...]).astype(BF16)
    next_ref[0] = values[:cols]
    next_ref[1] = values[cols:]
    mark_ref[...] = jnp.zeros_like(mark_ref)


def last_kernel(grad_ref, arrived_ref, wet_ref, terms_ref, *refs, cols):
    out_ref, mark_ref = refs[-2:]
    own = slice(cols, 3 * cols)
    wet = wet_ref[0:1, own], wet_ref[1:2, own]
    arrived = jnp.where(on_ocean(), arrived_ref[...] * wet_ref[2:3, own], arrived_ref[...])
    added = spread(arrived, wet, on_ocean(), terms_ref[0:8, :])
    values = (grad_ref[...] + added).astype(BF16)
    out_ref[0] = values[:cols]
    out_ref[1] = values[cols:]
    mark_ref[...] = jnp.zeros_like(mark_ref)


def swapped(value, axis, mask):
    pairs = [(source, source ^ mask) for source in range(lax.axis_size(axis))]
    return lax.ppermute(value, axis, pairs)


def far_halo(far):
    pairs = [(i, i + 1 if i % 2 else i - 1) for i in range(1, lax.axis_size("lat") - 1)]
    return lax.ppermute(far, "lat", pairs)


def local(
    fields,
    cotangent,
    ocean_kernels,
    atmos_kernels,
    ocean_surface,
    ocean_coupling,
    atmos_flux,
    atmos_coupling,
    row_map,
    wet_mask,
):
    x, g = fields[0], cotangent[0]
    bands, cols, channels = x.shape
    narrow = channels // 2
    cells = bands * cols
    count = lax.axis_size("lat")
    is_ocean = lax.axis_index("grp") == 0
    atmos_factor = 1.0 / math.sqrt(bands * count * cols)
    ocean_factor = 1.0 / math.sqrt(bands * count * 2 * cols)
    bound = functools.partial

    blank = jnp.zeros((4, narrow), BF16)
    gap = jnp.zeros((4, channels), BF16)
    surface = ocean_surface.T
    ocean_terms = jnp.concatenate(
        [
            jnp.concatenate([surface, blank], axis=1),
            jnp.concatenate([blank, surface], axis=1),
            jnp.concatenate([ocean_coupling, blank], axis=1),
            jnp.concatenate([blank, ocean_coupling], axis=1),
        ],
        axis=0,
    )
    atmos_terms = jnp.concatenate([atmos_flux.T, gap, atmos_coupling, gap], axis=0)
    terms = jnp.where(is_ocean, ocean_terms, atmos_terms).astype(F32)

    edge = shape((2 * cols + 16, channels), BF16)
    half = shape((cells, channels), BF16)
    near, far, own_early, own = call(
        bound(pack_kernel, cols=cols),
        [edge, edge, half, shape((2 * cells + 16, channels), BF16)],
        [x, g, wet_mask],
        [IN_PLACE] * 3,
        [
            pltpu.VMEM(x.shape, BF16),
            pltpu.VMEM(x.shape, BF16),
            pltpu.VMEM(wet_mask.shape, jnp.int32),
            pltpu.SemaphoreType.DMA((3,)),
        ],
        name="pack",
        limit=PACK_VMEM,
    )
    near, far = swapped(near, "lat", 1), far_halo(far)
    other_early = swapped(own_early, "grp", 1)
    wide = -(-narrow // 128) * 128
    own, atmos_flat, ocean_flat = call(
        hold_kernel,
        [
            shape(own.shape, BF16),
            shape((18, channels, channels), BF16),
            shape((18, wide, narrow), BF16),
        ],
        [own, atmos_kernels.reshape(18, channels, channels), ocean_kernels.reshape(18, narrow, narrow)],
        [WHOLE, IN_PLACE, IN_PLACE],
        [pltpu.SemaphoreType.DMA],
        flops=PACE * 10**8,
        name="hold",
        limit=HOLD_VMEM,
    )
    pad = shape((2 * cells, channels), BF16)
    xpad, gpad, wet, edges, sent = call(
        bound(outgoing_kernel, cols=cols),
        [pad, pad, shape((8, 2 * cells), F32), half, shape((4, 2 * cells), F32)],
        [own, near, far, terms],
        name="outgoing",
    )
    arrived = swapped(sent, "grp", 1)
    other_edges = swapped(edges, "grp", 1)
    conv_cost = dict(flops=PACE * 9 * cells * channels * channels, moved=9 * channels * channels * 2)
    back = call(
        bound(back_kernel, cols=cols),
        shape((cells, channels), F32),
        [gpad, atmos_flat, ocean_flat],
        **conv_cost,
        name="back",
    )
    upad, stay, give, near, far = call(
        bound(first_kernel, cols=cols),
        [pad, half, half, half, half],
        [xpad, wet, arrived, terms, back, atmos_flat, ocean_flat],
        None,
        [pltpu.VMEM((cells, channels), F32)],
        **conv_cost,
        name="first",
    )
    late = swapped(give, "grp", 1)

    far = far_halo(far)

    atmos_rows = 9 * channels // count
    ocean_rows = 9 * narrow // count
    chunked = count == 16 and 9 * channels % (8 * count) == 0 and ocean_rows % 2 == 0
    tall = -(-(atmos_rows + ocean_rows // 2) // 16) * 16
    spare = max(0, 2 * (tall - atmos_rows) - ocean_rows) if chunked else 0
    ocean_tall = 9 * narrow + -(-spare // 8) * 8
    sums = [shape((9 * channels, channels), F32), shape((wide // 128, ocean_tall, 128), F32)]
    atmos_sum, ocean_sum, lefts = call(
        bound(own_grads_kernel, cols=cols),
        [*sums, shape((3, channels, 2 * cells), BF16)],
        [upad, gpad, stay, other_early, other_edges, sent, atmos_coupling],
        **conv_cost,
        name="own_grads",
    )
    atmos_other, ocean_other = call(
        bound(other_grads_kernel, cols=cols),
        sums,
        [lefts, late, other_early, other_edges],
        **conv_cost,
        name="other_grads",
    )
    if chunked:
        taken = 2 * cols // (count // 2)
        sums = [atmos_sum, ocean_sum, atmos_other, ocean_other]
        send, keep = (
            call(
                bound(chunk_kernel, chunks=count, tall=tall, sent=sent),
                shape((count // 2, tall + taken * sent, channels), BF16),
                sums + [near, far] * sent,
                [WHOLE] * (4 + sent) + [ANYWHERE] * sent,
                moved=2 * count * tall * channels,
                name="chunk",
            )
            for sent in (True, False)
        )
        near = swapped(send, "lat", 1)
        kept, parts, split_mark = split(keep, near)
        after_split = [split_mark]
    else:
        near = swapped(near, "lat", 1)
        after_split = []

    grad, sent_back = call(
        bound(input_grad_kernel, cols=cols),
        [shape((cells, channels), F32), shape((4, cells), F32)],
        [stay, give, near, far, gpad, wet, terms, atmos_flat, ocean_flat, *after_split],
        [WHOLE] * 9 + [ANYWHERE] * len(after_split),
        **conv_cost,
        name="input_grad",
    )
    returned = swapped(sent_back, "grp", 1)
    next_field, next_mark = call(
        bound(next_kernel, cols=cols),
        [shape(x.shape, BF16), MARK],
        [stay, give, near, far, upad, atmos_flat, ocean_flat],
        None,
        [pltpu.VMEM((cells, channels), F32)],
        **conv_cost,
        name="next",
    )

    def field_grads(*after):
        return call(
            bound(last_kernel, cols=cols),
            [shape(x.shape, BF16), MARK],
            [grad, returned, wet, terms, *after],
            [WHOLE] * 4 + [ANYWHERE] * len(after),
            name="last",
        )

    if chunked:
        made = []

        def finish_last(mark):
            made.extend(field_grads(mark))
            return made[1]

        sums = scatter_sum(kept, parts, [returned, next_mark], finish_last)
        field_grad = made[0]
        atmos_chunk, ocean_chunk = call(
            bound(finish_kernel, atmos_factor=atmos_factor, ocean_factor=ocean_factor),
            [
                shape((atmos_rows * channels // 128, 128), F32),
                shape((ocean_rows * narrow // 128, 128), F32),
            ],
            sums,
            name="finish",
        )
        atmos_total, ocean_total = atmos_chunk.reshape(-1), ocean_chunk.reshape(-1)
    else:
        field_grad = field_grads()[0]
        atmos_all = jnp.where(is_ocean, atmos_other, atmos_sum)
        ocean_all = jnp.where(is_ocean, ocean_sum, ocean_other)
        atmos_total = atmos_factor * lax.psum_scatter(
            atmos_all.reshape(-1), "lat", scatter_dimension=0, tiled=True
        )
        ocean_all = jnp.concatenate([ocean_all[piece] for piece in range(wide // 128)], axis=1)
        ocean_total = ocean_factor * lax.psum_scatter(
            ocean_all[:, :narrow].reshape(-1), "lat", scatter_dimension=0, tiled=True
        )
    return (next_field[None], field_grad[None], ocean_total, atmos_total)


def solution(mesh):
    in_specs = (
        P("grp", "lat", None, None),
        P("grp", "lat", None, None),
        P(),
        P(),
        P(),
        P(),
        P(),
        P(),
        P("lat"),
        P("lat", None),
    )
    out_specs = (
        P("grp", "lat", None, None),
        P("grp", "lat", None, None),
        P(("grp", "lat")),
        P(("grp", "lat")),
    )
    return jax.shard_map(local, mesh=mesh, in_specs=in_specs, out_specs=out_specs, check_vma=False)
```

```python
import functools
import math

import jax
import jax.numpy as jnp
from jax import lax
from jax.experimental import pallas as pl
from jax.experimental.pallas import tpu as pltpu
from jax.sharding import PartitionSpec as P

HIGHEST = lax.Precision.HIGHEST
GELU_SCALE = 0.7978845608028654
GELU_CUBIC = 0.044715
F32 = jnp.float32
BF16 = jnp.bfloat16
WHOLE = pl.BlockSpec(memory_space=pltpu.VMEM)
IN_PLACE = pl.BlockSpec(memory_space=pltpu.HBM)
ANYWHERE = pl.BlockSpec(memory_space=pl.ANY)
VMEM_LIMIT = 20 * 1024 * 1024
PACE = 8
PACK_VMEM = 62 * 1024 * 1024
HOLD_VMEM = 42 * 1024 * 1024

NN = (((1,), (0,)), ((), ()))
NT = (((1,), (1,)), ((), ()))
TN = (((0,), (0,)), ((), ()))


def shape(dims, kind):
    return jax.ShapeDtypeStruct(dims, kind)


def call(kernel, outs, inputs, in_specs=None, scratch=(), flops=0, moved=0, name=None, limit=VMEM_LIMIT, out_spec=WHOLE):
    return pl.pallas_call(
        kernel,
        out_shape=outs,
        in_specs=in_specs or [WHOLE] * len(inputs),
        out_specs=jax.tree.map(lambda _: out_spec, outs),
        scratch_shapes=list(scratch),
        compiler_params=pltpu.CompilerParams(vmem_limit_bytes=limit),
        cost_estimate=pl.CostEstimate(flops=flops, bytes_accessed=moved, transcendentals=0),
        name=name,
    )(*inputs)


def on_ocean():
    return lax.axis_index("grp") == 0


def dot(left, right, dims=NN, precision=None):
    return lax.dot_general(left, right, dims, precision=precision, preferred_element_type=F32)


def moved_cells(values, axis, cols):
    count = values.shape[axis]
    place = lax.rem(lax.broadcasted_iota(jnp.int32, values.shape, axis), cols)
    before = jnp.where(place == 0, 0.0, pltpu.roll(values, 1, axis))
    after = jnp.where(place == cols - 1, 0.0, pltpu.roll(values, count - 1, axis))
    return before, after


def wet_halves(wet, cols, channels):
    source = lax.broadcasted_iota(jnp.int32, (2 * cols, 2 * cols), 0)
    target = lax.broadcasted_iota(jnp.int32, (2 * cols, 2 * cols), 1)
    wanted = 2 * lax.rem(target, cols) + jnp.where(target >= cols, 1, 0)
    chooser = (source == wanted).astype(F32).astype(BF16)
    padded = jnp.concatenate([wet.astype(F32), jnp.zeros((14, 2 * cols), F32)], axis=0)
    apart = dot(padded.astype(BF16), chooser)
    return jnp.concatenate([apart, jnp.zeros((16, channels - 2 * cols), F32)], axis=1)


def own_bit(bit):
    return lax.rem(lax.shift_right_logical(lax.axis_index("lat"), bit), 2)


def pack_kernel(
    x_any, g_any, wet_any, near_ref, far_ref, early_ref, own_ref, x_ref, g_ref, wet_ref, sems, *, cols
):
    pairs = ((wet_any, wet_ref), (x_any, x_ref), (g_any, g_ref))
    copies = [pltpu.make_async_copy(*pair, sems.at[index]) for index, pair in enumerate(pairs)]
    for copy in copies:
        copy.start()
    core = own_bit(0)
    copies[0].wait()
    wide = wet_halves(wet_ref[...], cols, x_ref.shape[2])
    other = pltpu.roll(wide, 15, 0)
    own_ref[4 * cols :, :] = wide.astype(BF16)
    far_ref[2 * cols :, :] = jnp.where(core == 0, wide, other).astype(BF16)
    near_ref[2 * cols :, :] = jnp.where(core == 0, other, wide).astype(BF16)
    copies[1].wait()
    copies[2].wait()
    for part, ref in enumerate((x_ref, g_ref)):
        far_ref[part * cols : (part + 1) * cols, :] = ref[core]
        near_ref[part * cols : (part + 1) * cols, :] = ref[1 - core]
        own_ref[2 * part * cols : (2 * part + 1) * cols, :] = ref[0]
        own_ref[(2 * part + 1) * cols : (2 * part + 2) * cols, :] = ref[1]
    for row in range(2):
        early_ref[row * cols : (row + 1) * cols, :] = jnp.where(on_ocean(), g_ref[row], x_ref[row])


def hold_kernel(own_in, atmos_any, ocean_any, own_ref, atmos_ref, ocean_ref, sem):
    narrow = ocean_ref.shape[2]
    ocean_copy = pltpu.make_async_copy(ocean_any, ocean_ref.at[:, pl.ds(0, narrow), :], sem)
    atmos_copy = pltpu.make_async_copy(atmos_any, atmos_ref, sem)

    @pl.when(on_ocean())
    def _():
        ocean_copy.start()
        gap = ocean_ref.shape[1] - narrow
        if gap:
            ocean_ref[:, narrow:, :] = jnp.zeros((ocean_ref.shape[0], gap, narrow), BF16)

    @pl.when(jnp.logical_not(on_ocean()))
    def _():
        atmos_copy.start()

    own_ref[...] = own_in[...]

    @pl.when(on_ocean())
    def _():
        ocean_copy.wait()

    @pl.when(jnp.logical_not(on_ocean()))
    def _():
        atmos_copy.wait()


def low_and_high(near, far):
    core = own_bit(0)
    return jnp.where(core == 0, far, near), jnp.where(core == 0, near, far)


def outgoing_kernel(
    own_ref, near_ref, far_ref, terms_ref, xpad_ref, gpad_ref, wet_ref, edge_ref, sent_ref, *, cols
):
    low, high = low_and_high(near_ref[...], far_ref[...])
    for part, pad_ref in enumerate((xpad_ref, gpad_ref)):
        pad_ref[0:cols, :] = low[part * cols : (part + 1) * cols]
        pad_ref[cols : 3 * cols, :] = own_ref[2 * part * cols : 2 * (part + 1) * cols, :]
        pad_ref[3 * cols : 4 * cols, :] = high[part * cols : (part + 1) * cols]
    low_wet = low[2 * cols :].astype(F32)
    high_wet = high[2 * cols :].astype(F32)
    own_wet = own_ref[4 * cols :, :].astype(F32)
    halves = []
    for start in (0, cols):
        lanes = slice(start, start + cols)
        rows = (low_wet[0:1, lanes], own_wet[0:1, lanes], own_wet[1:2, lanes], high_wet[0:1, lanes])
        halves.append(jnp.concatenate(rows, axis=1))
    first_wet, second_wet = halves
    inverse = 1.0 / jnp.maximum(first_wet + second_wet, 1.0)
    wet_ref[0:1, :] = first_wet
    wet_ref[1:2, :] = second_wet
    wet_ref[2:3, :] = inverse
    wet_ref[3:8, :] = jnp.zeros((5, 4 * cols), F32)
    xpad = xpad_ref[...]
    projected = dot(terms_ref[0:8, :].astype(BF16), xpad, NT)
    mixed = (projected[0:4] * first_wet + projected[4:8] * second_wet) * inverse
    sent_ref[...] = jnp.where(on_ocean(), mixed, projected[0:4])
    edge_ref[0:cols, :] = jnp.where(on_ocean(), gpad_ref[0:cols, :], xpad_ref[0:cols, :])
    edge_ref[cols:, :] = jnp.where(on_ocean(), gpad_ref[3 * cols :, :], xpad_ref[3 * cols :, :])


def halves_apart(values, narrow):
    wide = -(-narrow // 128) * 128
    lane = lax.broadcasted_iota(jnp.int32, values.shape, 1)
    even = jnp.where(lane < narrow, values, 0.0)
    odd = jnp.where(lane < narrow, pltpu.roll(values, narrow, 1), 0.0)
    return even[:, :wide], odd[:, :wide]


def halves_with_columns(pad, cols):
    even, odd = halves_apart(pad.astype(F32), pad.shape[1] // 2)
    odd_before = moved_cells(odd, 0, cols)[0].astype(BF16)
    even_after = moved_cells(even, 0, cols)[1].astype(BF16)
    even, odd = even.astype(BF16), odd.astype(BF16)
    return (odd_before, even, odd), (even, odd, even_after)


def with_columns(pad, cols):
    before, after = moved_cells(pad.astype(F32), 0, cols)
    return before.astype(BF16), pad, after.astype(BF16)


def convolve(pad, out_ref, atmos_ref, ocean_ref, layer, flipped, cols):
    base = 9 * layer
    channels = atmos_ref.shape[2]
    wide, narrow = ocean_ref.shape[1:]
    rows = out_ref.shape[0]

    def summed(pick):
        total = None
        for row_tap in range(3):
            part = pick(row_tap, slice(cols * row_tap, cols * row_tap + rows))
            total = part if total is None else total + part
        return total

    @pl.when(on_ocean())
    def _():
        evens, odds = halves_with_columns(pad, cols)
        if flipped:

            def pick(row_tap, span):
                part = None
                for col_tap in range(3):
                    left = jnp.concatenate([evens[col_tap][span], odds[col_tap][span]], axis=0)
                    kernel = ocean_ref[base + 8 - (3 * row_tap + col_tap), 0:narrow, :]
                    piece = dot(left[:, :narrow], kernel, NT)
                    part = piece if part is None else part + piece
                return part

        else:
            even, odd = jnp.concatenate(evens, axis=1), jnp.concatenate(odds, axis=1)

            def pick(row_tap, span):
                first = base + 3 * row_tap
                kernel = ocean_ref[first : first + 3].reshape(3 * wide, narrow)
                return dot(jnp.concatenate([even[span], odd[span]], axis=0), kernel)

        total = summed(pick)
        out_ref[...] = jnp.concatenate([total[:rows], total[rows:]], axis=1)

    @pl.when(jnp.logical_not(on_ocean()))
    def _():
        taps = with_columns(pad, cols)
        if flipped:

            def pick(row_tap, span):
                part = None
                for col_tap in range(3):
                    piece = dot(taps[col_tap][span], atmos_ref[base + 8 - (3 * row_tap + col_tap)], NT)
                    part = piece if part is None else part + piece
                return part

        else:
            joined = jnp.concatenate(taps, axis=1)

            def pick(row_tap, span):
                first = base + 3 * row_tap
                return dot(joined[span], atmos_ref[first : first + 3].reshape(3 * channels, channels))

        out_ref[...] = summed(pick)


def back_kernel(gpad_ref, atmos_ref, ocean_ref, out_ref, *, cols):
    convolve(gpad_ref[...], out_ref, atmos_ref, ocean_ref, 1, True, cols)


def spread(arrived, wet, mixing, terms):
    first_wet, second_wet = wet
    both = jnp.concatenate([arrived * first_wet, arrived * second_wet], axis=0)
    alone = jnp.concatenate([arrived, jnp.zeros_like(arrived)], axis=0)
    return dot(jnp.where(mixing, both, alone), terms, TN, HIGHEST)


def first_kernel(
    xpad_ref, wet_ref, arrived_ref, terms_ref, back_ref, atmos_ref, ocean_ref,
    u_ref, stay_ref, give_ref, near_ref, far_ref, first_ref, *, cols,
):
    wet = wet_ref[0:1, :], wet_ref[1:2, :]
    coupled = spread(arrived_ref[...], wet, on_ocean(), terms_ref[8:16, :])
    u = (xpad_ref[...].astype(F32) + coupled).astype(BF16)
    u_ref[...] = u
    convolve(u, first_ref, atmos_ref, ocean_ref, 0, False, cols)
    first = first_ref[...]
    tangent = jnp.tanh(GELU_SCALE * (first + GELU_CUBIC * first * first * first))
    hidden = (0.5 * first * (1.0 + tangent)).astype(BF16)
    slope = 0.5 * (1.0 + tangent) + 0.5 * first * (1.0 - tangent * tangent) * GELU_SCALE * (
        1.0 + 3.0 * GELU_CUBIC * first * first
    )
    first_grad = (back_ref[...] * slope).astype(BF16)
    stay_ref[...] = jnp.where(on_ocean(), first_grad, hidden)
    give_ref[...] = jnp.where(on_ocean(), hidden, first_grad)
    core = own_bit(0)
    for part, values in enumerate((hidden, first_grad)):
        target = slice(part * cols, (part + 1) * cols)
        far_ref[target, :] = jnp.where(core == 0, values[:cols], values[cols:])
        near_ref[target, :] = jnp.where(core == 0, values[cols:], values[:cols])


def whole_pad(early_ref, edge_ref, cols):
    parts = [edge_ref[0:cols, :], early_ref[...], edge_ref[cols:, :]]
    return jnp.concatenate(parts, axis=0).astype(F32)


def grad_atmos(pad, own, cols, store):
    rows = own.shape[0]
    left = own.T.astype(BF16)
    before, after = moved_cells(pad, 0, cols)
    rights = [part.astype(BF16) for part in (after, pad, before)]
    for tap in range(9):
        start = cols * (2 - tap // 3)
        store(tap, dot(left, rights[tap % 3][start : start + rows]))


def grad_ocean(pad, own, pad_is_input, cols, store):
    rows, channels = own.shape
    narrow = channels // 2

    if pad_is_input:
        middle = pad.T
        before, after = moved_cells(middle, 1, cols)
        even, odd = middle[:narrow].astype(BF16), middle[narrow:].astype(BF16)
        pairs = (
            (before[narrow:].astype(BF16), even),
            (even, odd),
            (odd, after[:narrow].astype(BF16)),
        )
        right = jnp.concatenate(halves_apart(own, narrow), axis=0).astype(BF16)
        for tap in range(9):
            start = cols * (tap // 3)
            pieces = [part[:, start : start + rows] for part in pairs[tap % 3]]
            store(tap, dot(jnp.concatenate(pieces, axis=1), right))
    else:
        turned = own.T.astype(BF16)
        left = jnp.concatenate([turned[:narrow], turned[narrow:]], axis=1)
        even, odd = halves_apart(pad, narrow)
        odd_before = moved_cells(odd, 0, cols)[0].astype(BF16)
        even_after = moved_cells(even, 0, cols)[1].astype(BF16)
        even, odd = even.astype(BF16), odd.astype(BF16)
        pairs = ((odd, even_after), (even, odd), (odd_before, even))
        for tap in range(9):
            start = cols * (2 - tap // 3)
            pieces = [part[start : start + rows] for part in pairs[tap % 3]]
            store(tap, dot(left, jnp.concatenate(pieces, axis=0)))


def store_into(out_ref):
    def store(tap, value):
        if len(out_ref.shape) == 2:
            rows = value.shape[0]
            out_ref[rows * tap : rows * (tap + 1), :] = value
        else:
            rows = value.shape[0]
            for piece in range(out_ref.shape[0]):
                lanes = slice(128 * piece, 128 * (piece + 1))
                out_ref[piece, rows * tap : rows * (tap + 1), :] = value[:, lanes]

    return store


def near_rows(near_ref, part, cols):
    if len(near_ref.shape) == 2:
        return near_ref[part * cols : (part + 1) * cols, :]
    count, tall = near_ref.shape[0] // 2, near_ref.shape[1]
    taken = cols // count
    pieces = [near_ref[index, tall - taken :, :] for index in range(part * count, (part + 1) * count)]
    return jnp.concatenate(pieces, axis=0)


def hidden_and_grad(stay_ref, give_ref):
    stay = stay_ref[...]
    give = give_ref[0 : stay.shape[0], :]
    return jnp.where(on_ocean(), give, stay), jnp.where(on_ocean(), stay, give)


def shifted_inputs(pad, cols):
    middle = pad.T
    before, after = moved_cells(middle, 1, cols)
    return [part.astype(BF16) for part in (before, middle, after)]


def own_grads_kernel(
    upad_ref, gpad_ref, stay_ref, early_ref, edge_ref, sent_ref, coupling_ref,
    atmos_out, ocean_out, left_ref, *, cols,
):
    stay = stay_ref[...].astype(F32)

    @pl.when(on_ocean())
    def _():
        grad_ocean(upad_ref[...].astype(F32), stay, True, cols, store_into(ocean_out))
        added = dot(sent_ref[...], coupling_ref[...].astype(F32), TN, HIGHEST)
        other = (whole_pad(early_ref, edge_ref, cols) + added).astype(BF16).astype(F32)
        for tap, left in enumerate(shifted_inputs(other, cols)):
            left_ref[tap] = left

    @pl.when(jnp.logical_not(on_ocean()))
    def _():
        grad_atmos(gpad_ref[...].astype(F32), stay, cols, store_into(atmos_out))


def other_grads_kernel(left_ref, late_ref, early_ref, edge_ref, atmos_out, ocean_out, *, cols):
    rows = early_ref.shape[0]

    @pl.when(on_ocean())
    def _():
        store = store_into(atmos_out)
        for tap in range(9):
            start = cols * (tap // 3)
            store(tap, dot(left_ref[tap % 3, :, start : start + rows], late_ref[0:rows, :]))

    @pl.when(jnp.logical_not(on_ocean()))
    def _():
        late = late_ref[0:rows, :].astype(F32)
        grad_ocean(whole_pad(early_ref, edge_ref, cols), late, False, cols, store_into(ocean_out))


def chunk_rows(out_ref, side, tall, atmos_all, ocean_all, chunks):
    channels = out_ref.shape[2]
    pieces = ocean_all.shape[0]
    atmos_rows = atmos_all.shape[0] // chunks
    ocean_rows = atmos_rows // 2
    taken = tall - atmos_rows
    blank = jnp.zeros((taken, channels - 128 * pieces), F32)
    for pair in range(chunks // 2):
        start = pl.multiple_of(atmos_rows * (2 * pair + side), 8)
        upper = atmos_all[pl.ds(start, atmos_rows), :]
        start = ocean_rows * (2 * pair + side)
        halves = []
        for odd in range(2):
            parts = [ocean_all.at[piece][pl.ds(start + odd, taken, 2), :] for piece in range(pieces)]
            halves.append(jnp.concatenate(parts + [blank], axis=1))
        lower = halves[0] + pltpu.roll(halves[1], channels // 2, 1)
        out_ref[pair, 0:tall, :] = jnp.concatenate([upper, lower], axis=0).astype(BF16)


def chunk_kernel(atmos_own, ocean_own, atmos_other, ocean_other, *refs, chunks, tall, sent):
    out_ref = refs[-1]
    core = own_bit(0)
    side = 1 - core if sent else core
    if sent:
        near_ref = refs[0]
        taken = out_ref.shape[1] - tall
        for pair in range(chunks // 2):
            out_ref[pair, tall:, :] = near_ref[pair * taken : (pair + 1) * taken, :]

    @pl.when(on_ocean())
    def _():
        chunk_rows(out_ref, side, tall, atmos_other, ocean_own, chunks)

    @pl.when(jnp.logical_not(on_ocean()))
    def _():
        chunk_rows(out_ref, side, tall, atmos_own, ocean_other, chunks)


def halve(keep_ref, came_ref, out_ref, side, rows):
    for outer in range(keep_ref.shape[0]):
        for inner in range(keep_ref.shape[2]):
            total = keep_ref[outer, side, inner, rows, :].astype(F32)
            total = total + came_ref[outer, side, inner, rows, :].astype(F32)
            out_ref[outer, inner] = total.astype(BF16)


def split_kernel(keep_ref, came_ref, *refs, cuts, sent):
    by_z = [ref.reshape(2, 2, 2, *ref.shape[3:]) for ref in (keep_ref, came_ref)]
    start = 0
    for index, rows in enumerate(cuts):
        pair, bit = (by_z, 2) if index == 1 else ((keep_ref, came_ref), 1)
        own = own_bit(bit)
        halve(*pair, refs[index], 1 - own if sent else own, slice(start, start + rows))
        start += rows
    if sent:
        refs[-1][...] = jnp.zeros_like(refs[-1])


def halve_kernel(keep_ref, came_ref, *refs, bit, marked):
    outs = refs[-3:] if marked else refs[-2:]
    own = own_bit(bit)
    halve(keep_ref, came_ref, outs[1], 1 - own, slice(None))
    halve(keep_ref, came_ref, outs[0], own, slice(None))
    if marked:
        outs[2][...] = jnp.zeros_like(outs[2])


MARK = shape((8, 128), F32)


def halved(keep, came, bit, dims, after, marked=True):
    outer, inner, rows, channels = dims[0], dims[1], keep.shape[-2], keep.shape[-1]
    keep, came = (part.reshape(outer, 2, inner, rows, channels) for part in (keep, came))
    out = shape((outer, inner, rows, channels), BF16)
    return call(
        functools.partial(halve_kernel, bit=bit, marked=marked),
        [out, out] + [MARK] * marked,
        [keep, came, *after],
        [WHOLE] * 2 + [ANYWHERE] * len(after),
        moved=8 * outer * inner * rows * channels,
        name="halve",
    )


def halve_both_kernel(a_keep, a_came, b_keep, b_came, *refs, bits):
    for index, (pair, bit) in enumerate((((a_keep, a_came), bits[0]), ((b_keep, b_came), bits[1]))):
        own = own_bit(bit)
        keep_out, send_out = refs[2 * index - 5 : 2 * index - 3]
        halve(*pair, send_out, 1 - own, slice(None))
        halve(*pair, keep_out, own, slice(None))
    refs[-1][...] = jnp.zeros_like(refs[-1])


def halved_both(a_keep, a_came, a_bit, b_keep, b_came, b_bit, after):
    inputs, outs = [], []
    for keep, came in ((a_keep, a_came), (b_keep, b_came)):
        rows, channels = keep.shape[-2:]
        inputs += [part.reshape(1, 2, 1, rows, channels) for part in (keep, came)]
        outs += [shape((1, 1, rows, channels), BF16)] * 2
    return call(
        functools.partial(halve_both_kernel, bits=(a_bit, b_bit)),
        [*outs, MARK],
        [*inputs, after],
        [WHOLE] * 4 + [ANYWHERE],
        name="halve_both",
    )


def split(keep, came):
    pairs, tall, channels = keep.shape
    cuts = [16 * (tall // 16 * part // 17) for part in (6, 7)]
    cuts.append(tall - sum(cuts))
    outs = [
        shape(((2, 2) if index == 1 else (4, 1)) + (rows, channels), BF16) for index, rows in enumerate(cuts)
    ]
    inputs = [part.reshape(4, 2, 1, *part.shape[1:]) for part in (keep, came)]
    kept, sent = (
        call(
            functools.partial(split_kernel, cuts=cuts, sent=is_sent),
            outs + [MARK] * is_sent,
            inputs,
            moved=3 * pairs * tall * channels,
            name="split",
        )
        for is_sent in (False, True)
    )
    return kept, sent[:3], sent[3]


def scatter_sum(kept, sent, before_b, finish_last):
    (a_keep, b_keep, c_keep), (a_send, b_send, c_send) = kept, sent
    channels = a_keep.shape[-1]
    a_came = swapped(a_send, "lat", 2)
    b_came = swapped(b_send, "lat", 4)
    c_came = swapped(c_send, "lat", 2)
    b_keep, b_send, mark = halved(b_keep, b_came, 3, (1, 2), before_b)
    b_came = swapped(b_send, "lat", 8)
    mark = finish_last(mark)
    a_keep, a_send, mark = halved(a_keep, a_came, 2, (2, 1), [mark])
    a_came = swapped(a_send, "lat", 4)
    c_keep, c_send, mark = halved(c_keep, c_came, 2, (2, 1), [mark])
    c_came = swapped(c_send, "lat", 4)
    a_keep, a_send, b_keep, b_send, mark = halved_both(a_keep, a_came, 3, b_keep, b_came, 1, mark)
    a_came = swapped(a_send, "lat", 8)
    b_came = swapped(b_send, "lat", 2)
    c_keep, c_send = halved(c_keep, c_came, 3, (1, 1), [mark], False)
    c_came = swapped(c_send, "lat", 8)
    return [part.reshape(-1, channels) for part in (a_keep, a_came, b_keep, b_came, c_keep, c_came)]


def finish_kernel(*refs, atmos_factor, ocean_factor):
    parts, (atmos_ref, ocean_ref) = refs[:-2], refs[-2:]
    channels = parts[0].shape[1]
    pieces = channels // 128
    atmos_rows = atmos_ref.shape[0] // pieces
    ocean_rows = ocean_ref.shape[0] // pieces
    sums = [
        parts[index][...].astype(F32) + parts[index + 1][...].astype(F32)
        for index in range(0, len(parts), 2)
    ]
    total = jnp.concatenate(sums, axis=0)
    for piece in range(pieces):
        lanes = slice(128 * piece, 128 * (piece + 1))
        atmos_ref[pl.ds(piece, atmos_rows, pieces), :] = total[:atmos_rows, lanes] * atmos_factor
        ocean_ref[pl.ds(piece, ocean_rows, pieces), :] = (
            total[atmos_rows : atmos_rows + ocean_rows, lanes] * ocean_factor
        )


def input_grad_kernel(
    stay_ref, give_ref, near_ref, far_ref, gpad_ref, wet_ref, terms_ref, atmos_ref, ocean_ref, *refs, cols
):
    grad_ref, sent_ref = refs[-2:]
    middle = hidden_and_grad(stay_ref, give_ref)[1]
    low, high = low_and_high(near_rows(near_ref, 1, cols), far_ref[cols:, :])
    pad = jnp.concatenate([low, middle, high], axis=0)
    own = slice(cols, 3 * cols)
    convolve(pad, grad_ref, atmos_ref, ocean_ref, 0, True, cols)
    grad = gpad_ref[own, :].astype(F32) + grad_ref[...]
    grad_ref[...] = grad
    weighted = dot(terms_ref[8:16, :], grad, NT, HIGHEST)
    mixed = weighted[0:4] * wet_ref[0:1, own] + weighted[4:8] * wet_ref[1:2, own]
    sent_ref[...] = jnp.where(on_ocean(), mixed, weighted[0:4])


def next_kernel(
    stay_ref, give_ref, near_ref, far_ref, upad_ref, atmos_ref, ocean_ref,
    next_ref, mark_ref, second_ref, *, cols,
):
    middle = hidden_and_grad(stay_ref, give_ref)[0]
    low, high = low_and_high(near_rows(near_ref, 0, cols), far_ref[0:cols, :])
    pad = jnp.concatenate([low, middle, high], axis=0)
    own = slice(cols, 3 * cols)
    convolve(pad, second_ref, atmos_ref, ocean_ref, 1, False, cols)
    values = (upad_ref[own, :].astype(F32) + second_ref[...]).astype(BF16)
    next_ref[0] = values[:cols]
    next_ref[1] = values[cols:]
    mark_ref[...] = jnp.zeros_like(mark_ref)


def last_kernel(grad_ref, arrived_ref, wet_ref, terms_ref, *refs, cols):
    out_ref, mark_ref = refs[-2:]
    own = slice(cols, 3 * cols)
    wet = wet_ref[0:1, own], wet_ref[1:2, own]
    arrived = jnp.where(on_ocean(), arrived_ref[...] * wet_ref[2:3, own], arrived_ref[...])
    added = spread(arrived, wet, on_ocean(), terms_ref[0:8, :])
    values = (grad_ref[...] + added).astype(BF16)
    out_ref[0] = values[:cols]
    out_ref[1] = values[cols:]
    mark_ref[...] = jnp.zeros_like(mark_ref)


def swapped(value, axis, mask):
    pairs = [(source, source ^ mask) for source in range(lax.axis_size(axis))]
    return lax.ppermute(value, axis, pairs)


def far_halo(far):
    pairs = [(i, i + 1 if i % 2 else i - 1) for i in range(1, lax.axis_size("lat") - 1)]
    return lax.ppermute(far, "lat", pairs)


def local(
    fields,
    cotangent,
    ocean_kernels,
    atmos_kernels,
    ocean_surface,
    ocean_coupling,
    atmos_flux,
    atmos_coupling,
    row_map,
    wet_mask,
):
    x, g = fields[0], cotangent[0]
    bands, cols, channels = x.shape
    narrow = channels // 2
    cells = bands * cols
    count = lax.axis_size("lat")
    is_ocean = lax.axis_index("grp") == 0
    atmos_factor = 1.0 / math.sqrt(bands * count * cols)
    ocean_factor = 1.0 / math.sqrt(bands * count * 2 * cols)
    bound = functools.partial

    blank = jnp.zeros((4, narrow), BF16)
    gap = jnp.zeros((4, channels), BF16)
    surface = ocean_surface.T
    ocean_terms = jnp.concatenate(
        [
            jnp.concatenate([surface, blank], axis=1),
            jnp.concatenate([blank, surface], axis=1),
            jnp.concatenate([ocean_coupling, blank], axis=1),
            jnp.concatenate([blank, ocean_coupling], axis=1),
        ],
        axis=0,
    )
    atmos_terms = jnp.concatenate([atmos_flux.T, gap, atmos_coupling, gap], axis=0)
    terms = jnp.where(is_ocean, ocean_terms, atmos_terms).astype(F32)

    edge = shape((2 * cols + 16, channels), BF16)
    half = shape((cells, channels), BF16)
    near, far, own_early, own = call(
        bound(pack_kernel, cols=cols),
        [edge, edge, half, shape((2 * cells + 16, channels), BF16)],
        [x, g, wet_mask],
        [IN_PLACE] * 3,
        [
            pltpu.VMEM(x.shape, BF16),
            pltpu.VMEM(x.shape, BF16),
            pltpu.VMEM(wet_mask.shape, jnp.int32),
            pltpu.SemaphoreType.DMA((3,)),
        ],
        name="pack",
        limit=PACK_VMEM,
    )
    near, far = swapped(near, "lat", 1), far_halo(far)
    other_early = swapped(own_early, "grp", 1)
    wide = -(-narrow // 128) * 128
    own, atmos_flat, ocean_flat = call(
        hold_kernel,
        [
            shape(own.shape, BF16),
            shape((18, channels, channels), BF16),
            shape((18, wide, narrow), BF16),
        ],
        [own, atmos_kernels.reshape(18, channels, channels), ocean_kernels.reshape(18, narrow, narrow)],
        [WHOLE, IN_PLACE, IN_PLACE],
        [pltpu.SemaphoreType.DMA],
        flops=PACE * 10**8,
        name="hold",
        limit=HOLD_VMEM,
    )
    pad = shape((2 * cells, channels), BF16)
    xpad, gpad, wet, edges, sent = call(
        bound(outgoing_kernel, cols=cols),
        [pad, pad, shape((8, 2 * cells), F32), half, shape((4, 2 * cells), F32)],
        [own, near, far, terms],
        name="outgoing",
    )
    arrived = swapped(sent, "grp", 1)
    other_edges = swapped(edges, "grp", 1)
    conv_cost = dict(flops=PACE * 9 * cells * channels * channels, moved=9 * channels * channels * 2)
    back = call(
        bound(back_kernel, cols=cols),
        shape((cells, channels), F32),
        [gpad, atmos_flat, ocean_flat],
        **conv_cost,
        name="back",
    )
    upad, stay, give, near, far = call(
        bound(first_kernel, cols=cols),
        [pad, half, half, half, half],
        [xpad, wet, arrived, terms, back, atmos_flat, ocean_flat],
        None,
        [pltpu.VMEM((cells, channels), F32)],
        **conv_cost,
        name="first",
    )
    late = swapped(give, "grp", 1)

    far = far_halo(far)

    atmos_rows = 9 * channels // count
    ocean_rows = 9 * narrow // count
    chunked = count == 16 and 9 * channels % (8 * count) == 0 and ocean_rows % 2 == 0
    tall = -(-(atmos_rows + ocean_rows // 2) // 16) * 16
    spare = max(0, 2 * (tall - atmos_rows) - ocean_rows) if chunked else 0
    ocean_tall = 9 * narrow + -(-spare // 8) * 8
    sums = [shape((9 * channels, channels), F32), shape((wide // 128, ocean_tall, 128), F32)]
    atmos_sum, ocean_sum, lefts = call(
        bound(own_grads_kernel, cols=cols),
        [*sums, shape((3, channels, 2 * cells), BF16)],
        [upad, gpad, stay, other_early, other_edges, sent, atmos_coupling],
        **conv_cost,
        name="own_grads",
    )
    atmos_other, ocean_other = call(
        bound(other_grads_kernel, cols=cols),
        sums,
        [lefts, late, other_early, other_edges],
        **conv_cost,
        name="other_grads",
    )
    if chunked:
        taken = 2 * cols // (count // 2)
        sums = [atmos_sum, ocean_sum, atmos_other, ocean_other]
        send, keep = (
            call(
                bound(chunk_kernel, chunks=count, tall=tall, sent=sent),
                shape((count // 2, tall + taken * sent, channels), BF16),
                sums + [near, far] * sent,
                [WHOLE] * (4 + sent) + [ANYWHERE] * sent,
                moved=2 * count * tall * channels,
                name="chunk",
            )
            for sent in (True, False)
        )
        near = swapped(send, "lat", 1)
        kept, parts, split_mark = split(keep, near)
        after_split = [split_mark]
    else:
        near = swapped(near, "lat", 1)
        after_split = []

    grad, sent_back = call(
        bound(input_grad_kernel, cols=cols),
        [shape((cells, channels), F32), shape((4, cells), F32)],
        [stay, give, near, far, gpad, wet, terms, atmos_flat, ocean_flat, *after_split],
        [WHOLE] * 9 + [ANYWHERE] * len(after_split),
        **conv_cost,
        name="input_grad",
    )
    returned = swapped(sent_back, "grp", 1)
    next_field, next_mark = call(
        bound(next_kernel, cols=cols),
        [shape(x.shape, BF16), MARK],
        [stay, give, near, far, upad, atmos_flat, ocean_flat],
        None,
        [pltpu.VMEM((cells, channels), F32)],
        **conv_cost,
        name="next",
    )

    def field_grads(*after):
        return call(
            bound(last_kernel, cols=cols),
            [shape(x.shape, BF16), MARK],
            [grad, returned, wet, terms, *after],
            [WHOLE] * 4 + [ANYWHERE] * len(after),
            name="last",
        )

    if chunked:
        made = []

        def finish_last(mark):
            made.extend(field_grads(mark))
            return made[1]

        sums = scatter_sum(kept, parts, [returned, next_mark], finish_last)
        field_grad = made[0]
        atmos_chunk, ocean_chunk = call(
            bound(finish_kernel, atmos_factor=atmos_factor, ocean_factor=ocean_factor),
            [
                shape((atmos_rows * channels // 128, 128), F32),
                shape((ocean_rows * narrow // 128, 128), F32),
            ],
            sums,
            name="finish",
        )
        atmos_total, ocean_total = atmos_chunk.reshape(-1), ocean_chunk.reshape(-1)
    else:
        field_grad = field_grads()[0]
        atmos_all = jnp.where(is_ocean, atmos_other, atmos_sum)
        ocean_all = jnp.where(is_ocean, ocean_sum, ocean_other)
        atmos_total = atmos_factor * lax.psum_scatter(
            atmos_all.reshape(-1), "lat", scatter_dimension=0, tiled=True
        )
        ocean_all = jnp.concatenate([ocean_all[piece] for piece in range(wide // 128)], axis=1)
        ocean_total = ocean_factor * lax.psum_scatter(
            ocean_all[:, :narrow].reshape(-1), "lat", scatter_dimension=0, tiled=True
        )
    return (next_field[None], field_grad[None], ocean_total, atmos_total)


def solution(mesh):
    in_specs = (
        P("grp", "lat", None, None),
        P("grp", "lat", None, None),
        P(),
        P(),
        P(),
        P(),
        P(),
        P(),
        P("lat"),
        P("lat", None),
    )
    out_specs = (
        P("grp", "lat", None, None),
        P("grp", "lat", None, None),
        P(("grp", "lat")),
        P(("grp", "lat")),
    )
    return jax.shard_map(local, mesh=mesh, in_specs=in_specs, out_specs=out_specs, check_vma=False)
```

```python
import functools
import math

import jax
import jax.numpy as jnp
from jax import lax
from jax.experimental import pallas as pl
from jax.experimental.pallas import tpu as pltpu
from jax.sharding import PartitionSpec as P

HIGHEST = lax.Precision.HIGHEST
GELU_SCALE = 0.7978845608028654
GELU_CUBIC = 0.044715
F32 = jnp.float32
BF16 = jnp.bfloat16
WHOLE = pl.BlockSpec(memory_space=pltpu.VMEM)
IN_PLACE = pl.BlockSpec(memory_space=pltpu.HBM)
ANYWHERE = pl.BlockSpec(memory_space=pl.ANY)
VMEM_LIMIT = 20 * 1024 * 1024
PACE = 8
PACK_VMEM = 62 * 1024 * 1024
HOLD_VMEM = 42 * 1024 * 1024

NN = (((1,), (0,)), ((), ()))
NT = (((1,), (1,)), ((), ()))
TN = (((0,), (0,)), ((), ()))


def shape(dims, kind):
    return jax.ShapeDtypeStruct(dims, kind)


def call(kernel, outs, inputs, in_specs=None, scratch=(), flops=0, moved=0, name=None, limit=VMEM_LIMIT, out_spec=WHOLE):
    return pl.pallas_call(
        kernel,
        out_shape=outs,
        in_specs=in_specs or [WHOLE] * len(inputs),
        out_specs=jax.tree.map(lambda _: out_spec, outs),
        scratch_shapes=list(scratch),
        compiler_params=pltpu.CompilerParams(vmem_limit_bytes=limit),
        cost_estimate=pl.CostEstimate(flops=flops, bytes_accessed=moved, transcendentals=0),
        name=name,
    )(*inputs)


def on_ocean():
    return lax.axis_index("grp") == 0


def dot(left, right, dims=NN, precision=None):
    return lax.dot_general(left, right, dims, precision=precision, preferred_element_type=F32)


def moved_cells(values, axis, cols):
    count = values.shape[axis]
    place = lax.rem(lax.broadcasted_iota(jnp.int32, values.shape, axis), cols)
    before = jnp.where(place == 0, 0.0, pltpu.roll(values, 1, axis))
    after = jnp.where(place == cols - 1, 0.0, pltpu.roll(values, count - 1, axis))
    return before, after


def wet_halves(wet, cols, channels):
    source = lax.broadcasted_iota(jnp.int32, (2 * cols, 2 * cols), 0)
    target = lax.broadcasted_iota(jnp.int32, (2 * cols, 2 * cols), 1)
    wanted = 2 * lax.rem(target, cols) + jnp.where(target >= cols, 1, 0)
    chooser = (source == wanted).astype(F32).astype(BF16)
    padded = jnp.concatenate([wet.astype(F32), jnp.zeros((14, 2 * cols), F32)], axis=0)
    apart = dot(padded.astype(BF16), chooser)
    return jnp.concatenate([apart, jnp.zeros((16, channels - 2 * cols), F32)], axis=1)


def own_bit(bit):
    return lax.rem(lax.shift_right_logical(lax.axis_index("lat"), bit), 2)


def pack_kernel(
    x_any, g_any, wet_any, near_ref, far_ref, early_ref, own_ref, x_ref, g_ref, wet_ref, sems, *, cols
):
    pairs = ((wet_any, wet_ref), (x_any, x_ref), (g_any, g_ref))
    copies = [pltpu.make_async_copy(*pair, sems.at[index]) for index, pair in enumerate(pairs)]
    for copy in copies:
        copy.start()
    core = own_bit(0)
    copies[0].wait()
    wide = wet_halves(wet_ref[...], cols, x_ref.shape[2])
    other = pltpu.roll(wide, 15, 0)
    own_ref[4 * cols :, :] = wide.astype(BF16)
    far_ref[2 * cols :, :] = jnp.where(core == 0, wide, other).astype(BF16)
    near_ref[2 * cols :, :] = jnp.where(core == 0, other, wide).astype(BF16)
    copies[1].wait()
    copies[2].wait()
    for part, ref in enumerate((x_ref, g_ref)):
        far_ref[part * cols : (part + 1) * cols, :] = ref[core]
        near_ref[part * cols : (part + 1) * cols, :] = ref[1 - core]
        own_ref[2 * part * cols : (2 * part + 1) * cols, :] = ref[0]
        own_ref[(2 * part + 1) * cols : (2 * part + 2) * cols, :] = ref[1]
    for row in range(2):
        early_ref[row * cols : (row + 1) * cols, :] = jnp.where(on_ocean(), g_ref[row], x_ref[row])


def hold_kernel(own_in, atmos_any, ocean_any, own_ref, atmos_ref, ocean_ref, sem):
    narrow = ocean_ref.shape[2]
    ocean_copy = pltpu.make_async_copy(ocean_any, ocean_ref.at[:, pl.ds(0, narrow), :], sem)
    atmos_copy = pltpu.make_async_copy(atmos_any, atmos_ref, sem)

    @pl.when(on_ocean())
    def _():
        ocean_copy.start()
        gap = ocean_ref.shape[1] - narrow
        if gap:
            ocean_ref[:, narrow:, :] = jnp.zeros((ocean_ref.shape[0], gap, narrow), BF16)

    @pl.when(jnp.logical_not(on_ocean()))
    def _():
        atmos_copy.start()

    own_ref[...] = own_in[...]

    @pl.when(on_ocean())
    def _():
        ocean_copy.wait()

    @pl.when(jnp.logical_not(on_ocean()))
    def _():
        atmos_copy.wait()


def low_and_high(near, far):
    core = own_bit(0)
    return jnp.where(core == 0, far, near), jnp.where(core == 0, near, far)


def outgoing_kernel(
    own_ref, near_ref, far_ref, terms_ref, xpad_ref, gpad_ref, wet_ref, edge_ref, sent_ref, *, cols
):
    low, high = low_and_high(near_ref[...], far_ref[...])
    for part, pad_ref in enumerate((xpad_ref, gpad_ref)):
        pad_ref[0:cols, :] = low[part * cols : (part + 1) * cols]
        pad_ref[cols : 3 * cols, :] = own_ref[2 * part * cols : 2 * (part + 1) * cols, :]
        pad_ref[3 * cols : 4 * cols, :] = high[part * cols : (part + 1) * cols]
    low_wet = low[2 * cols :].astype(F32)
    high_wet = high[2 * cols :].astype(F32)
    own_wet = own_ref[4 * cols :, :].astype(F32)
    halves = []
    for start in (0, cols):
        lanes = slice(start, start + cols)
        rows = (low_wet[0:1, lanes], own_wet[0:1, lanes], own_wet[1:2, lanes], high_wet[0:1, lanes])
        halves.append(jnp.concatenate(rows, axis=1))
    first_wet, second_wet = halves
    inverse = 1.0 / jnp.maximum(first_wet + second_wet, 1.0)
    wet_ref[0:1, :] = first_wet
    wet_ref[1:2, :] = second_wet
    wet_ref[2:3, :] = inverse
    wet_ref[3:8, :] = jnp.zeros((5, 4 * cols), F32)
    xpad = xpad_ref[...]
    projected = dot(terms_ref[0:8, :].astype(BF16), xpad, NT)
    mixed = (projected[0:4] * first_wet + projected[4:8] * second_wet) * inverse
    sent_ref[...] = jnp.where(on_ocean(), mixed, projected[0:4])
    edge_ref[0:cols, :] = jnp.where(on_ocean(), gpad_ref[0:cols, :], xpad_ref[0:cols, :])
    edge_ref[cols:, :] = jnp.where(on_ocean(), gpad_ref[3 * cols :, :], xpad_ref[3 * cols :, :])


def halves_apart(values, narrow):
    wide = -(-narrow // 128) * 128
    lane = lax.broadcasted_iota(jnp.int32, values.shape, 1)
    even = jnp.where(lane < narrow, values, 0.0)
    odd = jnp.where(lane < narrow, pltpu.roll(values, narrow, 1), 0.0)
    return even[:, :wide], odd[:, :wide]


def halves_with_columns(pad, cols):
    even, odd = halves_apart(pad.astype(F32), pad.shape[1] // 2)
    odd_before = moved_cells(odd, 0, cols)[0].astype(BF16)
    even_after = moved_cells(even, 0, cols)[1].astype(BF16)
    even, odd = even.astype(BF16), odd.astype(BF16)
    return (odd_before, even, odd), (even, odd, even_after)


def with_columns(pad, cols):
    before, after = moved_cells(pad.astype(F32), 0, cols)
    return before.astype(BF16), pad, after.astype(BF16)


def convolve(pad, out_ref, atmos_ref, ocean_ref, layer, flipped, cols):
    base = 9 * layer
    channels = atmos_ref.shape[2]
    wide, narrow = ocean_ref.shape[1:]
    rows = out_ref.shape[0]

    def summed(pick):
        total = None
        for row_tap in range(3):
            part = pick(row_tap, slice(cols * row_tap, cols * row_tap + rows))
            total = part if total is None else total + part
        return total

    @pl.when(on_ocean())
    def _():
        evens, odds = halves_with_columns(pad, cols)
        if flipped:

            def pick(row_tap, span):
                part = None
                for col_tap in range(3):
                    left = jnp.concatenate([evens[col_tap][span], odds[col_tap][span]], axis=0)
                    kernel = ocean_ref[base + 8 - (3 * row_tap + col_tap), 0:narrow, :]
                    piece = dot(left[:, :narrow], kernel, NT)
                    part = piece if part is None else part + piece
                return part

        else:
            even, odd = jnp.concatenate(evens, axis=1), jnp.concatenate(odds, axis=1)

            def pick(row_tap, span):
                first = base + 3 * row_tap
                kernel = ocean_ref[first : first + 3].reshape(3 * wide, narrow)
                return dot(jnp.concatenate([even[span], odd[span]], axis=0), kernel)

        total = summed(pick)
        out_ref[...] = jnp.concatenate([total[:rows], total[rows:]], axis=1)

    @pl.when(jnp.logical_not(on_ocean()))
    def _():
        taps = with_columns(pad, cols)
        if flipped:

            def pick(row_tap, span):
                part = None
                for col_tap in range(3):
                    piece = dot(taps[col_tap][span], atmos_ref[base + 8 - (3 * row_tap + col_tap)], NT)
                    part = piece if part is None else part + piece
                return part

        else:
            joined = jnp.concatenate(taps, axis=1)

            def pick(row_tap, span):
                first = base + 3 * row_tap
                return dot(joined[span], atmos_ref[first : first + 3].reshape(3 * channels, channels))

        out_ref[...] = summed(pick)


def back_kernel(gpad_ref, atmos_ref, ocean_ref, out_ref, *, cols):
    convolve(gpad_ref[...], out_ref, atmos_ref, ocean_ref, 1, True, cols)


def spread(arrived, wet, mixing, terms):
    first_wet, second_wet = wet
    both = jnp.concatenate([arrived * first_wet, arrived * second_wet], axis=0)
    alone = jnp.concatenate([arrived, jnp.zeros_like(arrived)], axis=0)
    return dot(jnp.where(mixing, both, alone), terms, TN, HIGHEST)


def first_kernel(
    xpad_ref, wet_ref, arrived_ref, terms_ref, back_ref, atmos_ref, ocean_ref,
    u_ref, stay_ref, give_ref, first_ref, *, cols,
):
    wet = wet_ref[0:1, :], wet_ref[1:2, :]
    coupled = spread(arrived_ref[...], wet, on_ocean(), terms_ref[8:16, :])
    u = (xpad_ref[...].astype(F32) + coupled).astype(BF16)
    u_ref[...] = u
    convolve(u, first_ref, atmos_ref, ocean_ref, 0, False, cols)
    first = first_ref[...]
    tangent = jnp.tanh(GELU_SCALE * (first + GELU_CUBIC * first * first * first))
    hidden = (0.5 * first * (1.0 + tangent)).astype(BF16)
    slope = 0.5 * (1.0 + tangent) + 0.5 * first * (1.0 - tangent * tangent) * GELU_SCALE * (
        1.0 + 3.0 * GELU_CUBIC * first * first
    )
    first_grad = (back_ref[...] * slope).astype(BF16)
    stay_ref[...] = jnp.where(on_ocean(), first_grad, hidden)
    give_ref[...] = jnp.where(on_ocean(), hidden, first_grad)


def whole_pad(early_ref, edge_ref, cols):
    parts = [edge_ref[0:cols, :], early_ref[...], edge_ref[cols:, :]]
    return jnp.concatenate(parts, axis=0).astype(F32)


def grad_atmos(pad, own, cols, store):
    rows = own.shape[0]
    left = own.T.astype(BF16)
    before, after = moved_cells(pad, 0, cols)
    rights = [part.astype(BF16) for part in (after, pad, before)]
    for tap in range(9):
        start = cols * (2 - tap // 3)
        store(tap, dot(left, rights[tap % 3][start : start + rows]))


def grad_ocean(pad, own, pad_is_input, cols, store):
    rows, channels = own.shape
    narrow = channels // 2

    if pad_is_input:
        middle = pad.T
        before, after = moved_cells(middle, 1, cols)
        even, odd = middle[:narrow].astype(BF16), middle[narrow:].astype(BF16)
        pairs = (
            (before[narrow:].astype(BF16), even),
            (even, odd),
            (odd, after[:narrow].astype(BF16)),
        )
        right = jnp.concatenate(halves_apart(own, narrow), axis=0).astype(BF16)
        for tap in range(9):
            start = cols * (tap // 3)
            pieces = [part[:, start : start + rows] for part in pairs[tap % 3]]
            store(tap, dot(jnp.concatenate(pieces, axis=1), right))
    else:
        turned = own.T.astype(BF16)
        left = jnp.concatenate([turned[:narrow], turned[narrow:]], axis=1)
        even, odd = halves_apart(pad, narrow)
        odd_before = moved_cells(odd, 0, cols)[0].astype(BF16)
        even_after = moved_cells(even, 0, cols)[1].astype(BF16)
        even, odd = even.astype(BF16), odd.astype(BF16)
        pairs = ((odd, even_after), (even, odd), (odd_before, even))
        for tap in range(9):
            start = cols * (2 - tap // 3)
            pieces = [part[start : start + rows] for part in pairs[tap % 3]]
            store(tap, dot(left, jnp.concatenate(pieces, axis=0)))


def store_into(out_ref):
    def store(tap, value):
        if len(out_ref.shape) == 2:
            rows = value.shape[0]
            out_ref[rows * tap : rows * (tap + 1), :] = value
        else:
            rows = value.shape[0]
            for piece in range(out_ref.shape[0]):
                lanes = slice(128 * piece, 128 * (piece + 1))
                out_ref[piece, rows * tap : rows * (tap + 1), :] = value[:, lanes]

    return store


def near_rows(near_ref, part, cols):
    if len(near_ref.shape) == 2:
        return near_ref[part * cols : (part + 1) * cols, :]
    count, tall = near_ref.shape[0] // 2, near_ref.shape[1]
    taken = cols // count
    pieces = [near_ref[index, tall - taken :, :] for index in range(part * count, (part + 1) * count)]
    return jnp.concatenate(pieces, axis=0)


def hidden_and_grad(stay_ref, give_ref):
    stay, give = stay_ref[...], give_ref[...]
    return jnp.where(on_ocean(), give, stay), jnp.where(on_ocean(), stay, give)


def shifted_inputs(pad, cols):
    middle = pad.T
    before, after = moved_cells(middle, 1, cols)
    return [part.astype(BF16) for part in (before, middle, after)]


def own_grads_kernel(
    upad_ref, gpad_ref, stay_ref, give_ref, atmos_out, ocean_out, near_ref, far_ref, *, cols
):
    stay = stay_ref[...].astype(F32)
    hidden, first_grad = hidden_and_grad(stay_ref, give_ref)
    core = own_bit(0)
    for part, values in enumerate((hidden, first_grad)):
        target = slice(part * cols, (part + 1) * cols)
        far_ref[target, :] = jnp.where(core == 0, values[:cols], values[cols:])
        near_ref[target, :] = jnp.where(core == 0, values[cols:], values[:cols])

    @pl.when(on_ocean())
    def _():
        grad_ocean(upad_ref[...].astype(F32), stay, True, cols, store_into(ocean_out))

    @pl.when(jnp.logical_not(on_ocean()))
    def _():
        grad_atmos(gpad_ref[...].astype(F32), stay, cols, store_into(atmos_out))


def shift_kernel(early_ref, edge_ref, sent_ref, coupling_ref, left_ref, *, cols):
    @pl.when(on_ocean())
    def _():
        added = dot(sent_ref[...], coupling_ref[...].astype(F32), TN, HIGHEST)
        other = (whole_pad(early_ref, edge_ref, cols) + added).astype(BF16).astype(F32)
        for tap, left in enumerate(shifted_inputs(other, cols)):
            left_ref[tap] = left


def other_grads_kernel(left_ref, late_ref, early_ref, edge_ref, atmos_out, ocean_out, *, cols):
    rows = late_ref.shape[0]

    @pl.when(on_ocean())
    def _():
        store = store_into(atmos_out)
        for tap in range(9):
            start = cols * (tap // 3)
            store(tap, dot(left_ref[tap % 3, :, start : start + rows], late_ref[...]))

    @pl.when(jnp.logical_not(on_ocean()))
    def _():
        late = late_ref[...].astype(F32)
        grad_ocean(whole_pad(early_ref, edge_ref, cols), late, False, cols, store_into(ocean_out))


def chunk_rows(out_ref, side, tall, atmos_all, ocean_all, chunks):
    channels = out_ref.shape[2]
    pieces = ocean_all.shape[0]
    atmos_rows = atmos_all.shape[0] // chunks
    ocean_rows = atmos_rows // 2
    taken = tall - atmos_rows
    blank = jnp.zeros((taken, channels - 128 * pieces), F32)
    for pair in range(chunks // 2):
        start = pl.multiple_of(atmos_rows * (2 * pair + side), 8)
        upper = atmos_all[pl.ds(start, atmos_rows), :]
        start = ocean_rows * (2 * pair + side)
        halves = []
        for odd in range(2):
            parts = [ocean_all.at[piece][pl.ds(start + odd, taken, 2), :] for piece in range(pieces)]
            halves.append(jnp.concatenate(parts + [blank], axis=1))
        lower = halves[0] + pltpu.roll(halves[1], channels // 2, 1)
        out_ref[pair, 0:tall, :] = jnp.concatenate([upper, lower], axis=0).astype(BF16)


def chunk_kernel(atmos_own, ocean_own, atmos_other, ocean_other, *refs, chunks, tall, sent):
    out_ref = refs[-1]
    core = own_bit(0)
    side = 1 - core if sent else core
    if sent:
        near_ref = refs[0]
        taken = out_ref.shape[1] - tall
        for pair in range(chunks // 2):
            out_ref[pair, tall:, :] = near_ref[pair * taken : (pair + 1) * taken, :]

    @pl.when(on_ocean())
    def _():
        chunk_rows(out_ref, side, tall, atmos_other, ocean_own, chunks)

    @pl.when(jnp.logical_not(on_ocean()))
    def _():
        chunk_rows(out_ref, side, tall, atmos_own, ocean_other, chunks)


def halve(keep_ref, came_ref, out_ref, side, rows):
    for outer in range(keep_ref.shape[0]):
        for inner in range(keep_ref.shape[2]):
            total = keep_ref[outer, side, inner, rows, :].astype(F32)
            total = total + came_ref[outer, side, inner, rows, :].astype(F32)
            out_ref[outer, inner] = total.astype(BF16)


def split_kernel(keep_ref, came_ref, *refs, cuts, sent):
    by_z = [ref.reshape(2, 2, 2, *ref.shape[3:]) for ref in (keep_ref, came_ref)]
    start = 0
    for index, rows in enumerate(cuts):
        pair, bit = (by_z, 2) if index == 1 else ((keep_ref, came_ref), 1)
        own = own_bit(bit)
        halve(*pair, refs[index], 1 - own if sent else own, slice(start, start + rows))
        start += rows
    if sent:
        refs[-1][...] = jnp.zeros_like(refs[-1])


def halve_kernel(keep_ref, came_ref, *refs, bit, marked):
    outs = refs[-3:] if marked else refs[-2:]
    own = own_bit(bit)
    halve(keep_ref, came_ref, outs[1], 1 - own, slice(None))
    halve(keep_ref, came_ref, outs[0], own, slice(None))
    if marked:
        outs[2][...] = jnp.zeros_like(outs[2])


MARK = shape((8, 128), F32)


def halved(keep, came, bit, dims, after, marked=True):
    outer, inner, rows, channels = dims[0], dims[1], keep.shape[-2], keep.shape[-1]
    keep, came = (part.reshape(outer, 2, inner, rows, channels) for part in (keep, came))
    out = shape((outer, inner, rows, channels), BF16)
    return call(
        functools.partial(halve_kernel, bit=bit, marked=marked),
        [out, out] + [MARK] * marked,
        [keep, came, *after],
        [WHOLE] * 2 + [ANYWHERE] * len(after),
        moved=8 * outer * inner * rows * channels,
        name="halve",
    )


def split(keep, came):
    pairs, tall, channels = keep.shape
    cuts = [16 * (tall // 16 * part // 17) for part in (6, 6)]
    cuts.append(tall - sum(cuts))
    outs = [
        shape(((2, 2) if index == 1 else (4, 1)) + (rows, channels), BF16) for index, rows in enumerate(cuts)
    ]
    inputs = [part.reshape(4, 2, 1, *part.shape[1:]) for part in (keep, came)]
    kept, sent = (
        call(
            functools.partial(split_kernel, cuts=cuts, sent=is_sent),
            outs + [MARK] * is_sent,
            inputs,
            moved=3 * pairs * tall * channels,
            name="split",
        )
        for is_sent in (False, True)
    )
    return kept, sent[:3], sent[3]


def scatter_sum(kept, sent, before_a):
    (a_keep, b_keep, c_keep), (a_send, b_send, c_send) = kept, sent
    channels = a_keep.shape[-1]
    a_came = swapped(a_send, "lat", 2)
    b_came = swapped(b_send, "lat", 4)
    c_came = swapped(c_send, "lat", 2)
    a_keep, a_send, mark = halved(a_keep, a_came, 2, (2, 1), before_a)
    a_came = swapped(a_send, "lat", 4)
    b_keep, b_send, mark = halved(b_keep, b_came, 3, (1, 2), [mark])
    b_came = swapped(b_send, "lat", 8)
    c_keep, c_send, mark = halved(c_keep, c_came, 2, (2, 1), [mark])
    c_came = swapped(c_send, "lat", 4)
    a_keep, a_send, mark = halved(a_keep, a_came, 3, (1, 1), [mark])
    a_came = swapped(a_send, "lat", 8)
    b_keep, b_send, mark = halved(b_keep, b_came, 1, (1, 1), [mark])
    b_came = swapped(b_send, "lat", 2)
    c_keep, c_send = halved(c_keep, c_came, 3, (1, 1), [mark], False)
    c_came = swapped(c_send, "lat", 8)
    return [part.reshape(-1, channels) for part in (a_keep, a_came, b_keep, b_came, c_keep, c_came)]


def finish_kernel(*refs, atmos_factor, ocean_factor):
    parts, (atmos_ref, ocean_ref) = refs[:-2], refs[-2:]
    channels = parts[0].shape[1]
    pieces = channels // 128
    atmos_rows = atmos_ref.shape[0] // pieces
    ocean_rows = ocean_ref.shape[0] // pieces
    sums = [
        parts[index][...].astype(F32) + parts[index + 1][...].astype(F32)
        for index in range(0, len(parts), 2)
    ]
    total = jnp.concatenate(sums, axis=0)
    for piece in range(pieces):
        lanes = slice(128 * piece, 128 * (piece + 1))
        atmos_ref[pl.ds(piece, atmos_rows, pieces), :] = total[:atmos_rows, lanes] * atmos_factor
        ocean_ref[pl.ds(piece, ocean_rows, pieces), :] = (
            total[atmos_rows : atmos_rows + ocean_rows, lanes] * ocean_factor
        )


def input_grad_kernel(
    stay_ref, give_ref, near_ref, far_ref, gpad_ref, wet_ref, terms_ref, atmos_ref, ocean_ref, *refs, cols
):
    grad_ref, sent_ref = refs[-2:]
    middle = hidden_and_grad(stay_ref, give_ref)[1]
    low, high = low_and_high(near_rows(near_ref, 1, cols), far_ref[cols:, :])
    pad = jnp.concatenate([low, middle, high], axis=0)
    own = slice(cols, 3 * cols)
    convolve(pad, grad_ref, atmos_ref, ocean_ref, 0, True, cols)
    grad = gpad_ref[own, :].astype(F32) + grad_ref[...]
    grad_ref[...] = grad
    weighted = dot(terms_ref[8:16, :], grad, NT, HIGHEST)
    mixed = weighted[0:4] * wet_ref[0:1, own] + weighted[4:8] * wet_ref[1:2, own]
    sent_ref[...] = jnp.where(on_ocean(), mixed, weighted[0:4])


def next_kernel(
    stay_ref, give_ref, near_ref, far_ref, upad_ref, atmos_ref, ocean_ref,
    next_ref, mark_ref, second_ref, *, cols,
):
    middle = hidden_and_grad(stay_ref, give_ref)[0]
    low, high = low_and_high(near_rows(near_ref, 0, cols), far_ref[0:cols, :])
    pad = jnp.concatenate([low, middle, high], axis=0)
    own = slice(cols, 3 * cols)
    convolve(pad, second_ref, atmos_ref, ocean_ref, 1, False, cols)
    values = (upad_ref[own, :].astype(F32) + second_ref[...]).astype(BF16)
    next_ref[0] = values[:cols]
    next_ref[1] = values[cols:]
    mark_ref[...] = jnp.zeros_like(mark_ref)


def last_kernel(grad_ref, arrived_ref, wet_ref, terms_ref, *refs, cols):
    out_ref, mark_ref = refs[-2:]
    own = slice(cols, 3 * cols)
    wet = wet_ref[0:1, own], wet_ref[1:2, own]
    arrived = jnp.where(on_ocean(), arrived_ref[...] * wet_ref[2:3, own], arrived_ref[...])
    added = spread(arrived, wet, on_ocean(), terms_ref[0:8, :])
    values = (grad_ref[...] + added).astype(BF16)
    out_ref[0] = values[:cols]
    out_ref[1] = values[cols:]
    mark_ref[...] = jnp.zeros_like(mark_ref)


def swapped(value, axis, mask):
    pairs = [(source, source ^ mask) for source in range(lax.axis_size(axis))]
    return lax.ppermute(value, axis, pairs)


def far_halo(far):
    pairs = [(i, i + 1 if i % 2 else i - 1) for i in range(1, lax.axis_size("lat") - 1)]
    return lax.ppermute(far, "lat", pairs)


def local(
    fields,
    cotangent,
    ocean_kernels,
    atmos_kernels,
    ocean_surface,
    ocean_coupling,
    atmos_flux,
    atmos_coupling,
    row_map,
    wet_mask,
):
    x, g = fields[0], cotangent[0]
    bands, cols, channels = x.shape
    narrow = channels // 2
    cells = bands * cols
    count = lax.axis_size("lat")
    is_ocean = lax.axis_index("grp") == 0
    atmos_factor = 1.0 / math.sqrt(bands * count * cols)
    ocean_factor = 1.0 / math.sqrt(bands * count * 2 * cols)
    bound = functools.partial

    blank = jnp.zeros((4, narrow), BF16)
    gap = jnp.zeros((4, channels), BF16)
    surface = ocean_surface.T
    ocean_terms = jnp.concatenate(
        [
            jnp.concatenate([surface, blank], axis=1),
            jnp.concatenate([blank, surface], axis=1),
            jnp.concatenate([ocean_coupling, blank], axis=1),
            jnp.concatenate([blank, ocean_coupling], axis=1),
        ],
        axis=0,
    )
    atmos_terms = jnp.concatenate([atmos_flux.T, gap, atmos_coupling, gap], axis=0)
    terms = jnp.where(is_ocean, ocean_terms, atmos_terms).astype(F32)

    edge = shape((2 * cols + 16, channels), BF16)
    half = shape((cells, channels), BF16)
    near, far, own_early, own = call(
        bound(pack_kernel, cols=cols),
        [edge, edge, half, shape((2 * cells + 16, channels), BF16)],
        [x, g, wet_mask],
        [IN_PLACE] * 3,
        [
            pltpu.VMEM(x.shape, BF16),
            pltpu.VMEM(x.shape, BF16),
            pltpu.VMEM(wet_mask.shape, jnp.int32),
            pltpu.SemaphoreType.DMA((3,)),
        ],
        name="pack",
        limit=PACK_VMEM,
    )
    near, far = swapped(near, "lat", 1), far_halo(far)
    other_early = swapped(own_early, "grp", 1)
    wide = -(-narrow // 128) * 128
    own, atmos_flat, ocean_flat = call(
        hold_kernel,
        [
            shape(own.shape, BF16),
            shape((18, channels, channels), BF16),
            shape((18, wide, narrow), BF16),
        ],
        [own, atmos_kernels.reshape(18, channels, channels), ocean_kernels.reshape(18, narrow, narrow)],
        [WHOLE, IN_PLACE, IN_PLACE],
        [pltpu.SemaphoreType.DMA],
        flops=PACE * 10**8,
        name="hold",
        limit=HOLD_VMEM,
    )
    pad = shape((2 * cells, channels), BF16)
    xpad, gpad, wet, edges, sent = call(
        bound(outgoing_kernel, cols=cols),
        [pad, pad, shape((8, 2 * cells), F32), half, shape((4, 2 * cells), F32)],
        [own, near, far, terms],
        name="outgoing",
    )
    arrived = swapped(sent, "grp", 1)
    other_edges = swapped(edges, "grp", 1)
    conv_cost = dict(flops=PACE * 9 * cells * channels * channels, moved=9 * channels * channels * 2)
    back = call(
        bound(back_kernel, cols=cols),
        shape((cells, channels), F32),
        [gpad, atmos_flat, ocean_flat],
        **conv_cost,
        name="back",
    )
    upad, stay, give = call(
        bound(first_kernel, cols=cols),
        [pad, half, half],
        [xpad, wet, arrived, terms, back, atmos_flat, ocean_flat],
        None,
        [pltpu.VMEM((cells, channels), F32)],
        **conv_cost,
        name="first",
    )
    late = swapped(give, "grp", 1)

    atmos_rows = 9 * channels // count
    ocean_rows = 9 * narrow // count
    chunked = count == 16 and 9 * channels % (8 * count) == 0 and ocean_rows % 2 == 0
    tall = -(-(atmos_rows + ocean_rows // 2) // 16) * 16
    spare = max(0, 2 * (tall - atmos_rows) - ocean_rows) if chunked else 0
    ocean_tall = 9 * narrow + -(-spare // 8) * 8
    sums = [shape((9 * channels, channels), F32), shape((wide // 128, ocean_tall, 128), F32)]
    atmos_sum, ocean_sum, near, far = call(
        bound(own_grads_kernel, cols=cols),
        [*sums, half, half],
        [upad, gpad, stay, give],
        **conv_cost,
        name="own_grads",
    )
    far = far_halo(far)
    lefts = call(
        bound(shift_kernel, cols=cols),
        shape((3, channels, 2 * cells), BF16),
        [other_early, other_edges, sent, atmos_coupling],
        name="shift",
    )
    atmos_other, ocean_other = call(
        bound(other_grads_kernel, cols=cols),
        sums,
        [lefts, late, other_early, other_edges],
        **conv_cost,
        name="other_grads",
    )
    if chunked:
        taken = 2 * cols // (count // 2)
        sums = [atmos_sum, ocean_sum, atmos_other, ocean_other]
        send, keep = (
            call(
                bound(chunk_kernel, chunks=count, tall=tall, sent=sent),
                shape((count // 2, tall + taken * sent, channels), BF16),
                sums + [near, far] * sent,
                [WHOLE] * (4 + sent) + [ANYWHERE] * sent,
                moved=2 * count * tall * channels,
                name="chunk",
            )
            for sent in (True, False)
        )
        near = swapped(send, "lat", 1)
        kept, parts, split_mark = split(keep, near)
        after_split = [split_mark]
    else:
        near = swapped(near, "lat", 1)
        after_split = []

    grad, sent_back = call(
        bound(input_grad_kernel, cols=cols),
        [shape((cells, channels), F32), shape((4, cells), F32)],
        [stay, give, near, far, gpad, wet, terms, atmos_flat, ocean_flat, *after_split],
        [WHOLE] * 9 + [ANYWHERE] * len(after_split),
        **conv_cost,
        name="input_grad",
    )
    returned = swapped(sent_back, "grp", 1)
    next_field, next_mark = call(
        bound(next_kernel, cols=cols),
        [shape(x.shape, BF16), MARK],
        [stay, give, near, far, upad, atmos_flat, ocean_flat],
        None,
        [pltpu.VMEM((cells, channels), F32)],
        **conv_cost,
        name="next",
    )

    field_grad, last_mark = call(
        bound(last_kernel, cols=cols),
        [shape(x.shape, BF16), MARK],
        [grad, returned, wet, terms],
        name="last",
    )
    if chunked:
        sums = scatter_sum(kept, parts, [next_mark, last_mark])
        atmos_chunk, ocean_chunk = call(
            bound(finish_kernel, atmos_factor=atmos_factor, ocean_factor=ocean_factor),
            [
                shape((atmos_rows * channels // 128, 128), F32),
                shape((ocean_rows * narrow // 128, 128), F32),
            ],
            sums,
            name="finish",
        )
        atmos_total, ocean_total = atmos_chunk.reshape(-1), ocean_chunk.reshape(-1)
    else:
        atmos_all = jnp.where(is_ocean, atmos_other, atmos_sum)
        ocean_all = jnp.where(is_ocean, ocean_sum, ocean_other)
        atmos_total = atmos_factor * lax.psum_scatter(
            atmos_all.reshape(-1), "lat", scatter_dimension=0, tiled=True
        )
        ocean_all = jnp.concatenate([ocean_all[piece] for piece in range(wide // 128)], axis=1)
        ocean_total = ocean_factor * lax.psum_scatter(
            ocean_all[:, :narrow].reshape(-1), "lat", scatter_dimension=0, tiled=True
        )
    return (next_field[None], field_grad[None], ocean_total, atmos_total)


def solution(mesh):
    in_specs = (
        P("grp", "lat", None, None),
        P("grp", "lat", None, None),
        P(),
        P(),
        P(),
        P(),
        P(),
        P(),
        P("lat"),
        P("lat", None),
    )
    out_specs = (
        P("grp", "lat", None, None),
        P("grp", "lat", None, None),
        P(("grp", "lat")),
        P(("grp", "lat")),
    )
    return jax.shard_map(local, mesh=mesh, in_specs=in_specs, out_specs=out_specs, check_vma=False)
```

```python
import functools
import math

import jax
import jax.numpy as jnp
from jax import lax
from jax.experimental import pallas as pl
from jax.experimental.pallas import tpu as pltpu
from jax.sharding import PartitionSpec as P

HIGHEST = lax.Precision.HIGHEST
GELU_SCALE = 0.7978845608028654
GELU_CUBIC = 0.044715
F32 = jnp.float32
BF16 = jnp.bfloat16
WHOLE = pl.BlockSpec(memory_space=pltpu.VMEM)
IN_PLACE = pl.BlockSpec(memory_space=pltpu.HBM)
ANYWHERE = pl.BlockSpec(memory_space=pl.ANY)
VMEM_LIMIT = 20 * 1024 * 1024
PACE = 8
PACK_VMEM = 62 * 1024 * 1024
HOLD_VMEM = 42 * 1024 * 1024

NN = (((1,), (0,)), ((), ()))
NT = (((1,), (1,)), ((), ()))
TN = (((0,), (0,)), ((), ()))


def shape(dims, kind):
    return jax.ShapeDtypeStruct(dims, kind)


def call(kernel, outs, inputs, in_specs=None, scratch=(), flops=0, moved=0, name=None, limit=VMEM_LIMIT, out_spec=WHOLE):
    return pl.pallas_call(
        kernel,
        out_shape=outs,
        in_specs=in_specs or [WHOLE] * len(inputs),
        out_specs=jax.tree.map(lambda _: out_spec, outs),
        scratch_shapes=list(scratch),
        compiler_params=pltpu.CompilerParams(vmem_limit_bytes=limit),
        cost_estimate=pl.CostEstimate(flops=flops, bytes_accessed=moved, transcendentals=0),
        name=name,
    )(*inputs)


def on_ocean():
    return lax.axis_index("grp") == 0


def dot(left, right, dims=NN, precision=None):
    return lax.dot_general(left, right, dims, precision=precision, preferred_element_type=F32)


def moved_cells(values, axis, cols):
    count = values.shape[axis]
    place = lax.rem(lax.broadcasted_iota(jnp.int32, values.shape, axis), cols)
    before = jnp.where(place == 0, 0.0, pltpu.roll(values, 1, axis))
    after = jnp.where(place == cols - 1, 0.0, pltpu.roll(values, count - 1, axis))
    return before, after


def wet_halves(wet, cols, channels):
    source = lax.broadcasted_iota(jnp.int32, (2 * cols, 2 * cols), 0)
    target = lax.broadcasted_iota(jnp.int32, (2 * cols, 2 * cols), 1)
    wanted = 2 * lax.rem(target, cols) + jnp.where(target >= cols, 1, 0)
    chooser = (source == wanted).astype(F32).astype(BF16)
    padded = jnp.concatenate([wet.astype(F32), jnp.zeros((14, 2 * cols), F32)], axis=0)
    apart = dot(padded.astype(BF16), chooser)
    return jnp.concatenate([apart, jnp.zeros((16, channels - 2 * cols), F32)], axis=1)


def own_bit(bit):
    return lax.rem(lax.shift_right_logical(lax.axis_index("lat"), bit), 2)


def pack_kernel(
    x_any, g_any, wet_any, near_ref, far_x, far_g, early_ref, own_ref, x_ref, g_ref, wet_ref, sems, *, cols
):
    pairs = ((wet_any, wet_ref), (x_any, x_ref), (g_any, g_ref))
    copies = [pltpu.make_async_copy(*pair, sems.at[index]) for index, pair in enumerate(pairs)]
    for copy in copies:
        copy.start()
    core = own_bit(0)
    copies[0].wait()
    wide = wet_halves(wet_ref[...], cols, x_ref.shape[2])
    other = pltpu.roll(wide, 15, 0)
    own_ref[4 * cols :, :] = wide.astype(BF16)
    far_x[cols:, :] = jnp.where(core == 0, wide, other).astype(BF16)
    near_ref[2 * cols :, :] = jnp.where(core == 0, other, wide).astype(BF16)
    far_g[cols:, :] = jnp.zeros((far_g.shape[0] - cols, far_g.shape[1]), BF16)
    copies[1].wait()
    copies[2].wait()
    for part, ref in enumerate((x_ref, g_ref)):
        (far_x, far_g)[part][0:cols, :] = ref[core]
        near_ref[part * cols : (part + 1) * cols, :] = ref[1 - core]
        own_ref[2 * part * cols : (2 * part + 1) * cols, :] = ref[0]
        own_ref[(2 * part + 1) * cols : (2 * part + 2) * cols, :] = ref[1]
    for row in range(2):
        early_ref[row * cols : (row + 1) * cols, :] = jnp.where(on_ocean(), g_ref[row], x_ref[row])


def hold_kernel(own_in, atmos_any, ocean_any, own_ref, atmos_ref, ocean_ref, sem):
    narrow = ocean_ref.shape[2]
    ocean_copy = pltpu.make_async_copy(ocean_any, ocean_ref.at[:, pl.ds(0, narrow), :], sem)
    atmos_copy = pltpu.make_async_copy(atmos_any, atmos_ref, sem)

    @pl.when(on_ocean())
    def _():
        ocean_copy.start()
        gap = ocean_ref.shape[1] - narrow
        if gap:
            ocean_ref[:, narrow:, :] = jnp.zeros((ocean_ref.shape[0], gap, narrow), BF16)

    @pl.when(jnp.logical_not(on_ocean()))
    def _():
        atmos_copy.start()

    own_ref[...] = own_in[...]

    @pl.when(on_ocean())
    def _():
        ocean_copy.wait()

    @pl.when(jnp.logical_not(on_ocean()))
    def _():
        atmos_copy.wait()


def low_and_high(near, far):
    core = own_bit(0)
    return jnp.where(core == 0, far, near), jnp.where(core == 0, near, far)


def outgoing_kernel(own_ref, near_ref, far_x, terms_ref, xpad_ref, wet_ref, sent_ref, *, cols):
    low, high = low_and_high(near_ref[0:cols, :], far_x[0:cols, :])
    xpad_ref[0:cols, :] = low
    xpad_ref[cols : 3 * cols, :] = own_ref[0 : 2 * cols, :]
    xpad_ref[3 * cols :, :] = high
    low_wet, high_wet = low_and_high(near_ref[2 * cols :, :].astype(F32), far_x[cols:, :].astype(F32))
    own_wet = own_ref[4 * cols :, :].astype(F32)
    halves = []
    for start in (0, cols):
        lanes = slice(start, start + cols)
        rows = (low_wet[0:1, lanes], own_wet[0:1, lanes], own_wet[1:2, lanes], high_wet[0:1, lanes])
        halves.append(jnp.concatenate(rows, axis=1))
    first_wet, second_wet = halves
    inverse = 1.0 / jnp.maximum(first_wet + second_wet, 1.0)
    wet_ref[0:1, :] = first_wet
    wet_ref[1:2, :] = second_wet
    wet_ref[2:3, :] = inverse
    wet_ref[3:8, :] = jnp.zeros((5, 4 * cols), F32)
    xpad = xpad_ref[...]
    projected = dot(terms_ref[0:8, :].astype(BF16), xpad, NT)
    mixed = (projected[0:4] * first_wet + projected[4:8] * second_wet) * inverse
    sent_ref[...] = jnp.where(on_ocean(), mixed, projected[0:4])


def halves_apart(values, narrow):
    wide = -(-narrow // 128) * 128
    lane = lax.broadcasted_iota(jnp.int32, values.shape, 1)
    even = jnp.where(lane < narrow, values, 0.0)
    odd = jnp.where(lane < narrow, pltpu.roll(values, narrow, 1), 0.0)
    return even[:, :wide], odd[:, :wide]


def halves_with_columns(pad, cols):
    even, odd = halves_apart(pad.astype(F32), pad.shape[1] // 2)
    odd_before = moved_cells(odd, 0, cols)[0].astype(BF16)
    even_after = moved_cells(even, 0, cols)[1].astype(BF16)
    even, odd = even.astype(BF16), odd.astype(BF16)
    return (odd_before, even, odd), (even, odd, even_after)


def with_columns(pad, cols):
    before, after = moved_cells(pad.astype(F32), 0, cols)
    return before.astype(BF16), pad, after.astype(BF16)


def convolve(pad, out_ref, atmos_ref, ocean_ref, layer, flipped, cols):
    base = 9 * layer
    channels = atmos_ref.shape[2]
    wide, narrow = ocean_ref.shape[1:]
    rows = out_ref.shape[0]

    def summed(pick):
        total = None
        for row_tap in range(3):
            part = pick(row_tap, slice(cols * row_tap, cols * row_tap + rows))
            total = part if total is None else total + part
        return total

    @pl.when(on_ocean())
    def _():
        evens, odds = halves_with_columns(pad, cols)
        if flipped:

            def pick(row_tap, span):
                part = None
                for col_tap in range(3):
                    left = jnp.concatenate([evens[col_tap][span], odds[col_tap][span]], axis=0)
                    kernel = ocean_ref[base + 8 - (3 * row_tap + col_tap), 0:narrow, :]
                    piece = dot(left[:, :narrow], kernel, NT)
                    part = piece if part is None else part + piece
                return part

        else:
            even, odd = jnp.concatenate(evens, axis=1), jnp.concatenate(odds, axis=1)

            def pick(row_tap, span):
                first = base + 3 * row_tap
                kernel = ocean_ref[first : first + 3].reshape(3 * wide, narrow)
                return dot(jnp.concatenate([even[span], odd[span]], axis=0), kernel)

        total = summed(pick)
        out_ref[...] = jnp.concatenate([total[:rows], total[rows:]], axis=1)

    @pl.when(jnp.logical_not(on_ocean()))
    def _():
        taps = with_columns(pad, cols)
        if flipped:

            def pick(row_tap, span):
                part = None
                for col_tap in range(3):
                    piece = dot(taps[col_tap][span], atmos_ref[base + 8 - (3 * row_tap + col_tap)], NT)
                    part = piece if part is None else part + piece
                return part

        else:
            joined = jnp.concatenate(taps, axis=1)

            def pick(row_tap, span):
                first = base + 3 * row_tap
                return dot(joined[span], atmos_ref[first : first + 3].reshape(3 * channels, channels))

        out_ref[...] = summed(pick)


def back_kernel(
    own_ref, near_ref, far_g, xpad_ref, atmos_ref, ocean_ref, out_ref, gpad_ref, edge_ref, *, cols
):
    low, high = low_and_high(near_ref[cols : 2 * cols, :], far_g[0:cols, :])
    pad = jnp.concatenate([low, own_ref[2 * cols : 4 * cols, :], high], axis=0)
    gpad_ref[...] = pad
    edge_ref[0:cols, :] = jnp.where(on_ocean(), low, xpad_ref[0:cols, :])
    edge_ref[cols:, :] = jnp.where(on_ocean(), high, xpad_ref[3 * cols :, :])
    convolve(pad, out_ref, atmos_ref, ocean_ref, 1, True, cols)


def spread(arrived, wet, mixing, terms):
    first_wet, second_wet = wet
    both = jnp.concatenate([arrived * first_wet, arrived * second_wet], axis=0)
    alone = jnp.concatenate([arrived, jnp.zeros_like(arrived)], axis=0)
    return dot(jnp.where(mixing, both, alone), terms, TN, HIGHEST)


def first_kernel(
    xpad_ref, wet_ref, arrived_ref, terms_ref, back_ref, atmos_ref, ocean_ref,
    u_ref, stay_ref, give_ref, first_ref, *, cols,
):
    wet = wet_ref[0:1, :], wet_ref[1:2, :]
    coupled = spread(arrived_ref[...], wet, on_ocean(), terms_ref[8:16, :])
    u = (xpad_ref[...].astype(F32) + coupled).astype(BF16)
    u_ref[...] = u
    convolve(u, first_ref, atmos_ref, ocean_ref, 0, False, cols)
    first = first_ref[...]
    tangent = jnp.tanh(GELU_SCALE * (first + GELU_CUBIC * first * first * first))
    hidden = (0.5 * first * (1.0 + tangent)).astype(BF16)
    slope = 0.5 * (1.0 + tangent) + 0.5 * first * (1.0 - tangent * tangent) * GELU_SCALE * (
        1.0 + 3.0 * GELU_CUBIC * first * first
    )
    first_grad = (back_ref[...] * slope).astype(BF16)
    stay_ref[...] = jnp.where(on_ocean(), first_grad, hidden)
    give_ref[...] = jnp.where(on_ocean(), hidden, first_grad)


def whole_pad(early_ref, edge_ref, cols):
    parts = [edge_ref[0:cols, :], early_ref[...], edge_ref[cols:, :]]
    return jnp.concatenate(parts, axis=0).astype(F32)


def grad_atmos(pad, own, cols, store):
    rows = own.shape[0]
    left = own.T.astype(BF16)
    before, after = moved_cells(pad, 0, cols)
    rights = [part.astype(BF16) for part in (after, pad, before)]
    for tap in range(9):
        start = cols * (2 - tap // 3)
        store(tap, dot(left, rights[tap % 3][start : start + rows]))


def grad_ocean(pad, own, pad_is_input, cols, store):
    rows, channels = own.shape
    narrow = channels // 2

    if pad_is_input:
        middle = pad.T
        before, after = moved_cells(middle, 1, cols)
        even, odd = middle[:narrow].astype(BF16), middle[narrow:].astype(BF16)
        pairs = (
            (before[narrow:].astype(BF16), even),
            (even, odd),
            (odd, after[:narrow].astype(BF16)),
        )
        right = jnp.concatenate(halves_apart(own, narrow), axis=0).astype(BF16)
        for tap in range(9):
            start = cols * (tap // 3)
            pieces = [part[:, start : start + rows] for part in pairs[tap % 3]]
            store(tap, dot(jnp.concatenate(pieces, axis=1), right))
    else:
        turned = own.T.astype(BF16)
        left = jnp.concatenate([turned[:narrow], turned[narrow:]], axis=1)
        even, odd = halves_apart(pad, narrow)
        odd_before = moved_cells(odd, 0, cols)[0].astype(BF16)
        even_after = moved_cells(even, 0, cols)[1].astype(BF16)
        even, odd = even.astype(BF16), odd.astype(BF16)
        pairs = ((odd, even_after), (even, odd), (odd_before, even))
        for tap in range(9):
            start = cols * (2 - tap // 3)
            pieces = [part[start : start + rows] for part in pairs[tap % 3]]
            store(tap, dot(left, jnp.concatenate(pieces, axis=0)))


def store_into(out_ref):
    def store(tap, value):
        if len(out_ref.shape) == 2:
            rows = value.shape[0]
            out_ref[rows * tap : rows * (tap + 1), :] = value
        else:
            rows = value.shape[0]
            for piece in range(out_ref.shape[0]):
                lanes = slice(128 * piece, 128 * (piece + 1))
                out_ref[piece, rows * tap : rows * (tap + 1), :] = value[:, lanes]

    return store


def near_rows(near_ref, part, cols):
    if len(near_ref.shape) == 2:
        return near_ref[part * cols : (part + 1) * cols, :]
    count, tall = near_ref.shape[0] // 2, near_ref.shape[1]
    taken = cols // count
    pieces = [near_ref[index, tall - taken :, :] for index in range(part * count, (part + 1) * count)]
    return jnp.concatenate(pieces, axis=0)


def hidden_and_grad(stay_ref, give_ref):
    stay, give = stay_ref[...], give_ref[...]
    return jnp.where(on_ocean(), give, stay), jnp.where(on_ocean(), stay, give)


def shifted_inputs(pad, cols):
    middle = pad.T
    before, after = moved_cells(middle, 1, cols)
    return [part.astype(BF16) for part in (before, middle, after)]


def own_grads_kernel(
    upad_ref, gpad_ref, stay_ref, give_ref, atmos_out, ocean_out, near_ref, far_hidden, far_grad, *, cols
):
    stay = stay_ref[...].astype(F32)
    hidden, first_grad = hidden_and_grad(stay_ref, give_ref)
    core = own_bit(0)
    for part, values in enumerate((hidden, first_grad)):
        target = slice(part * cols, (part + 1) * cols)
        (far_hidden, far_grad)[part][...] = jnp.where(core == 0, values[:cols], values[cols:])
        near_ref[target, :] = jnp.where(core == 0, values[cols:], values[:cols])

    @pl.when(on_ocean())
    def _():
        grad_ocean(upad_ref[...].astype(F32), stay, True, cols, store_into(ocean_out))

    @pl.when(jnp.logical_not(on_ocean()))
    def _():
        grad_atmos(gpad_ref[...].astype(F32), stay, cols, store_into(atmos_out))


def shift_kernel(early_ref, edge_ref, sent_ref, coupling_ref, left_ref, *, cols):
    @pl.when(on_ocean())
    def _():
        added = dot(sent_ref[...], coupling_ref[...].astype(F32), TN, HIGHEST)
        other = (whole_pad(early_ref, edge_ref, cols) + added).astype(BF16).astype(F32)
        for tap, left in enumerate(shifted_inputs(other, cols)):
            left_ref[tap] = left


def other_grads_kernel(left_ref, late_ref, early_ref, edge_ref, atmos_out, ocean_out, *, cols):
    rows = late_ref.shape[0]

    @pl.when(on_ocean())
    def _():
        store = store_into(atmos_out)
        for tap in range(9):
            start = cols * (tap // 3)
            store(tap, dot(left_ref[tap % 3, :, start : start + rows], late_ref[...]))

    @pl.when(jnp.logical_not(on_ocean()))
    def _():
        late = late_ref[...].astype(F32)
        grad_ocean(whole_pad(early_ref, edge_ref, cols), late, False, cols, store_into(ocean_out))


def chunk_rows(out_ref, side, tall, atmos_all, ocean_all, chunks):
    channels = out_ref.shape[2]
    pieces = ocean_all.shape[0]
    atmos_rows = atmos_all.shape[0] // chunks
    ocean_rows = atmos_rows // 2
    taken = tall - atmos_rows
    blank = jnp.zeros((taken, channels - 128 * pieces), F32)
    for pair in range(chunks // 2):
        start = pl.multiple_of(atmos_rows * (2 * pair + side), 8)
        upper = atmos_all[pl.ds(start, atmos_rows), :]
        start = ocean_rows * (2 * pair + side)
        halves = []
        for odd in range(2):
            parts = [ocean_all.at[piece][pl.ds(start + odd, taken, 2), :] for piece in range(pieces)]
            halves.append(jnp.concatenate(parts + [blank], axis=1))
        lower = halves[0] + pltpu.roll(halves[1], channels // 2, 1)
        out_ref[pair, 0:tall, :] = jnp.concatenate([upper, lower], axis=0).astype(BF16)


def chunk_kernel(atmos_own, ocean_own, atmos_other, ocean_other, *refs, chunks, tall, sent):
    out_ref = refs[-1]
    core = own_bit(0)
    side = 1 - core if sent else core
    if sent:
        near_ref = refs[0]
        taken = out_ref.shape[1] - tall
        for pair in range(chunks // 2):
            out_ref[pair, tall:, :] = near_ref[pair * taken : (pair + 1) * taken, :]

    @pl.when(on_ocean())
    def _():
        chunk_rows(out_ref, side, tall, atmos_other, ocean_own, chunks)

    @pl.when(jnp.logical_not(on_ocean()))
    def _():
        chunk_rows(out_ref, side, tall, atmos_own, ocean_other, chunks)


def halve(keep_ref, came_ref, out_ref, side, rows):
    for outer in range(keep_ref.shape[0]):
        for inner in range(keep_ref.shape[2]):
            total = keep_ref[outer, side, inner, rows, :].astype(F32)
            total = total + came_ref[outer, side, inner, rows, :].astype(F32)
            out_ref[outer, inner] = total.astype(BF16)


def split_kernel(keep_ref, came_ref, *refs, cuts, sent):
    by_z = [ref.reshape(2, 2, 2, *ref.shape[3:]) for ref in (keep_ref, came_ref)]
    start = 0
    for index, rows in enumerate(cuts):
        pair, bit = (by_z, 2) if index == 1 else ((keep_ref, came_ref), 1)
        own = own_bit(bit)
        halve(*pair, refs[index], 1 - own if sent else own, slice(start, start + rows))
        start += rows
    if sent:
        refs[-1][...] = jnp.zeros_like(refs[-1])


def halve_kernel(keep_ref, came_ref, *refs, bit, marked):
    outs = refs[-3:] if marked else refs[-2:]
    own = own_bit(bit)
    halve(keep_ref, came_ref, outs[1], 1 - own, slice(None))
    halve(keep_ref, came_ref, outs[0], own, slice(None))
    if marked:
        outs[2][...] = jnp.zeros_like(outs[2])


MARK = shape((8, 128), F32)


def halved(keep, came, bit, dims, after, marked=True):
    outer, inner, rows, channels = dims[0], dims[1], keep.shape[-2], keep.shape[-1]
    keep, came = (part.reshape(outer, 2, inner, rows, channels) for part in (keep, came))
    out = shape((outer, inner, rows, channels), BF16)
    return call(
        functools.partial(halve_kernel, bit=bit, marked=marked),
        [out, out] + [MARK] * marked,
        [keep, came, *after],
        [WHOLE] * 2 + [ANYWHERE] * len(after),
        moved=8 * outer * inner * rows * channels,
        name="halve",
    )


def split(keep, came):
    pairs, tall, channels = keep.shape
    cuts = [16 * (tall // 16 * part // 17) for part in (6, 6)]
    cuts.append(tall - sum(cuts))
    outs = [
        shape(((2, 2) if index == 1 else (4, 1)) + (rows, channels), BF16) for index, rows in enumerate(cuts)
    ]
    inputs = [part.reshape(4, 2, 1, *part.shape[1:]) for part in (keep, came)]
    kept, sent = (
        call(
            functools.partial(split_kernel, cuts=cuts, sent=is_sent),
            outs + [MARK] * is_sent,
            inputs,
            moved=3 * pairs * tall * channels,
            name="split",
        )
        for is_sent in (False, True)
    )
    return kept, sent[:3], sent[3]


def scatter_sum(kept, sent, before_a):
    (a_keep, b_keep, c_keep), (a_send, b_send, c_send) = kept, sent
    channels = a_keep.shape[-1]
    a_came = swapped(a_send, "lat", 2)
    b_came = swapped(b_send, "lat", 4)
    c_came = swapped(c_send, "lat", 2)
    a_keep, a_send, mark = halved(a_keep, a_came, 2, (2, 1), before_a)
    a_came = swapped(a_send, "lat", 4)
    b_keep, b_send, mark = halved(b_keep, b_came, 3, (1, 2), [mark])
    b_came = swapped(b_send, "lat", 8)
    c_keep, c_send, mark = halved(c_keep, c_came, 2, (2, 1), [mark])
    c_came = swapped(c_send, "lat", 4)
    a_keep, a_send, mark = halved(a_keep, a_came, 3, (1, 1), [mark])
    a_came = swapped(a_send, "lat", 8)
    b_keep, b_send, mark = halved(b_keep, b_came, 1, (1, 1), [mark])
    b_came = swapped(b_send, "lat", 2)
    c_keep, c_send = halved(c_keep, c_came, 3, (1, 1), [mark], False)
    c_came = swapped(c_send, "lat", 8)
    return [part.reshape(-1, channels) for part in (a_keep, a_came, b_keep, b_came, c_keep, c_came)]


def finish_kernel(*refs, atmos_factor, ocean_factor):
    parts, (atmos_ref, ocean_ref) = refs[:-2], refs[-2:]
    channels = parts[0].shape[1]
    pieces = channels // 128
    atmos_rows = atmos_ref.shape[0] // pieces
    ocean_rows = ocean_ref.shape[0] // pieces
    sums = [
        parts[index][...].astype(F32) + parts[index + 1][...].astype(F32)
        for index in range(0, len(parts), 2)
    ]
    total = jnp.concatenate(sums, axis=0)
    for piece in range(pieces):
        lanes = slice(128 * piece, 128 * (piece + 1))
        atmos_ref[pl.ds(piece, atmos_rows, pieces), :] = total[:atmos_rows, lanes] * atmos_factor
        ocean_ref[pl.ds(piece, ocean_rows, pieces), :] = (
            total[atmos_rows : atmos_rows + ocean_rows, lanes] * ocean_factor
        )


def input_grad_kernel(
    stay_ref, give_ref, near_ref, far_ref, gpad_ref, wet_ref, terms_ref, atmos_ref, ocean_ref, *refs, cols
):
    grad_ref, sent_ref = refs[-2:]
    middle = hidden_and_grad(stay_ref, give_ref)[1]
    low, high = low_and_high(near_rows(near_ref, 1, cols), far_ref[...])
    pad = jnp.concatenate([low, middle, high], axis=0)
    own = slice(cols, 3 * cols)
    convolve(pad, grad_ref, atmos_ref, ocean_ref, 0, True, cols)
    grad = gpad_ref[own, :].astype(F32) + grad_ref[...]
    grad_ref[...] = grad
    weighted = dot(terms_ref[8:16, :], grad, NT, HIGHEST)
    mixed = weighted[0:4] * wet_ref[0:1, own] + weighted[4:8] * wet_ref[1:2, own]
    sent_ref[...] = jnp.where(on_ocean(), mixed, weighted[0:4])


def next_kernel(
    stay_ref, give_ref, near_ref, far_ref, upad_ref, atmos_ref, ocean_ref,
    next_ref, mark_ref, second_ref, *, cols,
):
    middle = hidden_and_grad(stay_ref, give_ref)[0]
    low, high = low_and_high(near_rows(near_ref, 0, cols), far_ref[...])
    pad = jnp.concatenate([low, middle, high], axis=0)
    own = slice(cols, 3 * cols)
    convolve(pad, second_ref, atmos_ref, ocean_ref, 1, False, cols)
    values = (upad_ref[own, :].astype(F32) + second_ref[...]).astype(BF16)
    next_ref[0] = values[:cols]
    next_ref[1] = values[cols:]
    mark_ref[...] = jnp.zeros_like(mark_ref)


def last_kernel(grad_ref, arrived_ref, wet_ref, terms_ref, *refs, cols):
    out_ref, mark_ref = refs[-2:]
    own = slice(cols, 3 * cols)
    wet = wet_ref[0:1, own], wet_ref[1:2, own]
    arrived = jnp.where(on_ocean(), arrived_ref[...] * wet_ref[2:3, own], arrived_ref[...])
    added = spread(arrived, wet, on_ocean(), terms_ref[0:8, :])
    values = (grad_ref[...] + added).astype(BF16)
    out_ref[0] = values[:cols]
    out_ref[1] = values[cols:]
    mark_ref[...] = jnp.zeros_like(mark_ref)


def swapped(value, axis, mask):
    pairs = [(source, source ^ mask) for source in range(lax.axis_size(axis))]
    return lax.ppermute(value, axis, pairs)


def far_halo(far):
    pairs = [(i, i + 1 if i % 2 else i - 1) for i in range(1, lax.axis_size("lat") - 1)]
    return lax.ppermute(far, "lat", pairs)


def local(
    fields,
    cotangent,
    ocean_kernels,
    atmos_kernels,
    ocean_surface,
    ocean_coupling,
    atmos_flux,
    atmos_coupling,
    row_map,
    wet_mask,
):
    x, g = fields[0], cotangent[0]
    bands, cols, channels = x.shape
    narrow = channels // 2
    cells = bands * cols
    count = lax.axis_size("lat")
    is_ocean = lax.axis_index("grp") == 0
    atmos_factor = 1.0 / math.sqrt(bands * count * cols)
    ocean_factor = 1.0 / math.sqrt(bands * count * 2 * cols)
    bound = functools.partial

    blank = jnp.zeros((4, narrow), BF16)
    gap = jnp.zeros((4, channels), BF16)
    surface = ocean_surface.T
    ocean_terms = jnp.concatenate(
        [
            jnp.concatenate([surface, blank], axis=1),
            jnp.concatenate([blank, surface], axis=1),
            jnp.concatenate([ocean_coupling, blank], axis=1),
            jnp.concatenate([blank, ocean_coupling], axis=1),
        ],
        axis=0,
    )
    atmos_terms = jnp.concatenate([atmos_flux.T, gap, atmos_coupling, gap], axis=0)
    terms = jnp.where(is_ocean, ocean_terms, atmos_terms).astype(F32)

    edge = shape((2 * cols + 16, channels), BF16)
    half = shape((cells, channels), BF16)
    row = shape((cols, channels), BF16)
    near, far_x, far_g, own_early, own = call(
        bound(pack_kernel, cols=cols),
        [edge, shape((cols + 16, channels), BF16), shape((cols + 32, channels), BF16), half, shape((2 * cells + 16, channels), BF16)],
        [x, g, wet_mask],
        [IN_PLACE] * 3,
        [
            pltpu.VMEM(x.shape, BF16),
            pltpu.VMEM(x.shape, BF16),
            pltpu.VMEM(wet_mask.shape, jnp.int32),
            pltpu.SemaphoreType.DMA((3,)),
        ],
        name="pack",
        limit=PACK_VMEM,
    )
    near, far_x, far_g = swapped(near, "lat", 1), far_halo(far_x), far_halo(far_g)
    other_early = swapped(own_early, "grp", 1)
    wide = -(-narrow // 128) * 128
    own, atmos_flat, ocean_flat = call(
        hold_kernel,
        [
            shape(own.shape, BF16),
            shape((18, channels, channels), BF16),
            shape((18, wide, narrow), BF16),
        ],
        [own, atmos_kernels.reshape(18, channels, channels), ocean_kernels.reshape(18, narrow, narrow)],
        [WHOLE, IN_PLACE, IN_PLACE],
        [pltpu.SemaphoreType.DMA],
        flops=PACE * 10**8,
        name="hold",
        limit=HOLD_VMEM,
    )
    pad = shape((2 * cells, channels), BF16)
    xpad, wet, sent = call(
        bound(outgoing_kernel, cols=cols),
        [pad, shape((8, 2 * cells), F32), shape((4, 2 * cells), F32)],
        [own, near, far_x, terms],
        name="outgoing",
    )
    arrived = swapped(sent, "grp", 1)
    conv_cost = dict(flops=PACE * 9 * cells * channels * channels, moved=9 * channels * channels * 2)
    back, gpad, edges = call(
        bound(back_kernel, cols=cols),
        [shape((cells, channels), F32), pad, half],
        [own, near, far_g, xpad, atmos_flat, ocean_flat],
        **conv_cost,
        name="back",
    )
    other_edges = swapped(edges, "grp", 1)
    upad, stay, give = call(
        bound(first_kernel, cols=cols),
        [pad, half, half],
        [xpad, wet, arrived, terms, back, atmos_flat, ocean_flat],
        None,
        [pltpu.VMEM((cells, channels), F32)],
        **conv_cost,
        name="first",
    )
    late = swapped(give, "grp", 1)

    atmos_rows = 9 * channels // count
    ocean_rows = 9 * narrow // count
    chunked = count == 16 and 9 * channels % (8 * count) == 0 and ocean_rows % 2 == 0
    tall = -(-(atmos_rows + ocean_rows // 2) // 16) * 16
    spare = max(0, 2 * (tall - atmos_rows) - ocean_rows) if chunked else 0
    ocean_tall = 9 * narrow + -(-spare // 8) * 8
    sums = [shape((9 * channels, channels), F32), shape((wide // 128, ocean_tall, 128), F32)]
    atmos_sum, ocean_sum, near, far_hidden, far_grad = call(
        bound(own_grads_kernel, cols=cols),
        [*sums, half, row, row],
        [upad, gpad, stay, give],
        **conv_cost,
        name="own_grads",
    )
    far_hidden, far_grad = far_halo(far_hidden), far_halo(far_grad)
    lefts = call(
        bound(shift_kernel, cols=cols),
        shape((3, channels, 2 * cells), BF16),
        [other_early, other_edges, sent, atmos_coupling],
        name="shift",
    )
    atmos_other, ocean_other = call(
        bound(other_grads_kernel, cols=cols),
        sums,
        [lefts, late, other_early, other_edges],
        **conv_cost,
        name="other_grads",
    )
    if chunked:
        taken = 2 * cols // (count // 2)
        sums = [atmos_sum, ocean_sum, atmos_other, ocean_other]
        send, keep = (
            call(
                bound(chunk_kernel, chunks=count, tall=tall, sent=sent),
                shape((count // 2, tall + taken * sent, channels), BF16),
                sums + [near, far_grad] * sent,
                [WHOLE] * (4 + sent) + [ANYWHERE] * sent,
                moved=2 * count * tall * channels,
                name="chunk",
            )
            for sent in (True, False)
        )
        near = swapped(send, "lat", 1)
        kept, parts, split_mark = split(keep, near)
        after_split = [split_mark]
    else:
        near = swapped(near, "lat", 1)
        after_split = []

    grad, sent_back = call(
        bound(input_grad_kernel, cols=cols),
        [shape((cells, channels), F32), shape((4, cells), F32)],
        [stay, give, near, far_grad, gpad, wet, terms, atmos_flat, ocean_flat, *after_split],
        [WHOLE] * 9 + [ANYWHERE] * len(after_split),
        **conv_cost,
        name="input_grad",
    )
    returned = swapped(sent_back, "grp", 1)
    next_field, next_mark = call(
        bound(next_kernel, cols=cols),
        [shape(x.shape, BF16), MARK],
        [stay, give, near, far_hidden, upad, atmos_flat, ocean_flat],
        None,
        [pltpu.VMEM((cells, channels), F32)],
        **conv_cost,
        name="next",
    )

    field_grad, last_mark = call(
        bound(last_kernel, cols=cols),
        [shape(x.shape, BF16), MARK],
        [grad, returned, wet, terms],
        name="last",
    )
    if chunked:
        sums = scatter_sum(kept, parts, [next_mark, last_mark])
        atmos_chunk, ocean_chunk = call(
            bound(finish_kernel, atmos_factor=atmos_factor, ocean_factor=ocean_factor),
            [
                shape((atmos_rows * channels // 128, 128), F32),
                shape((ocean_rows * narrow // 128, 128), F32),
            ],
            sums,
            name="finish",
        )
        atmos_total, ocean_total = atmos_chunk.reshape(-1), ocean_chunk.reshape(-1)
    else:
        atmos_all = jnp.where(is_ocean, atmos_other, atmos_sum)
        ocean_all = jnp.where(is_ocean, ocean_sum, ocean_other)
        atmos_total = atmos_factor * lax.psum_scatter(
            atmos_all.reshape(-1), "lat", scatter_dimension=0, tiled=True
        )
        ocean_all = jnp.concatenate([ocean_all[piece] for piece in range(wide // 128)], axis=1)
        ocean_total = ocean_factor * lax.psum_scatter(
            ocean_all[:, :narrow].reshape(-1), "lat", scatter_dimension=0, tiled=True
        )
    return (next_field[None], field_grad[None], ocean_total, atmos_total)


def solution(mesh):
    in_specs = (
        P("grp", "lat", None, None),
        P("grp", "lat", None, None),
        P(),
        P(),
        P(),
        P(),
        P(),
        P(),
        P("lat"),
        P("lat", None),
    )
    out_specs = (
        P("grp", "lat", None, None),
        P("grp", "lat", None, None),
        P(("grp", "lat")),
        P(("grp", "lat")),
    )
    return jax.shard_map(local, mesh=mesh, in_specs=in_specs, out_specs=out_specs, check_vma=False)
```

```python
import functools
import math

import jax
import jax.numpy as jnp
from jax import lax
from jax.experimental import pallas as pl
from jax.experimental.pallas import tpu as pltpu
from jax.sharding import PartitionSpec as P

HIGHEST = lax.Precision.HIGHEST
GELU_SCALE = 0.7978845608028654
GELU_CUBIC = 0.044715
F32 = jnp.float32
BF16 = jnp.bfloat16
WHOLE = pl.BlockSpec(memory_space=pltpu.VMEM)
IN_PLACE = pl.BlockSpec(memory_space=pltpu.HBM)
ANYWHERE = pl.BlockSpec(memory_space=pl.ANY)
VMEM_LIMIT = 20 * 1024 * 1024
PACE = 8
PACK_VMEM = 62 * 1024 * 1024
HOLD_VMEM = 42 * 1024 * 1024

NN = (((1,), (0,)), ((), ()))
NT = (((1,), (1,)), ((), ()))
TN = (((0,), (0,)), ((), ()))


def shape(dims, kind):
    return jax.ShapeDtypeStruct(dims, kind)


def call(kernel, outs, inputs, in_specs=None, scratch=(), flops=0, moved=0, name=None, limit=VMEM_LIMIT, out_spec=WHOLE):
    return pl.pallas_call(
        kernel,
        out_shape=outs,
        in_specs=in_specs or [WHOLE] * len(inputs),
        out_specs=jax.tree.map(lambda _: out_spec, outs),
        scratch_shapes=list(scratch),
        compiler_params=pltpu.CompilerParams(vmem_limit_bytes=limit),
        cost_estimate=pl.CostEstimate(flops=flops, bytes_accessed=moved, transcendentals=0),
        name=name,
    )(*inputs)


def on_ocean():
    return lax.axis_index("grp") == 0


def dot(left, right, dims=NN, precision=None):
    return lax.dot_general(left, right, dims, precision=precision, preferred_element_type=F32)


def moved_cells(values, axis, cols):
    count = values.shape[axis]
    place = lax.rem(lax.broadcasted_iota(jnp.int32, values.shape, axis), cols)
    before = jnp.where(place == 0, 0.0, pltpu.roll(values, 1, axis))
    after = jnp.where(place == cols - 1, 0.0, pltpu.roll(values, count - 1, axis))
    return before, after


def wet_halves(wet, cols, channels):
    source = lax.broadcasted_iota(jnp.int32, (2 * cols, 2 * cols), 0)
    target = lax.broadcasted_iota(jnp.int32, (2 * cols, 2 * cols), 1)
    wanted = 2 * lax.rem(target, cols) + jnp.where(target >= cols, 1, 0)
    chooser = (source == wanted).astype(F32).astype(BF16)
    padded = jnp.concatenate([wet.astype(F32), jnp.zeros((14, 2 * cols), F32)], axis=0)
    apart = dot(padded.astype(BF16), chooser)
    return jnp.concatenate([apart, jnp.zeros((16, channels - 2 * cols), F32)], axis=1)


def own_bit(bit):
    return lax.rem(lax.shift_right_logical(lax.axis_index("lat"), bit), 2)


def pack_kernel(
    x_any, g_any, wet_any, near_ref, far_ref, early_ref, own_ref, x_ref, g_ref, wet_ref, sems, *, cols
):
    pairs = ((wet_any, wet_ref), (x_any, x_ref), (g_any, g_ref))
    copies = [pltpu.make_async_copy(*pair, sems.at[index]) for index, pair in enumerate(pairs)]
    for copy in copies:
        copy.start()
    core = own_bit(0)
    copies[0].wait()
    wide = wet_halves(wet_ref[...], cols, x_ref.shape[2])
    other = pltpu.roll(wide, 15, 0)
    own_ref[4 * cols :, :] = wide.astype(BF16)
    far_ref[2 * cols :, :] = jnp.where(core == 0, wide, other).astype(BF16)
    near_ref[2 * cols :, :] = jnp.where(core == 0, other, wide).astype(BF16)
    copies[1].wait()
    copies[2].wait()
    for part, ref in enumerate((x_ref, g_ref)):
        far_ref[part * cols : (part + 1) * cols, :] = ref[core]
        near_ref[part * cols : (part + 1) * cols, :] = ref[1 - core]
        own_ref[2 * part * cols : (2 * part + 1) * cols, :] = ref[0]
        own_ref[(2 * part + 1) * cols : (2 * part + 2) * cols, :] = ref[1]
    for row in range(2):
        early_ref[row * cols : (row + 1) * cols, :] = jnp.where(on_ocean(), g_ref[row], x_ref[row])


def hold_kernel(own_in, atmos_any, ocean_any, own_ref, atmos_ref, ocean_ref, sem):
    narrow = ocean_ref.shape[2]
    ocean_copy = pltpu.make_async_copy(ocean_any, ocean_ref.at[:, pl.ds(0, narrow), :], sem)
    atmos_copy = pltpu.make_async_copy(atmos_any, atmos_ref, sem)

    @pl.when(on_ocean())
    def _():
        ocean_copy.start()
        gap = ocean_ref.shape[1] - narrow
        if gap:
            ocean_ref[:, narrow:, :] = jnp.zeros((ocean_ref.shape[0], gap, narrow), BF16)

    @pl.when(jnp.logical_not(on_ocean()))
    def _():
        atmos_copy.start()

    own_ref[...] = own_in[...]

    @pl.when(on_ocean())
    def _():
        ocean_copy.wait()

    @pl.when(jnp.logical_not(on_ocean()))
    def _():
        atmos_copy.wait()


def low_and_high(near, far):
    core = own_bit(0)
    return jnp.where(core == 0, far, near), jnp.where(core == 0, near, far)


def outgoing_kernel(
    own_ref, near_ref, far_ref, terms_ref, xpad_ref, gpad_ref, wet_ref, edge_ref, sent_ref, *, cols
):
    low, high = low_and_high(near_ref[...], far_ref[...])
    for part, pad_ref in enumerate((xpad_ref, gpad_ref)):
        pad_ref[0:cols, :] = low[part * cols : (part + 1) * cols]
        pad_ref[cols : 3 * cols, :] = own_ref[2 * part * cols : 2 * (part + 1) * cols, :]
        pad_ref[3 * cols : 4 * cols, :] = high[part * cols : (part + 1) * cols]
    low_wet = low[2 * cols :].astype(F32)
    high_wet = high[2 * cols :].astype(F32)
    own_wet = own_ref[4 * cols :, :].astype(F32)
    halves = []
    for start in (0, cols):
        lanes = slice(start, start + cols)
        rows = (low_wet[0:1, lanes], own_wet[0:1, lanes], own_wet[1:2, lanes], high_wet[0:1, lanes])
        halves.append(jnp.concatenate(rows, axis=1))
    first_wet, second_wet = halves
    inverse = 1.0 / jnp.maximum(first_wet + second_wet, 1.0)
    wet_ref[0:1, :] = first_wet
    wet_ref[1:2, :] = second_wet
    wet_ref[2:3, :] = inverse
    wet_ref[3:8, :] = jnp.zeros((5, 4 * cols), F32)
    xpad = xpad_ref[...]
    projected = dot(terms_ref[0:8, :].astype(BF16), xpad, NT)
    mixed = (projected[0:4] * first_wet + projected[4:8] * second_wet) * inverse
    sent_ref[...] = jnp.where(on_ocean(), mixed, projected[0:4])
    edge_ref[0:cols, :] = jnp.where(on_ocean(), gpad_ref[0:cols, :], xpad_ref[0:cols, :])
    edge_ref[cols:, :] = jnp.where(on_ocean(), gpad_ref[3 * cols :, :], xpad_ref[3 * cols :, :])


def halves_apart(values, narrow):
    wide = -(-narrow // 128) * 128
    lane = lax.broadcasted_iota(jnp.int32, values.shape, 1)
    even = jnp.where(lane < narrow, values, 0.0)
    odd = jnp.where(lane < narrow, pltpu.roll(values, narrow, 1), 0.0)
    return even[:, :wide], odd[:, :wide]


def halves_with_columns(pad, cols):
    even, odd = halves_apart(pad.astype(F32), pad.shape[1] // 2)
    odd_before = moved_cells(odd, 0, cols)[0].astype(BF16)
    even_after = moved_cells(even, 0, cols)[1].astype(BF16)
    even, odd = even.astype(BF16), odd.astype(BF16)
    return (odd_before, even, odd), (even, odd, even_after)


def with_columns(pad, cols):
    before, after = moved_cells(pad.astype(F32), 0, cols)
    return before.astype(BF16), pad, after.astype(BF16)


def convolve(pad, out_ref, atmos_ref, ocean_ref, layer, flipped, cols):
    base = 9 * layer
    channels = atmos_ref.shape[2]
    wide, narrow = ocean_ref.shape[1:]
    rows = out_ref.shape[0]

    def summed(pick):
        total = None
        for row_tap in range(3):
            part = pick(row_tap, slice(cols * row_tap, cols * row_tap + rows))
            total = part if total is None else total + part
        return total

    @pl.when(on_ocean())
    def _():
        evens, odds = halves_with_columns(pad, cols)
        if flipped:

            def pick(row_tap, span):
                part = None
                for col_tap in range(3):
                    left = jnp.concatenate([evens[col_tap][span], odds[col_tap][span]], axis=0)
                    kernel = ocean_ref[base + 8 - (3 * row_tap + col_tap), 0:narrow, :]
                    piece = dot(left[:, :narrow], kernel, NT)
                    part = piece if part is None else part + piece
                return part

        else:
            even, odd = jnp.concatenate(evens, axis=1), jnp.concatenate(odds, axis=1)

            def pick(row_tap, span):
                first = base + 3 * row_tap
                kernel = ocean_ref[first : first + 3].reshape(3 * wide, narrow)
                return dot(jnp.concatenate([even[span], odd[span]], axis=0), kernel)

        total = summed(pick)
        out_ref[...] = jnp.concatenate([total[:rows], total[rows:]], axis=1)

    @pl.when(jnp.logical_not(on_ocean()))
    def _():
        taps = with_columns(pad, cols)
        if flipped:

            def pick(row_tap, span):
                part = None
                for col_tap in range(3):
                    piece = dot(taps[col_tap][span], atmos_ref[base + 8 - (3 * row_tap + col_tap)], NT)
                    part = piece if part is None else part + piece
                return part

        else:
            joined = jnp.concatenate(taps, axis=1)

            def pick(row_tap, span):
                first = base + 3 * row_tap
                return dot(joined[span], atmos_ref[first : first + 3].reshape(3 * channels, channels))

        out_ref[...] = summed(pick)


def back_kernel(gpad_ref, atmos_ref, ocean_ref, out_ref, *, cols):
    convolve(gpad_ref[...], out_ref, atmos_ref, ocean_ref, 1, True, cols)


def spread(arrived, wet, mixing, terms):
    first_wet, second_wet = wet
    both = jnp.concatenate([arrived * first_wet, arrived * second_wet], axis=0)
    alone = jnp.concatenate([arrived, jnp.zeros_like(arrived)], axis=0)
    return dot(jnp.where(mixing, both, alone), terms, TN, HIGHEST)


def first_kernel(
    xpad_ref, wet_ref, arrived_ref, terms_ref, back_ref, atmos_ref, ocean_ref,
    u_ref, stay_ref, give_ref, first_ref, *, cols,
):
    wet = wet_ref[0:1, :], wet_ref[1:2, :]
    coupled = spread(arrived_ref[...], wet, on_ocean(), terms_ref[8:16, :])
    u = (xpad_ref[...].astype(F32) + coupled).astype(BF16)
    u_ref[...] = u
    convolve(u, first_ref, atmos_ref, ocean_ref, 0, False, cols)
    first = first_ref[...]
    tangent = jnp.tanh(GELU_SCALE * (first + GELU_CUBIC * first * first * first))
    hidden = (0.5 * first * (1.0 + tangent)).astype(BF16)
    slope = 0.5 * (1.0 + tangent) + 0.5 * first * (1.0 - tangent * tangent) * GELU_SCALE * (
        1.0 + 3.0 * GELU_CUBIC * first * first
    )
    first_grad = (back_ref[...] * slope).astype(BF16)
    stay_ref[...] = jnp.where(on_ocean(), first_grad, hidden)
    give_ref[...] = jnp.where(on_ocean(), hidden, first_grad)


def whole_pad(early_ref, edge_ref, cols):
    parts = [edge_ref[0:cols, :], early_ref[...], edge_ref[cols:, :]]
    return jnp.concatenate(parts, axis=0).astype(F32)


def grad_atmos(pad, own, cols, store):
    rows = own.shape[0]
    left = own.T.astype(BF16)
    before, after = moved_cells(pad, 0, cols)
    rights = [part.astype(BF16) for part in (after, pad, before)]
    for tap in range(9):
        start = cols * (2 - tap // 3)
        store(tap, dot(left, rights[tap % 3][start : start + rows]))


def grad_ocean(pad, own, pad_is_input, cols, store):
    rows, channels = own.shape
    narrow = channels // 2

    if pad_is_input:
        middle = pad.T
        before, after = moved_cells(middle, 1, cols)
        even, odd = middle[:narrow].astype(BF16), middle[narrow:].astype(BF16)
        pairs = (
            (before[narrow:].astype(BF16), even),
            (even, odd),
            (odd, after[:narrow].astype(BF16)),
        )
        right = jnp.concatenate(halves_apart(own, narrow), axis=0).astype(BF16)
        for tap in range(9):
            start = cols * (tap // 3)
            pieces = [part[:, start : start + rows] for part in pairs[tap % 3]]
            store(tap, dot(jnp.concatenate(pieces, axis=1), right))
    else:
        turned = own.T.astype(BF16)
        left = jnp.concatenate([turned[:narrow], turned[narrow:]], axis=1)
        even, odd = halves_apart(pad, narrow)
        odd_before = moved_cells(odd, 0, cols)[0].astype(BF16)
        even_after = moved_cells(even, 0, cols)[1].astype(BF16)
        even, odd = even.astype(BF16), odd.astype(BF16)
        pairs = ((odd, even_after), (even, odd), (odd_before, even))
        for tap in range(9):
            start = cols * (2 - tap // 3)
            pieces = [part[start : start + rows] for part in pairs[tap % 3]]
            store(tap, dot(left, jnp.concatenate(pieces, axis=0)))


def store_into(out_ref):
    def store(tap, value):
        if len(out_ref.shape) == 2:
            rows = value.shape[0]
            out_ref[rows * tap : rows * (tap + 1), :] = value
        else:
            rows = value.shape[0]
            for piece in range(out_ref.shape[0]):
                lanes = slice(128 * piece, 128 * (piece + 1))
                out_ref[piece, rows * tap : rows * (tap + 1), :] = value[:, lanes]

    return store


def near_rows(near_ref, part, cols):
    if len(near_ref.shape) == 2:
        return near_ref[part * cols : (part + 1) * cols, :]
    count, tall = near_ref.shape[0] // 2, near_ref.shape[1]
    taken = cols // count
    pieces = [near_ref[index, tall - taken :, :] for index in range(part * count, (part + 1) * count)]
    return jnp.concatenate(pieces, axis=0)


def hidden_and_grad(stay_ref, give_ref):
    stay, give = stay_ref[...], give_ref[...]
    return jnp.where(on_ocean(), give, stay), jnp.where(on_ocean(), stay, give)


def shifted_inputs(pad, cols):
    middle = pad.T
    before, after = moved_cells(middle, 1, cols)
    return [part.astype(BF16) for part in (before, middle, after)]


def own_grads_kernel(
    upad_ref, gpad_ref, stay_ref, give_ref, atmos_out, ocean_out, near_ref, far_hidden, far_grad, *, cols
):
    stay = stay_ref[...].astype(F32)
    hidden, first_grad = hidden_and_grad(stay_ref, give_ref)
    core = own_bit(0)
    for part, values in enumerate((hidden, first_grad)):
        target = slice(part * cols, (part + 1) * cols)
        (far_hidden, far_grad)[part][...] = jnp.where(core == 0, values[:cols], values[cols:])
        near_ref[target, :] = jnp.where(core == 0, values[cols:], values[:cols])

    @pl.when(on_ocean())
    def _():
        grad_ocean(upad_ref[...].astype(F32), stay, True, cols, store_into(ocean_out))

    @pl.when(jnp.logical_not(on_ocean()))
    def _():
        grad_atmos(gpad_ref[...].astype(F32), stay, cols, store_into(atmos_out))


def shift_kernel(early_ref, edge_ref, sent_ref, coupling_ref, left_ref, *, cols):
    @pl.when(on_ocean())
    def _():
        added = dot(sent_ref[...], coupling_ref[...].astype(F32), TN, HIGHEST)
        other = (whole_pad(early_ref, edge_ref, cols) + added).astype(BF16).astype(F32)
        for tap, left in enumerate(shifted_inputs(other, cols)):
            left_ref[tap] = left


def other_grads_kernel(left_ref, late_ref, early_ref, edge_ref, atmos_out, ocean_out, *, cols):
    rows = late_ref.shape[0]

    @pl.when(on_ocean())
    def _():
        store = store_into(atmos_out)
        for tap in range(9):
            start = cols * (tap // 3)
            store(tap, dot(left_ref[tap % 3, :, start : start + rows], late_ref[...]))

    @pl.when(jnp.logical_not(on_ocean()))
    def _():
        late = late_ref[...].astype(F32)
        grad_ocean(whole_pad(early_ref, edge_ref, cols), late, False, cols, store_into(ocean_out))


def chunk_rows(out_ref, side, tall, atmos_all, ocean_all, chunks):
    channels = out_ref.shape[2]
    pieces = ocean_all.shape[0]
    atmos_rows = atmos_all.shape[0] // chunks
    ocean_rows = atmos_rows // 2
    taken = tall - atmos_rows
    blank = jnp.zeros((taken, channels - 128 * pieces), F32)
    for pair in range(chunks // 2):
        start = pl.multiple_of(atmos_rows * (2 * pair + side), 8)
        upper = atmos_all[pl.ds(start, atmos_rows), :]
        start = ocean_rows * (2 * pair + side)
        halves = []
        for odd in range(2):
            parts = [ocean_all.at[piece][pl.ds(start + odd, taken, 2), :] for piece in range(pieces)]
            halves.append(jnp.concatenate(parts + [blank], axis=1))
        lower = halves[0] + pltpu.roll(halves[1], channels // 2, 1)
        out_ref[pair, 0:tall, :] = jnp.concatenate([upper, lower], axis=0).astype(BF16)


def chunk_kernel(atmos_own, ocean_own, atmos_other, ocean_other, *refs, chunks, tall, sent):
    out_ref = refs[-1]
    core = own_bit(0)
    side = 1 - core if sent else core
    if sent:
        near_ref = refs[0]
        taken = out_ref.shape[1] - tall
        for pair in range(chunks // 2):
            out_ref[pair, tall:, :] = near_ref[pair * taken : (pair + 1) * taken, :]

    @pl.when(on_ocean())
    def _():
        chunk_rows(out_ref, side, tall, atmos_other, ocean_own, chunks)

    @pl.when(jnp.logical_not(on_ocean()))
    def _():
        chunk_rows(out_ref, side, tall, atmos_own, ocean_other, chunks)


def halve(keep_ref, came_ref, out_ref, side, rows):
    for outer in range(keep_ref.shape[0]):
        for inner in range(keep_ref.shape[2]):
            total = keep_ref[outer, side, inner, rows, :].astype(F32)
            total = total + came_ref[outer, side, inner, rows, :].astype(F32)
            out_ref[outer, inner] = total.astype(BF16)


def split_kernel(keep_ref, came_ref, *refs, cuts, sent):
    by_z = [ref.reshape(2, 2, 2, *ref.shape[3:]) for ref in (keep_ref, came_ref)]
    start = 0
    for index, rows in enumerate(cuts):
        pair, bit = (by_z, 2) if index == 1 else ((keep_ref, came_ref), 1)
        own = own_bit(bit)
        halve(*pair, refs[index], 1 - own if sent else own, slice(start, start + rows))
        start += rows
    if sent:
        refs[-1][...] = jnp.zeros_like(refs[-1])


def halve_kernel(keep_ref, came_ref, *refs, bit, marked):
    outs = refs[-3:] if marked else refs[-2:]
    own = own_bit(bit)
    halve(keep_ref, came_ref, outs[1], 1 - own, slice(None))
    halve(keep_ref, came_ref, outs[0], own, slice(None))
    if marked:
        outs[2][...] = jnp.zeros_like(outs[2])


MARK = shape((8, 128), F32)


def halved(keep, came, bit, dims, after, marked=True):
    outer, inner, rows, channels = dims[0], dims[1], keep.shape[-2], keep.shape[-1]
    keep, came = (part.reshape(outer, 2, inner, rows, channels) for part in (keep, came))
    out = shape((outer, inner, rows, channels), BF16)
    return call(
        functools.partial(halve_kernel, bit=bit, marked=marked),
        [out, out] + [MARK] * marked,
        [keep, came, *after],
        [WHOLE] * 2 + [ANYWHERE] * len(after),
        moved=8 * outer * inner * rows * channels,
        name="halve",
    )


def split(keep, came):
    pairs, tall, channels = keep.shape
    cuts = [16 * (tall // 16 * part // 17) for part in (6, 6)]
    cuts.append(tall - sum(cuts))
    outs = [
        shape(((2, 2) if index == 1 else (4, 1)) + (rows, channels), BF16) for index, rows in enumerate(cuts)
    ]
    inputs = [part.reshape(4, 2, 1, *part.shape[1:]) for part in (keep, came)]
    kept, sent = (
        call(
            functools.partial(split_kernel, cuts=cuts, sent=is_sent),
            outs + [MARK] * is_sent,
            inputs,
            moved=3 * pairs * tall * channels,
            name="split",
        )
        for is_sent in (False, True)
    )
    return kept, sent[:3], sent[3]


def scatter_sum(kept, sent, before_a):
    (a_keep, b_keep, c_keep), (a_send, b_send, c_send) = kept, sent
    channels = a_keep.shape[-1]
    a_came = swapped(a_send, "lat", 2)
    b_came = swapped(b_send, "lat", 4)
    c_came = swapped(c_send, "lat", 2)
    a_keep, a_send, mark = halved(a_keep, a_came, 2, (2, 1), before_a)
    a_came = swapped(a_send, "lat", 4)
    b_keep, b_send, mark = halved(b_keep, b_came, 3, (1, 2), [mark])
    b_came = swapped(b_send, "lat", 8)
    c_keep, c_send, mark = halved(c_keep, c_came, 2, (2, 1), [mark])
    c_came = swapped(c_send, "lat", 4)
    a_keep, a_send, mark = halved(a_keep, a_came, 3, (1, 1), [mark])
    a_came = swapped(a_send, "lat", 8)
    b_keep, b_send, mark = halved(b_keep, b_came, 1, (1, 1), [mark])
    b_came = swapped(b_send, "lat", 2)
    c_keep, c_send = halved(c_keep, c_came, 3, (1, 1), [mark], False)
    c_came = swapped(c_send, "lat", 8)
    return [part.reshape(-1, channels) for part in (a_keep, a_came, b_keep, b_came, c_keep, c_came)]


def finish_kernel(*refs, atmos_factor, ocean_factor):
    parts, (atmos_ref, ocean_ref) = refs[:-2], refs[-2:]
    channels = parts[0].shape[1]
    pieces = channels // 128
    atmos_rows = atmos_ref.shape[0] // pieces
    ocean_rows = ocean_ref.shape[0] // pieces
    sums = [
        parts[index][...].astype(F32) + parts[index + 1][...].astype(F32)
        for index in range(0, len(parts), 2)
    ]
    total = jnp.concatenate(sums, axis=0)
    for piece in range(pieces):
        lanes = slice(128 * piece, 128 * (piece + 1))
        atmos_ref[pl.ds(piece, atmos_rows, pieces), :] = total[:atmos_rows, lanes] * atmos_factor
        ocean_ref[pl.ds(piece, ocean_rows, pieces), :] = (
            total[atmos_rows : atmos_rows + ocean_rows, lanes] * ocean_factor
        )


def input_grad_kernel(
    stay_ref, give_ref, near_ref, far_ref, gpad_ref, wet_ref, terms_ref, atmos_ref, ocean_ref, *refs, cols
):
    grad_ref, sent_ref = refs[-2:]
    middle = hidden_and_grad(stay_ref, give_ref)[1]
    low, high = low_and_high(near_rows(near_ref, 1, cols), far_ref[...])
    pad = jnp.concatenate([low, middle, high], axis=0)
    own = slice(cols, 3 * cols)
    convolve(pad, grad_ref, atmos_ref, ocean_ref, 0, True, cols)
    grad = gpad_ref[own, :].astype(F32) + grad_ref[...]
    grad_ref[...] = grad
    weighted = dot(terms_ref[8:16, :], grad, NT, HIGHEST)
    mixed = weighted[0:4] * wet_ref[0:1, own] + weighted[4:8] * wet_ref[1:2, own]
    sent_ref[...] = jnp.where(on_ocean(), mixed, weighted[0:4])


def next_kernel(
    stay_ref, give_ref, near_ref, far_ref, upad_ref, atmos_ref, ocean_ref,
    next_ref, mark_ref, second_ref, *, cols,
):
    middle = hidden_and_grad(stay_ref, give_ref)[0]
    low, high = low_and_high(near_rows(near_ref, 0, cols), far_ref[...])
    pad = jnp.concatenate([low, middle, high], axis=0)
    own = slice(cols, 3 * cols)
    convolve(pad, second_ref, atmos_ref, ocean_ref, 1, False, cols)
    values = (upad_ref[own, :].astype(F32) + second_ref[...]).astype(BF16)
    next_ref[0] = values[:cols]
    next_ref[1] = values[cols:]
    mark_ref[...] = jnp.zeros_like(mark_ref)


def last_kernel(grad_ref, arrived_ref, wet_ref, terms_ref, *refs, cols):
    out_ref, mark_ref = refs[-2:]
    own = slice(cols, 3 * cols)
    wet = wet_ref[0:1, own], wet_ref[1:2, own]
    arrived = jnp.where(on_ocean(), arrived_ref[...] * wet_ref[2:3, own], arrived_ref[...])
    added = spread(arrived, wet, on_ocean(), terms_ref[0:8, :])
    values = (grad_ref[...] + added).astype(BF16)
    out_ref[0] = values[:cols]
    out_ref[1] = values[cols:]
    mark_ref[...] = jnp.zeros_like(mark_ref)


def swapped(value, axis, mask):
    pairs = [(source, source ^ mask) for source in range(lax.axis_size(axis))]
    return lax.ppermute(value, axis, pairs)


def far_halo(far):
    pairs = [(i, i + 1 if i % 2 else i - 1) for i in range(1, lax.axis_size("lat") - 1)]
    return lax.ppermute(far, "lat", pairs)


def local(
    fields,
    cotangent,
    ocean_kernels,
    atmos_kernels,
    ocean_surface,
    ocean_coupling,
    atmos_flux,
    atmos_coupling,
    row_map,
    wet_mask,
):
    x, g = fields[0], cotangent[0]
    bands, cols, channels = x.shape
    narrow = channels // 2
    cells = bands * cols
    count = lax.axis_size("lat")
    is_ocean = lax.axis_index("grp") == 0
    atmos_factor = 1.0 / math.sqrt(bands * count * cols)
    ocean_factor = 1.0 / math.sqrt(bands * count * 2 * cols)
    bound = functools.partial

    blank = jnp.zeros((4, narrow), BF16)
    gap = jnp.zeros((4, channels), BF16)
    surface = ocean_surface.T
    ocean_terms = jnp.concatenate(
        [
            jnp.concatenate([surface, blank], axis=1),
            jnp.concatenate([blank, surface], axis=1),
            jnp.concatenate([ocean_coupling, blank], axis=1),
            jnp.concatenate([blank, ocean_coupling], axis=1),
        ],
        axis=0,
    )
    atmos_terms = jnp.concatenate([atmos_flux.T, gap, atmos_coupling, gap], axis=0)
    terms = jnp.where(is_ocean, ocean_terms, atmos_terms).astype(F32)

    edge = shape((2 * cols + 16, channels), BF16)
    half = shape((cells, channels), BF16)
    near, far, own_early, own = call(
        bound(pack_kernel, cols=cols),
        [edge, edge, half, shape((2 * cells + 16, channels), BF16)],
        [x, g, wet_mask],
        [IN_PLACE] * 3,
        [
            pltpu.VMEM(x.shape, BF16),
            pltpu.VMEM(x.shape, BF16),
            pltpu.VMEM(wet_mask.shape, jnp.int32),
            pltpu.SemaphoreType.DMA((3,)),
        ],
        name="pack",
        limit=PACK_VMEM,
    )
    near, far = swapped(near, "lat", 1), far_halo(far)
    other_early = swapped(own_early, "grp", 1)
    wide = -(-narrow // 128) * 128
    own, atmos_flat, ocean_flat = call(
        hold_kernel,
        [
            shape(own.shape, BF16),
            shape((18, channels, channels), BF16),
            shape((18, wide, narrow), BF16),
        ],
        [own, atmos_kernels.reshape(18, channels, channels), ocean_kernels.reshape(18, narrow, narrow)],
        [WHOLE, IN_PLACE, IN_PLACE],
        [pltpu.SemaphoreType.DMA],
        flops=PACE * 10**8,
        name="hold",
        limit=HOLD_VMEM,
    )
    pad = shape((2 * cells, channels), BF16)
    xpad, gpad, wet, edges, sent = call(
        bound(outgoing_kernel, cols=cols),
        [pad, pad, shape((8, 2 * cells), F32), half, shape((4, 2 * cells), F32)],
        [own, near, far, terms],
        name="outgoing",
    )
    arrived = swapped(sent, "grp", 1)
    other_edges = swapped(edges, "grp", 1)
    conv_cost = dict(flops=PACE * 9 * cells * channels * channels, moved=9 * channels * channels * 2)
    back = call(
        bound(back_kernel, cols=cols),
        shape((cells, channels), F32),
        [gpad, atmos_flat, ocean_flat],
        **conv_cost,
        name="back",
    )
    upad, stay, give = call(
        bound(first_kernel, cols=cols),
        [pad, half, half],
        [xpad, wet, arrived, terms, back, atmos_flat, ocean_flat],
        None,
        [pltpu.VMEM((cells, channels), F32)],
        **conv_cost,
        name="first",
    )
    late = swapped(give, "grp", 1)

    atmos_rows = 9 * channels // count
    ocean_rows = 9 * narrow // count
    chunked = count == 16 and 9 * channels % (8 * count) == 0 and ocean_rows % 2 == 0
    tall = -(-(atmos_rows + ocean_rows // 2) // 16) * 16
    spare = max(0, 2 * (tall - atmos_rows) - ocean_rows) if chunked else 0
    ocean_tall = 9 * narrow + -(-spare // 8) * 8
    sums = [shape((9 * channels, channels), F32), shape((wide // 128, ocean_tall, 128), F32)]
    row = shape((cols, channels), BF16)
    atmos_sum, ocean_sum, near, far_hidden, far_grad = call(
        bound(own_grads_kernel, cols=cols),
        [*sums, half, row, row],
        [upad, gpad, stay, give],
        **conv_cost,
        name="own_grads",
    )
    far_hidden, far_grad = far_halo(far_hidden), far_halo(far_grad)
    lefts = call(
        bound(shift_kernel, cols=cols),
        shape((3, channels, 2 * cells), BF16),
        [other_early, other_edges, sent, atmos_coupling],
        name="shift",
    )
    atmos_other, ocean_other = call(
        bound(other_grads_kernel, cols=cols),
        sums,
        [lefts, late, other_early, other_edges],
        **conv_cost,
        name="other_grads",
    )
    if chunked:
        taken = 2 * cols // (count // 2)
        sums = [atmos_sum, ocean_sum, atmos_other, ocean_other]
        send, keep = (
            call(
                bound(chunk_kernel, chunks=count, tall=tall, sent=sent),
                shape((count // 2, tall + taken * sent, channels), BF16),
                sums + [near, far_grad] * sent,
                [WHOLE] * (4 + sent) + [ANYWHERE] * sent,
                moved=2 * count * tall * channels,
                name="chunk",
            )
            for sent in (True, False)
        )
        near = swapped(send, "lat", 1)
        kept, parts, split_mark = split(keep, near)
        after_split = [split_mark]
    else:
        near = swapped(near, "lat", 1)
        after_split = []

    grad, sent_back = call(
        bound(input_grad_kernel, cols=cols),
        [shape((cells, channels), F32), shape((4, cells), F32)],
        [stay, give, near, far_grad, gpad, wet, terms, atmos_flat, ocean_flat, *after_split],
        [WHOLE] * 9 + [ANYWHERE] * len(after_split),
        **conv_cost,
        name="input_grad",
    )
    returned = swapped(sent_back, "grp", 1)
    next_field, next_mark = call(
        bound(next_kernel, cols=cols),
        [shape(x.shape, BF16), MARK],
        [stay, give, near, far_hidden, upad, atmos_flat, ocean_flat],
        None,
        [pltpu.VMEM((cells, channels), F32)],
        **conv_cost,
        name="next",
    )

    field_grad, last_mark = call(
        bound(last_kernel, cols=cols),
        [shape(x.shape, BF16), MARK],
        [grad, returned, wet, terms],
        name="last",
    )
    if chunked:
        sums = scatter_sum(kept, parts, [next_mark, last_mark])
        atmos_chunk, ocean_chunk = call(
            bound(finish_kernel, atmos_factor=atmos_factor, ocean_factor=ocean_factor),
            [
                shape((atmos_rows * channels // 128, 128), F32),
                shape((ocean_rows * narrow // 128, 128), F32),
            ],
            sums,
            name="finish",
        )
        atmos_total, ocean_total = atmos_chunk.reshape(-1), ocean_chunk.reshape(-1)
    else:
        atmos_all = jnp.where(is_ocean, atmos_other, atmos_sum)
        ocean_all = jnp.where(is_ocean, ocean_sum, ocean_other)
        atmos_total = atmos_factor * lax.psum_scatter(
            atmos_all.reshape(-1), "lat", scatter_dimension=0, tiled=True
        )
        ocean_all = jnp.concatenate([ocean_all[piece] for piece in range(wide // 128)], axis=1)
        ocean_total = ocean_factor * lax.psum_scatter(
            ocean_all[:, :narrow].reshape(-1), "lat", scatter_dimension=0, tiled=True
        )
    return (next_field[None], field_grad[None], ocean_total, atmos_total)


def solution(mesh):
    in_specs = (
        P("grp", "lat", None, None),
        P("grp", "lat", None, None),
        P(),
        P(),
        P(),
        P(),
        P(),
        P(),
        P("lat"),
        P("lat", None),
    )
    out_specs = (
        P("grp", "lat", None, None),
        P("grp", "lat", None, None),
        P(("grp", "lat")),
        P(("grp", "lat")),
    )
    return jax.shard_map(local, mesh=mesh, in_specs=in_specs, out_specs=out_specs, check_vma=False)
```

```python
import functools
import math

import jax
import jax.numpy as jnp
from jax import lax
from jax.experimental import pallas as pl
from jax.experimental.pallas import tpu as pltpu
from jax.sharding import PartitionSpec as P

HIGHEST = lax.Precision.HIGHEST
GELU_SCALE = 0.7978845608028654
GELU_CUBIC = 0.044715
F32 = jnp.float32
BF16 = jnp.bfloat16
WHOLE = pl.BlockSpec(memory_space=pltpu.VMEM)
IN_PLACE = pl.BlockSpec(memory_space=pltpu.HBM)
ANYWHERE = pl.BlockSpec(memory_space=pl.ANY)
VMEM_LIMIT = 20 * 1024 * 1024
PACE = 8
PACK_VMEM = 62 * 1024 * 1024
HOLD_VMEM = 42 * 1024 * 1024

NN = (((1,), (0,)), ((), ()))
NT = (((1,), (1,)), ((), ()))
TN = (((0,), (0,)), ((), ()))


def shape(dims, kind):
    return jax.ShapeDtypeStruct(dims, kind)


def call(kernel, outs, inputs, in_specs=None, scratch=(), flops=0, moved=0, name=None, limit=VMEM_LIMIT, out_spec=WHOLE):
    return pl.pallas_call(
        kernel,
        out_shape=outs,
        in_specs=in_specs or [WHOLE] * len(inputs),
        out_specs=jax.tree.map(lambda _: out_spec, outs),
        scratch_shapes=list(scratch),
        compiler_params=pltpu.CompilerParams(vmem_limit_bytes=limit),
        cost_estimate=pl.CostEstimate(flops=flops, bytes_accessed=moved, transcendentals=0),
        name=name,
    )(*inputs)


def on_ocean():
    return lax.axis_index("grp") == 0


def dot(left, right, dims=NN, precision=None):
    return lax.dot_general(left, right, dims, precision=precision, preferred_element_type=F32)


def moved_cells(values, axis, cols):
    count = values.shape[axis]
    place = lax.rem(lax.broadcasted_iota(jnp.int32, values.shape, axis), cols)
    before = jnp.where(place == 0, 0.0, pltpu.roll(values, 1, axis))
    after = jnp.where(place == cols - 1, 0.0, pltpu.roll(values, count - 1, axis))
    return before, after


def wet_halves(wet, cols, channels):
    source = lax.broadcasted_iota(jnp.int32, (2 * cols, 2 * cols), 0)
    target = lax.broadcasted_iota(jnp.int32, (2 * cols, 2 * cols), 1)
    wanted = 2 * lax.rem(target, cols) + jnp.where(target >= cols, 1, 0)
    chooser = (source == wanted).astype(F32).astype(BF16)
    padded = jnp.concatenate([wet.astype(F32), jnp.zeros((14, 2 * cols), F32)], axis=0)
    apart = dot(padded.astype(BF16), chooser)
    return jnp.concatenate([apart, jnp.zeros((16, channels - 2 * cols), F32)], axis=1)


def own_bit(bit):
    return lax.rem(lax.shift_right_logical(lax.axis_index("lat"), bit), 2)


def pack_kernel(
    x_any, g_any, wet_any, near_ref, far_ref, early_ref, own_ref, x_ref, g_ref, wet_ref, sems, *, cols
):
    pairs = ((wet_any, wet_ref), (x_any, x_ref), (g_any, g_ref))
    copies = [pltpu.make_async_copy(*pair, sems.at[index]) for index, pair in enumerate(pairs)]
    for copy in copies:
        copy.start()
    core = own_bit(0)
    copies[0].wait()
    wide = wet_halves(wet_ref[...], cols, x_ref.shape[2])
    other = pltpu.roll(wide, 15, 0)
    own_ref[4 * cols :, :] = wide.astype(BF16)
    far_ref[2 * cols :, :] = jnp.where(core == 0, wide, other).astype(BF16)
    near_ref[2 * cols :, :] = jnp.where(core == 0, other, wide).astype(BF16)
    copies[1].wait()
    copies[2].wait()
    for part, ref in enumerate((x_ref, g_ref)):
        far_ref[part * cols : (part + 1) * cols, :] = ref[core]
        near_ref[part * cols : (part + 1) * cols, :] = ref[1 - core]
        own_ref[2 * part * cols : (2 * part + 1) * cols, :] = ref[0]
        own_ref[(2 * part + 1) * cols : (2 * part + 2) * cols, :] = ref[1]
    for row in range(2):
        early_ref[row * cols : (row + 1) * cols, :] = jnp.where(on_ocean(), g_ref[row], x_ref[row])


def hold_kernel(own_in, atmos_any, ocean_any, own_ref, atmos_ref, ocean_ref, sem):
    narrow = ocean_ref.shape[2]
    ocean_copy = pltpu.make_async_copy(ocean_any, ocean_ref.at[:, pl.ds(0, narrow), :], sem)
    atmos_copy = pltpu.make_async_copy(atmos_any, atmos_ref, sem)

    @pl.when(on_ocean())
    def _():
        ocean_copy.start()
        gap = ocean_ref.shape[1] - narrow
        if gap:
            ocean_ref[:, narrow:, :] = jnp.zeros((ocean_ref.shape[0], gap, narrow), BF16)

    @pl.when(jnp.logical_not(on_ocean()))
    def _():
        atmos_copy.start()

    own_ref[...] = own_in[...]

    @pl.when(on_ocean())
    def _():
        ocean_copy.wait()

    @pl.when(jnp.logical_not(on_ocean()))
    def _():
        atmos_copy.wait()


def low_and_high(near, far):
    core = own_bit(0)
    return jnp.where(core == 0, far, near), jnp.where(core == 0, near, far)


def outgoing_kernel(
    own_ref, near_ref, far_ref, terms_ref, xpad_ref, gpad_ref, wet_ref, edge_ref, sent_ref, *, cols
):
    low, high = low_and_high(near_ref[...], far_ref[...])
    for part, pad_ref in enumerate((xpad_ref, gpad_ref)):
        pad_ref[0:cols, :] = low[part * cols : (part + 1) * cols]
        pad_ref[cols : 3 * cols, :] = own_ref[2 * part * cols : 2 * (part + 1) * cols, :]
        pad_ref[3 * cols : 4 * cols, :] = high[part * cols : (part + 1) * cols]
    low_wet = low[2 * cols :].astype(F32)
    high_wet = high[2 * cols :].astype(F32)
    own_wet = own_ref[4 * cols :, :].astype(F32)
    halves = []
    for start in (0, cols):
        lanes = slice(start, start + cols)
        rows = (low_wet[0:1, lanes], own_wet[0:1, lanes], own_wet[1:2, lanes], high_wet[0:1, lanes])
        halves.append(jnp.concatenate(rows, axis=1))
    first_wet, second_wet = halves
    inverse = 1.0 / jnp.maximum(first_wet + second_wet, 1.0)
    wet_ref[0:1, :] = first_wet
    wet_ref[1:2, :] = second_wet
    wet_ref[2:3, :] = inverse
    wet_ref[3:8, :] = jnp.zeros((5, 4 * cols), F32)
    xpad = xpad_ref[...]
    projected = dot(terms_ref[0:8, :].astype(BF16), xpad, NT)
    mixed = (projected[0:4] * first_wet + projected[4:8] * second_wet) * inverse
    sent_ref[...] = jnp.where(on_ocean(), mixed, projected[0:4])
    edge_ref[0:cols, :] = jnp.where(on_ocean(), gpad_ref[0:cols, :], xpad_ref[0:cols, :])
    edge_ref[cols:, :] = jnp.where(on_ocean(), gpad_ref[3 * cols :, :], xpad_ref[3 * cols :, :])


def halves_apart(values, narrow):
    wide = -(-narrow // 128) * 128
    lane = lax.broadcasted_iota(jnp.int32, values.shape, 1)
    even = jnp.where(lane < narrow, values, 0.0)
    odd = jnp.where(lane < narrow, pltpu.roll(values, narrow, 1), 0.0)
    return even[:, :wide], odd[:, :wide]


def halves_with_columns(pad, cols):
    even, odd = halves_apart(pad.astype(F32), pad.shape[1] // 2)
    odd_before = moved_cells(odd, 0, cols)[0].astype(BF16)
    even_after = moved_cells(even, 0, cols)[1].astype(BF16)
    even, odd = even.astype(BF16), odd.astype(BF16)
    return (odd_before, even, odd), (even, odd, even_after)


def with_columns(pad, cols):
    before, after = moved_cells(pad.astype(F32), 0, cols)
    return before.astype(BF16), pad, after.astype(BF16)


def convolve(pad, out_ref, atmos_ref, ocean_ref, layer, flipped, cols):
    base = 9 * layer
    channels = atmos_ref.shape[2]
    wide, narrow = ocean_ref.shape[1:]
    rows = out_ref.shape[0]

    def summed(pick):
        total = None
        for row_tap in range(3):
            part = pick(row_tap, slice(cols * row_tap, cols * row_tap + rows))
            total = part if total is None else total + part
        return total

    @pl.when(on_ocean())
    def _():
        evens, odds = halves_with_columns(pad, cols)
        if flipped:

            def pick(row_tap, span):
                part = None
                for col_tap in range(3):
                    left = jnp.concatenate([evens[col_tap][span], odds[col_tap][span]], axis=0)
                    kernel = ocean_ref[base + 8 - (3 * row_tap + col_tap), 0:narrow, :]
                    piece = dot(left[:, :narrow], kernel, NT)
                    part = piece if part is None else part + piece
                return part

        else:
            even, odd = jnp.concatenate(evens, axis=1), jnp.concatenate(odds, axis=1)

            def pick(row_tap, span):
                first = base + 3 * row_tap
                kernel = ocean_ref[first : first + 3].reshape(3 * wide, narrow)
                return dot(jnp.concatenate([even[span], odd[span]], axis=0), kernel)

        total = summed(pick)
        out_ref[...] = jnp.concatenate([total[:rows], total[rows:]], axis=1)

    @pl.when(jnp.logical_not(on_ocean()))
    def _():
        taps = with_columns(pad, cols)
        if flipped:

            def pick(row_tap, span):
                part = None
                for col_tap in range(3):
                    piece = dot(taps[col_tap][span], atmos_ref[base + 8 - (3 * row_tap + col_tap)], NT)
                    part = piece if part is None else part + piece
                return part

        else:
            joined = jnp.concatenate(taps, axis=1)

            def pick(row_tap, span):
                first = base + 3 * row_tap
                return dot(joined[span], atmos_ref[first : first + 3].reshape(3 * channels, channels))

        out_ref[...] = summed(pick)


def back_kernel(gpad_ref, atmos_ref, ocean_ref, out_ref, *, cols):
    convolve(gpad_ref[...], out_ref, atmos_ref, ocean_ref, 1, True, cols)


def spread(arrived, wet, mixing, terms):
    first_wet, second_wet = wet
    both = jnp.concatenate([arrived * first_wet, arrived * second_wet], axis=0)
    alone = jnp.concatenate([arrived, jnp.zeros_like(arrived)], axis=0)
    return dot(jnp.where(mixing, both, alone), terms, TN, HIGHEST)


def first_kernel(
    xpad_ref, wet_ref, arrived_ref, terms_ref, back_ref, atmos_ref, ocean_ref,
    u_ref, stay_ref, give_ref, first_ref, *, cols,
):
    wet = wet_ref[0:1, :], wet_ref[1:2, :]
    coupled = spread(arrived_ref[...], wet, on_ocean(), terms_ref[8:16, :])
    u = (xpad_ref[...].astype(F32) + coupled).astype(BF16)
    u_ref[...] = u
    convolve(u, first_ref, atmos_ref, ocean_ref, 0, False, cols)
    first = first_ref[...]
    tangent = jnp.tanh(GELU_SCALE * (first + GELU_CUBIC * first * first * first))
    hidden = (0.5 * first * (1.0 + tangent)).astype(BF16)
    slope = 0.5 * (1.0 + tangent) + 0.5 * first * (1.0 - tangent * tangent) * GELU_SCALE * (
        1.0 + 3.0 * GELU_CUBIC * first * first
    )
    first_grad = (back_ref[...] * slope).astype(BF16)
    stay_ref[...] = jnp.where(on_ocean(), first_grad, hidden)
    give_ref[...] = jnp.where(on_ocean(), hidden, first_grad)


def whole_pad(early_ref, edge_ref, cols):
    parts = [edge_ref[0:cols, :], early_ref[...], edge_ref[cols:, :]]
    return jnp.concatenate(parts, axis=0).astype(F32)


def grad_atmos(pad, own, cols, store):
    rows = own.shape[0]
    left = own.T.astype(BF16)
    before, after = moved_cells(pad, 0, cols)
    rights = [part.astype(BF16) for part in (after, pad, before)]
    for tap in range(9):
        start = cols * (2 - tap // 3)
        store(tap, dot(left, rights[tap % 3][start : start + rows]))


def grad_ocean(pad, own, pad_is_input, cols, store):
    rows, channels = own.shape
    narrow = channels // 2

    if pad_is_input:
        middle = pad.T
        before, after = moved_cells(middle, 1, cols)
        even, odd = middle[:narrow].astype(BF16), middle[narrow:].astype(BF16)
        pairs = (
            (before[narrow:].astype(BF16), even),
            (even, odd),
            (odd, after[:narrow].astype(BF16)),
        )
        right = jnp.concatenate(halves_apart(own, narrow), axis=0).astype(BF16)
        for tap in range(9):
            start = cols * (tap // 3)
            pieces = [part[:, start : start + rows] for part in pairs[tap % 3]]
            store(tap, dot(jnp.concatenate(pieces, axis=1), right))
    else:
        turned = own.T.astype(BF16)
        left = jnp.concatenate([turned[:narrow], turned[narrow:]], axis=1)
        even, odd = halves_apart(pad, narrow)
        odd_before = moved_cells(odd, 0, cols)[0].astype(BF16)
        even_after = moved_cells(even, 0, cols)[1].astype(BF16)
        even, odd = even.astype(BF16), odd.astype(BF16)
        pairs = ((odd, even_after), (even, odd), (odd_before, even))
        for tap in range(9):
            start = cols * (2 - tap // 3)
            pieces = [part[start : start + rows] for part in pairs[tap % 3]]
            store(tap, dot(left, jnp.concatenate(pieces, axis=0)))


def store_into(out_ref):
    def store(tap, value):
        if len(out_ref.shape) == 2:
            rows = value.shape[0]
            out_ref[rows * tap : rows * (tap + 1), :] = value
        else:
            rows = value.shape[0]
            for piece in range(out_ref.shape[0]):
                lanes = slice(128 * piece, 128 * (piece + 1))
                out_ref[piece, rows * tap : rows * (tap + 1), :] = value[:, lanes]

    return store


def near_rows(near_ref, part, cols):
    if len(near_ref.shape) == 2:
        return near_ref[part * cols : (part + 1) * cols, :]
    count, tall = near_ref.shape[0] // 2, near_ref.shape[1]
    taken = cols // count
    pieces = [near_ref[index, tall - taken :, :] for index in range(part * count, (part + 1) * count)]
    return jnp.concatenate(pieces, axis=0)


def hidden_and_grad(stay_ref, give_ref):
    stay, give = stay_ref[...], give_ref[...]
    return jnp.where(on_ocean(), give, stay), jnp.where(on_ocean(), stay, give)


def shifted_inputs(pad, cols):
    middle = pad.T
    before, after = moved_cells(middle, 1, cols)
    return [part.astype(BF16) for part in (before, middle, after)]


def own_grads_kernel(
    upad_ref, gpad_ref, stay_ref, give_ref, atmos_out, ocean_out, near_ref, far_hidden, far_grad, *, cols
):
    stay = stay_ref[...].astype(F32)
    hidden, first_grad = hidden_and_grad(stay_ref, give_ref)
    core = own_bit(0)
    for part, values in enumerate((hidden, first_grad)):
        target = slice(part * cols, (part + 1) * cols)
        (far_hidden, far_grad)[part][...] = jnp.where(core == 0, values[:cols], values[cols:])
        near_ref[target, :] = jnp.where(core == 0, values[cols:], values[:cols])

    @pl.when(on_ocean())
    def _():
        grad_ocean(upad_ref[...].astype(F32), stay, True, cols, store_into(ocean_out))

    @pl.when(jnp.logical_not(on_ocean()))
    def _():
        grad_atmos(gpad_ref[...].astype(F32), stay, cols, store_into(atmos_out))


def shift_kernel(early_ref, edge_ref, sent_ref, coupling_ref, left_ref, *, cols):
    @pl.when(on_ocean())
    def _():
        added = dot(sent_ref[...], coupling_ref[...].astype(F32), TN, HIGHEST)
        other = (whole_pad(early_ref, edge_ref, cols) + added).astype(BF16).astype(F32)
        for tap, left in enumerate(shifted_inputs(other, cols)):
            left_ref[tap] = left


def other_grads_kernel(left_ref, late_ref, early_ref, edge_ref, atmos_out, ocean_out, *, cols):
    rows = late_ref.shape[0]

    @pl.when(on_ocean())
    def _():
        store = store_into(atmos_out)
        for tap in range(9):
            start = cols * (tap // 3)
            store(tap, dot(left_ref[tap % 3, :, start : start + rows], late_ref[...]))

    @pl.when(jnp.logical_not(on_ocean()))
    def _():
        late = late_ref[...].astype(F32)
        grad_ocean(whole_pad(early_ref, edge_ref, cols), late, False, cols, store_into(ocean_out))


def chunk_rows(out_ref, side, tall, atmos_all, ocean_all, chunks):
    channels = out_ref.shape[2]
    pieces = ocean_all.shape[0]
    atmos_rows = atmos_all.shape[0] // chunks
    ocean_rows = atmos_rows // 2
    taken = tall - atmos_rows
    blank = jnp.zeros((taken, channels - 128 * pieces), F32)
    for pair in range(chunks // 2):
        start = pl.multiple_of(atmos_rows * (2 * pair + side), 8)
        upper = atmos_all[pl.ds(start, atmos_rows), :]
        start = ocean_rows * (2 * pair + side)
        halves = []
        for odd in range(2):
            parts = [ocean_all.at[piece][pl.ds(start + odd, taken, 2), :] for piece in range(pieces)]
            halves.append(jnp.concatenate(parts + [blank], axis=1))
        lower = halves[0] + pltpu.roll(halves[1], channels // 2, 1)
        out_ref[pair, 0:tall, :] = jnp.concatenate([upper, lower], axis=0).astype(BF16)


def chunk_kernel(atmos_own, ocean_own, atmos_other, ocean_other, *refs, chunks, tall, sent):
    out_ref = refs[-1]
    core = own_bit(0)
    side = 1 - core if sent else core
    if sent:
        near_ref = refs[0]
        taken = out_ref.shape[1] - tall
        for pair in range(chunks // 2):
            out_ref[pair, tall:, :] = near_ref[pair * taken : (pair + 1) * taken, :]

    @pl.when(on_ocean())
    def _():
        chunk_rows(out_ref, side, tall, atmos_other, ocean_own, chunks)

    @pl.when(jnp.logical_not(on_ocean()))
    def _():
        chunk_rows(out_ref, side, tall, atmos_own, ocean_other, chunks)


def halve(keep_ref, came_ref, out_ref, side, rows):
    for outer in range(keep_ref.shape[0]):
        for inner in range(keep_ref.shape[2]):
            total = keep_ref[outer, side, inner, rows, :].astype(F32)
            total = total + came_ref[outer, side, inner, rows, :].astype(F32)
            out_ref[outer, inner] = total.astype(BF16)


def split_kernel(keep_ref, came_ref, *refs, cuts, sent):
    by_z = [ref.reshape(2, 2, 2, *ref.shape[3:]) for ref in (keep_ref, came_ref)]
    start = 0
    for index, rows in enumerate(cuts):
        pair, bit = (by_z, 2) if index == 1 else ((keep_ref, came_ref), 1)
        own = own_bit(bit)
        halve(*pair, refs[index], 1 - own if sent else own, slice(start, start + rows))
        start += rows
    if sent:
        refs[-1][...] = jnp.zeros_like(refs[-1])


def halve_kernel(keep_ref, came_ref, *refs, bit, marked):
    outs = refs[-3:] if marked else refs[-2:]
    own = own_bit(bit)
    halve(keep_ref, came_ref, outs[1], 1 - own, slice(None))
    halve(keep_ref, came_ref, outs[0], own, slice(None))
    if marked:
        outs[2][...] = jnp.zeros_like(outs[2])


MARK = shape((8, 128), F32)


def halved(keep, came, bit, dims, after, marked=True):
    outer, inner, rows, channels = dims[0], dims[1], keep.shape[-2], keep.shape[-1]
    keep, came = (part.reshape(outer, 2, inner, rows, channels) for part in (keep, came))
    out = shape((outer, inner, rows, channels), BF16)
    return call(
        functools.partial(halve_kernel, bit=bit, marked=marked),
        [out, out] + [MARK] * marked,
        [keep, came, *after],
        [WHOLE] * 2 + [ANYWHERE] * len(after),
        moved=8 * outer * inner * rows * channels,
        name="halve",
    )


def split(keep, came):
    pairs, tall, channels = keep.shape
    cuts = [16 * (tall // 16 * part // 17) for part in (7, 5)]
    cuts.append(tall - sum(cuts))
    outs = [
        shape(((2, 2) if index == 1 else (4, 1)) + (rows, channels), BF16) for index, rows in enumerate(cuts)
    ]
    inputs = [part.reshape(4, 2, 1, *part.shape[1:]) for part in (keep, came)]
    kept, sent = (
        call(
            functools.partial(split_kernel, cuts=cuts, sent=is_sent),
            outs + [MARK] * is_sent,
            inputs,
            moved=3 * pairs * tall * channels,
            name="split",
        )
        for is_sent in (False, True)
    )
    return kept, sent[:3], sent[3]


def scatter_sum(kept, sent, before_a):
    (a_keep, b_keep, c_keep), (a_send, b_send, c_send) = kept, sent
    channels = a_keep.shape[-1]
    a_came = swapped(a_send, "lat", 2)
    b_came = swapped(b_send, "lat", 4)
    c_came = swapped(c_send, "lat", 2)
    a_keep, a_send, mark = halved(a_keep, a_came, 2, (2, 1), before_a)
    a_came = swapped(a_send, "lat", 4)
    b_keep, b_send, mark = halved(b_keep, b_came, 3, (1, 2), [mark])
    b_came = swapped(b_send, "lat", 8)
    c_keep, c_send, mark = halved(c_keep, c_came, 2, (2, 1), [mark])
    c_came = swapped(c_send, "lat", 4)
    a_keep, a_send, mark = halved(a_keep, a_came, 3, (1, 1), [mark])
    a_came = swapped(a_send, "lat", 8)
    b_keep, b_send, mark = halved(b_keep, b_came, 1, (1, 1), [mark])
    b_came = swapped(b_send, "lat", 2)
    c_keep, c_send = halved(c_keep, c_came, 3, (1, 1), [mark], False)
    c_came = swapped(c_send, "lat", 8)
    return [part.reshape(-1, channels) for part in (a_keep, a_came, b_keep, b_came, c_keep, c_came)]


def finish_kernel(*refs, atmos_factor, ocean_factor):
    parts, (atmos_ref, ocean_ref) = refs[:-2], refs[-2:]
    channels = parts[0].shape[1]
    pieces = channels // 128
    atmos_rows = atmos_ref.shape[0] // pieces
    ocean_rows = ocean_ref.shape[0] // pieces
    sums = [
        parts[index][...].astype(F32) + parts[index + 1][...].astype(F32)
        for index in range(0, len(parts), 2)
    ]
    total = jnp.concatenate(sums, axis=0)
    for piece in range(pieces):
        lanes = slice(128 * piece, 128 * (piece + 1))
        atmos_ref[pl.ds(piece, atmos_rows, pieces), :] = total[:atmos_rows, lanes] * atmos_factor
        ocean_ref[pl.ds(piece, ocean_rows, pieces), :] = (
            total[atmos_rows : atmos_rows + ocean_rows, lanes] * ocean_factor
        )


def input_grad_kernel(
    stay_ref, give_ref, near_ref, far_ref, gpad_ref, wet_ref, terms_ref, atmos_ref, ocean_ref, *refs, cols
):
    grad_ref, sent_ref = refs[-2:]
    middle = hidden_and_grad(stay_ref, give_ref)[1]
    low, high = low_and_high(near_rows(near_ref, 1, cols), far_ref[...])
    pad = jnp.concatenate([low, middle, high], axis=0)
    own = slice(cols, 3 * cols)
    convolve(pad, grad_ref, atmos_ref, ocean_ref, 0, True, cols)
    grad = gpad_ref[own, :].astype(F32) + grad_ref[...]
    grad_ref[...] = grad
    weighted = dot(terms_ref[8:16, :], grad, NT, HIGHEST)
    mixed = weighted[0:4] * wet_ref[0:1, own] + weighted[4:8] * wet_ref[1:2, own]
    sent_ref[...] = jnp.where(on_ocean(), mixed, weighted[0:4])


def next_kernel(
    stay_ref, give_ref, near_ref, far_ref, upad_ref, atmos_ref, ocean_ref,
    next_ref, mark_ref, second_ref, *, cols,
):
    middle = hidden_and_grad(stay_ref, give_ref)[0]
    low, high = low_and_high(near_rows(near_ref, 0, cols), far_ref[...])
    pad = jnp.concatenate([low, middle, high], axis=0)
    own = slice(cols, 3 * cols)
    convolve(pad, second_ref, atmos_ref, ocean_ref, 1, False, cols)
    values = (upad_ref[own, :].astype(F32) + second_ref[...]).astype(BF16)
    next_ref[0] = values[:cols]
    next_ref[1] = values[cols:]
    mark_ref[...] = jnp.zeros_like(mark_ref)


def last_kernel(grad_ref, arrived_ref, wet_ref, terms_ref, *refs, cols):
    out_ref, mark_ref = refs[-2:]
    own = slice(cols, 3 * cols)
    wet = wet_ref[0:1, own], wet_ref[1:2, own]
    arrived = jnp.where(on_ocean(), arrived_ref[...] * wet_ref[2:3, own], arrived_ref[...])
    added = spread(arrived, wet, on_ocean(), terms_ref[0:8, :])
    values = (grad_ref[...] + added).astype(BF16)
    out_ref[0] = values[:cols]
    out_ref[1] = values[cols:]
    mark_ref[...] = jnp.zeros_like(mark_ref)


def swapped(value, axis, mask):
    pairs = [(source, source ^ mask) for source in range(lax.axis_size(axis))]
    return lax.ppermute(value, axis, pairs)


def far_halo(far):
    pairs = [(i, i + 1 if i % 2 else i - 1) for i in range(1, lax.axis_size("lat") - 1)]
    return lax.ppermute(far, "lat", pairs)


def local(
    fields,
    cotangent,
    ocean_kernels,
    atmos_kernels,
    ocean_surface,
    ocean_coupling,
    atmos_flux,
    atmos_coupling,
    row_map,
    wet_mask,
):
    x, g = fields[0], cotangent[0]
    bands, cols, channels = x.shape
    narrow = channels // 2
    cells = bands * cols
    count = lax.axis_size("lat")
    is_ocean = lax.axis_index("grp") == 0
    atmos_factor = 1.0 / math.sqrt(bands * count * cols)
    ocean_factor = 1.0 / math.sqrt(bands * count * 2 * cols)
    bound = functools.partial

    blank = jnp.zeros((4, narrow), BF16)
    gap = jnp.zeros((4, channels), BF16)
    surface = ocean_surface.T
    ocean_terms = jnp.concatenate(
        [
            jnp.concatenate([surface, blank], axis=1),
            jnp.concatenate([blank, surface], axis=1),
            jnp.concatenate([ocean_coupling, blank], axis=1),
            jnp.concatenate([blank, ocean_coupling], axis=1),
        ],
        axis=0,
    )
    atmos_terms = jnp.concatenate([atmos_flux.T, gap, atmos_coupling, gap], axis=0)
    terms = jnp.where(is_ocean, ocean_terms, atmos_terms).astype(F32)

    edge = shape((2 * cols + 16, channels), BF16)
    half = shape((cells, channels), BF16)
    near, far, own_early, own = call(
        bound(pack_kernel, cols=cols),
        [edge, edge, half, shape((2 * cells + 16, channels), BF16)],
        [x, g, wet_mask],
        [IN_PLACE] * 3,
        [
            pltpu.VMEM(x.shape, BF16),
            pltpu.VMEM(x.shape, BF16),
            pltpu.VMEM(wet_mask.shape, jnp.int32),
            pltpu.SemaphoreType.DMA((3,)),
        ],
        name="pack",
        limit=PACK_VMEM,
    )
    near, far = swapped(near, "lat", 1), far_halo(far)
    other_early = swapped(own_early, "grp", 1)
    wide = -(-narrow // 128) * 128
    own, atmos_flat, ocean_flat = call(
        hold_kernel,
        [
            shape(own.shape, BF16),
            shape((18, channels, channels), BF16),
            shape((18, wide, narrow), BF16),
        ],
        [own, atmos_kernels.reshape(18, channels, channels), ocean_kernels.reshape(18, narrow, narrow)],
        [WHOLE, IN_PLACE, IN_PLACE],
        [pltpu.SemaphoreType.DMA],
        flops=PACE * 10**8,
        name="hold",
        limit=HOLD_VMEM,
    )
    pad = shape((2 * cells, channels), BF16)
    xpad, gpad, wet, edges, sent = call(
        bound(outgoing_kernel, cols=cols),
        [pad, pad, shape((8, 2 * cells), F32), half, shape((4, 2 * cells), F32)],
        [own, near, far, terms],
        name="outgoing",
    )
    arrived = swapped(sent, "grp", 1)
    other_edges = swapped(edges, "grp", 1)
    conv_cost = dict(flops=PACE * 9 * cells * channels * channels, moved=9 * channels * channels * 2)
    back = call(
        bound(back_kernel, cols=cols),
        shape((cells, channels), F32),
        [gpad, atmos_flat, ocean_flat],
        **conv_cost,
        name="back",
    )
    upad, stay, give = call(
        bound(first_kernel, cols=cols),
        [pad, half, half],
        [xpad, wet, arrived, terms, back, atmos_flat, ocean_flat],
        None,
        [pltpu.VMEM((cells, channels), F32)],
        **conv_cost,
        name="first",
    )
    late = swapped(give, "grp", 1)

    atmos_rows = 9 * channels // count
    ocean_rows = 9 * narrow // count
    chunked = count == 16 and 9 * channels % (8 * count) == 0 and ocean_rows % 2 == 0
    tall = -(-(atmos_rows + ocean_rows // 2) // 16) * 16
    spare = max(0, 2 * (tall - atmos_rows) - ocean_rows) if chunked else 0
    ocean_tall = 9 * narrow + -(-spare // 8) * 8
    sums = [shape((9 * channels, channels), F32), shape((wide // 128, ocean_tall, 128), F32)]
    row = shape((cols, channels), BF16)
    atmos_sum, ocean_sum, near, far_hidden, far_grad = call(
        bound(own_grads_kernel, cols=cols),
        [*sums, half, row, row],
        [upad, gpad, stay, give],
        **conv_cost,
        name="own_grads",
    )
    far_hidden, far_grad = far_halo(far_hidden), far_halo(far_grad)
    lefts = call(
        bound(shift_kernel, cols=cols),
        shape((3, channels, 2 * cells), BF16),
        [other_early, other_edges, sent, atmos_coupling],
        name="shift",
    )
    atmos_other, ocean_other = call(
        bound(other_grads_kernel, cols=cols),
        sums,
        [lefts, late, other_early, other_edges],
        **conv_cost,
        name="other_grads",
    )
    if chunked:
        taken = 2 * cols // (count // 2)
        sums = [atmos_sum, ocean_sum, atmos_other, ocean_other]
        send, keep = (
            call(
                bound(chunk_kernel, chunks=count, tall=tall, sent=sent),
                shape((count // 2, tall + taken * sent, channels), BF16),
                sums + [near, far_grad] * sent,
                [WHOLE] * (4 + sent) + [ANYWHERE] * sent,
                moved=2 * count * tall * channels,
                name="chunk",
            )
            for sent in (True, False)
        )
        near = swapped(send, "lat", 1)
        kept, parts, split_mark = split(keep, near)
        after_split = [split_mark]
    else:
        near = swapped(near, "lat", 1)
        after_split = []

    grad, sent_back = call(
        bound(input_grad_kernel, cols=cols),
        [shape((cells, channels), F32), shape((4, cells), F32)],
        [stay, give, near, far_grad, gpad, wet, terms, atmos_flat, ocean_flat, *after_split],
        [WHOLE] * 9 + [ANYWHERE] * len(after_split),
        **conv_cost,
        name="input_grad",
    )
    returned = swapped(sent_back, "grp", 1)
    next_field, next_mark = call(
        bound(next_kernel, cols=cols),
        [shape(x.shape, BF16), MARK],
        [stay, give, near, far_hidden, upad, atmos_flat, ocean_flat],
        None,
        [pltpu.VMEM((cells, channels), F32)],
        **conv_cost,
        name="next",
    )

    field_grad, last_mark = call(
        bound(last_kernel, cols=cols),
        [shape(x.shape, BF16), MARK],
        [grad, returned, wet, terms],
        name="last",
    )
    if chunked:
        sums = scatter_sum(kept, parts, [next_mark, last_mark])
        atmos_chunk, ocean_chunk = call(
            bound(finish_kernel, atmos_factor=atmos_factor, ocean_factor=ocean_factor),
            [
                shape((atmos_rows * channels // 128, 128), F32),
                shape((ocean_rows * narrow // 128, 128), F32),
            ],
            sums,
            name="finish",
        )
        atmos_total, ocean_total = atmos_chunk.reshape(-1), ocean_chunk.reshape(-1)
    else:
        atmos_all = jnp.where(is_ocean, atmos_other, atmos_sum)
        ocean_all = jnp.where(is_ocean, ocean_sum, ocean_other)
        atmos_total = atmos_factor * lax.psum_scatter(
            atmos_all.reshape(-1), "lat", scatter_dimension=0, tiled=True
        )
        ocean_all = jnp.concatenate([ocean_all[piece] for piece in range(wide // 128)], axis=1)
        ocean_total = ocean_factor * lax.psum_scatter(
            ocean_all[:, :narrow].reshape(-1), "lat", scatter_dimension=0, tiled=True
        )
    return (next_field[None], field_grad[None], ocean_total, atmos_total)


def solution(mesh):
    in_specs = (
        P("grp", "lat", None, None),
        P("grp", "lat", None, None),
        P(),
        P(),
        P(),
        P(),
        P(),
        P(),
        P("lat"),
        P("lat", None),
    )
    out_specs = (
        P("grp", "lat", None, None),
        P("grp", "lat", None, None),
        P(("grp", "lat")),
        P(("grp", "lat")),
    )
    return jax.shard_map(local, mesh=mesh, in_specs=in_specs, out_specs=out_specs, check_vma=False)
```

```python
import functools
import math

import jax
import jax.numpy as jnp
from jax import lax
from jax.experimental import pallas as pl
from jax.experimental.pallas import tpu as pltpu
from jax.sharding import PartitionSpec as P

HIGHEST = lax.Precision.HIGHEST
GELU_SCALE = 0.7978845608028654
GELU_CUBIC = 0.044715
F32 = jnp.float32
BF16 = jnp.bfloat16
WHOLE = pl.BlockSpec(memory_space=pltpu.VMEM)
IN_PLACE = pl.BlockSpec(memory_space=pltpu.HBM)
ANYWHERE = pl.BlockSpec(memory_space=pl.ANY)
VMEM_LIMIT = 20 * 1024 * 1024
PACE = 8
PACK_VMEM = 62 * 1024 * 1024
HOLD_VMEM = 42 * 1024 * 1024

NN = (((1,), (0,)), ((), ()))
NT = (((1,), (1,)), ((), ()))
TN = (((0,), (0,)), ((), ()))


def shape(dims, kind):
    return jax.ShapeDtypeStruct(dims, kind)


def call(kernel, outs, inputs, in_specs=None, scratch=(), flops=0, moved=0, name=None, limit=VMEM_LIMIT, out_spec=WHOLE):
    return pl.pallas_call(
        kernel,
        out_shape=outs,
        in_specs=in_specs or [WHOLE] * len(inputs),
        out_specs=jax.tree.map(lambda _: out_spec, outs),
        scratch_shapes=list(scratch),
        compiler_params=pltpu.CompilerParams(vmem_limit_bytes=limit),
        cost_estimate=pl.CostEstimate(flops=flops, bytes_accessed=moved, transcendentals=0),
        name=name,
    )(*inputs)


def on_ocean():
    return lax.axis_index("grp") == 0


def dot(left, right, dims=NN, precision=None):
    return lax.dot_general(left, right, dims, precision=precision, preferred_element_type=F32)


def moved_cells(values, axis, cols):
    count = values.shape[axis]
    place = lax.rem(lax.broadcasted_iota(jnp.int32, values.shape, axis), cols)
    before = jnp.where(place == 0, 0.0, pltpu.roll(values, 1, axis))
    after = jnp.where(place == cols - 1, 0.0, pltpu.roll(values, count - 1, axis))
    return before, after


def wet_halves(wet, cols, channels):
    source = lax.broadcasted_iota(jnp.int32, (2 * cols, 2 * cols), 0)
    target = lax.broadcasted_iota(jnp.int32, (2 * cols, 2 * cols), 1)
    wanted = 2 * lax.rem(target, cols) + jnp.where(target >= cols, 1, 0)
    chooser = (source == wanted).astype(F32).astype(BF16)
    padded = jnp.concatenate([wet.astype(F32), jnp.zeros((14, 2 * cols), F32)], axis=0)
    apart = dot(padded.astype(BF16), chooser)
    return jnp.concatenate([apart, jnp.zeros((16, channels - 2 * cols), F32)], axis=1)


def own_bit(bit):
    return lax.rem(lax.shift_right_logical(lax.axis_index("lat"), bit), 2)


def pack_kernel(
    x_any, g_any, wet_any, near_ref, far_ref, early_ref, own_ref, x_ref, g_ref, wet_ref, sems, *, cols
):
    pairs = ((wet_any, wet_ref), (x_any, x_ref), (g_any, g_ref))
    copies = [pltpu.make_async_copy(*pair, sems.at[index]) for index, pair in enumerate(pairs)]
    for copy in copies:
        copy.start()
    core = own_bit(0)
    copies[0].wait()
    wide = wet_halves(wet_ref[...], cols, x_ref.shape[2])
    other = pltpu.roll(wide, 15, 0)
    own_ref[4 * cols :, :] = wide.astype(BF16)
    far_ref[2 * cols :, :] = jnp.where(core == 0, wide, other).astype(BF16)
    near_ref[2 * cols :, :] = jnp.where(core == 0, other, wide).astype(BF16)
    copies[1].wait()
    copies[2].wait()
    for part, ref in enumerate((x_ref, g_ref)):
        far_ref[part * cols : (part + 1) * cols, :] = ref[core]
        near_ref[part * cols : (part + 1) * cols, :] = ref[1 - core]
        own_ref[2 * part * cols : (2 * part + 1) * cols, :] = ref[0]
        own_ref[(2 * part + 1) * cols : (2 * part + 2) * cols, :] = ref[1]
    for row in range(2):
        early_ref[row * cols : (row + 1) * cols, :] = jnp.where(on_ocean(), g_ref[row], x_ref[row])


def hold_kernel(own_in, atmos_any, ocean_any, own_ref, atmos_ref, ocean_ref, sem):
    narrow = ocean_ref.shape[2]
    ocean_copy = pltpu.make_async_copy(ocean_any, ocean_ref.at[:, pl.ds(0, narrow), :], sem)
    atmos_copy = pltpu.make_async_copy(atmos_any, atmos_ref, sem)

    @pl.when(on_ocean())
    def _():
        ocean_copy.start()
        gap = ocean_ref.shape[1] - narrow
        if gap:
            ocean_ref[:, narrow:, :] = jnp.zeros((ocean_ref.shape[0], gap, narrow), BF16)

    @pl.when(jnp.logical_not(on_ocean()))
    def _():
        atmos_copy.start()

    own_ref[...] = own_in[...]

    @pl.when(on_ocean())
    def _():
        ocean_copy.wait()

    @pl.when(jnp.logical_not(on_ocean()))
    def _():
        atmos_copy.wait()


def low_and_high(near, far):
    core = own_bit(0)
    return jnp.where(core == 0, far, near), jnp.where(core == 0, near, far)


def outgoing_kernel(
    own_ref, near_ref, far_ref, terms_ref, xpad_ref, gpad_ref, wet_ref, edge_ref, sent_ref, *, cols
):
    low, high = low_and_high(near_ref[...], far_ref[...])
    for part, pad_ref in enumerate((xpad_ref, gpad_ref)):
        pad_ref[0:cols, :] = low[part * cols : (part + 1) * cols]
        pad_ref[cols : 3 * cols, :] = own_ref[2 * part * cols : 2 * (part + 1) * cols, :]
        pad_ref[3 * cols : 4 * cols, :] = high[part * cols : (part + 1) * cols]
    low_wet = low[2 * cols :].astype(F32)
    high_wet = high[2 * cols :].astype(F32)
    own_wet = own_ref[4 * cols :, :].astype(F32)
    halves = []
    for start in (0, cols):
        lanes = slice(start, start + cols)
        rows = (low_wet[0:1, lanes], own_wet[0:1, lanes], own_wet[1:2, lanes], high_wet[0:1, lanes])
        halves.append(jnp.concatenate(rows, axis=1))
    first_wet, second_wet = halves
    inverse = 1.0 / jnp.maximum(first_wet + second_wet, 1.0)
    wet_ref[0:1, :] = first_wet
    wet_ref[1:2, :] = second_wet
    wet_ref[2:3, :] = inverse
    wet_ref[3:8, :] = jnp.zeros((5, 4 * cols), F32)
    xpad = xpad_ref[...]
    projected = dot(terms_ref[0:8, :].astype(BF16), xpad, NT)
    mixed = (projected[0:4] * first_wet + projected[4:8] * second_wet) * inverse
    sent_ref[...] = jnp.where(on_ocean(), mixed, projected[0:4])
    edge_ref[0:cols, :] = jnp.where(on_ocean(), gpad_ref[0:cols, :], xpad_ref[0:cols, :])
    edge_ref[cols:, :] = jnp.where(on_ocean(), gpad_ref[3 * cols :, :], xpad_ref[3 * cols :, :])


def halves_apart(values, narrow):
    wide = -(-narrow // 128) * 128
    lane = lax.broadcasted_iota(jnp.int32, values.shape, 1)
    even = jnp.where(lane < narrow, values, 0.0)
    odd = jnp.where(lane < narrow, pltpu.roll(values, narrow, 1), 0.0)
    return even[:, :wide], odd[:, :wide]


def halves_with_columns(pad, cols):
    even, odd = halves_apart(pad.astype(F32), pad.shape[1] // 2)
    odd_before = moved_cells(odd, 0, cols)[0].astype(BF16)
    even_after = moved_cells(even, 0, cols)[1].astype(BF16)
    even, odd = even.astype(BF16), odd.astype(BF16)
    return (odd_before, even, odd), (even, odd, even_after)


def with_columns(pad, cols):
    before, after = moved_cells(pad.astype(F32), 0, cols)
    return before.astype(BF16), pad, after.astype(BF16)


def convolve(pad, out_ref, atmos_ref, ocean_ref, layer, flipped, cols):
    base = 9 * layer
    channels = atmos_ref.shape[2]
    wide, narrow = ocean_ref.shape[1:]
    rows = out_ref.shape[0]

    def summed(pick):
        total = None
        for row_tap in range(3):
            part = pick(row_tap, slice(cols * row_tap, cols * row_tap + rows))
            total = part if total is None else total + part
        return total

    @pl.when(on_ocean())
    def _():
        evens, odds = halves_with_columns(pad, cols)
        if flipped:

            def pick(row_tap, span):
                part = None
                for col_tap in range(3):
                    left = jnp.concatenate([evens[col_tap][span], odds[col_tap][span]], axis=0)
                    kernel = ocean_ref[base + 8 - (3 * row_tap + col_tap), 0:narrow, :]
                    piece = dot(left[:, :narrow], kernel, NT)
                    part = piece if part is None else part + piece
                return part

        else:
            even, odd = jnp.concatenate(evens, axis=1), jnp.concatenate(odds, axis=1)

            def pick(row_tap, span):
                first = base + 3 * row_tap
                kernel = ocean_ref[first : first + 3].reshape(3 * wide, narrow)
                return dot(jnp.concatenate([even[span], odd[span]], axis=0), kernel)

        total = summed(pick)
        out_ref[...] = jnp.concatenate([total[:rows], total[rows:]], axis=1)

    @pl.when(jnp.logical_not(on_ocean()))
    def _():
        taps = with_columns(pad, cols)
        if flipped:

            def pick(row_tap, span):
                part = None
                for col_tap in range(3):
                    piece = dot(taps[col_tap][span], atmos_ref[base + 8 - (3 * row_tap + col_tap)], NT)
                    part = piece if part is None else part + piece
                return part

        else:
            joined = jnp.concatenate(taps, axis=1)

            def pick(row_tap, span):
                first = base + 3 * row_tap
                return dot(joined[span], atmos_ref[first : first + 3].reshape(3 * channels, channels))

        out_ref[...] = summed(pick)


def back_kernel(gpad_ref, atmos_ref, ocean_ref, out_ref, *, cols):
    convolve(gpad_ref[...], out_ref, atmos_ref, ocean_ref, 1, True, cols)


def spread(arrived, wet, mixing, terms):
    first_wet, second_wet = wet
    both = jnp.concatenate([arrived * first_wet, arrived * second_wet], axis=0)
    alone = jnp.concatenate([arrived, jnp.zeros_like(arrived)], axis=0)
    return dot(jnp.where(mixing, both, alone), terms, TN, HIGHEST)


def first_kernel(
    xpad_ref, wet_ref, arrived_ref, terms_ref, back_ref, atmos_ref, ocean_ref,
    u_ref, stay_ref, give_ref, first_ref, *, cols,
):
    wet = wet_ref[0:1, :], wet_ref[1:2, :]
    coupled = spread(arrived_ref[...], wet, on_ocean(), terms_ref[8:16, :])
    u = (xpad_ref[...].astype(F32) + coupled).astype(BF16)
    u_ref[...] = u
    convolve(u, first_ref, atmos_ref, ocean_ref, 0, False, cols)
    first = first_ref[...]
    tangent = jnp.tanh(GELU_SCALE * (first + GELU_CUBIC * first * first * first))
    hidden = (0.5 * first * (1.0 + tangent)).astype(BF16)
    slope = 0.5 * (1.0 + tangent) + 0.5 * first * (1.0 - tangent * tangent) * GELU_SCALE * (
        1.0 + 3.0 * GELU_CUBIC * first * first
    )
    first_grad = (back_ref[...] * slope).astype(BF16)
    stay_ref[...] = jnp.where(on_ocean(), first_grad, hidden)
    give_ref[...] = jnp.where(on_ocean(), hidden, first_grad)


def whole_pad(early_ref, edge_ref, cols):
    parts = [edge_ref[0:cols, :], early_ref[...], edge_ref[cols:, :]]
    return jnp.concatenate(parts, axis=0).astype(F32)


def grad_atmos(pad, own, cols, store):
    rows = own.shape[0]
    left = own.T.astype(BF16)
    before, after = moved_cells(pad, 0, cols)
    rights = [part.astype(BF16) for part in (after, pad, before)]
    for tap in range(9):
        start = cols * (2 - tap // 3)
        store(tap, dot(left, rights[tap % 3][start : start + rows]))


def grad_ocean(pad, own, pad_is_input, cols, store):
    rows, channels = own.shape
    narrow = channels // 2

    if pad_is_input:
        middle = pad.T
        before, after = moved_cells(middle, 1, cols)
        even, odd = middle[:narrow].astype(BF16), middle[narrow:].astype(BF16)
        pairs = (
            (before[narrow:].astype(BF16), even),
            (even, odd),
            (odd, after[:narrow].astype(BF16)),
        )
        right = jnp.concatenate(halves_apart(own, narrow), axis=0).astype(BF16)
        for tap in range(9):
            start = cols * (tap // 3)
            pieces = [part[:, start : start + rows] for part in pairs[tap % 3]]
            store(tap, dot(jnp.concatenate(pieces, axis=1), right))
    else:
        turned = own.T.astype(BF16)
        left = jnp.concatenate([turned[:narrow], turned[narrow:]], axis=1)
        even, odd = halves_apart(pad, narrow)
        odd_before = moved_cells(odd, 0, cols)[0].astype(BF16)
        even_after = moved_cells(even, 0, cols)[1].astype(BF16)
        even, odd = even.astype(BF16), odd.astype(BF16)
        pairs = ((odd, even_after), (even, odd), (odd_before, even))
        for tap in range(9):
            start = cols * (2 - tap // 3)
            pieces = [part[start : start + rows] for part in pairs[tap % 3]]
            store(tap, dot(left, jnp.concatenate(pieces, axis=0)))


def store_into(out_ref):
    def store(tap, value):
        if len(out_ref.shape) == 2:
            rows = value.shape[0]
            out_ref[rows * tap : rows * (tap + 1), :] = value
        else:
            rows = value.shape[0]
            for piece in range(out_ref.shape[0]):
                lanes = slice(128 * piece, 128 * (piece + 1))
                out_ref[piece, rows * tap : rows * (tap + 1), :] = value[:, lanes]

    return store


def near_rows(near_ref, part, cols):
    if len(near_ref.shape) == 2:
        return near_ref[part * cols : (part + 1) * cols, :]
    count, tall = near_ref.shape[0] // 2, near_ref.shape[1]
    taken = cols // count
    pieces = [near_ref[index, tall - taken :, :] for index in range(part * count, (part + 1) * count)]
    return jnp.concatenate(pieces, axis=0)


def hidden_and_grad(stay_ref, give_ref):
    stay, give = stay_ref[...], give_ref[...]
    return jnp.where(on_ocean(), give, stay), jnp.where(on_ocean(), stay, give)


def shifted_inputs(pad, cols):
    middle = pad.T
    before, after = moved_cells(middle, 1, cols)
    return [part.astype(BF16) for part in (before, middle, after)]


def own_grads_kernel(
    upad_ref, gpad_ref, stay_ref, give_ref, atmos_out, ocean_out, near_ref, far_hidden, far_grad, *, cols
):
    stay = stay_ref[...].astype(F32)
    hidden, first_grad = hidden_and_grad(stay_ref, give_ref)
    core = own_bit(0)
    for part, values in enumerate((hidden, first_grad)):
        target = slice(part * cols, (part + 1) * cols)
        (far_hidden, far_grad)[part][...] = jnp.where(core == 0, values[:cols], values[cols:])
        near_ref[target, :] = jnp.where(core == 0, values[cols:], values[:cols])

    @pl.when(on_ocean())
    def _():
        grad_ocean(upad_ref[...].astype(F32), stay, True, cols, store_into(ocean_out))

    @pl.when(jnp.logical_not(on_ocean()))
    def _():
        grad_atmos(gpad_ref[...].astype(F32), stay, cols, store_into(atmos_out))


def shift_kernel(early_ref, edge_ref, sent_ref, coupling_ref, left_ref, *, cols):
    @pl.when(on_ocean())
    def _():
        added = dot(sent_ref[...], coupling_ref[...].astype(F32), TN, HIGHEST)
        other = (whole_pad(early_ref, edge_ref, cols) + added).astype(BF16).astype(F32)
        for tap, left in enumerate(shifted_inputs(other, cols)):
            left_ref[tap] = left


def other_grads_kernel(left_ref, late_ref, early_ref, edge_ref, atmos_out, ocean_out, *, cols):
    rows = late_ref.shape[0]

    @pl.when(on_ocean())
    def _():
        store = store_into(atmos_out)
        for tap in range(9):
            start = cols * (tap // 3)
            store(tap, dot(left_ref[tap % 3, :, start : start + rows], late_ref[...]))

    @pl.when(jnp.logical_not(on_ocean()))
    def _():
        late = late_ref[...].astype(F32)
        grad_ocean(whole_pad(early_ref, edge_ref, cols), late, False, cols, store_into(ocean_out))


def chunk_rows(out_ref, side, tall, atmos_all, ocean_all, chunks):
    channels = out_ref.shape[2]
    pieces = ocean_all.shape[0]
    atmos_rows = atmos_all.shape[0] // chunks
    ocean_rows = atmos_rows // 2
    taken = tall - atmos_rows
    blank = jnp.zeros((taken, channels - 128 * pieces), F32)
    for pair in range(chunks // 2):
        start = pl.multiple_of(atmos_rows * (2 * pair + side), 8)
        upper = atmos_all[pl.ds(start, atmos_rows), :]
        start = ocean_rows * (2 * pair + side)
        halves = []
        for odd in range(2):
            parts = [ocean_all.at[piece][pl.ds(start + odd, taken, 2), :] for piece in range(pieces)]
            halves.append(jnp.concatenate(parts + [blank], axis=1))
        lower = halves[0] + pltpu.roll(halves[1], channels // 2, 1)
        out_ref[pair, 0:tall, :] = jnp.concatenate([upper, lower], axis=0).astype(BF16)


def chunk_kernel(atmos_own, ocean_own, atmos_other, ocean_other, *refs, chunks, tall, sent):
    out_ref = refs[-1]
    core = own_bit(0)
    side = 1 - core if sent else core
    if sent:
        near_ref = refs[0]
        taken = out_ref.shape[1] - tall
        for pair in range(chunks // 2):
            out_ref[pair, tall:, :] = near_ref[pair * taken : (pair + 1) * taken, :]

    @pl.when(on_ocean())
    def _():
        chunk_rows(out_ref, side, tall, atmos_other, ocean_own, chunks)

    @pl.when(jnp.logical_not(on_ocean()))
    def _():
        chunk_rows(out_ref, side, tall, atmos_own, ocean_other, chunks)


def halve(keep_ref, came_ref, out_ref, side, rows):
    for outer in range(keep_ref.shape[0]):
        for inner in range(keep_ref.shape[2]):
            total = keep_ref[outer, side, inner, rows, :].astype(F32)
            total = total + came_ref[outer, side, inner, rows, :].astype(F32)
            out_ref[outer, inner] = total.astype(BF16)


def split_kernel(keep_ref, came_ref, *refs, cuts, sent):
    by_z = [ref.reshape(2, 2, 2, *ref.shape[3:]) for ref in (keep_ref, came_ref)]
    start = 0
    for index, rows in enumerate(cuts):
        pair, bit = (by_z, 2) if index == 1 else ((keep_ref, came_ref), 1)
        own = own_bit(bit)
        halve(*pair, refs[index], 1 - own if sent else own, slice(start, start + rows))
        start += rows
    if sent:
        refs[-1][...] = jnp.zeros_like(refs[-1])


def halve_kernel(keep_ref, came_ref, *refs, bit, marked):
    outs = refs[-3:] if marked else refs[-2:]
    own = own_bit(bit)
    halve(keep_ref, came_ref, outs[1], 1 - own, slice(None))
    halve(keep_ref, came_ref, outs[0], own, slice(None))
    if marked:
        outs[2][...] = jnp.zeros_like(outs[2])


MARK = shape((8, 128), F32)


def halved(keep, came, bit, dims, after, marked=True):
    outer, inner, rows, channels = dims[0], dims[1], keep.shape[-2], keep.shape[-1]
    keep, came = (part.reshape(outer, 2, inner, rows, channels) for part in (keep, came))
    out = shape((outer, inner, rows, channels), BF16)
    return call(
        functools.partial(halve_kernel, bit=bit, marked=marked),
        [out, out] + [MARK] * marked,
        [keep, came, *after],
        [WHOLE] * 2 + [ANYWHERE] * len(after),
        moved=8 * outer * inner * rows * channels,
        name="halve",
    )


def split(keep, came):
    pairs, tall, channels = keep.shape
    cuts = [16 * (tall // 16 * part // 17) for part in (6, 5)]
    cuts.append(tall - sum(cuts))
    outs = [
        shape(((2, 2) if index == 1 else (4, 1)) + (rows, channels), BF16) for index, rows in enumerate(cuts)
    ]
    inputs = [part.reshape(4, 2, 1, *part.shape[1:]) for part in (keep, came)]
    kept, sent = (
        call(
            functools.partial(split_kernel, cuts=cuts, sent=is_sent),
            outs + [MARK] * is_sent,
            inputs,
            moved=3 * pairs * tall * channels,
            name="split",
        )
        for is_sent in (False, True)
    )
    return kept, sent[:3], sent[3]


def scatter_sum(kept, sent, before_a):
    (a_keep, b_keep, c_keep), (a_send, b_send, c_send) = kept, sent
    channels = a_keep.shape[-1]
    a_came = swapped(a_send, "lat", 2)
    b_came = swapped(b_send, "lat", 4)
    c_came = swapped(c_send, "lat", 2)
    a_keep, a_send, mark = halved(a_keep, a_came, 2, (2, 1), before_a)
    a_came = swapped(a_send, "lat", 4)
    b_keep, b_send, mark = halved(b_keep, b_came, 3, (1, 2), [mark])
    b_came = swapped(b_send, "lat", 8)
    c_keep, c_send, mark = halved(c_keep, c_came, 2, (2, 1), [mark])
    c_came = swapped(c_send, "lat", 4)
    a_keep, a_send, mark = halved(a_keep, a_came, 3, (1, 1), [mark])
    a_came = swapped(a_send, "lat", 8)
    c_keep, c_send, mark = halved(c_keep, c_came, 3, (1, 1), [mark])
    c_came = swapped(c_send, "lat", 8)
    b_keep, b_send = halved(b_keep, b_came, 1, (1, 1), [mark], False)
    b_came = swapped(b_send, "lat", 2)
    return [part.reshape(-1, channels) for part in (a_keep, a_came, b_keep, b_came, c_keep, c_came)]


def finish_kernel(*refs, atmos_factor, ocean_factor):
    parts, (atmos_ref, ocean_ref) = refs[:-2], refs[-2:]
    channels = parts[0].shape[1]
    pieces = channels // 128
    atmos_rows = atmos_ref.shape[0] // pieces
    ocean_rows = ocean_ref.shape[0] // pieces
    sums = [
        parts[index][...].astype(F32) + parts[index + 1][...].astype(F32)
        for index in range(0, len(parts), 2)
    ]
    total = jnp.concatenate(sums, axis=0)
    for piece in range(pieces):
        lanes = slice(128 * piece, 128 * (piece + 1))
        atmos_ref[pl.ds(piece, atmos_rows, pieces), :] = total[:atmos_rows, lanes] * atmos_factor
        ocean_ref[pl.ds(piece, ocean_rows, pieces), :] = (
            total[atmos_rows : atmos_rows + ocean_rows, lanes] * ocean_factor
        )


def input_grad_kernel(
    stay_ref, give_ref, near_ref, far_ref, gpad_ref, wet_ref, terms_ref, atmos_ref, ocean_ref, *refs, cols
):
    grad_ref, sent_ref = refs[-2:]
    middle = hidden_and_grad(stay_ref, give_ref)[1]
    low, high = low_and_high(near_rows(near_ref, 1, cols), far_ref[...])
    pad = jnp.concatenate([low, middle, high], axis=0)
    own = slice(cols, 3 * cols)
    convolve(pad, grad_ref, atmos_ref, ocean_ref, 0, True, cols)
    grad = gpad_ref[own, :].astype(F32) + grad_ref[...]
    grad_ref[...] = grad
    weighted = dot(terms_ref[8:16, :], grad, NT, HIGHEST)
    mixed = weighted[0:4] * wet_ref[0:1, own] + weighted[4:8] * wet_ref[1:2, own]
    sent_ref[...] = jnp.where(on_ocean(), mixed, weighted[0:4])


def next_kernel(
    stay_ref, give_ref, near_ref, far_ref, upad_ref, atmos_ref, ocean_ref,
    next_ref, mark_ref, second_ref, *, cols,
):
    middle = hidden_and_grad(stay_ref, give_ref)[0]
    low, high = low_and_high(near_rows(near_ref, 0, cols), far_ref[...])
    pad = jnp.concatenate([low, middle, high], axis=0)
    own = slice(cols, 3 * cols)
    convolve(pad, second_ref, atmos_ref, ocean_ref, 1, False, cols)
    values = (upad_ref[own, :].astype(F32) + second_ref[...]).astype(BF16)
    next_ref[0] = values[:cols]
    next_ref[1] = values[cols:]
    mark_ref[...] = jnp.zeros_like(mark_ref)


def last_kernel(grad_ref, arrived_ref, wet_ref, terms_ref, *refs, cols):
    out_ref, mark_ref = refs[-2:]
    own = slice(cols, 3 * cols)
    wet = wet_ref[0:1, own], wet_ref[1:2, own]
    arrived = jnp.where(on_ocean(), arrived_ref[...] * wet_ref[2:3, own], arrived_ref[...])
    added = spread(arrived, wet, on_ocean(), terms_ref[0:8, :])
    values = (grad_ref[...] + added).astype(BF16)
    out_ref[0] = values[:cols]
    out_ref[1] = values[cols:]
    mark_ref[...] = jnp.zeros_like(mark_ref)


def swapped(value, axis, mask):
    pairs = [(source, source ^ mask) for source in range(lax.axis_size(axis))]
    return lax.ppermute(value, axis, pairs)


def far_halo(far):
    pairs = [(i, i + 1 if i % 2 else i - 1) for i in range(1, lax.axis_size("lat") - 1)]
    return lax.ppermute(far, "lat", pairs)


def local(
    fields,
    cotangent,
    ocean_kernels,
    atmos_kernels,
    ocean_surface,
    ocean_coupling,
    atmos_flux,
    atmos_coupling,
    row_map,
    wet_mask,
):
    x, g = fields[0], cotangent[0]
    bands, cols, channels = x.shape
    narrow = channels // 2
    cells = bands * cols
    count = lax.axis_size("lat")
    is_ocean = lax.axis_index("grp") == 0
    atmos_factor = 1.0 / math.sqrt(bands * count * cols)
    ocean_factor = 1.0 / math.sqrt(bands * count * 2 * cols)
    bound = functools.partial

    blank = jnp.zeros((4, narrow), BF16)
    gap = jnp.zeros((4, channels), BF16)
    surface = ocean_surface.T
    ocean_terms = jnp.concatenate(
        [
            jnp.concatenate([surface, blank], axis=1),
            jnp.concatenate([blank, surface], axis=1),
            jnp.concatenate([ocean_coupling, blank], axis=1),
            jnp.concatenate([blank, ocean_coupling], axis=1),
        ],
        axis=0,
    )
    atmos_terms = jnp.concatenate([atmos_flux.T, gap, atmos_coupling, gap], axis=0)
    terms = jnp.where(is_ocean, ocean_terms, atmos_terms).astype(F32)

    edge = shape((2 * cols + 16, channels), BF16)
    half = shape((cells, channels), BF16)
    near, far, own_early, own = call(
        bound(pack_kernel, cols=cols),
        [edge, edge, half, shape((2 * cells + 16, channels), BF16)],
        [x, g, wet_mask],
        [IN_PLACE] * 3,
        [
            pltpu.VMEM(x.shape, BF16),
            pltpu.VMEM(x.shape, BF16),
            pltpu.VMEM(wet_mask.shape, jnp.int32),
            pltpu.SemaphoreType.DMA((3,)),
        ],
        name="pack",
        limit=PACK_VMEM,
    )
    near, far = swapped(near, "lat", 1), far_halo(far)
    other_early = swapped(own_early, "grp", 1)
    wide = -(-narrow // 128) * 128
    own, atmos_flat, ocean_flat = call(
        hold_kernel,
        [
            shape(own.shape, BF16),
            shape((18, channels, channels), BF16),
            shape((18, wide, narrow), BF16),
        ],
        [own, atmos_kernels.reshape(18, channels, channels), ocean_kernels.reshape(18, narrow, narrow)],
        [WHOLE, IN_PLACE, IN_PLACE],
        [pltpu.SemaphoreType.DMA],
        flops=PACE * 10**8,
        name="hold",
        limit=HOLD_VMEM,
    )
    pad = shape((2 * cells, channels), BF16)
    xpad, gpad, wet, edges, sent = call(
        bound(outgoing_kernel, cols=cols),
        [pad, pad, shape((8, 2 * cells), F32), half, shape((4, 2 * cells), F32)],
        [own, near, far, terms],
        name="outgoing",
    )
    arrived = swapped(sent, "grp", 1)
    other_edges = swapped(edges, "grp", 1)
    conv_cost = dict(flops=PACE * 9 * cells * channels * channels, moved=9 * channels * channels * 2)
    back = call(
        bound(back_kernel, cols=cols),
        shape((cells, channels), F32),
        [gpad, atmos_flat, ocean_flat],
        **conv_cost,
        name="back",
    )
    upad, stay, give = call(
        bound(first_kernel, cols=cols),
        [pad, half, half],
        [xpad, wet, arrived, terms, back, atmos_flat, ocean_flat],
        None,
        [pltpu.VMEM((cells, channels), F32)],
        **conv_cost,
        name="first",
    )
    late = swapped(give, "grp", 1)

    atmos_rows = 9 * channels // count
    ocean_rows = 9 * narrow // count
    chunked = count == 16 and 9 * channels % (8 * count) == 0 and ocean_rows % 2 == 0
    tall = -(-(atmos_rows + ocean_rows // 2) // 16) * 16
    spare = max(0, 2 * (tall - atmos_rows) - ocean_rows) if chunked else 0
    ocean_tall = 9 * narrow + -(-spare // 8) * 8
    sums = [shape((9 * channels, channels), F32), shape((wide // 128, ocean_tall, 128), F32)]
    row = shape((cols, channels), BF16)
    atmos_sum, ocean_sum, near, far_hidden, far_grad = call(
        bound(own_grads_kernel, cols=cols),
        [*sums, half, row, row],
        [upad, gpad, stay, give],
        **conv_cost,
        name="own_grads",
    )
    far_hidden, far_grad = far_halo(far_hidden), far_halo(far_grad)
    lefts = call(
        bound(shift_kernel, cols=cols),
        shape((3, channels, 2 * cells), BF16),
        [other_early, other_edges, sent, atmos_coupling],
        name="shift",
    )
    atmos_other, ocean_other = call(
        bound(other_grads_kernel, cols=cols),
        sums,
        [lefts, late, other_early, other_edges],
        **conv_cost,
        name="other_grads",
    )
    if chunked:
        taken = 2 * cols // (count // 2)
        sums = [atmos_sum, ocean_sum, atmos_other, ocean_other]
        send, keep = (
            call(
                bound(chunk_kernel, chunks=count, tall=tall, sent=sent),
                shape((count // 2, tall + taken * sent, channels), BF16),
                sums + [near, far_grad] * sent,
                [WHOLE] * (4 + sent) + [ANYWHERE] * sent,
                moved=2 * count * tall * channels,
                name="chunk",
            )
            for sent in (True, False)
        )
        near = swapped(send, "lat", 1)
        kept, parts, split_mark = split(keep, near)
        after_split = [split_mark]
    else:
        near = swapped(near, "lat", 1)
        after_split = []

    grad, sent_back = call(
        bound(input_grad_kernel, cols=cols),
        [shape((cells, channels), F32), shape((4, cells), F32)],
        [stay, give, near, far_grad, gpad, wet, terms, atmos_flat, ocean_flat, *after_split],
        [WHOLE] * 9 + [ANYWHERE] * len(after_split),
        **conv_cost,
        name="input_grad",
    )
    returned = swapped(sent_back, "grp", 1)
    next_field, next_mark = call(
        bound(next_kernel, cols=cols),
        [shape(x.shape, BF16), MARK],
        [stay, give, near, far_hidden, upad, atmos_flat, ocean_flat],
        None,
        [pltpu.VMEM((cells, channels), F32)],
        **conv_cost,
        name="next",
    )

    field_grad, last_mark = call(
        bound(last_kernel, cols=cols),
        [shape(x.shape, BF16), MARK],
        [grad, returned, wet, terms],
        name="last",
    )
    if chunked:
        sums = scatter_sum(kept, parts, [next_mark, last_mark])
        atmos_chunk, ocean_chunk = call(
            bound(finish_kernel, atmos_factor=atmos_factor, ocean_factor=ocean_factor),
            [
                shape((atmos_rows * channels // 128, 128), F32),
                shape((ocean_rows * narrow // 128, 128), F32),
            ],
            sums,
            name="finish",
        )
        atmos_total, ocean_total = atmos_chunk.reshape(-1), ocean_chunk.reshape(-1)
    else:
        atmos_all = jnp.where(is_ocean, atmos_other, atmos_sum)
        ocean_all = jnp.where(is_ocean, ocean_sum, ocean_other)
        atmos_total = atmos_factor * lax.psum_scatter(
            atmos_all.reshape(-1), "lat", scatter_dimension=0, tiled=True
        )
        ocean_all = jnp.concatenate([ocean_all[piece] for piece in range(wide // 128)], axis=1)
        ocean_total = ocean_factor * lax.psum_scatter(
            ocean_all[:, :narrow].reshape(-1), "lat", scatter_dimension=0, tiled=True
        )
    return (next_field[None], field_grad[None], ocean_total, atmos_total)


def solution(mesh):
    in_specs = (
        P("grp", "lat", None, None),
        P("grp", "lat", None, None),
        P(),
        P(),
        P(),
        P(),
        P(),
        P(),
        P("lat"),
        P("lat", None),
    )
    out_specs = (
        P("grp", "lat", None, None),
        P("grp", "lat", None, None),
        P(("grp", "lat")),
        P(("grp", "lat")),
    )
    return jax.shard_map(local, mesh=mesh, in_specs=in_specs, out_specs=out_specs, check_vma=False)
```

```python
import functools
import math

import jax
import jax.numpy as jnp
from jax import lax
from jax.experimental import pallas as pl
from jax.experimental.pallas import tpu as pltpu
from jax.sharding import PartitionSpec as P

HIGHEST = lax.Precision.HIGHEST
GELU_SCALE = 0.7978845608028654
GELU_CUBIC = 0.044715
F32 = jnp.float32
BF16 = jnp.bfloat16
WHOLE = pl.BlockSpec(memory_space=pltpu.VMEM)
IN_PLACE = pl.BlockSpec(memory_space=pltpu.HBM)
ANYWHERE = pl.BlockSpec(memory_space=pl.ANY)
VMEM_LIMIT = 20 * 1024 * 1024
PACE = 8
PACK_VMEM = 62 * 1024 * 1024
HOLD_VMEM = 42 * 1024 * 1024

NN = (((1,), (0,)), ((), ()))
NT = (((1,), (1,)), ((), ()))
TN = (((0,), (0,)), ((), ()))


def shape(dims, kind):
    return jax.ShapeDtypeStruct(dims, kind)


def call(kernel, outs, inputs, in_specs=None, scratch=(), flops=0, moved=0, name=None, limit=VMEM_LIMIT, out_spec=WHOLE):
    return pl.pallas_call(
        kernel,
        out_shape=outs,
        in_specs=in_specs or [WHOLE] * len(inputs),
        out_specs=jax.tree.map(lambda _: out_spec, outs),
        scratch_shapes=list(scratch),
        compiler_params=pltpu.CompilerParams(vmem_limit_bytes=limit),
        cost_estimate=pl.CostEstimate(flops=flops, bytes_accessed=moved, transcendentals=0),
        name=name,
    )(*inputs)


def on_ocean():
    return lax.axis_index("grp") == 0


def dot(left, right, dims=NN, precision=None):
    return lax.dot_general(left, right, dims, precision=precision, preferred_element_type=F32)


def moved_cells(values, axis, cols):
    count = values.shape[axis]
    place = lax.rem(lax.broadcasted_iota(jnp.int32, values.shape, axis), cols)
    before = jnp.where(place == 0, 0.0, pltpu.roll(values, 1, axis))
    after = jnp.where(place == cols - 1, 0.0, pltpu.roll(values, count - 1, axis))
    return before, after


def wet_halves(wet, cols, channels):
    source = lax.broadcasted_iota(jnp.int32, (2 * cols, 2 * cols), 0)
    target = lax.broadcasted_iota(jnp.int32, (2 * cols, 2 * cols), 1)
    wanted = 2 * lax.rem(target, cols) + jnp.where(target >= cols, 1, 0)
    chooser = (source == wanted).astype(F32).astype(BF16)
    padded = jnp.concatenate([wet.astype(F32), jnp.zeros((14, 2 * cols), F32)], axis=0)
    apart = dot(padded.astype(BF16), chooser)
    return jnp.concatenate([apart, jnp.zeros((16, channels - 2 * cols), F32)], axis=1)


def own_bit(bit):
    return lax.rem(lax.shift_right_logical(lax.axis_index("lat"), bit), 2)


def pack_kernel(
    x_any, g_any, wet_any, near_ref, far_ref, early_ref, own_ref, x_ref, g_ref, wet_ref, sems, *, cols
):
    pairs = ((wet_any, wet_ref), (x_any, x_ref), (g_any, g_ref))
    copies = [pltpu.make_async_copy(*pair, sems.at[index]) for index, pair in enumerate(pairs)]
    for copy in copies:
        copy.start()
    core = own_bit(0)
    copies[0].wait()
    wide = wet_halves(wet_ref[...], cols, x_ref.shape[2])
    other = pltpu.roll(wide, 15, 0)
    own_ref[4 * cols :, :] = wide.astype(BF16)
    far_ref[2 * cols :, :] = jnp.where(core == 0, wide, other).astype(BF16)
    near_ref[2 * cols :, :] = jnp.where(core == 0, other, wide).astype(BF16)
    copies[1].wait()
    copies[2].wait()
    for part, ref in enumerate((x_ref, g_ref)):
        far_ref[part * cols : (part + 1) * cols, :] = ref[core]
        near_ref[part * cols : (part + 1) * cols, :] = ref[1 - core]
        own_ref[2 * part * cols : (2 * part + 1) * cols, :] = ref[0]
        own_ref[(2 * part + 1) * cols : (2 * part + 2) * cols, :] = ref[1]
    for row in range(2):
        early_ref[row * cols : (row + 1) * cols, :] = jnp.where(on_ocean(), g_ref[row], x_ref[row])


def hold_kernel(own_in, atmos_any, ocean_any, own_ref, atmos_ref, ocean_ref, sem):
    narrow = ocean_ref.shape[2]
    ocean_copy = pltpu.make_async_copy(ocean_any, ocean_ref.at[:, pl.ds(0, narrow), :], sem)
    atmos_copy = pltpu.make_async_copy(atmos_any, atmos_ref, sem)

    @pl.when(on_ocean())
    def _():
        ocean_copy.start()
        gap = ocean_ref.shape[1] - narrow
        if gap:
            ocean_ref[:, narrow:, :] = jnp.zeros((ocean_ref.shape[0], gap, narrow), BF16)

    @pl.when(jnp.logical_not(on_ocean()))
    def _():
        atmos_copy.start()

    own_ref[...] = own_in[...]

    @pl.when(on_ocean())
    def _():
        ocean_copy.wait()

    @pl.when(jnp.logical_not(on_ocean()))
    def _():
        atmos_copy.wait()


def low_and_high(near, far):
    core = own_bit(0)
    return jnp.where(core == 0, far, near), jnp.where(core == 0, near, far)


def outgoing_kernel(
    own_ref, near_ref, far_ref, terms_ref, xpad_ref, gpad_ref, wet_ref, edge_ref, sent_ref, *, cols
):
    low, high = low_and_high(near_ref[...], far_ref[...])
    for part, pad_ref in enumerate((xpad_ref, gpad_ref)):
        pad_ref[0:cols, :] = low[part * cols : (part + 1) * cols]
        pad_ref[cols : 3 * cols, :] = own_ref[2 * part * cols : 2 * (part + 1) * cols, :]
        pad_ref[3 * cols : 4 * cols, :] = high[part * cols : (part + 1) * cols]
    low_wet = low[2 * cols :].astype(F32)
    high_wet = high[2 * cols :].astype(F32)
    own_wet = own_ref[4 * cols :, :].astype(F32)
    halves = []
    for start in (0, cols):
        lanes = slice(start, start + cols)
        rows = (low_wet[0:1, lanes], own_wet[0:1, lanes], own_wet[1:2, lanes], high_wet[0:1, lanes])
        halves.append(jnp.concatenate(rows, axis=1))
    first_wet, second_wet = halves
    inverse = 1.0 / jnp.maximum(first_wet + second_wet, 1.0)
    wet_ref[0:1, :] = first_wet
    wet_ref[1:2, :] = second_wet
    wet_ref[2:3, :] = inverse
    wet_ref[3:8, :] = jnp.zeros((5, 4 * cols), F32)
    xpad = xpad_ref[...]
    projected = dot(terms_ref[0:8, :].astype(BF16), xpad, NT)
    mixed = (projected[0:4] * first_wet + projected[4:8] * second_wet) * inverse
    sent_ref[...] = jnp.where(on_ocean(), mixed, projected[0:4])
    edge_ref[0:cols, :] = jnp.where(on_ocean(), gpad_ref[0:cols, :], xpad_ref[0:cols, :])
    edge_ref[cols:, :] = jnp.where(on_ocean(), gpad_ref[3 * cols :, :], xpad_ref[3 * cols :, :])


def halves_apart(values, narrow):
    wide = -(-narrow // 128) * 128
    lane = lax.broadcasted_iota(jnp.int32, values.shape, 1)
    even = jnp.where(lane < narrow, values, 0.0)
    odd = jnp.where(lane < narrow, pltpu.roll(values, narrow, 1), 0.0)
    return even[:, :wide], odd[:, :wide]


def halves_with_columns(pad, cols):
    even, odd = halves_apart(pad.astype(F32), pad.shape[1] // 2)
    odd_before = moved_cells(odd, 0, cols)[0].astype(BF16)
    even_after = moved_cells(even, 0, cols)[1].astype(BF16)
    even, odd = even.astype(BF16), odd.astype(BF16)
    return (odd_before, even, odd), (even, odd, even_after)


def with_columns(pad, cols):
    before, after = moved_cells(pad.astype(F32), 0, cols)
    return before.astype(BF16), pad, after.astype(BF16)


def convolve(pad, out_ref, atmos_ref, ocean_ref, layer, flipped, cols):
    base = 9 * layer
    channels = atmos_ref.shape[2]
    wide, narrow = ocean_ref.shape[1:]
    rows = out_ref.shape[0]

    def summed(pick):
        total = None
        for row_tap in range(3):
            part = pick(row_tap, slice(cols * row_tap, cols * row_tap + rows))
            total = part if total is None else total + part
        return total

    @pl.when(on_ocean())
    def _():
        evens, odds = halves_with_columns(pad, cols)
        if flipped:

            def pick(row_tap, span):
                part = None
                for col_tap in range(3):
                    left = jnp.concatenate([evens[col_tap][span], odds[col_tap][span]], axis=0)
                    kernel = ocean_ref[base + 8 - (3 * row_tap + col_tap), 0:narrow, :]
                    piece = dot(left[:, :narrow], kernel, NT)
                    part = piece if part is None else part + piece
                return part

        else:
            even, odd = jnp.concatenate(evens, axis=1), jnp.concatenate(odds, axis=1)

            def pick(row_tap, span):
                first = base + 3 * row_tap
                kernel = ocean_ref[first : first + 3].reshape(3 * wide, narrow)
                return dot(jnp.concatenate([even[span], odd[span]], axis=0), kernel)

        total = summed(pick)
        out_ref[...] = jnp.concatenate([total[:rows], total[rows:]], axis=1)

    @pl.when(jnp.logical_not(on_ocean()))
    def _():
        taps = with_columns(pad, cols)
        if flipped:

            def pick(row_tap, span):
                part = None
                for col_tap in range(3):
                    piece = dot(taps[col_tap][span], atmos_ref[base + 8 - (3 * row_tap + col_tap)], NT)
                    part = piece if part is None else part + piece
                return part

        else:
            joined = jnp.concatenate(taps, axis=1)

            def pick(row_tap, span):
                first = base + 3 * row_tap
                return dot(joined[span], atmos_ref[first : first + 3].reshape(3 * channels, channels))

        out_ref[...] = summed(pick)


def back_kernel(gpad_ref, atmos_ref, ocean_ref, out_ref, *, cols):
    convolve(gpad_ref[...], out_ref, atmos_ref, ocean_ref, 1, True, cols)


def spread(arrived, wet, mixing, terms):
    first_wet, second_wet = wet
    both = jnp.concatenate([arrived * first_wet, arrived * second_wet], axis=0)
    alone = jnp.concatenate([arrived, jnp.zeros_like(arrived)], axis=0)
    return dot(jnp.where(mixing, both, alone), terms, TN, HIGHEST)


def first_kernel(
    xpad_ref, wet_ref, arrived_ref, terms_ref, back_ref, atmos_ref, ocean_ref,
    u_ref, stay_ref, give_ref, first_ref, *, cols,
):
    wet = wet_ref[0:1, :], wet_ref[1:2, :]
    coupled = spread(arrived_ref[...], wet, on_ocean(), terms_ref[8:16, :])
    u = (xpad_ref[...].astype(F32) + coupled).astype(BF16)
    u_ref[...] = u
    convolve(u, first_ref, atmos_ref, ocean_ref, 0, False, cols)
    first = first_ref[...]
    tangent = jnp.tanh(GELU_SCALE * (first + GELU_CUBIC * first * first * first))
    hidden = (0.5 * first * (1.0 + tangent)).astype(BF16)
    slope = 0.5 * (1.0 + tangent) + 0.5 * first * (1.0 - tangent * tangent) * GELU_SCALE * (
        1.0 + 3.0 * GELU_CUBIC * first * first
    )
    first_grad = (back_ref[...] * slope).astype(BF16)
    stay_ref[...] = jnp.where(on_ocean(), first_grad, hidden)
    give_ref[...] = jnp.where(on_ocean(), hidden, first_grad)


def whole_pad(early_ref, edge_ref, cols):
    parts = [edge_ref[0:cols, :], early_ref[...], edge_ref[cols:, :]]
    return jnp.concatenate(parts, axis=0).astype(F32)


def grad_atmos(pad, own, cols, store):
    rows = own.shape[0]
    left = own.T.astype(BF16)
    before, after = moved_cells(pad, 0, cols)
    rights = [part.astype(BF16) for part in (after, pad, before)]
    for tap in range(9):
        start = cols * (2 - tap // 3)
        store(tap, dot(left, rights[tap % 3][start : start + rows]))


def grad_ocean(pad, own, pad_is_input, cols, store):
    rows, channels = own.shape
    narrow = channels // 2

    if pad_is_input:
        middle = pad.T
        before, after = moved_cells(middle, 1, cols)
        even, odd = middle[:narrow].astype(BF16), middle[narrow:].astype(BF16)
        pairs = (
            (before[narrow:].astype(BF16), even),
            (even, odd),
            (odd, after[:narrow].astype(BF16)),
        )
        right = jnp.concatenate(halves_apart(own, narrow), axis=0).astype(BF16)
        for tap in range(9):
            start = cols * (tap // 3)
            pieces = [part[:, start : start + rows] for part in pairs[tap % 3]]
            store(tap, dot(jnp.concatenate(pieces, axis=1), right))
    else:
        turned = own.T.astype(BF16)
        left = jnp.concatenate([turned[:narrow], turned[narrow:]], axis=1)
        even, odd = halves_apart(pad, narrow)
        odd_before = moved_cells(odd, 0, cols)[0].astype(BF16)
        even_after = moved_cells(even, 0, cols)[1].astype(BF16)
        even, odd = even.astype(BF16), odd.astype(BF16)
        pairs = ((odd, even_after), (even, odd), (odd_before, even))
        for tap in range(9):
            start = cols * (2 - tap // 3)
            pieces = [part[start : start + rows] for part in pairs[tap % 3]]
            store(tap, dot(left, jnp.concatenate(pieces, axis=0)))


def store_into(out_ref):
    def store(tap, value):
        if len(out_ref.shape) == 2:
            rows = value.shape[0]
            out_ref[rows * tap : rows * (tap + 1), :] = value
        else:
            rows = value.shape[0]
            for piece in range(out_ref.shape[0]):
                lanes = slice(128 * piece, 128 * (piece + 1))
                out_ref[piece, rows * tap : rows * (tap + 1), :] = value[:, lanes]

    return store


def near_rows(near_ref, part, cols):
    if len(near_ref.shape) == 2:
        return near_ref[part * cols : (part + 1) * cols, :]
    count, tall = near_ref.shape[0] // 2, near_ref.shape[1]
    taken = cols // count
    pieces = [near_ref[index, tall - taken :, :] for index in range(part * count, (part + 1) * count)]
    return jnp.concatenate(pieces, axis=0)


def hidden_and_grad(stay_ref, give_ref):
    stay, give = stay_ref[...], give_ref[...]
    return jnp.where(on_ocean(), give, stay), jnp.where(on_ocean(), stay, give)


def shifted_inputs(pad, cols):
    middle = pad.T
    before, after = moved_cells(middle, 1, cols)
    return [part.astype(BF16) for part in (before, middle, after)]


def own_grads_kernel(
    upad_ref, gpad_ref, stay_ref, give_ref, atmos_out, ocean_out, near_ref, far_hidden, far_grad, *, cols
):
    stay = stay_ref[...].astype(F32)
    hidden, first_grad = hidden_and_grad(stay_ref, give_ref)
    core = own_bit(0)
    for part, values in enumerate((hidden, first_grad)):
        target = slice(part * cols, (part + 1) * cols)
        (far_hidden, far_grad)[part][...] = jnp.where(core == 0, values[:cols], values[cols:])
        near_ref[target, :] = jnp.where(core == 0, values[cols:], values[:cols])

    @pl.when(on_ocean())
    def _():
        grad_ocean(upad_ref[...].astype(F32), stay, True, cols, store_into(ocean_out))

    @pl.when(jnp.logical_not(on_ocean()))
    def _():
        grad_atmos(gpad_ref[...].astype(F32), stay, cols, store_into(atmos_out))


def shift_kernel(early_ref, edge_ref, sent_ref, coupling_ref, left_ref, *, cols):
    @pl.when(on_ocean())
    def _():
        added = dot(sent_ref[...], coupling_ref[...].astype(F32), TN, HIGHEST)
        other = (whole_pad(early_ref, edge_ref, cols) + added).astype(BF16).astype(F32)
        for tap, left in enumerate(shifted_inputs(other, cols)):
            left_ref[tap] = left


def other_grads_kernel(left_ref, late_ref, early_ref, edge_ref, atmos_out, ocean_out, *, cols):
    rows = late_ref.shape[0]

    @pl.when(on_ocean())
    def _():
        store = store_into(atmos_out)
        for tap in range(9):
            start = cols * (tap // 3)
            store(tap, dot(left_ref[tap % 3, :, start : start + rows], late_ref[...]))

    @pl.when(jnp.logical_not(on_ocean()))
    def _():
        late = late_ref[...].astype(F32)
        grad_ocean(whole_pad(early_ref, edge_ref, cols), late, False, cols, store_into(ocean_out))


def chunk_rows(out_ref, side, tall, atmos_all, ocean_all, chunks):
    channels = out_ref.shape[2]
    pieces = ocean_all.shape[0]
    atmos_rows = atmos_all.shape[0] // chunks
    ocean_rows = atmos_rows // 2
    taken = tall - atmos_rows
    blank = jnp.zeros((taken, channels - 128 * pieces), F32)
    for pair in range(chunks // 2):
        start = pl.multiple_of(atmos_rows * (2 * pair + side), 8)
        upper = atmos_all[pl.ds(start, atmos_rows), :]
        start = ocean_rows * (2 * pair + side)
        halves = []
        for odd in range(2):
            parts = [ocean_all.at[piece][pl.ds(start + odd, taken, 2), :] for piece in range(pieces)]
            halves.append(jnp.concatenate(parts + [blank], axis=1))
        lower = halves[0] + pltpu.roll(halves[1], channels // 2, 1)
        out_ref[pair, 0:tall, :] = jnp.concatenate([upper, lower], axis=0).astype(BF16)


def chunk_kernel(atmos_own, ocean_own, atmos_other, ocean_other, *refs, chunks, tall, sent):
    out_ref = refs[-1]
    core = own_bit(0)
    side = 1 - core if sent else core
    if sent:
        near_ref = refs[0]
        taken = out_ref.shape[1] - tall
        for pair in range(chunks // 2):
            out_ref[pair, tall:, :] = near_ref[pair * taken : (pair + 1) * taken, :]

    @pl.when(on_ocean())
    def _():
        chunk_rows(out_ref, side, tall, atmos_other, ocean_own, chunks)

    @pl.when(jnp.logical_not(on_ocean()))
    def _():
        chunk_rows(out_ref, side, tall, atmos_own, ocean_other, chunks)


def halve(keep_ref, came_ref, out_ref, side, rows):
    for outer in range(keep_ref.shape[0]):
        for inner in range(keep_ref.shape[2]):
            total = keep_ref[outer, side, inner, rows, :].astype(F32)
            total = total + came_ref[outer, side, inner, rows, :].astype(F32)
            out_ref[outer, inner] = total.astype(BF16)


def split_kernel(keep_ref, came_ref, *refs, cuts, sent):
    by_z = [ref.reshape(2, 2, 2, *ref.shape[3:]) for ref in (keep_ref, came_ref)]
    start = 0
    for index, rows in enumerate(cuts):
        pair, bit = (by_z, 2) if index == 1 else ((keep_ref, came_ref), 1)
        own = own_bit(bit)
        halve(*pair, refs[index], 1 - own if sent else own, slice(start, start + rows))
        start += rows
    if sent:
        refs[-1][...] = jnp.zeros_like(refs[-1])


def halve_kernel(keep_ref, came_ref, *refs, bit, marked):
    outs = refs[-3:] if marked else refs[-2:]
    own = own_bit(bit)
    halve(keep_ref, came_ref, outs[1], 1 - own, slice(None))
    halve(keep_ref, came_ref, outs[0], own, slice(None))
    if marked:
        outs[2][...] = jnp.zeros_like(outs[2])


MARK = shape((8, 128), F32)


def halved(keep, came, bit, dims, after, marked=True):
    outer, inner, rows, channels = dims[0], dims[1], keep.shape[-2], keep.shape[-1]
    keep, came = (part.reshape(outer, 2, inner, rows, channels) for part in (keep, came))
    out = shape((outer, inner, rows, channels), BF16)
    return call(
        functools.partial(halve_kernel, bit=bit, marked=marked),
        [out, out] + [MARK] * marked,
        [keep, came, *after],
        [WHOLE] * 2 + [ANYWHERE] * len(after),
        moved=8 * outer * inner * rows * channels,
        name="halve",
    )


def split(keep, came):
    pairs, tall, channels = keep.shape
    cuts = [16 * (tall // 16 * part // 17) for part in (6, 6)]
    cuts.append(tall - sum(cuts))
    outs = [
        shape(((2, 2) if index == 1 else (4, 1)) + (rows, channels), BF16) for index, rows in enumerate(cuts)
    ]
    inputs = [part.reshape(4, 2, 1, *part.shape[1:]) for part in (keep, came)]
    kept, sent = (
        call(
            functools.partial(split_kernel, cuts=cuts, sent=is_sent),
            outs + [MARK] * is_sent,
            inputs,
            moved=3 * pairs * tall * channels,
            name="split",
        )
        for is_sent in (False, True)
    )
    return kept, sent[:3], sent[3]


def scatter_sum(kept, sent, before_a):
    (a_keep, b_keep, c_keep), (a_send, b_send, c_send) = kept, sent
    channels = a_keep.shape[-1]
    a_came = swapped(a_send, "lat", 2)
    b_came = swapped(b_send, "lat", 4)
    c_came = swapped(c_send, "lat", 2)
    a_keep, a_send, mark = halved(a_keep, a_came, 2, (2, 1), before_a)
    a_came = swapped(a_send, "lat", 4)
    b_keep, b_send, mark = halved(b_keep, b_came, 3, (1, 2), [mark])
    b_came = swapped(b_send, "lat", 8)
    c_keep, c_send, mark = halved(c_keep, c_came, 2, (2, 1), [mark])
    c_came = swapped(c_send, "lat", 4)
    a_keep, a_send, mark = halved(a_keep, a_came, 3, (1, 1), [mark])
    a_came = swapped(a_send, "lat", 8)
    c_keep, c_send, mark = halved(c_keep, c_came, 3, (1, 1), [mark])
    c_came = swapped(c_send, "lat", 8)
    b_keep, b_send = halved(b_keep, b_came, 1, (1, 1), [mark], False)
    b_came = swapped(b_send, "lat", 2)
    return [part.reshape(-1, channels) for part in (a_keep, a_came, b_keep, b_came, c_keep, c_came)]


def finish_kernel(*refs, atmos_factor, ocean_factor):
    parts, (atmos_ref, ocean_ref) = refs[:-2], refs[-2:]
    channels = parts[0].shape[1]
    pieces = channels // 128
    atmos_rows = atmos_ref.shape[0] // pieces
    ocean_rows = ocean_ref.shape[0] // pieces
    sums = [
        parts[index][...].astype(F32) + parts[index + 1][...].astype(F32)
        for index in range(0, len(parts), 2)
    ]
    total = jnp.concatenate(sums, axis=0)
    for piece in range(pieces):
        lanes = slice(128 * piece, 128 * (piece + 1))
        atmos_ref[pl.ds(piece, atmos_rows, pieces), :] = total[:atmos_rows, lanes] * atmos_factor
        ocean_ref[pl.ds(piece, ocean_rows, pieces), :] = (
            total[atmos_rows : atmos_rows + ocean_rows, lanes] * ocean_factor
        )


def input_grad_kernel(
    stay_ref, give_ref, near_ref, far_ref, gpad_ref, wet_ref, terms_ref, atmos_ref, ocean_ref, *refs, cols
):
    grad_ref, sent_ref = refs[-2:]
    middle = hidden_and_grad(stay_ref, give_ref)[1]
    low, high = low_and_high(near_rows(near_ref, 1, cols), far_ref[...])
    pad = jnp.concatenate([low, middle, high], axis=0)
    own = slice(cols, 3 * cols)
    convolve(pad, grad_ref, atmos_ref, ocean_ref, 0, True, cols)
    grad = gpad_ref[own, :].astype(F32) + grad_ref[...]
    grad_ref[...] = grad
    weighted = dot(terms_ref[8:16, :], grad, NT, HIGHEST)
    mixed = weighted[0:4] * wet_ref[0:1, own] + weighted[4:8] * wet_ref[1:2, own]
    sent_ref[...] = jnp.where(on_ocean(), mixed, weighted[0:4])


def next_kernel(
    stay_ref, give_ref, near_ref, far_ref, upad_ref, atmos_ref, ocean_ref,
    next_ref, mark_ref, second_ref, *, cols,
):
    middle = hidden_and_grad(stay_ref, give_ref)[0]
    low, high = low_and_high(near_rows(near_ref, 0, cols), far_ref[...])
    pad = jnp.concatenate([low, middle, high], axis=0)
    own = slice(cols, 3 * cols)
    convolve(pad, second_ref, atmos_ref, ocean_ref, 1, False, cols)
    values = (upad_ref[own, :].astype(F32) + second_ref[...]).astype(BF16)
    next_ref[0] = values[:cols]
    next_ref[1] = values[cols:]
    mark_ref[...] = jnp.zeros_like(mark_ref)


def last_kernel(grad_ref, arrived_ref, wet_ref, terms_ref, *refs, cols):
    out_ref, mark_ref = refs[-2:]
    own = slice(cols, 3 * cols)
    wet = wet_ref[0:1, own], wet_ref[1:2, own]
    arrived = jnp.where(on_ocean(), arrived_ref[...] * wet_ref[2:3, own], arrived_ref[...])
    added = spread(arrived, wet, on_ocean(), terms_ref[0:8, :])
    values = (grad_ref[...] + added).astype(BF16)
    out_ref[0] = values[:cols]
    out_ref[1] = values[cols:]
    mark_ref[...] = jnp.zeros_like(mark_ref)


def swapped(value, axis, mask):
    pairs = [(source, source ^ mask) for source in range(lax.axis_size(axis))]
    return lax.ppermute(value, axis, pairs)


def far_halo(far):
    pairs = [(i, i + 1 if i % 2 else i - 1) for i in range(1, lax.axis_size("lat") - 1)]
    return lax.ppermute(far, "lat", pairs)


def local(
    fields,
    cotangent,
    ocean_kernels,
    atmos_kernels,
    ocean_surface,
    ocean_coupling,
    atmos_flux,
    atmos_coupling,
    row_map,
    wet_mask,
):
    x, g = fields[0], cotangent[0]
    bands, cols, channels = x.shape
    narrow = channels // 2
    cells = bands * cols
    count = lax.axis_size("lat")
    is_ocean = lax.axis_index("grp") == 0
    atmos_factor = 1.0 / math.sqrt(bands * count * cols)
    ocean_factor = 1.0 / math.sqrt(bands * count * 2 * cols)
    bound = functools.partial

    blank = jnp.zeros((4, narrow), BF16)
    gap = jnp.zeros((4, channels), BF16)
    surface = ocean_surface.T
    ocean_terms = jnp.concatenate(
        [
            jnp.concatenate([surface, blank], axis=1),
            jnp.concatenate([blank, surface], axis=1),
            jnp.concatenate([ocean_coupling, blank], axis=1),
            jnp.concatenate([blank, ocean_coupling], axis=1),
        ],
        axis=0,
    )
    atmos_terms = jnp.concatenate([atmos_flux.T, gap, atmos_coupling, gap], axis=0)
    terms = jnp.where(is_ocean, ocean_terms, atmos_terms).astype(F32)

    edge = shape((2 * cols + 16, channels), BF16)
    half = shape((cells, channels), BF16)
    near, far, own_early, own = call(
        bound(pack_kernel, cols=cols),
        [edge, edge, half, shape((2 * cells + 16, channels), BF16)],
        [x, g, wet_mask],
        [IN_PLACE] * 3,
        [
            pltpu.VMEM(x.shape, BF16),
            pltpu.VMEM(x.shape, BF16),
            pltpu.VMEM(wet_mask.shape, jnp.int32),
            pltpu.SemaphoreType.DMA((3,)),
        ],
        name="pack",
        limit=PACK_VMEM,
    )
    near, far = swapped(near, "lat", 1), far_halo(far)
    other_early = swapped(own_early, "grp", 1)
    wide = -(-narrow // 128) * 128
    own, atmos_flat, ocean_flat = call(
        hold_kernel,
        [
            shape(own.shape, BF16),
            shape((18, channels, channels), BF16),
            shape((18, wide, narrow), BF16),
        ],
        [own, atmos_kernels.reshape(18, channels, channels), ocean_kernels.reshape(18, narrow, narrow)],
        [WHOLE, IN_PLACE, IN_PLACE],
        [pltpu.SemaphoreType.DMA],
        flops=PACE * 10**8,
        name="hold",
        limit=HOLD_VMEM,
    )
    pad = shape((2 * cells, channels), BF16)
    xpad, gpad, wet, edges, sent = call(
        bound(outgoing_kernel, cols=cols),
        [pad, pad, shape((8, 2 * cells), F32), half, shape((4, 2 * cells), F32)],
        [own, near, far, terms],
        name="outgoing",
    )
    arrived = swapped(sent, "grp", 1)
    other_edges = swapped(edges, "grp", 1)
    conv_cost = dict(flops=PACE * 9 * cells * channels * channels, moved=9 * channels * channels * 2)
    back = call(
        bound(back_kernel, cols=cols),
        shape((cells, channels), F32),
        [gpad, atmos_flat, ocean_flat],
        **conv_cost,
        name="back",
    )
    upad, stay, give = call(
        bound(first_kernel, cols=cols),
        [pad, half, half],
        [xpad, wet, arrived, terms, back, atmos_flat, ocean_flat],
        None,
        [pltpu.VMEM((cells, channels), F32)],
        **conv_cost,
        name="first",
    )
    late = swapped(give, "grp", 1)

    atmos_rows = 9 * channels // count
    ocean_rows = 9 * narrow // count
    chunked = count == 16 and 9 * channels % (8 * count) == 0 and ocean_rows % 2 == 0
    tall = -(-(atmos_rows + ocean_rows // 2) // 16) * 16
    spare = max(0, 2 * (tall - atmos_rows) - ocean_rows) if chunked else 0
    ocean_tall = 9 * narrow + -(-spare // 8) * 8
    sums = [shape((9 * channels, channels), F32), shape((wide // 128, ocean_tall, 128), F32)]
    row = shape((cols, channels), BF16)
    atmos_sum, ocean_sum, near, far_hidden, far_grad = call(
        bound(own_grads_kernel, cols=cols),
        [*sums, half, row, row],
        [upad, gpad, stay, give],
        **conv_cost,
        name="own_grads",
    )
    far_hidden, far_grad = far_halo(far_hidden), far_halo(far_grad)
    lefts = call(
        bound(shift_kernel, cols=cols),
        shape((3, channels, 2 * cells), BF16),
        [other_early, other_edges, sent, atmos_coupling],
        name="shift",
    )
    atmos_other, ocean_other = call(
        bound(other_grads_kernel, cols=cols),
        sums,
        [lefts, late, other_early, other_edges],
        **conv_cost,
        name="other_grads",
    )
    if chunked:
        taken = 2 * cols // (count // 2)
        sums = [atmos_sum, ocean_sum, atmos_other, ocean_other]
        send, keep = (
            call(
                bound(chunk_kernel, chunks=count, tall=tall, sent=sent),
                shape((count // 2, tall + taken * sent, channels), BF16),
                sums + [near, far_grad] * sent,
                [WHOLE] * (4 + sent) + [ANYWHERE] * sent,
                moved=2 * count * tall * channels,
                name="chunk",
            )
            for sent in (True, False)
        )
        near = swapped(send, "lat", 1)
        kept, parts, split_mark = split(keep, near)
        after_split = [split_mark]
    else:
        near = swapped(near, "lat", 1)
        after_split = []

    grad, sent_back = call(
        bound(input_grad_kernel, cols=cols),
        [shape((cells, channels), F32), shape((4, cells), F32)],
        [stay, give, near, far_grad, gpad, wet, terms, atmos_flat, ocean_flat, *after_split],
        [WHOLE] * 9 + [ANYWHERE] * len(after_split),
        **conv_cost,
        name="input_grad",
    )
    returned = swapped(sent_back, "grp", 1)
    next_field, next_mark = call(
        bound(next_kernel, cols=cols),
        [shape(x.shape, BF16), MARK],
        [stay, give, near, far_hidden, upad, atmos_flat, ocean_flat],
        None,
        [pltpu.VMEM((cells, channels), F32)],
        **conv_cost,
        name="next",
    )

    field_grad, last_mark = call(
        bound(last_kernel, cols=cols),
        [shape(x.shape, BF16), MARK],
        [grad, returned, wet, terms],
        name="last",
    )
    if chunked:
        sums = scatter_sum(kept, parts, [next_mark, last_mark])
        atmos_chunk, ocean_chunk = call(
            bound(finish_kernel, atmos_factor=atmos_factor, ocean_factor=ocean_factor),
            [
                shape((atmos_rows * channels // 128, 128), F32),
                shape((ocean_rows * narrow // 128, 128), F32),
            ],
            sums,
            name="finish",
        )
        atmos_total, ocean_total = atmos_chunk.reshape(-1), ocean_chunk.reshape(-1)
    else:
        atmos_all = jnp.where(is_ocean, atmos_other, atmos_sum)
        ocean_all = jnp.where(is_ocean, ocean_sum, ocean_other)
        atmos_total = atmos_factor * lax.psum_scatter(
            atmos_all.reshape(-1), "lat", scatter_dimension=0, tiled=True
        )
        ocean_all = jnp.concatenate([ocean_all[piece] for piece in range(wide // 128)], axis=1)
        ocean_total = ocean_factor * lax.psum_scatter(
            ocean_all[:, :narrow].reshape(-1), "lat", scatter_dimension=0, tiled=True
        )
    return (next_field[None], field_grad[None], ocean_total, atmos_total)


def solution(mesh):
    in_specs = (
        P("grp", "lat", None, None),
        P("grp", "lat", None, None),
        P(),
        P(),
        P(),
        P(),
        P(),
        P(),
        P("lat"),
        P("lat", None),
    )
    out_specs = (
        P("grp", "lat", None, None),
        P("grp", "lat", None, None),
        P(("grp", "lat")),
        P(("grp", "lat")),
    )
    return jax.shard_map(local, mesh=mesh, in_specs=in_specs, out_specs=out_specs, check_vma=False)
```
